32 devices in a mesh: blk: 16 (over z, x, core), ulysses: 2 (over y).
Axes of the slice: x: 2, y: 2, z: 4, core: 2. Of those that a mesh axis runs over, the one named last changes fastest.
Arguments:
- layer_input: bfloat16 [4096, 1536], P(('blk', 'ulysses'))
- grad_output: bfloat16 [4096, 1536], P(('blk', 'ulysses')), may hold values from -6 to 6
- gain_attn: bfloat16 [1536], P(('blk', 'ulysses')), may hold values from 0.5 to 1.5
- gain_moe: bfloat16 [1536], P(('blk', 'ulysses')), may hold values from 0.5 to 1.5
- w_query: bfloat16 [1536, 1536], P(('blk', 'ulysses')), may hold values from -0.15625 to 0.15625
- w_keyval: bfloat16 [1536, 512], P(('blk', 'ulysses')), may hold values from -0.15625 to 0.15625
- w_out: bfloat16 [1536, 1536], P(('blk', 'ulysses')), may hold values from -2.5 to 2.5
- w_gate: bfloat16 [1536, 6144], P('ulysses', 'blk'), may hold values from -0.15625 to 0.15625
- w_up: bfloat16 [1536, 6144], P('ulysses', 'blk'), may hold values from -0.15625 to 0.15625
- w_down: bfloat16 [1536, 6144], P('ulysses', 'blk'), may hold values from -0.21875 to 0.21875
- gate_weights: float32 [4096, 4], P(('blk', 'ulysses')), may hold values from 0.15 to 0.6
- expert_ids: int32 [4096, 4], P(('blk', 'ulysses')), may hold values from 0 to 7, all different within a row; in each aligned block of 128 rows (0 to 127, 128 to 255, ...) at most 128 rows name the same one
- doc_starts: int32 [8], replicated, may hold values from 0 to 4095, as said below
Outputs:
- layer_output: bfloat16 [4096, 1536], P(('blk', 'ulysses'))
- grad_input: float32 [4096, 1536], P(('blk', 'ulysses'))
- grad_gain_attn: float32 [1536], P(('blk', 'ulysses'))
- grad_gain_moe: float32 [1536], P(('blk', 'ulysses'))
- grad_query: float32 [1536, 1536], P('blk', 'ulysses')
- grad_keyval: float32 [1536, 512], P(('blk', 'ulysses'))
- grad_outproj: float32 [1536, 1536], P('blk', 'ulysses')
- grad_gate: float32 [1536, 6144], P('ulysses', 'blk')
- grad_up: float32 [1536, 6144], P('ulysses', 'blk')
- grad_down: float32 [1536, 6144], P('ulysses', 'blk')
- branch_rms: float32 [3], replicated
The draws below stay inside these ranges and needn't reach their ends.
Inputs may be any that keep to these rules, and one draw needn't show every extreme that they name: `expert_ids`: in the rows of one device each expert is named at most 128 times. `doc_starts`: strictly increasing, the first is 0. No document (from its start to the next start, or to the end of the stream) has more than min(8192, 4082) tokens, and one has exactly that many.
All inputs are finite; a program needn't handle non-finite values.
Results may differ from the reference program's by a relative error of at most 0.015.
Values may be sent and summed in bfloat16 or wider, within the bound.
A program may use at most 192 MiB of HBM per device.

```python
import math
import jax
import jax.numpy as jnp
import numpy as np
from jax import lax

D = 1536
HEADS = 12
KV_HEADS = 2
HEAD_DIM = 128
FF = 768
TOP = 4
TOK_DEV = 128
MAX_DOC = 8192
EXPERTS = 8
HQ = 1536
TOKENS = 4096
DOCS = 8
CAP = 128
N_ULYSSES = 2


def draw_layer_input(key, part):
    key = jax.random.fold_in(key, 11)
    ramp = 1.0 + 2.0 * jnp.arange(TOKENS, dtype=jnp.float32)[:, None] / TOKENS
    noise = jnp.clip(jax.random.normal(key, (TOKENS, D), jnp.float32), -5.0, 5.0)
    return (noise * ramp).astype(jnp.bfloat16)


def draw_doc_starts(key, part):
    key = jax.random.fold_in(key, 23)
    longest = min(MAX_DOC, TOKENS - 14)
    rest = TOKENS - longest
    base = rest // (DOCS - 1)
    shifts = jax.random.randint(jax.random.fold_in(key, 1), (DOCS - 2,), 0, base // 2 + 1)
    edges = jnp.concatenate([jnp.zeros((1,), jnp.int32), shifts.astype(jnp.int32), jnp.zeros((1,), jnp.int32)])
    others = base + edges[1:] - edges[:-1]
    others = others.at[0].add(rest - base * (DOCS - 1))
    place = jax.random.randint(jax.random.fold_in(key, 2), (), 0, DOCS).astype(jnp.int32)
    index = jnp.arange(DOCS, dtype=jnp.int32)
    source = jnp.clip(index - (index > place).astype(jnp.int32), 0, DOCS - 2)
    lengths = jnp.where(index == place, longest, others[source]).astype(jnp.int32)
    ends = jnp.cumsum(lengths).astype(jnp.int32)
    return jnp.concatenate([jnp.zeros((1,), jnp.int32), ends[:-1]])


def shard_levels(own_key, extent, pieces, low, top_value):
    def one(dim, parts):
        draws = jax.random.uniform(jax.random.fold_in(jax.random.fold_in(own_key, 6), dim), (parts,), jnp.float32, low / len(pieces), top_value / len(pieces))
        return jnp.repeat(jnp.exp(draws), extent[dim] // parts).reshape((-1,) + (1,) * (len(extent) - dim - 1))

    gain = one(*pieces[0])
    for cut in pieces[1:]:
        gain = gain * one(*cut)
    return gain


def deal_out(own_key, own, number, rows, amount, top, bound, slope):
    order = jax.random.permutation(own_key, amount)
    heavy_load, ordinary = shares(amount, rows * top, bound, slope, True), shares(amount, rows * top, bound, slope, False)
    places = jnp.arange(amount)

    def named(tallies, offset_by):
        used = int((tallies > 0).sum())
        fixed = max(1, used // 4)
        moved = fixed + (places - fixed + offset_by * (used - fixed)) % max(1, amount - fixed)
        return jnp.zeros((amount,), jnp.int32).at[order[jnp.where(places < fixed, places, moved)]].set(jnp.asarray(tallies, jnp.int32))

    tallies = jnp.where(number % 4 == 0, named(heavy_load, number // 4), named(ordinary, number - number // 4 - 1))
    mixed = jax.random.permutation(jax.random.fold_in(own, 3), amount)
    source_of, taker = mixed[0:amount // 2 * 2:2], mixed[1:amount // 2 * 2:2]
    margin = jnp.minimum(tallies[source_of] - 1, bound - tallies[taker]) // 2
    margin = jnp.where((source_of == order[0]) | (taker == order[0]) | (tallies[taker] == 0), 0, jnp.maximum(margin, 0))
    moved = jax.random.randint(jax.random.fold_in(own, 4), (amount // 2,), 0, 1 << 20) % (margin + 1)
    tallies = tallies.at[source_of].add(-moved).at[taker].add(moved)
    items = jnp.searchsorted(jnp.cumsum(tallies), jnp.arange(rows * top), side="right").astype(jnp.int32)
    table = items.reshape(top, rows).T
    table = table[jax.random.permutation(jax.random.fold_in(own, 1), rows)]
    offset_by = jax.random.randint(jax.random.fold_in(own, 2), (rows, 1), 0, top)
    return jnp.take_along_axis(table, (jnp.arange(top)[None, :] + offset_by) % top, axis=1)


def shares(amount, total, bound, skew, full):
    weights = [(1 << 20) // math.isqrt(standing ** skew) + 1 for standing in range(1, amount + 1)]
    largest = bound if full else min(bound, max(-(-total // amount), total * weights[0] // sum(weights)))
    least = 1 if total - largest >= amount - 1 else 0
    holding, spare = [largest] + [least] * (amount - 1), total - largest - least * (amount - 1)
    while spare > 0:
        movable = [i for i in range(1, amount) if holding[i] < largest] or [i for i in range(1, amount) if holding[i] < bound]
        whole, budget = sum([weights[i] for i in movable]), spare
        for i in movable:
            addition = min(bound - holding[i], max(1, budget * weights[i] // whole), spare)
            holding[i] = holding[i] + addition
            spare = spare - addition
    return np.array(holding)


def centred(own_key, dims, deviation, bound, shards=(), held_as=jnp.bfloat16):
    level = shard_levels(own_key, dims, shards, -0.22, 0.18) if shards else 1.0
    drawn = jax.random.normal(own_key, dims, jnp.float32) * deviation * level
    return jnp.minimum(jnp.maximum(drawn, -bound), bound).astype(held_as)


def setup_inputs(seed: int = 0) -> dict:
    streams_of = jax.random.split(jax.random.key(seed), 14)
    layer_input = draw_layer_input(jax.random.fold_in(streams_of[13], 71), 0)
    grad_output = centred(streams_of[1], (TOKENS, D), 1.0, 6.0, ((0, 32),))
    gain_attn = jnp.clip(1.0 + 0.1 * jax.random.normal(streams_of[2], (D,), jnp.float32), 0.5, 1.5).astype(jnp.bfloat16)
    gain_moe = jnp.clip(1.0 + 0.1 * jax.random.normal(streams_of[3], (D,), jnp.float32), 0.5, 1.5).astype(jnp.bfloat16)
    w_query = centred(streams_of[4], (D, HQ), D ** -0.5, 0.15625, ((0, 32),))
    w_keyval = centred(streams_of[5], (D, 2 * KV_HEADS * HEAD_DIM), D ** -0.5, 0.15625, ((0, 32),))
    w_out = centred(streams_of[6], (D, HQ), (max(1, HQ // 256)) ** -0.5, 2.5, ((0, 32),))
    w_gate = centred(streams_of[7], (D, EXPERTS * FF), D ** -0.5, 0.15625, ((0, 2), (1, 16)))
    w_up = centred(streams_of[8], (D, EXPERTS * FF), D ** -0.5, 0.15625, ((0, 2), (1, 16)))
    w_down = centred(streams_of[9], (D, EXPERTS * FF), FF ** -0.5, 0.21875, ((0, 2), (1, 16)))
    gate_weights = jnp.clip(jnp.exp(math.log(0.6) - 1.3862944 * jax.random.uniform(streams_of[10], (TOKENS, TOP), jnp.float32) ** shard_levels(streams_of[10], (TOKENS, TOP), ((0, 32),), -0.2, 0.2)), 0.15, 0.6)
    expert_ids_keys = jax.random.split(jax.random.fold_in(streams_of[11], 1), TOKENS // TOK_DEV)
    expert_ids_turns = jax.random.permutation(jax.random.fold_in(streams_of[11], 3), TOKENS // TOK_DEV)
    expert_ids = jax.vmap(lambda own, number: deal_out(jax.random.fold_in(streams_of[11], 2), own, number, TOK_DEV, EXPERTS, TOP, CAP, 1))(expert_ids_keys, expert_ids_turns).reshape((TOKENS, TOP))
    doc_starts = draw_doc_starts(jax.random.fold_in(streams_of[13], 71), 0)
    return {"layer_input": layer_input, "grad_output": grad_output, "gain_attn": gain_attn, "gain_moe": gain_moe, "w_query": w_query, "w_keyval": w_keyval, "w_out": w_out, "w_gate": w_gate, "w_up": w_up, "w_down": w_down, "gate_weights": gate_weights, "expert_ids": expert_ids, "doc_starts": doc_starts}


EPS = 1e-06
ROPE_BASE = 1000000.0
NEG = -1e+30

@jax.custom_vjp
def low(v):
    return lax.optimization_barrier(v.astype(jnp.bfloat16)).astype(jnp.float32)

@jax.custom_vjp
def low_back(v):
    return v

def low_keep(v):
    return (low(v), None)

def low_pass(kept, grad):
    return (grad,)

def back_keep(v):
    return (v, None)

def back_low(kept, grad):
    return (low(grad),)
low.defvjp(low_keep, low_pass)
low_back.defvjp(back_keep, back_low)

def rotate(values, positions):
    half = values.shape[-1] // 2
    freq = ROPE_BASE ** (-jnp.arange(half, dtype=jnp.float32) * 2.0 / values.shape[-1])
    angle = positions.astype(jnp.float32)[:, None] * freq[None, :]
    cosine = jnp.cos(angle)[:, None, :]
    sine = jnp.sin(angle)[:, None, :]
    first = values[..., :half]
    second = values[..., half:]
    return jnp.concatenate([first * cosine - second * sine, second * cosine + first * sine], -1)

def doc_begin(positions, doc_starts):
    return lax.optimization_barrier(jnp.max(jnp.where(doc_starts[None, :] <= positions[:, None], doc_starts[None, :], 0), axis=1))

def layer(inputs, gain_a, gain_m, query_w, keyval_w, out_w, gate_w, up_w, down_w, gate_weights, expert_ids, doc_starts):
    highest = lax.Precision.HIGHEST
    count = inputs.shape[0]
    index = jnp.arange(count, dtype=jnp.int32)
    begins = doc_begin(index, doc_starts)
    places = index - begins
    factor_a = lax.rsqrt(lax.optimization_barrier(jnp.mean(inputs * inputs, -1, keepdims=True)) + EPS)
    normed_a = low(inputs * factor_a * gain_a)
    query_raw = low_back(jnp.dot(normed_a, query_w, precision=highest))
    keyval = jnp.dot(normed_a, keyval_w, precision=highest)
    width = KV_HEADS * HEAD_DIM
    key_raw = low_back(keyval[:, :width])
    value_raw = low_back(keyval[:, width:])
    queries = low_back(low(rotate(query_raw.reshape(count, HEADS, HEAD_DIM), places)))
    keys = low(rotate(key_raw.reshape(count, KV_HEADS, HEAD_DIM), places))
    values = low(value_raw.reshape(count, KV_HEADS, HEAD_DIM))
    share = HEADS // N_ULYSSES
    per_kv = HEADS // KV_HEADS
    which = [c * share // per_kv for c in range(N_ULYSSES)]
    key_copies = low_back(jnp.stack([keys[:, j] for j in which], 1))
    value_copies = low_back(jnp.stack([values[:, j] for j in which], 1))
    grouped = queries.reshape(count, N_ULYSSES, share, HEAD_DIM)
    block = min(512, count)
    scale = 1.0 / math.sqrt(HEAD_DIM)

    def attend(number):
        start = number * block
        rows = lax.dynamic_slice_in_dim(grouped, start, block, 0)
        q_pos = start + jnp.arange(block, dtype=jnp.int32)
        q_begin = lax.dynamic_slice_in_dim(begins, start, block, 0)
        scores = low_back(jnp.einsum('qchd,kcd->chqk', rows, key_copies, precision=highest) * scale)
        visible = (index[None, :] >= q_begin[:, None]) & (index[None, :] <= q_pos[:, None])
        scores = jnp.where(visible[None, None], scores, NEG)
        top = lax.optimization_barrier(jnp.max(scores, -1, keepdims=True))
        weights = jnp.exp(scores - top)
        total = lax.optimization_barrier(jnp.sum(weights, -1, keepdims=True))
        mixed = jnp.einsum('chqk,kcd->qchd', low(weights), value_copies, precision=highest)
        return mixed / jnp.transpose(total, (2, 0, 1, 3))
    blocks = lax.map(jax.checkpoint(attend), jnp.arange(count // block, dtype=jnp.int32))
    attended = low_back(low(blocks.reshape(count, HEADS * HEAD_DIM)))
    attn_branch = low_back(jnp.dot(attended, out_w.T, precision=highest))
    hidden = inputs + attn_branch
    factor_m = lax.rsqrt(lax.optimization_barrier(jnp.mean(hidden * hidden, -1, keepdims=True)) + EPS)
    normed_m = low(hidden * factor_m * gain_m)
    half = FF // 2

    def expert(total, number):
        gate_cols = lax.dynamic_slice_in_dim(gate_w, number * FF, FF, 1)
        up_cols = lax.dynamic_slice_in_dim(up_w, number * FF, FF, 1)
        down_cols = lax.dynamic_slice_in_dim(down_w, number * FF, FF, 1)
        weight = lax.optimization_barrier(jnp.sum(jnp.where(expert_ids == number, gate_weights, 0.0), -1))
        combined = jnp.zeros_like(total)
        for part in range(2):
            lo_col = part * half
            rows = low_back(normed_m)
            gate = low_back(jnp.dot(rows, gate_cols[:, lo_col:lo_col + half], precision=highest))
            up = low_back(jnp.dot(rows, up_cols[:, lo_col:lo_col + half], precision=highest))
            act = low(jax.nn.silu(gate) * up)
            combined = combined + low(low_back(jnp.dot(act, down_cols[:, lo_col:lo_col + half].T, precision=highest)))
        return (total + weight[:, None] * combined, None)
    moe_branch, _ = lax.scan(jax.checkpoint(expert), jnp.zeros_like(hidden), jnp.arange(EXPERTS, dtype=jnp.int32))
    result = hidden + moe_branch
    return (result, (attn_branch, moe_branch))

def reference(layer_input, grad_output, gain_attn, gain_moe, w_query, w_keyval, w_out, w_gate, w_up, w_down, gate_weights, expert_ids, doc_starts):
    floats = [v.astype(jnp.float32) for v in (layer_input, gain_attn, gain_moe, w_query, w_keyval, w_out, w_gate, w_up, w_down)]

    def forward(inputs, gain_a, gain_m, query_w, keyval_w, out_w, gate_w, up_w, down_w):
        return layer(inputs, gain_a, gain_m, query_w, keyval_w, out_w, gate_w, up_w, down_w, gate_weights.astype(jnp.float32), expert_ids, doc_starts)
    result, pull, branches = jax.vjp(forward, *floats, has_aux=True)
    grads = pull(grad_output.astype(jnp.float32))
    entries = result.shape[0] * result.shape[1]
    sums = jnp.stack([jnp.sum(branches[0] * branches[0]), jnp.sum(branches[1] * branches[1]), jnp.sum(result * result)])
    branch_rms = jnp.sqrt(sums / entries)
    return (result.astype(jnp.bfloat16), grads[0], grads[1], grads[2], grads[3], grads[4], grads[5], grads[6], grads[7], grads[8], branch_rms)
```

```python
import functools
import math

import jax
import jax.numpy as jnp
from jax import lax
from jax.experimental import pallas as pl
from jax.experimental.pallas import tpu as pltpu
from jax.sharding import PartitionSpec as P

D = 1536
HEADS = 12
KV_HEADS = 2
HEAD_DIM = 128
TOP = 4


EPS = 1e-06
ROPE_BASE = 1000000.0
NEG = -1e30


def rotate(values, positions, sign):
    half = values.shape[-1] // 2
    freq = ROPE_BASE ** (-jnp.arange(half, dtype=jnp.float32) * 2.0 / values.shape[-1])
    angle = positions.astype(jnp.float32)[:, None] * freq[None, :]
    cosine = jnp.cos(angle)[:, None, :]
    sine = sign * jnp.sin(angle)[:, None, :]
    first = values[..., :half]
    second = values[..., half:]
    return jnp.concatenate([first * cosine - second * sine, second * cosine + first * sine], -1)


def doc_begin(positions, doc_starts):
    return jnp.max(
        jnp.where(doc_starts[None, :] <= positions[:, None], doc_starts[None, :], 0), axis=1
    )


def norm_back(values, factor, gain, grad):
    weighted = grad * gain
    inner = jnp.mean(weighted * values, -1, keepdims=True)
    return factor * weighted - values * factor * factor * factor * inner


def visible_mask(q_pos, q_begin, k_pos):
    return (k_pos[None, :] >= q_begin[:, None]) & (k_pos[None, :] <= q_pos[:, None])


def split_blocks(array):
    rows = array.shape[0]
    size = min(rows, 512)
    return (array.reshape((rows // size, size) + array.shape[1:]), size)


def contract(left, right, left_dim, right_dim):
    return lax.dot_general(
        left, right, (((left_dim,), (right_dim,)), ((), ())), preferred_element_type=jnp.float32
    )


def reorder_rows(array, outer, inner):
    rows = array.shape[0]
    shaped = array.reshape((outer, inner, rows // (outer * inner)) + array.shape[1:])
    return jnp.swapaxes(shaped, 0, 1).reshape(array.shape)


def route(payload):
    return lax.all_to_all(payload, "blk", split_axis=0, concat_axis=0, tiled=True)


def backward_block(queries, grads, lse, delta, q_pos, q_begin, keys, values, k_start, scale):
    k_pos = k_start + jnp.arange(keys.shape[0], dtype=jnp.int32)
    visible = visible_mask(q_pos, q_begin, k_pos)[None]
    scores = jnp.einsum("qhd,kd->hqk", queries, keys, preferred_element_type=jnp.float32) * scale
    probs = jnp.where(visible, jnp.exp(scores - lse[:, :, None]), 0.0)
    probs_low = probs.astype(jnp.bfloat16)
    grad_probs = jnp.einsum("qhd,kd->hqk", grads, values, preferred_element_type=jnp.float32)
    grad_scores = (probs * (grad_probs - delta[:, :, None])).astype(jnp.bfloat16)
    part_q = (
        jnp.einsum("hqk,kd->qhd", grad_scores, keys, preferred_element_type=jnp.float32) * scale
    )
    part_k = (
        jnp.einsum("hqk,qhd->kd", grad_scores, queries, preferred_element_type=jnp.float32) * scale
    )
    part_v = jnp.einsum("hqk,qhd->kd", probs_low, grads, preferred_element_type=jnp.float32)
    return (part_q, part_k, part_v)


def local(
    layer_input,
    grad_output,
    gain_attn,
    gain_moe,
    w_query,
    w_keyval,
    w_out,
    w_gate,
    w_up,
    w_down,
    gate_weights,
    expert_ids,
    doc_starts,
):
    n_blk = lax.axis_size("blk")
    n_uly = lax.axis_size("ulysses")
    tok = layer_input.shape[0]
    group = tok * n_uly
    heads_dev = HEADS // n_uly
    per_kv = HEADS // KV_HEADS
    which = [c * heads_dev // per_kv for c in range(n_uly)]
    kv_width = KV_HEADS * HEAD_DIM
    q_width = HEADS * HEAD_DIM
    scale = 1.0 / math.sqrt(HEAD_DIM)
    blk_index = lax.axis_index("blk")
    device = blk_index * n_uly + lax.axis_index("ulysses")
    tok_pos = device * tok + jnp.arange(tok, dtype=jnp.int32)
    places = tok_pos - doc_begin(tok_pos, doc_starts)
    gain_a, gain_m, query_w, keyval_w, out_w = (
        lax.all_gather(gain_attn, ("blk", "ulysses"), axis=0, tiled=True),
        lax.all_gather(gain_moe, ("blk", "ulysses"), axis=0, tiled=True),
        lax.all_gather(w_query, ("blk", "ulysses"), axis=0, tiled=True),
        lax.all_gather(w_keyval, ("blk", "ulysses"), axis=0, tiled=True),
        lax.all_gather(w_out, ("blk", "ulysses"), axis=0, tiled=True),
    )
    gate_w, up_w, down_w = (
        lax.all_gather(w_gate, "ulysses", axis=0, tiled=True),
        lax.all_gather(w_up, "ulysses", axis=0, tiled=True),
        lax.all_gather(w_down, "ulysses", axis=0, tiled=True),
    )
    gain_a = gain_a.astype(jnp.float32)
    gain_m = gain_m.astype(jnp.float32)
    inputs = layer_input.astype(jnp.float32)
    factor_a = lax.rsqrt(jnp.mean(inputs * inputs, -1, keepdims=True) + EPS)
    normed_a = (inputs * factor_a * gain_a).astype(jnp.bfloat16)
    query_raw = jnp.dot(normed_a, query_w, preferred_element_type=jnp.float32)
    keyval_raw = jnp.dot(normed_a, keyval_w, preferred_element_type=jnp.float32)
    queries = rotate(query_raw.reshape(tok, HEADS, HEAD_DIM), places, 1.0).astype(jnp.bfloat16)
    keys = rotate(keyval_raw[:, :kv_width].reshape(tok, KV_HEADS, HEAD_DIM), places, 1.0).astype(
        jnp.bfloat16
    )
    values = keyval_raw[:, kv_width:].reshape(tok, KV_HEADS, HEAD_DIM).astype(jnp.bfloat16)
    key_copies = jnp.stack([keys[:, j] for j in which], 1)
    value_copies = jnp.stack([values[:, j] for j in which], 1)
    spread_normed = jnp.broadcast_to(normed_a[:, None, :], (tok, n_uly, D))
    head_q, head_k, head_v, head_normed = (
        lax.all_to_all(queries, "ulysses", split_axis=1, concat_axis=0, tiled=True),
        lax.all_to_all(key_copies, "ulysses", split_axis=1, concat_axis=0, tiled=True),
        lax.all_to_all(value_copies, "ulysses", split_axis=1, concat_axis=0, tiled=True),
        lax.all_to_all(spread_normed, "ulysses", split_axis=1, concat_axis=0, tiled=True),
    )
    key_local = head_k[:, 0, :]
    value_local = head_v[:, 0, :]
    normed_group = head_normed[:, 0, :]
    q_pos = blk_index * group + jnp.arange(group, dtype=jnp.int32)
    q_begin = doc_begin(q_pos, doc_starts)
    start_state = (
        jnp.full((heads_dev, group), NEG, jnp.float32),
        jnp.zeros((heads_dev, group), jnp.float32),
        jnp.zeros((group, heads_dev, HEAD_DIM), jnp.float32),
    )
    state = start_state
    key_rows = lax.all_gather(key_local, "blk", axis=0, tiled=True)
    value_rows = lax.all_gather(value_local, "blk", axis=0, tiled=True)
    key_blocks, size = split_blocks(key_rows)
    value_blocks, _ = split_blocks(value_rows)

    def attend_step(inner, item):
        key_blk, value_blk, number = item
        k_start = number * size
        live = (k_start <= q_pos[-1]) & (k_start + size - 1 >= q_begin[0])

        def attend_work(current):
            top, total, acc = current
            k_pos = k_start + jnp.arange(size, dtype=jnp.int32)
            visible = visible_mask(q_pos, q_begin, k_pos)[None]
            scores = (
                jnp.einsum("qhd,kd->hqk", head_q, key_blk, preferred_element_type=jnp.float32)
                * scale
            )
            scores = jnp.where(visible, scores, NEG)
            new_top = jnp.maximum(top, jnp.max(scores, -1))
            weights = jnp.where(visible, jnp.exp(scores - new_top[:, :, None]), 0.0)
            keep = jnp.exp(top - new_top)
            total = total * keep + jnp.sum(weights, -1)
            acc = acc * jnp.transpose(keep)[:, :, None] + jnp.einsum(
                "hqk,kd->qhd",
                weights.astype(jnp.bfloat16),
                value_blk,
                preferred_element_type=jnp.float32,
            )
            return (new_top, total, acc)

        return (lax.cond(live, attend_work, lambda current: current, inner), None)

    state, _ = lax.scan(
        attend_step,
        state,
        (key_blocks, value_blocks, jnp.arange(key_blocks.shape[0], dtype=jnp.int32)),
    )
    top, total, acc = state
    mixed = acc / jnp.transpose(total)[:, :, None]
    mixed_low = mixed.astype(jnp.bfloat16)
    lse = top + jnp.log(total)
    attended = lax.all_to_all(
        mixed_low, "ulysses", split_axis=0, concat_axis=1, tiled=True
    ).reshape(tok, q_width)
    attn_branch = contract(attended, out_w, 1, 1)
    hidden = inputs + attn_branch
    factor_m = lax.rsqrt(jnp.mean(hidden * hidden, -1, keepdims=True) + EPS)
    normed_m = (hidden * factor_m * gain_m).astype(jnp.bfloat16)
    experts = n_blk // 2
    capacity = min(tok, 2 * tok * TOP // experts)
    flat_ids = expert_ids.reshape(-1)
    picks = (flat_ids[:, None] == jnp.arange(experts, dtype=jnp.int32)[None, :]).astype(jnp.int32)
    slots = jnp.sum((jnp.cumsum(picks, 0) - 1) * picks, -1)

    def dispatch(rows):
        buffer = jnp.zeros((experts, capacity, D), jnp.bfloat16).at[flat_ids, slots].set(rows)
        return route(jnp.repeat(buffer, 2, axis=0)).reshape(n_blk * capacity, D)

    def collect(rows):
        back = route(rows.astype(jnp.bfloat16).reshape(n_blk, capacity, D))
        return back[2 * flat_ids, slots].astype(jnp.float32) + back[2 * flat_ids + 1, slots].astype(
            jnp.float32
        )

    expert_in = dispatch(jnp.repeat(normed_m, TOP, axis=0))
    gate_pre = jnp.dot(expert_in, gate_w, preferred_element_type=jnp.float32)
    up_pre = jnp.dot(expert_in, up_w, preferred_element_type=jnp.float32)
    act = (jax.nn.silu(gate_pre) * up_pre).astype(jnp.bfloat16)
    expert_out = contract(act, down_w, 1, 1)
    returned = collect(expert_out).reshape(tok, TOP, D)
    moe_branch = jnp.sum(gate_weights[:, :, None] * returned, 1)
    result = hidden + moe_branch
    layer_output = result.astype(jnp.bfloat16)
    grad_res = grad_output.astype(jnp.float32)
    routed_grad = (
        (gate_weights[:, :, None] * grad_res[:, None, :]).reshape(tok * TOP, D).astype(jnp.bfloat16)
    )
    expert_grad = dispatch(routed_grad)
    grad_act = jnp.dot(expert_grad, down_w, preferred_element_type=jnp.float32)
    grad_down = contract(expert_grad, act, 0, 0)
    sig = jax.nn.sigmoid(gate_pre)
    grad_gate_pre = (grad_act * up_pre * sig * (1.0 + gate_pre * (1.0 - sig))).astype(jnp.bfloat16)
    grad_up_pre = (grad_act * gate_pre * sig).astype(jnp.bfloat16)
    grad_gate = contract(expert_in, grad_gate_pre, 0, 0)
    grad_up = contract(expert_in, grad_up_pre, 0, 0)
    grad_in = contract(grad_gate_pre, gate_w, 1, 1) + contract(grad_up_pre, up_w, 1, 1)
    grad_normed_m = jnp.sum(collect(grad_in).reshape(tok, TOP, D), 1)
    grad_gain_m = jnp.sum(grad_normed_m * hidden * factor_m, 0)
    grad_hidden = grad_res + norm_back(hidden, factor_m, gain_m, grad_normed_m)
    grad_hidden_low = grad_hidden.astype(jnp.bfloat16)
    grad_attended = jnp.dot(grad_hidden_low, out_w, preferred_element_type=jnp.float32).astype(
        jnp.bfloat16
    )
    spread_hidden = jnp.broadcast_to(grad_hidden_low[:, None, :], (tok, n_uly, D))
    head_grad, head_hidden = (
        lax.all_to_all(
            grad_attended.reshape(tok, HEADS, HEAD_DIM),
            "ulysses",
            split_axis=1,
            concat_axis=0,
            tiled=True,
        ),
        lax.all_to_all(spread_hidden, "ulysses", split_axis=1, concat_axis=0, tiled=True),
    )
    grad_out_slice = contract(
        head_hidden[:, 0, :], mixed_low.reshape(group, heads_dev * HEAD_DIM), 0, 0
    )
    delta = jnp.transpose(jnp.sum(head_grad.astype(jnp.float32) * mixed, -1))
    total_keys = group * n_blk
    zero_q = jnp.zeros((group, heads_dev, HEAD_DIM), jnp.float32)
    fold_start = (
        zero_q,
        jnp.zeros((total_keys, HEAD_DIM), jnp.float32),
        jnp.zeros((total_keys, HEAD_DIM), jnp.float32),
    )
    state = fold_start
    key_rows = lax.all_gather(key_local, "blk", axis=0, tiled=True)
    value_rows = lax.all_gather(value_local, "blk", axis=0, tiled=True)
    key_blocks, grads_size = split_blocks(key_rows)
    value_blocks, _ = split_blocks(value_rows)

    def grads_step(inner, item):
        key_blk, value_blk, number = item
        k_start = number * grads_size
        live = (k_start <= q_pos[-1]) & (k_start + grads_size - 1 >= q_begin[0])

        def grads_work(current):
            part_q, part_k, part_v = backward_block(
                head_q, head_grad, lse, delta, q_pos, q_begin, key_blk, value_blk, k_start, scale
            )
            grad_q, grad_keys, grad_values = current
            grad_keys = lax.dynamic_update_slice_in_dim(
                grad_keys,
                lax.dynamic_slice_in_dim(grad_keys, k_start, grads_size, 0) + part_k,
                k_start,
                0,
            )
            grad_values = lax.dynamic_update_slice_in_dim(
                grad_values,
                lax.dynamic_slice_in_dim(grad_values, k_start, grads_size, 0) + part_v,
                k_start,
                0,
            )
            return (grad_q + part_q, grad_keys, grad_values)

        return (lax.cond(live, grads_work, lambda current: current, inner), None)

    state, _ = lax.scan(
        grads_step,
        state,
        (key_blocks, value_blocks, jnp.arange(key_blocks.shape[0], dtype=jnp.int32)),
    )
    grad_q = state[0]
    grad_k, grad_v = (
        lax.psum_scatter(state[1], "blk", scatter_dimension=0, tiled=True),
        lax.psum_scatter(state[2], "blk", scatter_dimension=0, tiled=True),
    )
    group_places = q_pos - q_begin
    grad_q_pre = rotate(grad_q.astype(jnp.bfloat16).astype(jnp.float32), group_places, -1.0).astype(
        jnp.bfloat16
    )
    grad_query_slice = contract(normed_group, grad_q_pre.reshape(group, heads_dev * HEAD_DIM), 0, 0)
    token_q, token_k, token_v = (
        lax.all_to_all(grad_q_pre, "ulysses", split_axis=0, concat_axis=1, tiled=True),
        lax.all_to_all(
            grad_k.astype(jnp.bfloat16)[:, None, :],
            "ulysses",
            split_axis=0,
            concat_axis=1,
            tiled=True,
        ),
        lax.all_to_all(
            grad_v.astype(jnp.bfloat16)[:, None, :],
            "ulysses",
            split_axis=0,
            concat_axis=1,
            tiled=True,
        ),
    )
    summed_k = []
    summed_v = []
    for head in range(KV_HEADS):
        members = [c for c in range(n_uly) if which[c] == head]
        summed_k.append(sum((token_k[:, c].astype(jnp.float32) for c in members)))
        summed_v.append(sum((token_v[:, c].astype(jnp.float32) for c in members)))
    grad_key_heads = jnp.stack(summed_k, 1)
    grad_value_heads = jnp.stack(summed_v, 1)
    grad_query_pre = token_q.reshape(tok, q_width)
    grad_key_pre = rotate(grad_key_heads, places, -1.0).reshape(tok, kv_width)
    grad_keyval_pre = jnp.concatenate(
        [grad_key_pre, grad_value_heads.reshape(tok, kv_width)], 1
    ).astype(jnp.bfloat16)
    grad_normed_a = contract(grad_query_pre, query_w, 1, 1) + contract(
        grad_keyval_pre, keyval_w, 1, 1
    )
    grad_keyval_w = contract(normed_a, grad_keyval_pre, 0, 0)
    grad_gain_a = jnp.sum(grad_normed_a * inputs * factor_a, 0)
    grad_input = grad_hidden + norm_back(inputs, factor_a, gain_a, grad_normed_a)
    n_dev = n_blk * n_uly
    squares = jnp.stack(
        [
            jnp.sum(attn_branch * attn_branch),
            jnp.sum(moe_branch * moe_branch),
            jnp.sum(result * result),
        ]
    )
    square_rows = jnp.broadcast_to(squares[None, :], (n_dev, 3))
    part_gate, part_up, part_down, uly_gain_a, uly_gain_m, uly_keyval, uly_squares = (
        lax.psum_scatter(
            grad_gate.astype(jnp.bfloat16), "ulysses", scatter_dimension=0, tiled=True
        ).astype(jnp.float32),
        lax.psum_scatter(
            grad_up.astype(jnp.bfloat16), "ulysses", scatter_dimension=0, tiled=True
        ).astype(jnp.float32),
        lax.psum_scatter(
            grad_down.astype(jnp.bfloat16), "ulysses", scatter_dimension=0, tiled=True
        ).astype(jnp.float32),
        lax.psum_scatter(
            reorder_rows(grad_gain_a, n_blk, n_uly).astype(jnp.bfloat16),
            "ulysses",
            scatter_dimension=0,
            tiled=True,
        ).astype(jnp.float32),
        lax.psum_scatter(
            reorder_rows(grad_gain_m, n_blk, n_uly).astype(jnp.bfloat16),
            "ulysses",
            scatter_dimension=0,
            tiled=True,
        ).astype(jnp.float32),
        lax.psum_scatter(
            reorder_rows(grad_keyval_w, n_blk, n_uly).astype(jnp.bfloat16),
            "ulysses",
            scatter_dimension=0,
            tiled=True,
        ).astype(jnp.float32),
        lax.psum_scatter(
            square_rows.astype(jnp.bfloat16), "ulysses", scatter_dimension=0, tiled=True
        ).astype(jnp.float32),
    )
    part_outw, part_query, part_gain_a, part_gain_m, part_keyval, square_row = (
        lax.psum_scatter(grad_out_slice, "blk", scatter_dimension=0, tiled=True),
        lax.psum_scatter(grad_query_slice, "blk", scatter_dimension=0, tiled=True),
        lax.psum_scatter(uly_gain_a, "blk", scatter_dimension=0, tiled=True),
        lax.psum_scatter(uly_gain_m, "blk", scatter_dimension=0, tiled=True),
        lax.psum_scatter(uly_keyval, "blk", scatter_dimension=0, tiled=True),
        lax.psum_scatter(uly_squares, "blk", scatter_dimension=0, tiled=True),
    )
    branch_rms = jnp.sqrt(square_row[0] / (tok * n_dev * D))
    return (
        layer_output,
        grad_input,
        part_gain_a,
        part_gain_m,
        part_query,
        part_keyval,
        part_outw,
        part_gate,
        part_up,
        part_down,
        branch_rms,
    )


MESH = pl.DeviceIdType.MESH
LANES = 128
LOG2E = 1.4426950408889634


class Place:
    def __init__(self, depth):
        self.blk = lax.axis_index("blk")
        self.u = lax.axis_index("ulysses")
        self.depth = depth
        self.z = self.blk // 4
        self.x = (self.blk // 2) % 2
        self.c = self.blk % 2
        self.up = (self.blk + 4, self.u)
        self.down = (self.blk - 4, self.u)
        self.across = (self.blk + 2 - 4 * self.x, self.u)
        self.sibling = (self.blk + 1 - 2 * self.c, self.u)
        self.other = (self.blk, 1 - self.u)
        self.has_up = self.z < depth - 1
        self.has_down = self.z > 0

    def slot(self, z, x, c):
        return z * 4 + x * 2 + c

    def greet(self, sibling=False, other=False, plane=True):
        barrier = pltpu.get_barrier_semaphore()

        def hail(device):
            pl.semaphore_signal(barrier, inc=1, device_id=device, device_id_type=MESH)

        count = 0
        if plane:
            hail(self.across)
            pl.when(self.has_up)(lambda: hail(self.up))
            pl.when(self.has_down)(lambda: hail(self.down))
            count = 1 + self.has_up.astype(jnp.int32) + self.has_down.astype(jnp.int32)
        if sibling:
            hail(self.sibling)
            count = count + 1
        if other:
            hail(self.other)
            count = count + 1
        pl.semaphore_wait(barrier, count)


class Wires:
    def __init__(self, sems):
        self.sems = sems
        self.used = 0

    def take(self, count):
        base = self.used
        self.used += count
        return lambda index: self.sems.at[base + index]


def remote(src, dst, send, recv, device):
    return pltpu.make_async_remote_copy(
        src_ref=src, dst_ref=dst, send_sem=send, recv_sem=recv, device_id=device, device_id_type=MESH
    )


class Gather:
    def __init__(self, place, wires, src, out, cores):
        self.p, self.src, self.out, self.cores = place, src, out, cores
        n = place.depth
        self.s_up, self.s_down, self.s_across = wires.take(n), wires.take(n), wires.take(n)
        self.r_z, self.r_x = wires.take(n), wires.take(n)
        if cores:
            self.s_core, self.r_core = wires.take(2 * n), wires.take(2 * n)
        self.own = wires.take(1)(0)

    def _send(self, zz, xx, kind, src=None):
        p = self.p
        dst = self.out(zz, xx, p.c)
        src = dst if src is None else src
        if kind == "up":
            return remote(src, dst, self.s_up(zz), self.r_z(zz), p.up)
        if kind == "down":
            return remote(src, dst, self.s_down(zz), self.r_z(zz), p.down)
        if kind == "across":
            return remote(src, dst, self.s_across(zz), self.r_x(zz), p.across)
        return remote(src, dst, self.s_core(zz * 2 + xx), self.r_core(zz * 2 + xx), p.sibling)

    def _keep(self):
        p = self.p
        return pltpu.make_async_copy(self.src, self.out(p.z, p.x, p.c), self.own)

    def start(self, in_place=False):
        p = self.p
        self.in_place = in_place
        src = None if in_place else self.src
        pl.when(p.has_up)(lambda: self._send(p.z, p.x, "up", src).start())
        pl.when(p.has_down)(lambda: self._send(p.z, p.x, "down", src).start())
        self._send(p.z, p.x, "across", src).start()
        if self.cores:
            self._send(p.z, p.x, "core", src).start()
        if not in_place:
            self._keep().start()

    def hop(self, d):
        p = self.p

        def low():
            zz = p.z - d
            self._send(zz, p.x, "up").wait_recv()
            pl.when(p.has_up)(lambda: self._send(zz, p.x, "up").start())
            self._send(zz, p.x, "across").start()
            if self.cores:
                self._send(zz, p.x, "core").start()

        def high():
            zz = p.z + d
            self._send(zz, p.x, "down").wait_recv()
            pl.when(p.has_down)(lambda: self._send(zz, p.x, "down").start())
            self._send(zz, p.x, "across").start()
            if self.cores:
                self._send(zz, p.x, "core").start()

        pl.when(p.z >= d)(low)
        pl.when(p.z + d < p.depth)(high)

    def cross(self, d):
        p = self.p

        def take(zz):
            self._send(zz, 1 - p.x, "across").wait_recv()
            if self.cores:
                self._send(zz, 1 - p.x, "core").start()

        if d == 0:
            take(p.z)
        else:
            pl.when(p.z >= d)(lambda: take(p.z - d))
            pl.when(p.z + d < p.depth)(lambda: take(p.z + d))

    def finish(self):
        p = self.p
        for zz in range(p.depth):
            if self.cores:
                for xx in range(2):
                    self._send(zz, xx, "core").wait()
            self._send(zz, p.x, "across").wait_send()
            pl.when(p.has_up & (p.z >= zz))(lambda zz=zz: self._send(zz, p.x, "up").wait_send())
            pl.when(p.has_down & (p.z <= zz))(lambda zz=zz: self._send(zz, p.x, "down").wait_send())
        if not self.in_place:
            self._keep().wait()


def gather_kernel(depth, cores, src, out, sems):
    place = Place(depth)
    place.greet(sibling=cores)
    wires = Wires(sems)
    if cores:
        view = lambda z, x, c: out.at[place.slot(z, x, c)]
    else:
        view = lambda z, x, c: out.at[z * 2 + x]
    g = Gather(place, wires, src, view, cores)
    g.start()
    for d in range(1, depth):
        g.hop(d)
        g.cross(d - 1)
    g.cross(depth - 1)
    g.finish()


def gather_plane(block, depth, cores, cid):
    slots = depth * (4 if cores else 2)
    return pl.pallas_call(
        functools.partial(gather_kernel, depth, cores),
        out_shape=jax.ShapeDtypeStruct((slots,) + block.shape, block.dtype),
        in_specs=[pl.BlockSpec(memory_space=pl.ANY)],
        out_specs=pl.BlockSpec(memory_space=pl.ANY),
        scratch_shapes=[pltpu.SemaphoreType.DMA((16 * depth,))],
        compiler_params=pltpu.CompilerParams(collective_id=cid, has_side_effects=True),
        name="gather_%d" % cid,
    )(block)


def opening_kernel(
    depth, w_own, x_own, dy_own, g_own, e0, e1, e2, w_all, x_all, dy_all, g_all, f0, f1, f2, sems
):
    p = Place(depth)
    p.greet(sibling=True, other=True)
    wires = Wires(sems)
    u = p.u
    mine = Gather(p, wires, w_own.at[u], lambda z, x, c: w_all.at[p.slot(z, x, c), u], True)
    peer = Gather(p, wires, None, lambda z, x, c: w_all.at[p.slot(z, x, c), 1 - u], True)
    dys = Gather(p, wires, dy_own, lambda z, x, c: dy_all.at[z * 2 + x], False)
    gws = Gather(p, wires, g_own, lambda z, x, c: g_all.at[z * 2 + x], False)
    ws, wr = wires.take(1)(0), wires.take(1)(0)
    xs, xr, xl = wires.take(1)(0), wires.take(1)(0), wires.take(1)(0)
    es, er, el = wires.take(3), wires.take(3), wires.take(3)
    cs, cr = wires.take(6), wires.take(6)
    half = e0.shape[0]
    cols = e0.shape[1]

    def part(ref, row, core):
        return ref.at[
            pl.ds(pl.multiple_of(row * half, half), half), pl.ds(pl.multiple_of(core * cols, LANES), cols)
        ]

    w_swap = remote(w_own.at[1 - u], w_all.at[p.blk, u], ws, wr, p.other)
    w_swap.start()
    mine.start()
    gws.start()
    x_swap = remote(x_own, x_all.at[u], xs, xr, p.other)
    x_swap.start()
    x_keep = pltpu.make_async_copy(x_own, x_all.at[u], xl)
    x_keep.start()
    experts = ((e0, f0), (e1, f1), (e2, f2))
    swaps = [remote(e, part(f, u, p.c), es(i), er(i), p.other) for i, (e, f) in enumerate(experts)]
    keeps = [pltpu.make_async_copy(e, part(f, u, p.c), el(i)) for i, (e, f) in enumerate(experts)]
    shares = [remote(e, part(f, u, p.c), cs(i), cr(i), p.sibling) for i, (e, f) in enumerate(experts)]
    passes = [
        remote(part(f, 1 - u, p.c), part(f, 1 - u, p.c), cs(3 + i), cr(3 + i), p.sibling)
        for i, (e, f) in enumerate(experts)
    ]
    for i in range(3):
        swaps[i].start()
        keeps[i].start()
        shares[i].start()
    w_swap.wait_recv()
    peer.start(in_place=True)
    dys.start()
    for d in range(1, depth):
        for g in (mine, peer, gws, dys):
            g.hop(d)
            g.cross(d - 1)
    for g in (mine, peer, gws, dys):
        g.cross(depth - 1)
    for i in range(3):
        swaps[i].wait_recv()
        passes[i].start()
    w_swap.wait_send()
    x_swap.wait()
    x_keep.wait()
    for i in range(3):
        swaps[i].wait_send()
        keeps[i].wait()
        shares[i].wait()
        passes[i].wait()
    for g in (mine, peer, gws, dys):
        g.finish()


def opening(w_own, x_own, dy_own, g_own, e0, e1, e2, depth, cid):
    shape = jax.ShapeDtypeStruct
    bf = jnp.bfloat16
    expert = shape((2 * e0.shape[0], 2 * e0.shape[1]), bf)
    return pl.pallas_call(
        functools.partial(opening_kernel, depth),
        out_shape=(
            shape((4 * depth,) + w_own.shape, bf),
            shape((2,) + x_own.shape, bf),
            shape((2 * depth,) + dy_own.shape, bf),
            shape((2 * depth,) + g_own.shape, jnp.float32),
            expert,
            expert,
            expert,
        ),
        in_specs=[pl.BlockSpec(memory_space=pl.ANY)] * 7,
        out_specs=tuple([pl.BlockSpec(memory_space=pl.ANY)] * 7),
        scratch_shapes=[pltpu.SemaphoreType.DMA((2 * 40 + 2 * 24 + 40,))],
        compiler_params=pltpu.CompilerParams(collective_id=cid, has_side_effects=True),
        name="opening",
    )(w_own, x_own, dy_own, g_own, e0, e1, e2)


class Scatter:
    def __init__(self, place, wires, part, keep, out, rx, ru, rd, send, mid, pieces):
        self.p, self.part, self.keep, self.out = place, part, keep, out
        self.rx, self.ru, self.rd, self.sendbuf, self.mid = rx, ru, rd, send, mid
        n = place.depth
        total = n * pieces
        self.pieces = pieces
        self.sx, self.cx = wires.take(total), wires.take(total)
        self.sz, self.cu, self.cd = wires.take(total), wires.take(total), wires.take(total)
        order = []
        low, high = 0, n - 1
        while low <= high:
            order.append(high)
            if low != high:
                order.append(low)
            low, high = low + 1, high - 1
        self.items = [(zz, k) for zz in order for k in range(pieces)]

    def _x(self, zz, k):
        i = zz * self.pieces + k
        return remote(self.part(zz, 1 - self.p.x, k), self.rx(zz, k), self.sx(i), self.cx(i), self.p.across)

    def _up(self, zz, k):
        i = zz * self.pieces + k
        return remote(self.sendbuf(zz, k), self.ru(zz, k), self.sz(i), self.cu(i), self.p.up)

    def _down(self, zz, k):
        i = zz * self.pieces + k
        return remote(self.sendbuf(zz, k), self.rd(zz, k), self.sz(i), self.cd(i), self.p.down)

    def begin(self, t):
        if t < len(self.items):
            self._x(*self.items[t]).start()

    def land(self, t):
        if t >= len(self.items):
            return
        p = self.p
        zz, k = self.items[t]
        self._x(zz, k).wait_recv()
        total = self.keep(zz, p.x, k)[...].astype(jnp.float32) + self.rx(zz, k)[...].astype(jnp.float32)
        self.mid(zz, k)[...] = total

        def climb():
            self.sendbuf(zz, k)[...] = total.astype(jnp.bfloat16)
            self._up(zz, k).start()

        def sink():
            self.sendbuf(zz, k)[...] = total.astype(jnp.bfloat16)
            self._down(zz, k).start()

        if zz > 0:
            pl.when(p.z == 0)(climb)
        if zz < p.depth - 1:
            pl.when(p.z == p.depth - 1)(sink)

    def chain(self, t, h):
        if t < 0 or t >= len(self.items):
            return
        p = self.p
        n = p.depth
        zz, k = self.items[t]

        def from_low():
            self._up(zz, k).wait_recv()
            total = self.mid(zz, k)[...] + self.ru(zz, k)[...].astype(jnp.float32)
            if zz == h:
                self.mid(zz, k)[...] = total
            else:
                self.sendbuf(zz, k)[...] = total.astype(jnp.bfloat16)
                self._up(zz, k).start()

        def from_high():
            self._down(zz, k).wait_recv()
            total = self.mid(zz, k)[...] + self.rd(zz, k)[...].astype(jnp.float32)
            if zz == n - 1 - h:
                self.mid(zz, k)[...] = total
            else:
                self.sendbuf(zz, k)[...] = total.astype(jnp.bfloat16)
                self._down(zz, k).start()

        if zz >= h:
            pl.when(p.z == h)(from_low)
        if zz <= n - 1 - h:
            pl.when(p.z == n - 1 - h)(from_high)

    def step(self, t):
        self.land(t)
        for h in range(1, self.p.depth):
            self.chain(t - h, h)

    def steps(self):
        return len(self.items) + self.p.depth - 1

    def finish(self):
        p = self.p
        for zz, k in self.items:
            self._x(zz, k).wait_send()
            pl.when(p.z < zz)(lambda zz=zz, k=k: self._up(zz, k).wait_send())
            pl.when(p.z > zz)(lambda zz=zz, k=k: self._down(zz, k).wait_send())

            def store(zz=zz, k=k):
                self.out(k)[...] = self.mid(zz, k)[...]

            pl.when(p.z == zz)(store)


def scatter_kernel(depth, pieces, cores, window, count, *refs):
    ins, outs = refs[:count], refs[count : 2 * count]
    rx, ru, rd, send, mid, sems = refs[2 * count : 2 * count + 6]
    rc = refs[2 * count + 6] if cores else None
    p = Place(depth)
    p.greet(sibling=cores)
    wires = Wires(sems)
    rows = outs[0].shape[0] // pieces

    def cut(ref, k):
        return ref.at[pl.ds(k * rows, rows)]

    jobs = []
    for a in range(count):
        src = ins[a]
        if cores:
            part = lambda zz, xx, k: cut(rc.at[zz * 2 + xx], k)
        else:
            part = lambda zz, xx, k, src=src: cut(src.at[zz * 2 + xx], k)
        jobs.append(
            Scatter(
                p, wires, part, part, lambda k, a=a: cut(outs[a], k),
                lambda zz, k, a=a: cut(rx.at[a, zz], k),
                lambda zz, k, a=a: cut(ru.at[a, zz], k),
                lambda zz, k, a=a: cut(rd.at[a, zz], k),
                lambda zz, k, a=a: cut(send.at[a, zz], k),
                lambda zz, k, a=a: cut(mid.at[a, zz], k),
                pieces,
            )
        )
    if cores:
        sc, cc = wires.take(2 * depth), wires.take(2 * depth)
        src = ins[0]

        def trade(zz, xx):
            i = zz * 2 + xx
            return remote(src.at[p.slot(zz, xx, 1 - p.c)], rc.at[i], sc(i), cc(i), p.sibling)

        order = list(dict.fromkeys(zz for zz, _ in jobs[0].items))
        for zz in order:
            for flip in range(2):
                xx = (1 - p.x) if flip == 0 else p.x
                trade(zz, xx).start()
        for zz in order:
            for flip in range(2):
                xx = (1 - p.x) if flip == 0 else p.x
                trade(zz, xx).wait_recv()
                at = zz * 2 + xx
                rc[at] = (
                    src[p.slot(zz, xx, p.c)].astype(jnp.float32) + rc[at].astype(jnp.float32)
                ).astype(jnp.bfloat16)
                if flip == 0:
                    for t, (z2, _) in enumerate(jobs[0].items):
                        if z2 == zz:
                            jobs[0].begin(t)
        for t in range(jobs[0].steps()):
            jobs[0].step(t)
        for zz in order:
            for xx in range(2):
                trade(zz, xx).wait_send()
    else:
        for t in range(window):
            jobs[0].begin(t)
        for a, job in enumerate(jobs):
            total = len(job.items)
            for t in range(job.steps()):
                job.step(t)
                if t + window < total:
                    job.begin(t + window)
                elif a + 1 < count and t + window - total < window:
                    jobs[a + 1].begin(t + window - total)
    for job in jobs:
        job.finish()


def scatter_plane(arrays, depth, pieces, cores, cid, window=3):
    count = len(arrays)
    block = arrays[0].shape[1:]
    bf = jnp.bfloat16
    total = depth * pieces
    scratch = [pltpu.VMEM((count, depth) + block, bf)] * 4 + [
        pltpu.VMEM((count, depth) + block, jnp.float32),
        pltpu.SemaphoreType.DMA((count * 5 * total + (4 * depth if cores else 0),)),
    ]
    if cores:
        scratch.append(pltpu.VMEM((2 * depth,) + block, bf))
    return pl.pallas_call(
        functools.partial(scatter_kernel, depth, pieces, cores, window, count),
        out_shape=tuple([jax.ShapeDtypeStruct(block, jnp.float32)] * count),
        in_specs=[pl.BlockSpec(memory_space=pltpu.VMEM)] * count,
        out_specs=tuple([pl.BlockSpec(memory_space=pltpu.VMEM)] * count),
        scratch_shapes=scratch,
        compiler_params=pltpu.CompilerParams(
            collective_id=cid, has_side_effects=True, vmem_limit_bytes=56 * 2**20
        ),
        name="scatter_%d" % cid,
    )(*arrays)


def mm(left, right):
    return jnp.dot(left, right, preferred_element_type=jnp.float32)


def flip(tile):
    return tile.astype(jnp.float32).T.astype(jnp.bfloat16)


def hidden_bias(first_key, first_query, begin, keys):
    queries = begin.shape[1]
    k_pos = first_key + lax.broadcasted_iota(jnp.int32, (keys, queries), 0)
    q_pos = first_query + lax.broadcasted_iota(jnp.int32, (keys, queries), 1)
    return jnp.where((k_pos >= begin) & (k_pos <= q_pos), 0.0, NEG)


def attend_kernel(scale, blk_ref, q_ref, kv_ref, begin_ref, o_ref, ot_ref, lse_ref, qt, top, total):
    group = q_ref.shape[0]
    heads = q_ref.shape[1] // HEAD_DIM
    blk = blk_ref[0]
    for h in range(heads):
        qt[:, h * group : (h + 1) * group] = flip(q_ref[:, h * HEAD_DIM : (h + 1) * HEAD_DIM])
    top[...] = jnp.full(top.shape, NEG, jnp.float32)
    total[...] = jnp.zeros(total.shape, jnp.float32)
    ot_ref[...] = jnp.zeros(ot_ref.shape, jnp.float32)

    def tile(j, carry):
        k = kv_ref[j, :, :HEAD_DIM]
        vt = flip(kv_ref[j, :, HEAD_DIM:])
        bias = hidden_bias(j * group, blk * group, begin_ref[0:1, :], group)
        for h in range(heads):
            at = slice(h * group, (h + 1) * group)
            s = mm(k, qt[:, at]) * (scale * LOG2E) + bias
            old = top[0:1, at]
            new = jnp.maximum(old, jnp.max(s, axis=0, keepdims=True))
            w = jnp.exp2(s - new)
            keep = jnp.exp2(old - new)
            total[0:1, at] = total[0:1, at] * keep + jnp.sum(w, axis=0, keepdims=True)
            ot_ref[:, at] = ot_ref[:, at] * keep + mm(vt, w.astype(jnp.bfloat16))
            top[0:1, at] = new
        return carry

    lax.fori_loop(0, blk + 1, tile, 0)
    sums = total[0:1, :]
    lse_ref[...] = jnp.broadcast_to(top[0:1, :] + jnp.log2(sums), lse_ref.shape)
    ot_ref[...] = ot_ref[...] / sums
    for h in range(heads):
        o_ref[:, h * HEAD_DIM : (h + 1) * HEAD_DIM] = ot_ref[:, h * group : (h + 1) * group].T.astype(
            jnp.bfloat16
        )


def attend(blk, q, kv, begin, scale):
    group, width = q.shape
    rows = width // HEAD_DIM * group
    vmem = pl.BlockSpec(memory_space=pltpu.VMEM)
    return pl.pallas_call(
        functools.partial(attend_kernel, scale),
        out_shape=(
            jax.ShapeDtypeStruct(q.shape, jnp.bfloat16),
            jax.ShapeDtypeStruct((HEAD_DIM, rows), jnp.float32),
            jax.ShapeDtypeStruct((8, rows), jnp.float32),
        ),
        in_specs=[pl.BlockSpec(memory_space=pltpu.SMEM), vmem, vmem, vmem],
        out_specs=(vmem, vmem, vmem),
        scratch_shapes=[
            pltpu.VMEM((HEAD_DIM, rows), jnp.bfloat16),
            pltpu.VMEM((8, rows), jnp.float32),
            pltpu.VMEM((8, rows), jnp.float32),
        ],
        compiler_params=pltpu.CompilerParams(vmem_limit_bytes=48 * 2**20),
        name="attend",
    )(blk, q, kv, begin)


def attend_back_kernel(
    scale, blk_ref, q_ref, do_ref, kv_ref, begin_ref, ot_ref, lse_ref, dq_ref, dkv_ref, qt, dot_, dqt, delta
):
    group = q_ref.shape[0]
    heads = q_ref.shape[1] // HEAD_DIM
    blocks = kv_ref.shape[0]
    blk = blk_ref[0]
    for h in range(heads):
        at = slice(h * group, (h + 1) * group)
        cols = slice(h * HEAD_DIM, (h + 1) * HEAD_DIM)
        qt[:, at] = flip(q_ref[:, cols])
        turned = do_ref[:, cols].astype(jnp.float32).T
        dot_[:, at] = turned.astype(jnp.bfloat16)
        delta[0:1, at] = jnp.sum(turned * ot_ref[:, at], axis=0, keepdims=True)
    dqt[...] = jnp.zeros(dqt.shape, jnp.float32)

    def tile(j, carry):
        k = kv_ref[j, :, :HEAD_DIM]
        v = kv_ref[j, :, HEAD_DIM:]
        kt = flip(k)
        bias = hidden_bias(j * group, blk * group, begin_ref[0:1, :], group)
        dk = jnp.zeros((group, HEAD_DIM), jnp.float32)
        dv = jnp.zeros((group, HEAD_DIM), jnp.float32)
        for h in range(heads):
            at = slice(h * group, (h + 1) * group)
            cols = slice(h * HEAD_DIM, (h + 1) * HEAD_DIM)
            s = mm(k, qt[:, at]) * (scale * LOG2E) + bias
            w = jnp.exp2(s - lse_ref[0:1, at])
            ds = (w * (mm(v, dot_[:, at]) - delta[0:1, at])).astype(jnp.bfloat16)
            dqt[:, at] += mm(kt, ds)
            dk += mm(ds, q_ref[:, cols])
            dv += mm(w.astype(jnp.bfloat16), do_ref[:, cols])
        dkv_ref[j, :, :HEAD_DIM] = (dk * scale).astype(jnp.bfloat16)
        dkv_ref[j, :, HEAD_DIM:] = dv.astype(jnp.bfloat16)
        return carry

    lax.fori_loop(0, blk + 1, tile, 0)

    def clear(j, carry):
        dkv_ref[j] = jnp.zeros(dkv_ref.shape[1:], jnp.bfloat16)
        return carry

    lax.fori_loop(blk + 1, blocks, clear, 0)
    for h in range(heads):
        at = slice(h * group, (h + 1) * group)
        dq_ref[:, h * HEAD_DIM : (h + 1) * HEAD_DIM] = (dqt[:, at] * scale).T.astype(jnp.bfloat16)


def attend_back(blk, q, do, kv, begin, ot, lse, scale):
    group, width = q.shape
    rows = width // HEAD_DIM * group
    vmem = pl.BlockSpec(memory_space=pltpu.VMEM)
    return pl.pallas_call(
        functools.partial(attend_back_kernel, scale),
        out_shape=(
            jax.ShapeDtypeStruct(q.shape, jnp.bfloat16),
            jax.ShapeDtypeStruct(kv.shape, jnp.bfloat16),
        ),
        in_specs=[pl.BlockSpec(memory_space=pltpu.SMEM)] + [vmem] * 6,
        out_specs=(vmem, vmem),
        scratch_shapes=[
            pltpu.VMEM((HEAD_DIM, rows), jnp.bfloat16),
            pltpu.VMEM((HEAD_DIM, rows), jnp.bfloat16),
            pltpu.VMEM((HEAD_DIM, rows), jnp.float32),
            pltpu.VMEM((8, rows), jnp.float32),
        ],
        compiler_params=pltpu.CompilerParams(vmem_limit_bytes=48 * 2**20),
        name="attend_back",
    )(blk, q, do, kv, begin, ot, lse)


def turn(values, cosine, sine):
    rows, width = values.shape
    heads = width // HEAD_DIM
    half = HEAD_DIM // 2
    shaped = values.reshape(rows, heads, HEAD_DIM)
    swapped = jnp.concatenate([shaped[..., half:], shaped[..., :half]], -1)
    return (shaped * cosine[:, None, :] + swapped * sine[:, None, :]).reshape(rows, width)


def other_half(values, u, rows):
    mine = lax.dynamic_slice_in_dim(values, u * rows, rows, 0)
    theirs = lax.dynamic_slice_in_dim(values, (1 - u) * rows, rows, 0).astype(jnp.bfloat16)
    return mine + lax.ppermute(theirs, "ulysses", [(0, 1), (1, 0)]).astype(jnp.float32)


def join_group(rows, u):
    theirs = lax.ppermute(rows, "ulysses", [(0, 1), (1, 0)])
    first = jnp.where(u == 0, rows, theirs)
    second = jnp.where(u == 0, theirs, rows)
    return jnp.concatenate([first, second], 0)


def planned(
    layer_input,
    grad_output,
    gain_attn,
    gain_moe,
    w_query,
    w_keyval,
    w_out,
    w_gate,
    w_up,
    w_down,
    gate_weights,
    expert_ids,
    doc_starts,
):
    bf, f32 = jnp.bfloat16, jnp.float32
    n_blk = lax.axis_size("blk")
    n_uly = lax.axis_size("ulysses")
    depth = n_blk // 4
    tok = layer_input.shape[0]
    group = tok * n_uly
    rows_dev = w_query.shape[0]
    q_half = HEADS // n_uly * HEAD_DIM
    kv_half = 2 * HEAD_DIM
    scale = 1.0 / math.sqrt(HEAD_DIM)
    blk = lax.axis_index("blk")
    u = lax.axis_index("ulysses")
    experts = n_blk // 2
    expert = blk // 2
    n_dev = n_blk * n_uly

    gains = jnp.concatenate(
        [gain_attn[:, None], gain_moe[:, None], jnp.zeros((rows_dev, LANES - 2), bf)], 1
    )
    w_own = jnp.concatenate(
        [
            w_query.reshape(rows_dev, n_uly, q_half),
            jnp.swapaxes(w_keyval.reshape(rows_dev, 2, n_uly, HEAD_DIM), 1, 2).reshape(
                rows_dev, n_uly, kv_half
            ),
            jnp.broadcast_to(gains[:, None, :], (rows_dev, n_uly, LANES)),
            w_out.reshape(rows_dev, n_uly, q_half),
        ],
        2,
    )
    w_own = jnp.swapaxes(w_own, 0, 1)
    named = expert_ids[:, :, None] == jnp.arange(experts, dtype=jnp.int32)[None, None, :]
    g_own = jnp.sum(jnp.where(named, gate_weights[:, :, None], 0.0), 1).T
    w_all, x_all, dy_all, g_all, gate_w, up_w, down_w = opening(
        w_own, layer_input, grad_output, g_own, w_gate, w_up, w_down, depth, 1
    )
    w_all = w_all.reshape(D, w_own.shape[2])
    query_w = w_all[:, :q_half]
    keyval_w = w_all[:, q_half : q_half + kv_half]
    gain_cols = w_all[:, q_half + kv_half : q_half + kv_half + 2].astype(f32).T
    out_w = w_all[:, q_half + kv_half + LANES :]
    gain_a, gain_m = gain_cols[0], gain_cols[1]

    positions = blk * group + jnp.arange(group, dtype=jnp.int32)
    begins = doc_begin(positions, doc_starts)
    half = HEAD_DIM // 2
    freq = ROPE_BASE ** (-jnp.arange(half, dtype=f32) * 2.0 / HEAD_DIM)
    angle = (positions - begins).astype(f32)[:, None] * freq[None, :]
    cosine = jnp.concatenate([jnp.cos(angle)] * 2, 1)
    sine = jnp.sin(angle)
    sine = jnp.concatenate([-sine, sine], 1)

    inputs_g = x_all.reshape(group, D).astype(f32)
    normed_a = (
        inputs_g * lax.rsqrt(jnp.mean(inputs_g * inputs_g, -1, keepdims=True) + EPS) * gain_a
    ).astype(bf)
    queries = turn(mm(normed_a, query_w), cosine, sine).astype(bf)
    keyval = mm(normed_a, keyval_w)
    kv_own = jnp.concatenate(
        [turn(keyval[:, :HEAD_DIM], cosine, sine).astype(bf), keyval[:, HEAD_DIM:].astype(bf)], 1
    )
    kv_all = gather_plane(kv_own, depth, True, 2)
    blk_word = jnp.full((1,), blk, jnp.int32)
    begin_rows = jnp.broadcast_to(begins[None, :], (8, group))
    mixed, mixed_t, lse = attend(blk_word, queries, kv_all, begin_rows, scale)

    attn_branch = other_half(contract(mixed, out_w, 1, 1), u, tok)
    inputs = layer_input.astype(f32)
    hidden = inputs + attn_branch
    factor_m = lax.rsqrt(jnp.mean(hidden * hidden, -1, keepdims=True) + EPS)
    normed_m = (hidden * factor_m * gain_m).astype(bf)

    rows_in = gather_plane(normed_m, depth, False, 3).reshape(2 * depth * tok, D)
    dy_in = dy_all.reshape(2 * depth * tok, D)
    weight = lax.dynamic_index_in_dim(g_all, expert, 1, keepdims=False).reshape(2 * depth * tok, 1)
    gate_pre = mm(rows_in, gate_w)
    up_pre = mm(rows_in, up_w)
    sig = jax.nn.sigmoid(gate_pre)
    act = (gate_pre * sig * up_pre).astype(bf)
    z_part = (weight * contract(act, down_w, 1, 1)).astype(bf)
    dyr = (weight * dy_in.astype(f32)).astype(bf)
    grad_act = mm(dyr, down_w)
    grad_gate_pre = (grad_act * up_pre * sig * (1.0 + gate_pre * (1.0 - sig))).astype(bf)
    grad_up_pre = (grad_act * gate_pre * sig).astype(bf)
    db_part = (contract(grad_gate_pre, gate_w, 1, 1) + contract(grad_up_pre, up_w, 1, 1)).astype(bf)
    block = (2 * depth, tok, D)
    grad_normed_m, moe_branch = scatter_plane(
        [db_part.reshape(block), z_part.reshape(block)], depth, 2, False, 4
    )
    grads_e = jnp.stack(
        [contract(rows_in, grad_gate_pre, 0, 0), contract(rows_in, grad_up_pre, 0, 0), contract(dyr, act, 0, 0)]
    )
    cols = w_gate.shape[1]
    core = blk % 2
    keep_cols = lax.dynamic_slice_in_dim(grads_e, core * cols, cols, 2)
    give_cols = lax.dynamic_slice_in_dim(grads_e, (1 - core) * cols, cols, 2).astype(bf)
    pairs = [(i, i ^ 1) for i in range(n_blk)]
    grads_e = keep_cols + lax.ppermute(give_cols, "blk", pairs).astype(f32)
    rows_e = w_gate.shape[0]
    keep_rows = lax.dynamic_slice_in_dim(grads_e, u * rows_e, rows_e, 1)
    give_rows = lax.dynamic_slice_in_dim(grads_e, (1 - u) * rows_e, rows_e, 1).astype(bf)
    grads_e = keep_rows + lax.ppermute(give_rows, "ulysses", [(0, 1), (1, 0)]).astype(f32)

    result = hidden + moe_branch
    layer_output = result.astype(bf)
    grad_res = grad_output.astype(f32)
    grad_hidden = grad_res + norm_back(hidden, factor_m, gain_m, grad_normed_m)
    hidden_low = join_group(grad_hidden.astype(bf), u)
    grad_mixed = mm(hidden_low, out_w).astype(bf)
    grad_out_half = contract(hidden_low, mixed, 0, 0)

    grad_q, grad_kv = attend_back(
        blk_word, queries, grad_mixed, kv_all, begin_rows, mixed_t, lse, scale
    )
    (kv_sum,) = scatter_plane([grad_kv], depth, 1, True, 5)
    kv_sum = kv_sum.astype(bf).astype(f32)
    grad_q_pre = turn(grad_q.astype(f32), cosine, -sine).astype(bf)
    grad_kv_pre = jnp.concatenate(
        [turn(kv_sum[:, :HEAD_DIM], cosine, -sine).astype(bf), kv_sum[:, HEAD_DIM:].astype(bf)], 1
    )
    grad_normed_a = other_half(
        contract(grad_q_pre, query_w, 1, 1) + contract(grad_kv_pre, keyval_w, 1, 1), u, tok
    )
    factor_a = lax.rsqrt(jnp.mean(inputs * inputs, -1, keepdims=True) + EPS)
    grad_input = grad_hidden + norm_back(inputs, factor_a, gain_a, grad_normed_a)
    spread = jnp.arange(LANES, dtype=jnp.int32)[None, :]
    pick_a = jnp.broadcast_to((spread == 0).astype(bf), (tok, LANES))
    pick_m = jnp.broadcast_to((spread == 1).astype(bf), (tok, LANES))
    gain_terms = contract((grad_normed_a * inputs * factor_a).astype(bf), pick_a, 0, 0) + contract(
        (grad_normed_m * hidden * factor_m).astype(bf), pick_m, 0, 0
    )
    payload = jnp.concatenate(
        [
            contract(normed_a, grad_q_pre, 0, 0).astype(bf),
            contract(normed_a, grad_kv_pre, 0, 0).astype(bf),
            gain_terms.astype(bf),
            grad_out_half.astype(bf),
        ],
        1,
    )
    (sums,) = scatter_plane([payload.reshape(n_blk, D // n_blk, payload.shape[1])], depth, 1, True, 6)
    part_query = sums[:, :q_half]
    part_out = sums[:, q_half + kv_half + LANES :]
    tail = sums[:, q_half : q_half + kv_half + LANES]
    mine = lax.dynamic_slice_in_dim(tail, u * rows_dev, rows_dev, 0)
    theirs = lax.ppermute(
        lax.dynamic_slice_in_dim(tail, (1 - u) * rows_dev, rows_dev, 0), "ulysses", [(0, 1), (1, 0)]
    )
    first = jnp.where(u == 0, mine, theirs)
    second = jnp.where(u == 0, theirs, mine)
    part_keyval = jnp.concatenate(
        [
            first[:, :HEAD_DIM],
            second[:, :HEAD_DIM],
            first[:, HEAD_DIM:kv_half],
            second[:, HEAD_DIM:kv_half],
        ],
        1,
    )
    gain_sums = mine[:, kv_half : kv_half + 2] + theirs[:, kv_half : kv_half + 2]
    squares = lax.psum(
        jnp.stack(
            [
                jnp.sum(attn_branch * attn_branch),
                jnp.sum(moe_branch * moe_branch),
                jnp.sum(result * result),
            ]
        ),
        ("blk", "ulysses"),
    )
    branch_rms = jnp.sqrt(squares / (tok * n_dev * D))
    return (
        layer_output,
        grad_input,
        gain_sums[:, 0],
        gain_sums[:, 1],
        part_query,
        part_keyval,
        part_out,
        grads_e[0],
        grads_e[1],
        grads_e[2],
        branch_rms,
    )


def solution(mesh):
    in_specs = (
        P(("blk", "ulysses"), None),
        P(("blk", "ulysses"), None),
        P(("blk", "ulysses")),
        P(("blk", "ulysses")),
        P(("blk", "ulysses"), None),
        P(("blk", "ulysses"), None),
        P(("blk", "ulysses"), None),
        P("ulysses", "blk"),
        P("ulysses", "blk"),
        P("ulysses", "blk"),
        P(("blk", "ulysses"), None),
        P(("blk", "ulysses"), None),
        P(),
    )
    out_specs = (
        P(("blk", "ulysses"), None),
        P(("blk", "ulysses"), None),
        P(("blk", "ulysses")),
        P(("blk", "ulysses")),
        P("blk", "ulysses"),
        P(("blk", "ulysses"), None),
        P("blk", "ulysses"),
        P("ulysses", "blk"),
        P("ulysses", "blk"),
        P("ulysses", "blk"),
        P(),
    )
    blocks, members = mesh.shape["blk"], mesh.shape["ulysses"]
    body = planned if blocks == 16 and members == KV_HEADS else local
    return jax.shard_map(body, mesh=mesh, in_specs=in_specs, out_specs=out_specs, check_vma=False)
```

```python
import functools
import math

import jax
import jax.numpy as jnp
from jax import lax
from jax.experimental import pallas as pl
from jax.experimental.pallas import tpu as pltpu
from jax.sharding import PartitionSpec as P

D = 1536
HEADS = 12
KV_HEADS = 2
HEAD_DIM = 128
TOP = 4


EPS = 1e-06
ROPE_BASE = 1000000.0
NEG = -1e30


def rotate(values, positions, sign):
    half = values.shape[-1] // 2
    freq = ROPE_BASE ** (-jnp.arange(half, dtype=jnp.float32) * 2.0 / values.shape[-1])
    angle = positions.astype(jnp.float32)[:, None] * freq[None, :]
    cosine = jnp.cos(angle)[:, None, :]
    sine = sign * jnp.sin(angle)[:, None, :]
    first = values[..., :half]
    second = values[..., half:]
    return jnp.concatenate([first * cosine - second * sine, second * cosine + first * sine], -1)


def doc_begin(positions, doc_starts):
    return jnp.max(
        jnp.where(doc_starts[None, :] <= positions[:, None], doc_starts[None, :], 0), axis=1
    )


def norm_back(values, factor, gain, grad):
    weighted = grad * gain
    inner = jnp.mean(weighted * values, -1, keepdims=True)
    return factor * weighted - values * factor * factor * factor * inner


def visible_mask(q_pos, q_begin, k_pos):
    return (k_pos[None, :] >= q_begin[:, None]) & (k_pos[None, :] <= q_pos[:, None])


def split_blocks(array):
    rows = array.shape[0]
    size = min(rows, 512)
    return (array.reshape((rows // size, size) + array.shape[1:]), size)


def contract(left, right, left_dim, right_dim):
    return lax.dot_general(
        left, right, (((left_dim,), (right_dim,)), ((), ())), preferred_element_type=jnp.float32
    )


def reorder_rows(array, outer, inner):
    rows = array.shape[0]
    shaped = array.reshape((outer, inner, rows // (outer * inner)) + array.shape[1:])
    return jnp.swapaxes(shaped, 0, 1).reshape(array.shape)


def route(payload):
    return lax.all_to_all(payload, "blk", split_axis=0, concat_axis=0, tiled=True)


def backward_block(queries, grads, lse, delta, q_pos, q_begin, keys, values, k_start, scale):
    k_pos = k_start + jnp.arange(keys.shape[0], dtype=jnp.int32)
    visible = visible_mask(q_pos, q_begin, k_pos)[None]
    scores = jnp.einsum("qhd,kd->hqk", queries, keys, preferred_element_type=jnp.float32) * scale
    probs = jnp.where(visible, jnp.exp(scores - lse[:, :, None]), 0.0)
    probs_low = probs.astype(jnp.bfloat16)
    grad_probs = jnp.einsum("qhd,kd->hqk", grads, values, preferred_element_type=jnp.float32)
    grad_scores = (probs * (grad_probs - delta[:, :, None])).astype(jnp.bfloat16)
    part_q = (
        jnp.einsum("hqk,kd->qhd", grad_scores, keys, preferred_element_type=jnp.float32) * scale
    )
    part_k = (
        jnp.einsum("hqk,qhd->kd", grad_scores, queries, preferred_element_type=jnp.float32) * scale
    )
    part_v = jnp.einsum("hqk,qhd->kd", probs_low, grads, preferred_element_type=jnp.float32)
    return (part_q, part_k, part_v)


def local(
    layer_input,
    grad_output,
    gain_attn,
    gain_moe,
    w_query,
    w_keyval,
    w_out,
    w_gate,
    w_up,
    w_down,
    gate_weights,
    expert_ids,
    doc_starts,
):
    n_blk = lax.axis_size("blk")
    n_uly = lax.axis_size("ulysses")
    tok = layer_input.shape[0]
    group = tok * n_uly
    heads_dev = HEADS // n_uly
    per_kv = HEADS // KV_HEADS
    which = [c * heads_dev // per_kv for c in range(n_uly)]
    kv_width = KV_HEADS * HEAD_DIM
    q_width = HEADS * HEAD_DIM
    scale = 1.0 / math.sqrt(HEAD_DIM)
    blk_index = lax.axis_index("blk")
    device = blk_index * n_uly + lax.axis_index("ulysses")
    tok_pos = device * tok + jnp.arange(tok, dtype=jnp.int32)
    places = tok_pos - doc_begin(tok_pos, doc_starts)
    gain_a, gain_m, query_w, keyval_w, out_w = (
        lax.all_gather(gain_attn, ("blk", "ulysses"), axis=0, tiled=True),
        lax.all_gather(gain_moe, ("blk", "ulysses"), axis=0, tiled=True),
        lax.all_gather(w_query, ("blk", "ulysses"), axis=0, tiled=True),
        lax.all_gather(w_keyval, ("blk", "ulysses"), axis=0, tiled=True),
        lax.all_gather(w_out, ("blk", "ulysses"), axis=0, tiled=True),
    )
    gate_w, up_w, down_w = (
        lax.all_gather(w_gate, "ulysses", axis=0, tiled=True),
        lax.all_gather(w_up, "ulysses", axis=0, tiled=True),
        lax.all_gather(w_down, "ulysses", axis=0, tiled=True),
    )
    gain_a = gain_a.astype(jnp.float32)
    gain_m = gain_m.astype(jnp.float32)
    inputs = layer_input.astype(jnp.float32)
    factor_a = lax.rsqrt(jnp.mean(inputs * inputs, -1, keepdims=True) + EPS)
    normed_a = (inputs * factor_a * gain_a).astype(jnp.bfloat16)
    query_raw = jnp.dot(normed_a, query_w, preferred_element_type=jnp.float32)
    keyval_raw = jnp.dot(normed_a, keyval_w, preferred_element_type=jnp.float32)
    queries = rotate(query_raw.reshape(tok, HEADS, HEAD_DIM), places, 1.0).astype(jnp.bfloat16)
    keys = rotate(keyval_raw[:, :kv_width].reshape(tok, KV_HEADS, HEAD_DIM), places, 1.0).astype(
        jnp.bfloat16
    )
    values = keyval_raw[:, kv_width:].reshape(tok, KV_HEADS, HEAD_DIM).astype(jnp.bfloat16)
    key_copies = jnp.stack([keys[:, j] for j in which], 1)
    value_copies = jnp.stack([values[:, j] for j in which], 1)
    spread_normed = jnp.broadcast_to(normed_a[:, None, :], (tok, n_uly, D))
    head_q, head_k, head_v, head_normed = (
        lax.all_to_all(queries, "ulysses", split_axis=1, concat_axis=0, tiled=True),
        lax.all_to_all(key_copies, "ulysses", split_axis=1, concat_axis=0, tiled=True),
        lax.all_to_all(value_copies, "ulysses", split_axis=1, concat_axis=0, tiled=True),
        lax.all_to_all(spread_normed, "ulysses", split_axis=1, concat_axis=0, tiled=True),
    )
    key_local = head_k[:, 0, :]
    value_local = head_v[:, 0, :]
    normed_group = head_normed[:, 0, :]
    q_pos = blk_index * group + jnp.arange(group, dtype=jnp.int32)
    q_begin = doc_begin(q_pos, doc_starts)
    start_state = (
        jnp.full((heads_dev, group), NEG, jnp.float32),
        jnp.zeros((heads_dev, group), jnp.float32),
        jnp.zeros((group, heads_dev, HEAD_DIM), jnp.float32),
    )
    state = start_state
    key_rows = lax.all_gather(key_local, "blk", axis=0, tiled=True)
    value_rows = lax.all_gather(value_local, "blk", axis=0, tiled=True)
    key_blocks, size = split_blocks(key_rows)
    value_blocks, _ = split_blocks(value_rows)

    def attend_step(inner, item):
        key_blk, value_blk, number = item
        k_start = number * size
        live = (k_start <= q_pos[-1]) & (k_start + size - 1 >= q_begin[0])

        def attend_work(current):
            top, total, acc = current
            k_pos = k_start + jnp.arange(size, dtype=jnp.int32)
            visible = visible_mask(q_pos, q_begin, k_pos)[None]
            scores = (
                jnp.einsum("qhd,kd->hqk", head_q, key_blk, preferred_element_type=jnp.float32)
                * scale
            )
            scores = jnp.where(visible, scores, NEG)
            new_top = jnp.maximum(top, jnp.max(scores, -1))
            weights = jnp.where(visible, jnp.exp(scores - new_top[:, :, None]), 0.0)
            keep = jnp.exp(top - new_top)
            total = total * keep + jnp.sum(weights, -1)
            acc = acc * jnp.transpose(keep)[:, :, None] + jnp.einsum(
                "hqk,kd->qhd",
                weights.astype(jnp.bfloat16),
                value_blk,
                preferred_element_type=jnp.float32,
            )
            return (new_top, total, acc)

        return (lax.cond(live, attend_work, lambda current: current, inner), None)

    state, _ = lax.scan(
        attend_step,
        state,
        (key_blocks, value_blocks, jnp.arange(key_blocks.shape[0], dtype=jnp.int32)),
    )
    top, total, acc = state
    mixed = acc / jnp.transpose(total)[:, :, None]
    mixed_low = mixed.astype(jnp.bfloat16)
    lse = top + jnp.log(total)
    attended = lax.all_to_all(
        mixed_low, "ulysses", split_axis=0, concat_axis=1, tiled=True
    ).reshape(tok, q_width)
    attn_branch = contract(attended, out_w, 1, 1)
    hidden = inputs + attn_branch
    factor_m = lax.rsqrt(jnp.mean(hidden * hidden, -1, keepdims=True) + EPS)
    normed_m = (hidden * factor_m * gain_m).astype(jnp.bfloat16)
    experts = n_blk // 2
    capacity = min(tok, 2 * tok * TOP // experts)
    flat_ids = expert_ids.reshape(-1)
    picks = (flat_ids[:, None] == jnp.arange(experts, dtype=jnp.int32)[None, :]).astype(jnp.int32)
    slots = jnp.sum((jnp.cumsum(picks, 0) - 1) * picks, -1)

    def dispatch(rows):
        buffer = jnp.zeros((experts, capacity, D), jnp.bfloat16).at[flat_ids, slots].set(rows)
        return route(jnp.repeat(buffer, 2, axis=0)).reshape(n_blk * capacity, D)

    def collect(rows):
        back = route(rows.astype(jnp.bfloat16).reshape(n_blk, capacity, D))
        return back[2 * flat_ids, slots].astype(jnp.float32) + back[2 * flat_ids + 1, slots].astype(
            jnp.float32
        )

    expert_in = dispatch(jnp.repeat(normed_m, TOP, axis=0))
    gate_pre = jnp.dot(expert_in, gate_w, preferred_element_type=jnp.float32)
    up_pre = jnp.dot(expert_in, up_w, preferred_element_type=jnp.float32)
    act = (jax.nn.silu(gate_pre) * up_pre).astype(jnp.bfloat16)
    expert_out = contract(act, down_w, 1, 1)
    returned = collect(expert_out).reshape(tok, TOP, D)
    moe_branch = jnp.sum(gate_weights[:, :, None] * returned, 1)
    result = hidden + moe_branch
    layer_output = result.astype(jnp.bfloat16)
    grad_res = grad_output.astype(jnp.float32)
    routed_grad = (
        (gate_weights[:, :, None] * grad_res[:, None, :]).reshape(tok * TOP, D).astype(jnp.bfloat16)
    )
    expert_grad = dispatch(routed_grad)
    grad_act = jnp.dot(expert_grad, down_w, preferred_element_type=jnp.float32)
    grad_down = contract(expert_grad, act, 0, 0)
    sig = jax.nn.sigmoid(gate_pre)
    grad_gate_pre = (grad_act * up_pre * sig * (1.0 + gate_pre * (1.0 - sig))).astype(jnp.bfloat16)
    grad_up_pre = (grad_act * gate_pre * sig).astype(jnp.bfloat16)
    grad_gate = contract(expert_in, grad_gate_pre, 0, 0)
    grad_up = contract(expert_in, grad_up_pre, 0, 0)
    grad_in = contract(grad_gate_pre, gate_w, 1, 1) + contract(grad_up_pre, up_w, 1, 1)
    grad_normed_m = jnp.sum(collect(grad_in).reshape(tok, TOP, D), 1)
    grad_gain_m = jnp.sum(grad_normed_m * hidden * factor_m, 0)
    grad_hidden = grad_res + norm_back(hidden, factor_m, gain_m, grad_normed_m)
    grad_hidden_low = grad_hidden.astype(jnp.bfloat16)
    grad_attended = jnp.dot(grad_hidden_low, out_w, preferred_element_type=jnp.float32).astype(
        jnp.bfloat16
    )
    spread_hidden = jnp.broadcast_to(grad_hidden_low[:, None, :], (tok, n_uly, D))
    head_grad, head_hidden = (
        lax.all_to_all(
            grad_attended.reshape(tok, HEADS, HEAD_DIM),
            "ulysses",
            split_axis=1,
            concat_axis=0,
            tiled=True,
        ),
        lax.all_to_all(spread_hidden, "ulysses", split_axis=1, concat_axis=0, tiled=True),
    )
    grad_out_slice = contract(
        head_hidden[:, 0, :], mixed_low.reshape(group, heads_dev * HEAD_DIM), 0, 0
    )
    delta = jnp.transpose(jnp.sum(head_grad.astype(jnp.float32) * mixed, -1))
    total_keys = group * n_blk
    zero_q = jnp.zeros((group, heads_dev, HEAD_DIM), jnp.float32)
    fold_start = (
        zero_q,
        jnp.zeros((total_keys, HEAD_DIM), jnp.float32),
        jnp.zeros((total_keys, HEAD_DIM), jnp.float32),
    )
    state = fold_start
    key_rows = lax.all_gather(key_local, "blk", axis=0, tiled=True)
    value_rows = lax.all_gather(value_local, "blk", axis=0, tiled=True)
    key_blocks, grads_size = split_blocks(key_rows)
    value_blocks, _ = split_blocks(value_rows)

    def grads_step(inner, item):
        key_blk, value_blk, number = item
        k_start = number * grads_size
        live = (k_start <= q_pos[-1]) & (k_start + grads_size - 1 >= q_begin[0])

        def grads_work(current):
            part_q, part_k, part_v = backward_block(
                head_q, head_grad, lse, delta, q_pos, q_begin, key_blk, value_blk, k_start, scale
            )
            grad_q, grad_keys, grad_values = current
            grad_keys = lax.dynamic_update_slice_in_dim(
                grad_keys,
                lax.dynamic_slice_in_dim(grad_keys, k_start, grads_size, 0) + part_k,
                k_start,
                0,
            )
            grad_values = lax.dynamic_update_slice_in_dim(
                grad_values,
                lax.dynamic_slice_in_dim(grad_values, k_start, grads_size, 0) + part_v,
                k_start,
                0,
            )
            return (grad_q + part_q, grad_keys, grad_values)

        return (lax.cond(live, grads_work, lambda current: current, inner), None)

    state, _ = lax.scan(
        grads_step,
        state,
        (key_blocks, value_blocks, jnp.arange(key_blocks.shape[0], dtype=jnp.int32)),
    )
    grad_q = state[0]
    grad_k, grad_v = (
        lax.psum_scatter(state[1], "blk", scatter_dimension=0, tiled=True),
        lax.psum_scatter(state[2], "blk", scatter_dimension=0, tiled=True),
    )
    group_places = q_pos - q_begin
    grad_q_pre = rotate(grad_q.astype(jnp.bfloat16).astype(jnp.float32), group_places, -1.0).astype(
        jnp.bfloat16
    )
    grad_query_slice = contract(normed_group, grad_q_pre.reshape(group, heads_dev * HEAD_DIM), 0, 0)
    token_q, token_k, token_v = (
        lax.all_to_all(grad_q_pre, "ulysses", split_axis=0, concat_axis=1, tiled=True),
        lax.all_to_all(
            grad_k.astype(jnp.bfloat16)[:, None, :],
            "ulysses",
            split_axis=0,
            concat_axis=1,
            tiled=True,
        ),
        lax.all_to_all(
            grad_v.astype(jnp.bfloat16)[:, None, :],
            "ulysses",
            split_axis=0,
            concat_axis=1,
            tiled=True,
        ),
    )
    summed_k = []
    summed_v = []
    for head in range(KV_HEADS):
        members = [c for c in range(n_uly) if which[c] == head]
        summed_k.append(sum((token_k[:, c].astype(jnp.float32) for c in members)))
        summed_v.append(sum((token_v[:, c].astype(jnp.float32) for c in members)))
    grad_key_heads = jnp.stack(summed_k, 1)
    grad_value_heads = jnp.stack(summed_v, 1)
    grad_query_pre = token_q.reshape(tok, q_width)
    grad_key_pre = rotate(grad_key_heads, places, -1.0).reshape(tok, kv_width)
    grad_keyval_pre = jnp.concatenate(
        [grad_key_pre, grad_value_heads.reshape(tok, kv_width)], 1
    ).astype(jnp.bfloat16)
    grad_normed_a = contract(grad_query_pre, query_w, 1, 1) + contract(
        grad_keyval_pre, keyval_w, 1, 1
    )
    grad_keyval_w = contract(normed_a, grad_keyval_pre, 0, 0)
    grad_gain_a = jnp.sum(grad_normed_a * inputs * factor_a, 0)
    grad_input = grad_hidden + norm_back(inputs, factor_a, gain_a, grad_normed_a)
    n_dev = n_blk * n_uly
    squares = jnp.stack(
        [
            jnp.sum(attn_branch * attn_branch),
            jnp.sum(moe_branch * moe_branch),
            jnp.sum(result * result),
        ]
    )
    square_rows = jnp.broadcast_to(squares[None, :], (n_dev, 3))
    part_gate, part_up, part_down, uly_gain_a, uly_gain_m, uly_keyval, uly_squares = (
        lax.psum_scatter(
            grad_gate.astype(jnp.bfloat16), "ulysses", scatter_dimension=0, tiled=True
        ).astype(jnp.float32),
        lax.psum_scatter(
            grad_up.astype(jnp.bfloat16), "ulysses", scatter_dimension=0, tiled=True
        ).astype(jnp.float32),
        lax.psum_scatter(
            grad_down.astype(jnp.bfloat16), "ulysses", scatter_dimension=0, tiled=True
        ).astype(jnp.float32),
        lax.psum_scatter(
            reorder_rows(grad_gain_a, n_blk, n_uly).astype(jnp.bfloat16),
            "ulysses",
            scatter_dimension=0,
            tiled=True,
        ).astype(jnp.float32),
        lax.psum_scatter(
            reorder_rows(grad_gain_m, n_blk, n_uly).astype(jnp.bfloat16),
            "ulysses",
            scatter_dimension=0,
            tiled=True,
        ).astype(jnp.float32),
        lax.psum_scatter(
            reorder_rows(grad_keyval_w, n_blk, n_uly).astype(jnp.bfloat16),
            "ulysses",
            scatter_dimension=0,
            tiled=True,
        ).astype(jnp.float32),
        lax.psum_scatter(
            square_rows.astype(jnp.bfloat16), "ulysses", scatter_dimension=0, tiled=True
        ).astype(jnp.float32),
    )
    part_outw, part_query, part_gain_a, part_gain_m, part_keyval, square_row = (
        lax.psum_scatter(grad_out_slice, "blk", scatter_dimension=0, tiled=True),
        lax.psum_scatter(grad_query_slice, "blk", scatter_dimension=0, tiled=True),
        lax.psum_scatter(uly_gain_a, "blk", scatter_dimension=0, tiled=True),
        lax.psum_scatter(uly_gain_m, "blk", scatter_dimension=0, tiled=True),
        lax.psum_scatter(uly_keyval, "blk", scatter_dimension=0, tiled=True),
        lax.psum_scatter(uly_squares, "blk", scatter_dimension=0, tiled=True),
    )
    branch_rms = jnp.sqrt(square_row[0] / (tok * n_dev * D))
    return (
        layer_output,
        grad_input,
        part_gain_a,
        part_gain_m,
        part_query,
        part_keyval,
        part_outw,
        part_gate,
        part_up,
        part_down,
        branch_rms,
    )


MESH = pl.DeviceIdType.MESH
LANES = 128
LOG2E = 1.4426950408889634


class Place:
    def __init__(self, depth):
        self.blk = lax.axis_index("blk")
        self.u = lax.axis_index("ulysses")
        self.depth = depth
        self.z = self.blk // 4
        self.x = (self.blk // 2) % 2
        self.c = self.blk % 2
        self.up = (self.blk + 4, self.u)
        self.down = (self.blk - 4, self.u)
        self.across = (self.blk + 2 - 4 * self.x, self.u)
        self.sibling = (self.blk + 1 - 2 * self.c, self.u)
        self.other = (self.blk, 1 - self.u)
        self.has_up = self.z < depth - 1
        self.has_down = self.z > 0

    def slot(self, z, x, c):
        return z * 4 + x * 2 + c

    def greet(self, sibling=False, other=False, plane=True):
        barrier = pltpu.get_barrier_semaphore()

        def hail(device):
            pl.semaphore_signal(barrier, inc=1, device_id=device, device_id_type=MESH)

        count = 0
        if plane:
            hail(self.across)
            pl.when(self.has_up)(lambda: hail(self.up))
            pl.when(self.has_down)(lambda: hail(self.down))
            count = 1 + self.has_up.astype(jnp.int32) + self.has_down.astype(jnp.int32)
        if sibling:
            hail(self.sibling)
            count = count + 1
        if other:
            hail(self.other)
            count = count + 1
        pl.semaphore_wait(barrier, count)


class Wires:
    def __init__(self, sems):
        self.sems = sems
        self.used = 0

    def take(self, count):
        base = self.used
        self.used += count
        return lambda index: self.sems.at[base + index]


def each(act, items):
    for item in items:
        act(item)


def remote(src, dst, send, recv, device):
    return pltpu.make_async_remote_copy(
        src_ref=src, dst_ref=dst, send_sem=send, recv_sem=recv, device_id=device, device_id_type=MESH
    )


class Gather:
    def __init__(self, place, wires, src, out, cores):
        self.p, self.src, self.out, self.cores = place, src, out, cores
        n = place.depth
        self.s_up, self.s_down, self.s_across = wires.take(n), wires.take(n), wires.take(n)
        self.r_z, self.r_x = wires.take(n), wires.take(n)
        if cores:
            self.s_core, self.r_core = wires.take(2 * n), wires.take(2 * n)
        self.own = wires.take(1)(0)

    def _send(self, zz, xx, kind, src=None):
        p = self.p
        dst = self.out(zz, xx, p.c)
        src = dst if src is None else src
        if kind == "up":
            return remote(src, dst, self.s_up(zz), self.r_z(zz), p.up)
        if kind == "down":
            return remote(src, dst, self.s_down(zz), self.r_z(zz), p.down)
        if kind == "across":
            return remote(src, dst, self.s_across(zz), self.r_x(zz), p.across)
        return remote(src, dst, self.s_core(zz * 2 + xx), self.r_core(zz * 2 + xx), p.sibling)

    def _keep(self):
        p = self.p
        return pltpu.make_async_copy(self.src, self.out(p.z, p.x, p.c), self.own)

    def start(self, in_place=False):
        p = self.p
        self.in_place = in_place
        src = None if in_place else self.src
        pl.when(p.has_up)(lambda: self._send(p.z, p.x, "up", src).start())
        pl.when(p.has_down)(lambda: self._send(p.z, p.x, "down", src).start())
        self._send(p.z, p.x, "across", src).start()
        if self.cores:
            self._send(p.z, p.x, "core", src).start()
        if not in_place:
            self._keep().start()

    def hop(self, d):
        p = self.p

        def low():
            zz = p.z - d
            self._send(zz, p.x, "up").wait_recv()
            pl.when(p.has_up)(lambda: self._send(zz, p.x, "up").start())
            self._send(zz, p.x, "across").start()
            if self.cores:
                self._send(zz, p.x, "core").start()

        def high():
            zz = p.z + d
            self._send(zz, p.x, "down").wait_recv()
            pl.when(p.has_down)(lambda: self._send(zz, p.x, "down").start())
            self._send(zz, p.x, "across").start()
            if self.cores:
                self._send(zz, p.x, "core").start()

        pl.when(p.z >= d)(low)
        pl.when(p.z + d < p.depth)(high)

    def cross(self, d):
        p = self.p

        def take(zz):
            self._send(zz, 1 - p.x, "across").wait_recv()
            if self.cores:
                self._send(zz, 1 - p.x, "core").start()

        if d == 0:
            take(p.z)
        else:
            pl.when(p.z >= d)(lambda: take(p.z - d))
            pl.when(p.z + d < p.depth)(lambda: take(p.z + d))

    def finish(self):
        p = self.p
        for zz in range(p.depth):
            if self.cores:
                for xx in range(2):
                    self._send(zz, xx, "core").wait()
            self._send(zz, p.x, "across").wait_send()
            pl.when(p.has_up & (p.z >= zz))(lambda zz=zz: self._send(zz, p.x, "up").wait_send())
            pl.when(p.has_down & (p.z <= zz))(lambda zz=zz: self._send(zz, p.x, "down").wait_send())
        if not self.in_place:
            self._keep().wait()


def gather_kernel(depth, cores, src, out, sems):
    place = Place(depth)
    place.greet(sibling=cores)
    wires = Wires(sems)
    if cores:
        view = lambda z, x, c: out.at[place.slot(z, x, c)]
    else:
        view = lambda z, x, c: out.at[z * 2 + x]
    g = Gather(place, wires, src, view, cores)
    g.start()
    for d in range(1, depth):
        g.hop(d)
        g.cross(d - 1)
    g.cross(depth - 1)
    g.finish()


def gather_plane(block, depth, cores, cid):
    slots = depth * (4 if cores else 2)
    return pl.pallas_call(
        functools.partial(gather_kernel, depth, cores),
        out_shape=jax.ShapeDtypeStruct((slots,) + block.shape, block.dtype),
        in_specs=[pl.BlockSpec(memory_space=pl.ANY)],
        out_specs=pl.BlockSpec(memory_space=pl.ANY),
        scratch_shapes=[pltpu.SemaphoreType.DMA((16 * depth,))],
        compiler_params=pltpu.CompilerParams(collective_id=cid, has_side_effects=True),
        name="gather_%d" % cid,
    )(block)


def opening_kernel(
    depth, w_own, x_own, dy_own, g_own, e0, e1, e2, w_all, x_all, dy_all, g_all, f0, f1, f2, sems
):
    p = Place(depth)
    p.greet(sibling=True, other=True)
    wires = Wires(sems)
    u = p.u
    mine = Gather(p, wires, w_own.at[u], lambda z, x, c: w_all.at[p.slot(z, x, c), u], True)
    peer = Gather(p, wires, None, lambda z, x, c: w_all.at[p.slot(z, x, c), 1 - u], True)
    dys = Gather(p, wires, dy_own, lambda z, x, c: dy_all.at[z * 2 + x], False)
    gws = Gather(p, wires, g_own, lambda z, x, c: g_all.at[z * 2 + x], False)
    ws, wr = wires.take(1)(0), wires.take(1)(0)
    xs, xr, xl = wires.take(1)(0), wires.take(1)(0), wires.take(1)(0)
    es, er, el = wires.take(3), wires.take(3), wires.take(3)
    cs, cr = wires.take(6), wires.take(6)
    half = e0.shape[0]
    cols = e0.shape[1]

    def part(ref, row, core):
        return ref.at[
            pl.ds(pl.multiple_of(row * half, half), half), pl.ds(pl.multiple_of(core * cols, LANES), cols)
        ]

    w_swap = remote(w_own.at[1 - u], w_all.at[p.blk, u], ws, wr, p.other)
    w_swap.start()
    mine.start()
    gws.start()
    x_swap = remote(x_own, x_all.at[u], xs, xr, p.other)
    x_swap.start()
    x_keep = pltpu.make_async_copy(x_own, x_all.at[u], xl)
    x_keep.start()
    experts = ((e0, f0), (e1, f1), (e2, f2))
    swaps = [remote(e, part(f, u, p.c), es(i), er(i), p.other) for i, (e, f) in enumerate(experts)]
    keeps = [pltpu.make_async_copy(e, part(f, u, p.c), el(i)) for i, (e, f) in enumerate(experts)]
    shares = [remote(e, part(f, u, p.c), cs(i), cr(i), p.sibling) for i, (e, f) in enumerate(experts)]
    passes = [
        remote(part(f, 1 - u, p.c), part(f, 1 - u, p.c), cs(3 + i), cr(3 + i), p.sibling)
        for i, (e, f) in enumerate(experts)
    ]
    for i in range(3):
        swaps[i].start()
        keeps[i].start()
        shares[i].start()
    w_swap.wait_recv()
    peer.start(in_place=True)
    dys.start()
    for d in range(1, depth):
        for g in (mine, peer, gws, dys):
            g.hop(d)
            g.cross(d - 1)
    for g in (mine, peer, gws, dys):
        g.cross(depth - 1)
    for i in range(3):
        swaps[i].wait_recv()
        passes[i].start()
    w_swap.wait_send()
    x_swap.wait()
    x_keep.wait()
    for i in range(3):
        swaps[i].wait_send()
        keeps[i].wait()
        shares[i].wait()
        passes[i].wait()
    for g in (mine, peer, gws, dys):
        g.finish()


def opening(w_own, x_own, dy_own, g_own, e0, e1, e2, depth, cid):
    shape = jax.ShapeDtypeStruct
    bf = jnp.bfloat16
    expert = shape((2 * e0.shape[0], 2 * e0.shape[1]), bf)
    return pl.pallas_call(
        functools.partial(opening_kernel, depth),
        out_shape=(
            shape((4 * depth,) + w_own.shape, bf),
            shape((2,) + x_own.shape, bf),
            shape((2 * depth,) + dy_own.shape, bf),
            shape((2 * depth,) + g_own.shape, jnp.float32),
            expert,
            expert,
            expert,
        ),
        in_specs=[pl.BlockSpec(memory_space=pl.ANY)] * 7,
        out_specs=tuple([pl.BlockSpec(memory_space=pl.ANY)] * 7),
        scratch_shapes=[pltpu.SemaphoreType.DMA((2 * 40 + 2 * 24 + 40,))],
        compiler_params=pltpu.CompilerParams(collective_id=cid, has_side_effects=True),
        name="opening",
    )(w_own, x_own, dy_own, g_own, e0, e1, e2)


class Scatter:
    def __init__(self, place, wires, part, out, rx, rz, pieces, down_only=False):
        self.p, self.part, self.out, self.rx, self.rz = place, part, out, rx, rz
        n = place.depth
        total = n * pieces
        self.pieces, self.down_only = pieces, down_only
        self.sx, self.cx = wires.take(total), wires.take(total)
        self.sz, self.cu, self.cd = wires.take(total), wires.take(total), wires.take(total)
        order = []
        low, high = 0, n - 1
        while low <= high:
            if not down_only:
                order.append(high)
            if low != high or down_only:
                order.append(low)
            if down_only:
                low = low + 1
            else:
                low, high = low + 1, high - 1
        self.order = order
        self.items = [(zz, k) for zz in order for k in range(pieces)]

    def _x(self, zz, k):
        i = zz * self.pieces + k
        return remote(self.part(zz, 1 - self.p.x, k), self.rx(zz, k), self.sx(i), self.cx(i), self.p.across)

    def _up(self, zz, k):
        i = zz * self.pieces + k
        return remote(self.rx(zz, k), self.rz(zz, k), self.sz(i), self.cu(i), self.p.up)

    def _down(self, zz, k, z):
        i = zz * self.pieces + k
        slot = self.p.depth if zz == z - 1 else zz
        return remote(self.rx(zz, k), self.rz(slot, k), self.sz(i), self.cd(i), self.p.down)

    def _live(self, zz, act):
        if self.down_only and zz > 0:
            pl.when(self.p.z >= zz)(act)
        else:
            act()

    def begin(self, t):
        if t < len(self.items):
            zz, k = self.items[t]
            self._live(zz, lambda: self._x(zz, k).start())

    def _pass(self, zz, k, more):
        p = self.p
        total = self.part(zz, p.x, k)[...].astype(jnp.float32) + self.rx(zz, k)[...].astype(jnp.float32)
        if more:
            total = total + self.rz(zz, k)[...].astype(jnp.float32)
        self.rx(zz, k)[...] = total.astype(jnp.bfloat16)

    def land(self, t):
        if t < 0 or t >= len(self.items):
            return
        p = self.p
        n = p.depth
        zz, k = self.items[t]
        self._live(zz, lambda: self._x(zz, k).wait_recv())

        def climb():
            self._pass(zz, k, False)
            self._up(zz, k).start()

        def sink():
            self._pass(zz, k, False)
            self._down(zz, k, n - 1).start()

        if zz > 0 and not self.down_only:
            pl.when(p.z == 0)(climb)
        if zz < n - 1:
            pl.when(p.z == n - 1)(sink)

    def chain(self, t, h):
        if t < 0 or t >= len(self.items):
            return
        p = self.p
        n = p.depth
        zz, k = self.items[t]
        low, high = h, n - 1 - h

        def from_low():
            self._up(zz, k).wait_recv()
            if zz > low:
                self._pass(zz, k, True)
                self._up(zz, k).start()

        def from_high():
            self._down(zz, k, high + 1).wait_recv()
            if zz < high:
                self._pass(zz, k, True)
                self._down(zz, k, high).start()

        if zz >= low and not self.down_only:
            pl.when(p.z == low)(from_low)
        if zz <= high:
            pl.when(p.z == high)(from_high)

    def step(self, t):
        self.land(t)
        for h in range(1, self.p.depth):
            self.chain(t - h, h)

    def steps(self):
        return len(self.items) + self.p.depth - 1

    def finish(self):
        p = self.p
        n = p.depth
        for zz, k in self.items:
            self._live(zz, lambda zz=zz, k=k: self._x(zz, k).wait_send())
            if not self.down_only:
                pl.when(p.z < zz)(lambda zz=zz, k=k: self._up(zz, k).wait_send())
            pl.when(p.z > zz)(lambda zz=zz, k=k: self._down(zz, k, zz + 1).wait_send())

            def store(zz=zz, k=k):
                total = self.part(zz, p.x, k)[...].astype(jnp.float32)
                total = total + self.rx(zz, k)[...].astype(jnp.float32)
                if zz > 0 and not self.down_only:
                    total = total + self.rz(zz, k)[...].astype(jnp.float32)
                if zz < n - 1:
                    total = total + self.rz(n, k)[...].astype(jnp.float32)
                self.out(k)[...] = total

            pl.when(p.z == zz)(store)


class CoreScatter:
    def __init__(self, place, wires, src, rc, out, rx, rz, down_only=False):
        self.p, self.src, self.rc = place, src, rc
        n = place.depth
        self.sc, self.cc = wires.take(2 * n), wires.take(2 * n)
        self.plane = Scatter(
            place, wires, lambda zz, xx, k: rc.at[zz * 2 + xx], lambda k: out,
            lambda zz, k: rx.at[zz], lambda slot, k: rz.at[slot], 1, down_only,
        )
        self.order = self.plane.order

    def _trade(self, zz, xx):
        p = self.p
        i = zz * 2 + xx
        return remote(self.src.at[p.slot(zz, xx, 1 - p.c)], self.rc.at[i], self.sc(i), self.cc(i), p.sibling)

    def trade(self, t):
        zz = self.order[t]
        self.plane._live(zz, lambda: each(lambda xx: self._trade(zz, xx).start(), (1 - self.p.x, self.p.x)))

    def join(self, t):
        p = self.p
        zz = self.order[t]

        def act():
            for xx in (1 - p.x, p.x):
                self._trade(zz, xx).wait_recv()
                at = zz * 2 + xx
                self.rc[at] = (
                    self.src[p.slot(zz, xx, p.c)].astype(jnp.float32) + self.rc[at].astype(jnp.float32)
                ).astype(jnp.bfloat16)

        self.plane._live(zz, act)
        self.plane.begin(t)

    def release(self):
        for zz in self.order:
            self.plane._live(zz, lambda zz=zz: each(lambda xx: self._trade(zz, xx).wait_send(), range(2)))

    def finish(self):
        self.plane.finish()


def scatter_kernel(depth, pieces, window, count, *refs):
    ins, outs = refs[:count], refs[count : 2 * count]
    rx, rz, sems = refs[2 * count :]
    p = Place(depth)
    p.greet()
    wires = Wires(sems)
    rows = outs[0].shape[0] // pieces

    def cut(ref, k):
        return ref.at[pl.ds(k * rows, rows)]

    jobs = []
    for a in range(count):
        jobs.append(
            Scatter(
                p, wires,
                lambda zz, xx, k, a=a: cut(ins[a].at[zz * 2 + xx], k),
                lambda k, a=a: cut(outs[a], k),
                lambda zz, k, a=a: cut(rx.at[a, zz], k),
                lambda slot, k, a=a: cut(rz.at[a, slot], k),
                pieces,
            )
        )
    for t in range(window):
        jobs[0].begin(t)
    for a, job in enumerate(jobs):
        total = len(job.items)
        for t in range(job.steps()):
            job.step(t)
            if t + window < total:
                job.begin(t + window)
            elif a + 1 < count and t + window - total < window:
                jobs[a + 1].begin(t + window - total)
    for job in jobs:
        job.finish()


def scatter_plane(arrays, depth, pieces, cid, window=3):
    count = len(arrays)
    block = arrays[0].shape[1:]
    bf = jnp.bfloat16
    return pl.pallas_call(
        functools.partial(scatter_kernel, depth, pieces, window, count),
        out_shape=tuple([jax.ShapeDtypeStruct(block, jnp.float32)] * count),
        in_specs=[pl.BlockSpec(memory_space=pltpu.VMEM)] * count,
        out_specs=tuple([pl.BlockSpec(memory_space=pltpu.VMEM)] * count),
        scratch_shapes=[
            pltpu.VMEM((count, depth) + block, bf),
            pltpu.VMEM((count, depth + 1) + block, bf),
            pltpu.SemaphoreType.DMA((count * 5 * depth * pieces,)),
        ],
        compiler_params=pltpu.CompilerParams(
            collective_id=cid, has_side_effects=True, vmem_limit_bytes=56 * 2**20
        ),
        name="scatter_%d" % cid,
    )(*arrays)


def mm(left, right):
    return jnp.dot(left, right, preferred_element_type=jnp.float32)


def flip(tile):
    return tile.astype(jnp.float32).T.astype(jnp.bfloat16)


def hidden_bias(first_key, first_query, begin, keys):
    queries = begin.shape[1]
    k_pos = first_key + lax.broadcasted_iota(jnp.int32, (keys, queries), 0)
    q_pos = first_query + lax.broadcasted_iota(jnp.int32, (keys, queries), 1)
    return jnp.where((k_pos >= begin) & (k_pos <= q_pos), 0.0, NEG)


def attend_kernel(scale, blk_ref, q_ref, kv_ref, begin_ref, o_ref, ot_ref, lse_ref, qt, top, total):
    group = q_ref.shape[0]
    heads = q_ref.shape[1] // HEAD_DIM
    blk = blk_ref[0]
    for h in range(heads):
        qt[:, h * group : (h + 1) * group] = flip(q_ref[:, h * HEAD_DIM : (h + 1) * HEAD_DIM])
    top[...] = jnp.full(top.shape, NEG, jnp.float32)
    total[...] = jnp.zeros(total.shape, jnp.float32)
    ot_ref[...] = jnp.zeros(ot_ref.shape, jnp.float32)

    def tile(j, carry):
        k = kv_ref[j, :, :HEAD_DIM]
        vt = flip(kv_ref[j, :, HEAD_DIM:])
        bias = hidden_bias(j * group, blk * group, begin_ref[0:1, :], group)
        for h in range(heads):
            at = slice(h * group, (h + 1) * group)
            s = mm(k, qt[:, at]) * (scale * LOG2E) + bias
            old = top[0:1, at]
            new = jnp.maximum(old, jnp.max(s, axis=0, keepdims=True))
            w = jnp.exp2(s - new)
            keep = jnp.exp2(old - new)
            total[0:1, at] = total[0:1, at] * keep + jnp.sum(w, axis=0, keepdims=True)
            ot_ref[:, at] = ot_ref[:, at] * keep + mm(vt, w.astype(jnp.bfloat16))
            top[0:1, at] = new
        return carry

    lax.fori_loop(0, blk + 1, tile, 0)
    sums = total[0:1, :]
    lse_ref[...] = jnp.broadcast_to(top[0:1, :] + jnp.log2(sums), lse_ref.shape)
    ot_ref[...] = ot_ref[...] / sums
    for h in range(heads):
        o_ref[:, h * HEAD_DIM : (h + 1) * HEAD_DIM] = ot_ref[:, h * group : (h + 1) * group].T.astype(
            jnp.bfloat16
        )


def attend(blk, q, kv, begin, scale):
    group, width = q.shape
    rows = width // HEAD_DIM * group
    vmem = pl.BlockSpec(memory_space=pltpu.VMEM)
    return pl.pallas_call(
        functools.partial(attend_kernel, scale),
        out_shape=(
            jax.ShapeDtypeStruct(q.shape, jnp.bfloat16),
            jax.ShapeDtypeStruct((HEAD_DIM, rows), jnp.float32),
            jax.ShapeDtypeStruct((8, rows), jnp.float32),
        ),
        in_specs=[pl.BlockSpec(memory_space=pltpu.SMEM), vmem, vmem, vmem],
        out_specs=(vmem, vmem, vmem),
        scratch_shapes=[
            pltpu.VMEM((HEAD_DIM, rows), jnp.bfloat16),
            pltpu.VMEM((8, rows), jnp.float32),
            pltpu.VMEM((8, rows), jnp.float32),
        ],
        compiler_params=pltpu.CompilerParams(vmem_limit_bytes=48 * 2**20),
        name="attend",
    )(blk, q, kv, begin)


def closing_kernel(
    depth, scale, attn_sq, dhr, dh, hid, x, gain, w, a, q, o, kv, begin, ot, lse, cosine, sine, zp, gm, e0, e1, e2,
    out, gin, gq, go, gkv, gg, f0, f1, f2, sq,
    dhr_all, qt, dot_, dqt, delta, dkv, do, dq, at, acc,
    z_sum, z_rx, z_rz, go_p, go_rc, go_rx, go_rz, kv_sum, kv_rc, kv_rx, kv_rz,
    gq_rc, gq_rx, gq_rz, gk_p, gk_sum, gk_rc, gk_rx, gk_rz,
    e_own, e_core, e_low, e_peer, da_out, da_in, t_out, t_in, sq_own, sems,
):
    f32, bf = jnp.float32, jnp.bfloat16
    p = Place(depth)
    p.greet(sibling=True, other=True)
    wires = Wires(sems)
    u, blk = p.u, p.blk
    tok = x.shape[0]
    group, q_half = q.shape
    heads = q_half // HEAD_DIM
    kv_half = 2 * HEAD_DIM
    blocks = kv.shape[0]
    out_at = q_half + kv_half + LANES
    rows_blk = gq.shape[0]

    cols = f0.shape[1]
    rows_e = f0.shape[0]
    es, er, el, ps, pr = wires.take(3), wires.take(3), wires.take(3), wires.take(3), wires.take(3)

    def e_cols(ref, core):
        return ref.at[:, pl.ds(pl.multiple_of(core * cols, LANES), cols)]

    def e_rows(member):
        return pl.ds(pl.multiple_of(member * rows_e, rows_e), rows_e)

    experts = (e0, e1, e2)
    e_trade = [remote(e_cols(e, 1 - p.c), e_core.at[i], es(i), er(i), p.sibling) for i, e in enumerate(experts)]
    e_keep = [pltpu.make_async_copy(e_cols(e, p.c), e_own.at[i], el(i)) for i, e in enumerate(experts)]
    e_swap = [remote(e_low.at[i], e_peer.at[i], ps(i), pr(i), p.other) for i in range(3)]

    def e_join(i):
        e_trade[i].wait_recv()
        e_keep[i].wait()
        theirs = e_rows(1 - u)
        e_low[i] = (e_own[i, theirs, :].astype(f32) + e_core[i, theirs, :].astype(f32)).astype(bf)
        e_swap[i].start()

    def e_done(i):
        e_swap[i].wait_recv()
        mine = e_rows(u)
        total = e_own[i, mine, :].astype(f32) + e_core[i, mine, :].astype(f32)
        (f0, f1, f2)[i][...] = total + e_peer[i].astype(f32)

    ds, dr, dl = wires.take(1)(0), wires.take(1)(0), wires.take(1)(0)
    swap = remote(dhr, dhr_all.at[u], ds, dr, p.other)
    keep = pltpu.make_async_copy(dhr, dhr_all.at[u], dl)

    pieces = 2
    z_rows = tok // pieces

    def cut(ref, k):
        return ref.at[pl.ds(k * z_rows, z_rows)]

    zs = Scatter(
        p, wires,
        lambda zz, xx, k: cut(zp.at[zz * 2 + xx], k),
        lambda k: cut(z_sum, k),
        lambda zz, k: cut(z_rx.at[zz], k),
        lambda slot, k: cut(z_rz.at[slot], k),
        pieces,
    )
    gos = CoreScatter(p, wires, go_p, go_rc, go, go_rx, go_rz)
    kvs = CoreScatter(p, wires, dkv, kv_rc, kv_sum, kv_rx, kv_rz, down_only=True)
    gqs = CoreScatter(p, wires, go_p, gq_rc, gq, gq_rx, gq_rz)
    gks = CoreScatter(p, wires, gk_p, gk_rc, gk_sum, gk_rx, gk_rz)
    sqs = Gather(p, wires, sq_own, lambda z, xx, c: sq.at[p.slot(z, xx, c), u], True)
    qs, qr = wires.take(1)(0), wires.take(1)(0)
    sq_swap = remote(sq.at[:, u], sq.at[:, u], qs, qr, p.other)

    swap.start()
    keep.start()
    window = 3
    for t in range(window):
        zs.begin(t)
    for i in range(3):
        e_trade[i].start()
        e_keep[i].start()

    def z_step(t):
        zs.step(t)
        zs.begin(t + window)

    for h in range(heads):
        qt[:, h * group : (h + 1) * group] = flip(q[:, h * HEAD_DIM : (h + 1) * HEAD_DIM])
    dqt[...] = jnp.zeros(dqt.shape, f32)
    dkv[...] = jnp.zeros(dkv.shape, bf)
    for i in range(3):
        e_join(i)
    z_step(0)
    keep.wait()
    swap.wait_recv()

    for h in range(heads):
        cs = slice(h * HEAD_DIM, (h + 1) * HEAD_DIM)
        hs = slice(h * group, (h + 1) * group)
        ws = slice(out_at + h * HEAD_DIM, out_at + (h + 1) * HEAD_DIM)
        part = jnp.concatenate([mm(dhr_all[m], w[:, ws]) for m in range(2)], 0).astype(bf)
        do[:, cs] = part
        turned = part.astype(f32).T
        dot_[:, hs] = turned.astype(bf)
        delta[0:1, hs] = jnp.sum(turned * ot[:, hs], axis=0, keepdims=True)
    for m in range(2):
        at[:, m * tok : (m + 1) * tok] = flip(dhr_all[m])

    def out_rows(i, carry):
        rows = pl.ds(pl.multiple_of(i * rows_blk, rows_blk), rows_blk)
        go_p[i] = mm(at[rows, :], o[...]).astype(bf)
        return carry

    lax.fori_loop(0, blocks, out_rows, 0)
    for t in range(depth):
        gos.trade(t)

    background = {}

    def at_tile(j, act):
        background.setdefault(j, []).append(act)

    for t in range(1, zs.steps()):
        at_tile(min(t, blocks - 1), lambda t=t: z_step(t))
    for t in range(depth):
        at_tile(3 + t, lambda t=t: gos.join(t))
    for t in range(gos.plane.steps()):
        at_tile(8 + t, lambda t=t: gos.plane.step(t))

    def tile(j, carry):
        def work():
            k = kv[j, :, :HEAD_DIM]
            v = kv[j, :, HEAD_DIM:]
            kt = flip(k)
            bias = hidden_bias(j * group, blk * group, begin[0:1, :], group)
            dk = jnp.zeros((group, HEAD_DIM), f32)
            dv = jnp.zeros((group, HEAD_DIM), f32)
            for h in range(heads):
                hs = slice(h * group, (h + 1) * group)
                cs = slice(h * HEAD_DIM, (h + 1) * HEAD_DIM)
                s = mm(k, qt[:, hs]) * (scale * LOG2E) + bias
                e = jnp.exp2(s - lse[0:1, hs])
                g = (e * (mm(v, dot_[:, hs]) - delta[0:1, hs])).astype(bf)
                dqt[:, hs] += mm(kt, g)
                dk += mm(g, q[:, cs])
                dv += mm(e.astype(bf), do[:, cs])
            dkv[j, :, :HEAD_DIM] = (dk * scale).astype(bf)
            dkv[j, :, HEAD_DIM:] = dv.astype(bf)

        pl.when(j <= blk)(work)
        for when, acts in background.items():
            pl.when(j == when)(lambda acts=acts: each(lambda act: act(), acts))
        return carry

    lax.fori_loop(0, blocks, tile, 0)

    for t in range(depth):
        kvs.trade(t)
    gos.release()

    def back_turn(values):
        return values * cosine[...] - pltpu.roll(values, HEAD_DIM // 2, 1) * sine[...]

    for h in range(heads):
        hs = slice(h * group, (h + 1) * group)
        cs = slice(h * HEAD_DIM, (h + 1) * HEAD_DIM)
        dq[:, cs] = back_turn((dqt[:, hs] * scale).T.astype(bf).astype(f32)).astype(bf)
    for t in range(depth):
        kvs.join(t)
    kvs.plane.step(0)
    for j in range(0, D, 256):
        at[j : j + 256, :] = flip(a[:, j : j + 256])
    kvs.plane.step(1)

    def query_rows(i, carry):
        rows = pl.ds(pl.multiple_of(i * rows_blk, rows_blk), rows_blk)
        go_p[i] = mm(at[rows, :], dq[...]).astype(bf)
        return carry

    lax.fori_loop(0, blocks // 2, query_rows, 0)
    kvs.plane.step(2)
    lax.fori_loop(blocks // 2, blocks, query_rows, 0)
    kvs.plane.step(3)
    for m in range(2):
        for cb in range(0, D, 512):
            acc[m * tok : (m + 1) * tok, cb : cb + 512] = contract(
                dq[m * tok : (m + 1) * tok, :], w[cb : cb + 512, :q_half], 1, 1
            )
    for t in range(4, kvs.plane.steps()):
        kvs.plane.step(t)
    kvs.release()
    kvs.finish()
    kv_low = kv_sum[...].astype(bf).astype(f32)
    kv_pre = jnp.concatenate([back_turn(kv_low[:, :HEAD_DIM]).astype(bf), kv_low[:, HEAD_DIM:].astype(bf)], 1)

    da_s, da_r = wires.take(3), wires.take(3)
    wide = D // 3
    da_swaps = []
    for i in range(3):
        cb = i * wide
        part = contract(kv_pre, w[cb : cb + wide, q_half : q_half + kv_half], 1, 1)
        acc[:, cb : cb + wide] += part
        theirs = pl.ds(pl.multiple_of((1 - u) * tok, tok), tok)
        da_out[i] = acc[theirs, cb : cb + wide].astype(bf)
        da_swaps.append(remote(da_out.at[i], da_in.at[i], da_s(i), da_r(i), p.other))
        da_swaps[i].start()
    for t in range(depth):
        gqs.trade(t)

    def keyval_rows(i, carry):
        rows = pl.ds(pl.multiple_of(i * rows_blk, rows_blk), rows_blk)
        gk_p[i, :, :kv_half] = mm(at[rows, :], kv_pre).astype(bf)
        return carry

    lax.fori_loop(0, blocks, keyval_rows, 0)
    for t in range(depth):
        gqs.join(t)

    zs.finish()
    result = hid[...] + z_sum[...]
    out[...] = result.astype(bf)
    spread = lax.broadcasted_iota(jnp.int32, (8, LANES), 1)
    z_sq = jnp.sum(z_sum[...] * z_sum[...])
    r_sq = jnp.sum(result * result)
    sq_own[...] = jnp.where(
        spread == 0, attn_sq[0], jnp.where(spread == 1, z_sq, jnp.where(spread == 2, r_sq, 0.0))
    )
    sqs.start()
    gos.finish()
    for i in range(3):
        e_done(i)

    mine = pl.ds(pl.multiple_of(u * tok, tok), tok)
    for i in range(3):
        da_swaps[i].wait_recv()
        acc[mine, i * wide : (i + 1) * wide] += da_in[i].astype(f32)
    da = acc[mine, :]
    xf = x[...].astype(f32)
    r1 = lax.rsqrt(jnp.mean(xf * xf, -1, keepdims=True) + EPS)
    terms = (da * xf * r1).T
    weighted = da * gain[...]
    inner = jnp.mean(weighted * xf, -1, keepdims=True)
    gin[...] = dh[...] + r1 * weighted - xf * (r1 * r1 * r1 * inner)
    column = jnp.sum(terms, axis=1, keepdims=True)
    lane = lax.broadcasted_iota(jnp.int32, (D, LANES), 1)
    gain_cols = (jnp.where(lane == 0, column, 0.0) + gm[...].astype(f32)).astype(bf)
    for i in range(blocks):
        gk_p[i, :, kv_half:] = gain_cols[i * rows_blk : (i + 1) * rows_blk, :]
    for t in range(depth):
        gks.trade(t)
    sqs.hop(1)
    for t in range(depth):
        gks.join(t)
    steps = gqs.plane.steps()
    for t in range(steps):
        gqs.plane.step(t)
        gks.plane.step(t)
        if t + 2 < depth:
            sqs.hop(t + 2)
        if t < depth:
            sqs.cross(t)
    sqs.finish()
    sq_swap.start()
    gks.release()
    gks.finish()
    rows_dev = gkv.shape[0]
    theirs = pl.ds(pl.multiple_of((1 - u) * rows_dev, rows_dev), rows_dev)
    own = pl.ds(pl.multiple_of(u * rows_dev, rows_dev), rows_dev)
    t_out[...] = gk_sum[theirs, :]
    ts, tr = wires.take(1)(0), wires.take(1)(0)
    t_swap = remote(t_out, t_in, ts, tr, p.other)
    t_swap.start()
    gqs.release()
    gqs.finish()
    t_swap.wait_recv()
    for part in range(2):
        here = slice(part * HEAD_DIM, (part + 1) * HEAD_DIM)
        base = part * kv_half
        gkv[:, pl.ds(pl.multiple_of(base + u * HEAD_DIM, LANES), HEAD_DIM)] = gk_sum[own, here]
        gkv[:, pl.ds(pl.multiple_of(base + (1 - u) * HEAD_DIM, LANES), HEAD_DIM)] = t_in[:, here]
    gg[...] = gk_sum[own, kv_half:] + t_in[:, kv_half:]
    sq_swap.wait()
    t_swap.wait_send()
    swap.wait_send()
    for i in range(3):
        e_trade[i].wait_send()
        e_swap[i].wait_send()
        da_swaps[i].wait_send()


def closing(attn_sq, dhr, dh, hid, x, gain, w, a, q, o, kv, begin, ot, lse, cosine, sine, zp, gm, grads, depth, scale, cid):
    f32, bf = jnp.float32, jnp.bfloat16
    tok, width = x.shape
    group, q_half = q.shape
    blocks = kv.shape[0]
    rows_blk = width // blocks
    rows_e, cols = grads[0].shape[0] // 2, grads[0].shape[1] // 2
    kv_half = 2 * HEAD_DIM
    shape = jax.ShapeDtypeStruct
    vmem = pl.BlockSpec(memory_space=pltpu.VMEM)
    hbm = pl.BlockSpec(memory_space=pl.ANY)
    V = pltpu.VMEM

    def buffers(block):
        return [
            V((blocks // 2,) + block, bf),
            V((depth,) + block, bf),
            V((depth + 1,) + block, bf),
        ]

    grad = shape((rows_e, cols), f32)
    rows = q_half // HEAD_DIM * group
    return pl.pallas_call(
        functools.partial(closing_kernel, depth, scale),
        out_shape=(
            shape((tok, width), bf),
            shape((tok, width), f32),
            shape((rows_blk, q_half), f32),
            shape((rows_blk, q_half), f32),
            shape((rows_blk // 2, 2 * kv_half), f32),
            shape((rows_blk // 2, LANES), f32),
            grad,
            grad,
            grad,
            shape((blocks, 2, 8, LANES), f32),
        ),
        in_specs=[pl.BlockSpec(memory_space=pltpu.SMEM)] + [vmem] * 17 + [hbm] * 3,
        out_specs=tuple([vmem] * 10),
        scratch_shapes=[
            V((2, tok, width), bf),
            V((HEAD_DIM, rows), bf),
            V((HEAD_DIM, rows), bf),
            V((HEAD_DIM, rows), f32),
            V((8, rows), f32),
            V(kv.shape, bf),
            V((group, q_half), bf),
            V((group, q_half), bf),
            V((width, group), bf),
            V((group, width), f32),
            V((tok, width), f32),
            V((depth, tok, width), bf),
            V((depth + 1, tok, width), bf),
            V((blocks, rows_blk, q_half), bf),
        ]
        + buffers((rows_blk, q_half))
        + [V((group, kv_half), f32)]
        + buffers((group, kv_half))
        + buffers((rows_blk, q_half))
        + [V((blocks, rows_blk, kv_half + LANES), bf), V((rows_blk, kv_half + LANES), f32)]
        + buffers((rows_blk, kv_half + LANES))
        + [
            V((3, 2 * rows_e, cols), bf),
            V((3, 2 * rows_e, cols), bf),
            V((3, rows_e, cols), bf),
            V((3, rows_e, cols), bf),
            V((3, tok, width // 3), bf),
            V((3, tok, width // 3), bf),
            V((rows_blk // 2, kv_half + LANES), f32),
            V((rows_blk // 2, kv_half + LANES), f32),
            V((8, LANES), f32),
            pltpu.SemaphoreType.DMA((320,)),
        ],
        compiler_params=pltpu.CompilerParams(
            collective_id=cid, has_side_effects=True, vmem_limit_bytes=60 * 2**20
        ),
        name="closing",
    )(attn_sq, dhr, dh, hid, x, gain, w, a, q, o, kv, begin, ot, lse, cosine, sine, zp, gm, *grads)


def turn(values, cosine, sine):
    rows, width = values.shape
    heads = width // HEAD_DIM
    half = HEAD_DIM // 2
    shaped = values.reshape(rows, heads, HEAD_DIM)
    swapped = jnp.concatenate([shaped[..., half:], shaped[..., :half]], -1)
    return (shaped * cosine[:, None, :] + swapped * sine[:, None, :]).reshape(rows, width)


def other_half(values, u, rows):
    mine = lax.dynamic_slice_in_dim(values, u * rows, rows, 0)
    theirs = lax.dynamic_slice_in_dim(values, (1 - u) * rows, rows, 0).astype(jnp.bfloat16)
    return mine + lax.ppermute(theirs, "ulysses", [(0, 1), (1, 0)]).astype(jnp.float32)


def planned(
    layer_input,
    grad_output,
    gain_attn,
    gain_moe,
    w_query,
    w_keyval,
    w_out,
    w_gate,
    w_up,
    w_down,
    gate_weights,
    expert_ids,
    doc_starts,
):
    bf, f32 = jnp.bfloat16, jnp.float32
    n_blk = lax.axis_size("blk")
    n_uly = lax.axis_size("ulysses")
    depth = n_blk // 4
    tok = layer_input.shape[0]
    group = tok * n_uly
    rows_dev = w_query.shape[0]
    q_half = HEADS // n_uly * HEAD_DIM
    kv_half = 2 * HEAD_DIM
    scale = 1.0 / math.sqrt(HEAD_DIM)
    blk = lax.axis_index("blk")
    u = lax.axis_index("ulysses")
    experts = n_blk // 2
    expert = blk // 2
    n_dev = n_blk * n_uly

    gains = jnp.concatenate(
        [gain_attn[:, None], gain_moe[:, None], jnp.zeros((rows_dev, LANES - 2), bf)], 1
    )
    w_own = jnp.concatenate(
        [
            w_query.reshape(rows_dev, n_uly, q_half),
            jnp.swapaxes(w_keyval.reshape(rows_dev, 2, n_uly, HEAD_DIM), 1, 2).reshape(
                rows_dev, n_uly, kv_half
            ),
            jnp.broadcast_to(gains[:, None, :], (rows_dev, n_uly, LANES)),
            w_out.reshape(rows_dev, n_uly, q_half),
        ],
        2,
    )
    w_own = jnp.swapaxes(w_own, 0, 1)
    named = expert_ids[:, :, None] == jnp.arange(experts, dtype=jnp.int32)[None, None, :]
    g_own = jnp.sum(jnp.where(named, gate_weights[:, :, None], 0.0), 1).T
    w_all, x_all, dy_all, g_all, gate_w, up_w, down_w = opening(
        w_own, layer_input, grad_output, g_own, w_gate, w_up, w_down, depth, 1
    )
    w_all = w_all.reshape(D, w_own.shape[2])
    query_w = w_all[:, :q_half]
    keyval_w = w_all[:, q_half : q_half + kv_half]
    gain_cols = w_all[:, q_half + kv_half : q_half + kv_half + 2].astype(f32).T
    out_w = w_all[:, q_half + kv_half + LANES :]
    gain_a, gain_m = gain_cols[0], gain_cols[1]

    positions = blk * group + jnp.arange(group, dtype=jnp.int32)
    begins = doc_begin(positions, doc_starts)
    half = HEAD_DIM // 2
    freq = ROPE_BASE ** (-jnp.arange(half, dtype=f32) * 2.0 / HEAD_DIM)
    angle = (positions - begins).astype(f32)[:, None] * freq[None, :]
    cosine = jnp.concatenate([jnp.cos(angle)] * 2, 1)
    sine = jnp.sin(angle)
    sine = jnp.concatenate([-sine, sine], 1)

    inputs_g = x_all.reshape(group, D).astype(f32)
    normed_a = (
        inputs_g * lax.rsqrt(jnp.mean(inputs_g * inputs_g, -1, keepdims=True) + EPS) * gain_a
    ).astype(bf)
    queries = turn(mm(normed_a, query_w), cosine, sine).astype(bf)
    keyval = mm(normed_a, keyval_w)
    kv_own = jnp.concatenate(
        [turn(keyval[:, :HEAD_DIM], cosine, sine).astype(bf), keyval[:, HEAD_DIM:].astype(bf)], 1
    )
    kv_all = gather_plane(kv_own, depth, True, 2)
    blk_word = jnp.full((1,), blk, jnp.int32)
    begin_rows = jnp.broadcast_to(begins[None, :], (8, group))
    mixed, mixed_t, lse = attend(blk_word, queries, kv_all, begin_rows, scale)

    attn_branch = other_half(contract(mixed, out_w, 1, 1), u, tok)
    inputs = layer_input.astype(f32)
    hidden = inputs + attn_branch
    factor_m = lax.rsqrt(jnp.mean(hidden * hidden, -1, keepdims=True) + EPS)
    normed_m = (hidden * factor_m * gain_m).astype(bf)

    rows_in = gather_plane(normed_m, depth, False, 3).reshape(2 * depth * tok, D)
    dy_in = dy_all.reshape(2 * depth * tok, D)
    weight = lax.dynamic_index_in_dim(g_all, expert, 1, keepdims=False).reshape(2 * depth * tok, 1)
    gate_pre = mm(rows_in, gate_w)
    up_pre = mm(rows_in, up_w)
    sig = jax.nn.sigmoid(gate_pre)
    act = (gate_pre * sig * up_pre).astype(bf)
    z_part = (weight * contract(act, down_w, 1, 1)).astype(bf)
    dyr = (weight * dy_in.astype(f32)).astype(bf)
    grad_act = mm(dyr, down_w)
    grad_gate_pre = (grad_act * up_pre * sig * (1.0 + gate_pre * (1.0 - sig))).astype(bf)
    grad_up_pre = (grad_act * gate_pre * sig).astype(bf)
    db_part = (contract(grad_gate_pre, gate_w, 1, 1) + contract(grad_up_pre, up_w, 1, 1)).astype(bf)
    block = (2 * depth, tok, D)
    (grad_normed_m,) = scatter_plane([db_part.reshape(block)], depth, 2, 4)
    grads_e = [
        contract(rows_in, grad_gate_pre, 0, 0).astype(bf),
        contract(rows_in, grad_up_pre, 0, 0).astype(bf),
        contract(dyr, act, 0, 0).astype(bf),
    ]
    grad_hidden = grad_output.astype(f32) + norm_back(hidden, factor_m, gain_m, grad_normed_m)
    spread = jnp.arange(LANES, dtype=jnp.int32)[None, :]
    pick_m = jnp.broadcast_to((spread == 1).astype(bf), (tok, LANES))
    gain_terms = contract((grad_normed_m * hidden * factor_m).astype(bf), pick_m, 0, 0).astype(bf)
    attn_sq = jnp.sum(attn_branch * attn_branch).reshape(1)
    (
        layer_output, grad_input, part_query, part_out, part_keyval, gain_sums, grad_gate, grad_up, grad_down, squares
    ) = closing(
        attn_sq, grad_hidden.astype(bf), grad_hidden, hidden, layer_input, gain_a[None, :], w_all, normed_a, queries,
        mixed, kv_all, begin_rows, mixed_t, lse, cosine, sine, z_part.reshape(block), gain_terms, grads_e,
        depth, scale, 5,
    )
    squares = jnp.sum(squares[:, :, 0, :3], (0, 1))
    branch_rms = jnp.sqrt(squares / (tok * n_dev * D))
    return (
        layer_output,
        grad_input,
        gain_sums[:, 0],
        gain_sums[:, 1],
        part_query,
        part_keyval,
        part_out,
        grad_gate,
        grad_up,
        grad_down,
        branch_rms,
    )


def solution(mesh):
    in_specs = (
        P(("blk", "ulysses"), None),
        P(("blk", "ulysses"), None),
        P(("blk", "ulysses")),
        P(("blk", "ulysses")),
        P(("blk", "ulysses"), None),
        P(("blk", "ulysses"), None),
        P(("blk", "ulysses"), None),
        P("ulysses", "blk"),
        P("ulysses", "blk"),
        P("ulysses", "blk"),
        P(("blk", "ulysses"), None),
        P(("blk", "ulysses"), None),
        P(),
    )
    out_specs = (
        P(("blk", "ulysses"), None),
        P(("blk", "ulysses"), None),
        P(("blk", "ulysses")),
        P(("blk", "ulysses")),
        P("blk", "ulysses"),
        P(("blk", "ulysses"), None),
        P("blk", "ulysses"),
        P("ulysses", "blk"),
        P("ulysses", "blk"),
        P("ulysses", "blk"),
        P(),
    )
    blocks, members = mesh.shape["blk"], mesh.shape["ulysses"]
    body = planned if blocks == 16 and members == KV_HEADS else local
    return jax.shard_map(body, mesh=mesh, in_specs=in_specs, out_specs=out_specs, check_vma=False)
```

```python
import functools
import math

import jax
import jax.numpy as jnp
from jax import lax
from jax.experimental import pallas as pl
from jax.experimental.pallas import tpu as pltpu
from jax.sharding import PartitionSpec as P

D = 1536
HEADS = 12
KV_HEADS = 2
HEAD_DIM = 128
TOP = 4


EPS = 1e-06
ROPE_BASE = 1000000.0
NEG = -1e30


def rotate(values, positions, sign):
    half = values.shape[-1] // 2
    freq = ROPE_BASE ** (-jnp.arange(half, dtype=jnp.float32) * 2.0 / values.shape[-1])
    angle = positions.astype(jnp.float32)[:, None] * freq[None, :]
    cosine = jnp.cos(angle)[:, None, :]
    sine = sign * jnp.sin(angle)[:, None, :]
    first = values[..., :half]
    second = values[..., half:]
    return jnp.concatenate([first * cosine - second * sine, second * cosine + first * sine], -1)


def doc_begin(positions, doc_starts):
    return jnp.max(
        jnp.where(doc_starts[None, :] <= positions[:, None], doc_starts[None, :], 0), axis=1
    )


def norm_back(values, factor, gain, grad):
    weighted = grad * gain
    inner = jnp.mean(weighted * values, -1, keepdims=True)
    return factor * weighted - values * factor * factor * factor * inner


def visible_mask(q_pos, q_begin, k_pos):
    return (k_pos[None, :] >= q_begin[:, None]) & (k_pos[None, :] <= q_pos[:, None])


def split_blocks(array):
    rows = array.shape[0]
    size = min(rows, 512)
    return (array.reshape((rows // size, size) + array.shape[1:]), size)


def contract(left, right, left_dim, right_dim):
    return lax.dot_general(
        left, right, (((left_dim,), (right_dim,)), ((), ())), preferred_element_type=jnp.float32
    )


def reorder_rows(array, outer, inner):
    rows = array.shape[0]
    shaped = array.reshape((outer, inner, rows // (outer * inner)) + array.shape[1:])
    return jnp.swapaxes(shaped, 0, 1).reshape(array.shape)


def route(payload):
    return lax.all_to_all(payload, "blk", split_axis=0, concat_axis=0, tiled=True)


def backward_block(queries, grads, lse, delta, q_pos, q_begin, keys, values, k_start, scale):
    k_pos = k_start + jnp.arange(keys.shape[0], dtype=jnp.int32)
    visible = visible_mask(q_pos, q_begin, k_pos)[None]
    scores = jnp.einsum("qhd,kd->hqk", queries, keys, preferred_element_type=jnp.float32) * scale
    probs = jnp.where(visible, jnp.exp(scores - lse[:, :, None]), 0.0)
    probs_low = probs.astype(jnp.bfloat16)
    grad_probs = jnp.einsum("qhd,kd->hqk", grads, values, preferred_element_type=jnp.float32)
    grad_scores = (probs * (grad_probs - delta[:, :, None])).astype(jnp.bfloat16)
    part_q = (
        jnp.einsum("hqk,kd->qhd", grad_scores, keys, preferred_element_type=jnp.float32) * scale
    )
    part_k = (
        jnp.einsum("hqk,qhd->kd", grad_scores, queries, preferred_element_type=jnp.float32) * scale
    )
    part_v = jnp.einsum("hqk,qhd->kd", probs_low, grads, preferred_element_type=jnp.float32)
    return (part_q, part_k, part_v)


def local(
    layer_input,
    grad_output,
    gain_attn,
    gain_moe,
    w_query,
    w_keyval,
    w_out,
    w_gate,
    w_up,
    w_down,
    gate_weights,
    expert_ids,
    doc_starts,
):
    n_blk = lax.axis_size("blk")
    n_uly = lax.axis_size("ulysses")
    tok = layer_input.shape[0]
    group = tok * n_uly
    heads_dev = HEADS // n_uly
    per_kv = HEADS // KV_HEADS
    which = [c * heads_dev // per_kv for c in range(n_uly)]
    kv_width = KV_HEADS * HEAD_DIM
    q_width = HEADS * HEAD_DIM
    scale = 1.0 / math.sqrt(HEAD_DIM)
    blk_index = lax.axis_index("blk")
    device = blk_index * n_uly + lax.axis_index("ulysses")
    tok_pos = device * tok + jnp.arange(tok, dtype=jnp.int32)
    places = tok_pos - doc_begin(tok_pos, doc_starts)
    gain_a, gain_m, query_w, keyval_w, out_w = (
        lax.all_gather(gain_attn, ("blk", "ulysses"), axis=0, tiled=True),
        lax.all_gather(gain_moe, ("blk", "ulysses"), axis=0, tiled=True),
        lax.all_gather(w_query, ("blk", "ulysses"), axis=0, tiled=True),
        lax.all_gather(w_keyval, ("blk", "ulysses"), axis=0, tiled=True),
        lax.all_gather(w_out, ("blk", "ulysses"), axis=0, tiled=True),
    )
    gate_w, up_w, down_w = (
        lax.all_gather(w_gate, "ulysses", axis=0, tiled=True),
        lax.all_gather(w_up, "ulysses", axis=0, tiled=True),
        lax.all_gather(w_down, "ulysses", axis=0, tiled=True),
    )
    gain_a = gain_a.astype(jnp.float32)
    gain_m = gain_m.astype(jnp.float32)
    inputs = layer_input.astype(jnp.float32)
    factor_a = lax.rsqrt(jnp.mean(inputs * inputs, -1, keepdims=True) + EPS)
    normed_a = (inputs * factor_a * gain_a).astype(jnp.bfloat16)
    query_raw = jnp.dot(normed_a, query_w, preferred_element_type=jnp.float32)
    keyval_raw = jnp.dot(normed_a, keyval_w, preferred_element_type=jnp.float32)
    queries = rotate(query_raw.reshape(tok, HEADS, HEAD_DIM), places, 1.0).astype(jnp.bfloat16)
    keys = rotate(keyval_raw[:, :kv_width].reshape(tok, KV_HEADS, HEAD_DIM), places, 1.0).astype(
        jnp.bfloat16
    )
    values = keyval_raw[:, kv_width:].reshape(tok, KV_HEADS, HEAD_DIM).astype(jnp.bfloat16)
    key_copies = jnp.stack([keys[:, j] for j in which], 1)
    value_copies = jnp.stack([values[:, j] for j in which], 1)
    spread_normed = jnp.broadcast_to(normed_a[:, None, :], (tok, n_uly, D))
    head_q, head_k, head_v, head_normed = (
        lax.all_to_all(queries, "ulysses", split_axis=1, concat_axis=0, tiled=True),
        lax.all_to_all(key_copies, "ulysses", split_axis=1, concat_axis=0, tiled=True),
        lax.all_to_all(value_copies, "ulysses", split_axis=1, concat_axis=0, tiled=True),
        lax.all_to_all(spread_normed, "ulysses", split_axis=1, concat_axis=0, tiled=True),
    )
    key_local = head_k[:, 0, :]
    value_local = head_v[:, 0, :]
    normed_group = head_normed[:, 0, :]
    q_pos = blk_index * group + jnp.arange(group, dtype=jnp.int32)
    q_begin = doc_begin(q_pos, doc_starts)
    start_state = (
        jnp.full((heads_dev, group), NEG, jnp.float32),
        jnp.zeros((heads_dev, group), jnp.float32),
        jnp.zeros((group, heads_dev, HEAD_DIM), jnp.float32),
    )
    state = start_state
    key_rows = lax.all_gather(key_local, "blk", axis=0, tiled=True)
    value_rows = lax.all_gather(value_local, "blk", axis=0, tiled=True)
    key_blocks, size = split_blocks(key_rows)
    value_blocks, _ = split_blocks(value_rows)

    def attend_step(inner, item):
        key_blk, value_blk, number = item
        k_start = number * size
        live = (k_start <= q_pos[-1]) & (k_start + size - 1 >= q_begin[0])

        def attend_work(current):
            top, total, acc = current
            k_pos = k_start + jnp.arange(size, dtype=jnp.int32)
            visible = visible_mask(q_pos, q_begin, k_pos)[None]
            scores = (
                jnp.einsum("qhd,kd->hqk", head_q, key_blk, preferred_element_type=jnp.float32)
                * scale
            )
            scores = jnp.where(visible, scores, NEG)
            new_top = jnp.maximum(top, jnp.max(scores, -1))
            weights = jnp.where(visible, jnp.exp(scores - new_top[:, :, None]), 0.0)
            keep = jnp.exp(top - new_top)
            total = total * keep + jnp.sum(weights, -1)
            acc = acc * jnp.transpose(keep)[:, :, None] + jnp.einsum(
                "hqk,kd->qhd",
                weights.astype(jnp.bfloat16),
                value_blk,
                preferred_element_type=jnp.float32,
            )
            return (new_top, total, acc)

        return (lax.cond(live, attend_work, lambda current: current, inner), None)

    state, _ = lax.scan(
        attend_step,
        state,
        (key_blocks, value_blocks, jnp.arange(key_blocks.shape[0], dtype=jnp.int32)),
    )
    top, total, acc = state
    mixed = acc / jnp.transpose(total)[:, :, None]
    mixed_low = mixed.astype(jnp.bfloat16)
    lse = top + jnp.log(total)
    attended = lax.all_to_all(
        mixed_low, "ulysses", split_axis=0, concat_axis=1, tiled=True
    ).reshape(tok, q_width)
    attn_branch = contract(attended, out_w, 1, 1)
    hidden = inputs + attn_branch
    factor_m = lax.rsqrt(jnp.mean(hidden * hidden, -1, keepdims=True) + EPS)
    normed_m = (hidden * factor_m * gain_m).astype(jnp.bfloat16)
    experts = n_blk // 2
    capacity = min(tok, 2 * tok * TOP // experts)
    flat_ids = expert_ids.reshape(-1)
    picks = (flat_ids[:, None] == jnp.arange(experts, dtype=jnp.int32)[None, :]).astype(jnp.int32)
    slots = jnp.sum((jnp.cumsum(picks, 0) - 1) * picks, -1)

    def dispatch(rows):
        buffer = jnp.zeros((experts, capacity, D), jnp.bfloat16).at[flat_ids, slots].set(rows)
        return route(jnp.repeat(buffer, 2, axis=0)).reshape(n_blk * capacity, D)

    def collect(rows):
        back = route(rows.astype(jnp.bfloat16).reshape(n_blk, capacity, D))
        return back[2 * flat_ids, slots].astype(jnp.float32) + back[2 * flat_ids + 1, slots].astype(
            jnp.float32
        )

    expert_in = dispatch(jnp.repeat(normed_m, TOP, axis=0))
    gate_pre = jnp.dot(expert_in, gate_w, preferred_element_type=jnp.float32)
    up_pre = jnp.dot(expert_in, up_w, preferred_element_type=jnp.float32)
    act = (jax.nn.silu(gate_pre) * up_pre).astype(jnp.bfloat16)
    expert_out = contract(act, down_w, 1, 1)
    returned = collect(expert_out).reshape(tok, TOP, D)
    moe_branch = jnp.sum(gate_weights[:, :, None] * returned, 1)
    result = hidden + moe_branch
    layer_output = result.astype(jnp.bfloat16)
    grad_res = grad_output.astype(jnp.float32)
    routed_grad = (
        (gate_weights[:, :, None] * grad_res[:, None, :]).reshape(tok * TOP, D).astype(jnp.bfloat16)
    )
    expert_grad = dispatch(routed_grad)
    grad_act = jnp.dot(expert_grad, down_w, preferred_element_type=jnp.float32)
    grad_down = contract(expert_grad, act, 0, 0)
    sig = jax.nn.sigmoid(gate_pre)
    grad_gate_pre = (grad_act * up_pre * sig * (1.0 + gate_pre * (1.0 - sig))).astype(jnp.bfloat16)
    grad_up_pre = (grad_act * gate_pre * sig).astype(jnp.bfloat16)
    grad_gate = contract(expert_in, grad_gate_pre, 0, 0)
    grad_up = contract(expert_in, grad_up_pre, 0, 0)
    grad_in = contract(grad_gate_pre, gate_w, 1, 1) + contract(grad_up_pre, up_w, 1, 1)
    grad_normed_m = jnp.sum(collect(grad_in).reshape(tok, TOP, D), 1)
    grad_gain_m = jnp.sum(grad_normed_m * hidden * factor_m, 0)
    grad_hidden = grad_res + norm_back(hidden, factor_m, gain_m, grad_normed_m)
    grad_hidden_low = grad_hidden.astype(jnp.bfloat16)
    grad_attended = jnp.dot(grad_hidden_low, out_w, preferred_element_type=jnp.float32).astype(
        jnp.bfloat16
    )
    spread_hidden = jnp.broadcast_to(grad_hidden_low[:, None, :], (tok, n_uly, D))
    head_grad, head_hidden = (
        lax.all_to_all(
            grad_attended.reshape(tok, HEADS, HEAD_DIM),
            "ulysses",
            split_axis=1,
            concat_axis=0,
            tiled=True,
        ),
        lax.all_to_all(spread_hidden, "ulysses", split_axis=1, concat_axis=0, tiled=True),
    )
    grad_out_slice = contract(
        head_hidden[:, 0, :], mixed_low.reshape(group, heads_dev * HEAD_DIM), 0, 0
    )
    delta = jnp.transpose(jnp.sum(head_grad.astype(jnp.float32) * mixed, -1))
    total_keys = group * n_blk
    zero_q = jnp.zeros((group, heads_dev, HEAD_DIM), jnp.float32)
    fold_start = (
        zero_q,
        jnp.zeros((total_keys, HEAD_DIM), jnp.float32),
        jnp.zeros((total_keys, HEAD_DIM), jnp.float32),
    )
    state = fold_start
    key_rows = lax.all_gather(key_local, "blk", axis=0, tiled=True)
    value_rows = lax.all_gather(value_local, "blk", axis=0, tiled=True)
    key_blocks, grads_size = split_blocks(key_rows)
    value_blocks, _ = split_blocks(value_rows)

    def grads_step(inner, item):
        key_blk, value_blk, number = item
        k_start = number * grads_size
        live = (k_start <= q_pos[-1]) & (k_start + grads_size - 1 >= q_begin[0])

        def grads_work(current):
            part_q, part_k, part_v = backward_block(
                head_q, head_grad, lse, delta, q_pos, q_begin, key_blk, value_blk, k_start, scale
            )
            grad_q, grad_keys, grad_values = current
            grad_keys = lax.dynamic_update_slice_in_dim(
                grad_keys,
                lax.dynamic_slice_in_dim(grad_keys, k_start, grads_size, 0) + part_k,
                k_start,
                0,
            )
            grad_values = lax.dynamic_update_slice_in_dim(
                grad_values,
                lax.dynamic_slice_in_dim(grad_values, k_start, grads_size, 0) + part_v,
                k_start,
                0,
            )
            return (grad_q + part_q, grad_keys, grad_values)

        return (lax.cond(live, grads_work, lambda current: current, inner), None)

    state, _ = lax.scan(
        grads_step,
        state,
        (key_blocks, value_blocks, jnp.arange(key_blocks.shape[0], dtype=jnp.int32)),
    )
    grad_q = state[0]
    grad_k, grad_v = (
        lax.psum_scatter(state[1], "blk", scatter_dimension=0, tiled=True),
        lax.psum_scatter(state[2], "blk", scatter_dimension=0, tiled=True),
    )
    group_places = q_pos - q_begin
    grad_q_pre = rotate(grad_q.astype(jnp.bfloat16).astype(jnp.float32), group_places, -1.0).astype(
        jnp.bfloat16
    )
    grad_query_slice = contract(normed_group, grad_q_pre.reshape(group, heads_dev * HEAD_DIM), 0, 0)
    token_q, token_k, token_v = (
        lax.all_to_all(grad_q_pre, "ulysses", split_axis=0, concat_axis=1, tiled=True),
        lax.all_to_all(
            grad_k.astype(jnp.bfloat16)[:, None, :],
            "ulysses",
            split_axis=0,
            concat_axis=1,
            tiled=True,
        ),
        lax.all_to_all(
            grad_v.astype(jnp.bfloat16)[:, None, :],
            "ulysses",
            split_axis=0,
            concat_axis=1,
            tiled=True,
        ),
    )
    summed_k = []
    summed_v = []
    for head in range(KV_HEADS):
        members = [c for c in range(n_uly) if which[c] == head]
        summed_k.append(sum((token_k[:, c].astype(jnp.float32) for c in members)))
        summed_v.append(sum((token_v[:, c].astype(jnp.float32) for c in members)))
    grad_key_heads = jnp.stack(summed_k, 1)
    grad_value_heads = jnp.stack(summed_v, 1)
    grad_query_pre = token_q.reshape(tok, q_width)
    grad_key_pre = rotate(grad_key_heads, places, -1.0).reshape(tok, kv_width)
    grad_keyval_pre = jnp.concatenate(
        [grad_key_pre, grad_value_heads.reshape(tok, kv_width)], 1
    ).astype(jnp.bfloat16)
    grad_normed_a = contract(grad_query_pre, query_w, 1, 1) + contract(
        grad_keyval_pre, keyval_w, 1, 1
    )
    grad_keyval_w = contract(normed_a, grad_keyval_pre, 0, 0)
    grad_gain_a = jnp.sum(grad_normed_a * inputs * factor_a, 0)
    grad_input = grad_hidden + norm_back(inputs, factor_a, gain_a, grad_normed_a)
    n_dev = n_blk * n_uly
    squares = jnp.stack(
        [
            jnp.sum(attn_branch * attn_branch),
            jnp.sum(moe_branch * moe_branch),
            jnp.sum(result * result),
        ]
    )
    square_rows = jnp.broadcast_to(squares[None, :], (n_dev, 3))
    part_gate, part_up, part_down, uly_gain_a, uly_gain_m, uly_keyval, uly_squares = (
        lax.psum_scatter(
            grad_gate.astype(jnp.bfloat16), "ulysses", scatter_dimension=0, tiled=True
        ).astype(jnp.float32),
        lax.psum_scatter(
            grad_up.astype(jnp.bfloat16), "ulysses", scatter_dimension=0, tiled=True
        ).astype(jnp.float32),
        lax.psum_scatter(
            grad_down.astype(jnp.bfloat16), "ulysses", scatter_dimension=0, tiled=True
        ).astype(jnp.float32),
        lax.psum_scatter(
            reorder_rows(grad_gain_a, n_blk, n_uly).astype(jnp.bfloat16),
            "ulysses",
            scatter_dimension=0,
            tiled=True,
        ).astype(jnp.float32),
        lax.psum_scatter(
            reorder_rows(grad_gain_m, n_blk, n_uly).astype(jnp.bfloat16),
            "ulysses",
            scatter_dimension=0,
            tiled=True,
        ).astype(jnp.float32),
        lax.psum_scatter(
            reorder_rows(grad_keyval_w, n_blk, n_uly).astype(jnp.bfloat16),
            "ulysses",
            scatter_dimension=0,
            tiled=True,
        ).astype(jnp.float32),
        lax.psum_scatter(
            square_rows.astype(jnp.bfloat16), "ulysses", scatter_dimension=0, tiled=True
        ).astype(jnp.float32),
    )
    part_outw, part_query, part_gain_a, part_gain_m, part_keyval, square_row = (
        lax.psum_scatter(grad_out_slice, "blk", scatter_dimension=0, tiled=True),
        lax.psum_scatter(grad_query_slice, "blk", scatter_dimension=0, tiled=True),
        lax.psum_scatter(uly_gain_a, "blk", scatter_dimension=0, tiled=True),
        lax.psum_scatter(uly_gain_m, "blk", scatter_dimension=0, tiled=True),
        lax.psum_scatter(uly_keyval, "blk", scatter_dimension=0, tiled=True),
        lax.psum_scatter(uly_squares, "blk", scatter_dimension=0, tiled=True),
    )
    branch_rms = jnp.sqrt(square_row[0] / (tok * n_dev * D))
    return (
        layer_output,
        grad_input,
        part_gain_a,
        part_gain_m,
        part_query,
        part_keyval,
        part_outw,
        part_gate,
        part_up,
        part_down,
        branch_rms,
    )


MESH = pl.DeviceIdType.MESH
LANES = 128
LOG2E = 1.4426950408889634


class Place:
    def __init__(self, depth):
        self.blk = lax.axis_index("blk")
        self.u = lax.axis_index("ulysses")
        self.depth = depth
        self.z = self.blk // 4
        self.x = (self.blk // 2) % 2
        self.c = self.blk % 2
        self.up = (self.blk + 4, self.u)
        self.down = (self.blk - 4, self.u)
        self.across = (self.blk + 2 - 4 * self.x, self.u)
        self.sibling = (self.blk + 1 - 2 * self.c, self.u)
        self.other = (self.blk, 1 - self.u)
        self.has_up = self.z < depth - 1
        self.has_down = self.z > 0

    def slot(self, z, x, c):
        return z * 4 + x * 2 + c

    def greet(self, sibling=False, other=False, plane=True):
        barrier = pltpu.get_barrier_semaphore()

        def hail(device):
            pl.semaphore_signal(barrier, inc=1, device_id=device, device_id_type=MESH)

        count = 0
        if plane:
            hail(self.across)
            pl.when(self.has_up)(lambda: hail(self.up))
            pl.when(self.has_down)(lambda: hail(self.down))
            count = 1 + self.has_up.astype(jnp.int32) + self.has_down.astype(jnp.int32)
        if sibling:
            hail(self.sibling)
            count = count + 1
        if other:
            hail(self.other)
            count = count + 1
        pl.semaphore_wait(barrier, count)


class Wires:
    def __init__(self, sems):
        self.sems = sems
        self.used = 0

    def take(self, count):
        base = self.used
        self.used += count
        return lambda index: self.sems.at[base + index]


def each(act, items):
    for item in items:
        act(item)


def remote(src, dst, send, recv, device):
    return pltpu.make_async_remote_copy(
        src_ref=src, dst_ref=dst, send_sem=send, recv_sem=recv, device_id=device, device_id_type=MESH
    )


class Gather:
    def __init__(self, place, wires, src, out, cores, up_only=False):
        self.p, self.src, self.out, self.cores, self.up_only = place, src, out, cores, up_only
        n = place.depth
        self.s_up, self.s_down, self.s_across = wires.take(n), wires.take(n), wires.take(n)
        self.r_z, self.r_x = wires.take(n), wires.take(n)
        if cores:
            self.s_core, self.r_core = wires.take(2 * n), wires.take(2 * n)
        self.own = wires.take(1)(0)

    def _send(self, zz, xx, kind, src=None):
        p = self.p
        dst = self.out(zz, xx, p.c)
        src = dst if src is None else src
        if kind == "up":
            return remote(src, dst, self.s_up(zz), self.r_z(zz), p.up)
        if kind == "down":
            return remote(src, dst, self.s_down(zz), self.r_z(zz), p.down)
        if kind == "across":
            return remote(src, dst, self.s_across(zz), self.r_x(zz), p.across)
        return remote(src, dst, self.s_core(zz * 2 + xx), self.r_core(zz * 2 + xx), p.sibling)

    def _keep(self):
        p = self.p
        return pltpu.make_async_copy(self.src, self.out(p.z, p.x, p.c), self.own)

    def start(self, in_place=False):
        p = self.p
        self.in_place = in_place
        src = None if in_place else self.src
        pl.when(p.has_up)(lambda: self._send(p.z, p.x, "up", src).start())
        if not self.up_only:
            pl.when(p.has_down)(lambda: self._send(p.z, p.x, "down", src).start())
        self._send(p.z, p.x, "across", src).start()
        if self.cores:
            self._send(p.z, p.x, "core", src).start()
        if not in_place:
            self._keep().start()

    def hop(self, d):
        p = self.p

        def low():
            zz = p.z - d
            self._send(zz, p.x, "up").wait_recv()
            pl.when(p.has_up)(lambda: self._send(zz, p.x, "up").start())
            self._send(zz, p.x, "across").start()
            if self.cores:
                self._send(zz, p.x, "core").start()

        def high():
            zz = p.z + d
            self._send(zz, p.x, "down").wait_recv()
            pl.when(p.has_down)(lambda: self._send(zz, p.x, "down").start())
            self._send(zz, p.x, "across").start()
            if self.cores:
                self._send(zz, p.x, "core").start()

        pl.when(p.z >= d)(low)
        if not self.up_only:
            pl.when(p.z + d < p.depth)(high)

    def cross(self, d):
        p = self.p

        def take(zz):
            self._send(zz, 1 - p.x, "across").wait_recv()
            if self.cores:
                self._send(zz, 1 - p.x, "core").start()

        if isinstance(d, int) and d == 0:
            take(p.z)
        else:
            pl.when(p.z >= d)(lambda: take(p.z - d))
            if not self.up_only:
                pl.when(p.z + d < p.depth)(lambda: take(p.z + d))

    def core(self, zz, xx):
        self._send(zz, xx, "core").wait_recv()

    def finish(self, cores_taken=False):
        p = self.p
        for zz in range(p.depth):

            def ends(zz=zz):
                if self.cores:
                    for xx in range(2):
                        if not cores_taken:
                            self._send(zz, xx, "core").wait_recv()
                        self._send(zz, xx, "core").wait_send()
                self._send(zz, p.x, "across").wait_send()

            if self.up_only and zz > 0:
                pl.when(p.z >= zz)(ends)
            else:
                ends()
            pl.when(p.has_up & (p.z >= zz))(lambda zz=zz: self._send(zz, p.x, "up").wait_send())
            if not self.up_only:
                pl.when(p.has_down & (p.z <= zz))(lambda zz=zz: self._send(zz, p.x, "down").wait_send())
        if not self.in_place:
            self._keep().wait()


def gather_kernel(depth, cores, src, out, sems):
    place = Place(depth)
    place.greet(sibling=cores)
    wires = Wires(sems)
    if cores:
        view = lambda z, x, c: out.at[place.slot(z, x, c)]
    else:
        view = lambda z, x, c: out.at[z * 2 + x]
    g = Gather(place, wires, src, view, cores)
    g.start()
    for d in range(1, depth):
        g.hop(d)
        g.cross(d - 1)
    g.cross(depth - 1)
    g.finish()


def gather_plane(block, depth, cores, cid):
    slots = depth * (4 if cores else 2)
    return pl.pallas_call(
        functools.partial(gather_kernel, depth, cores),
        out_shape=jax.ShapeDtypeStruct((slots,) + block.shape, block.dtype),
        in_specs=[pl.BlockSpec(memory_space=pl.ANY)],
        out_specs=pl.BlockSpec(memory_space=pl.ANY),
        scratch_shapes=[pltpu.SemaphoreType.DMA((16 * depth,))],
        compiler_params=pltpu.CompilerParams(collective_id=cid, has_side_effects=True),
        name="gather_%d" % cid,
    )(block)


class Scatter:
    def __init__(self, place, wires, part, out, rx, rz, pieces, down_only=False):
        self.p, self.part, self.out, self.rx, self.rz = place, part, out, rx, rz
        n = place.depth
        total = n * pieces
        self.pieces, self.down_only = pieces, down_only
        self.sx, self.cx = wires.take(total), wires.take(total)
        self.sz, self.cu, self.cd = wires.take(total), wires.take(total), wires.take(total)
        order = []
        low, high = 0, n - 1
        while low <= high:
            if not down_only:
                order.append(high)
            if low != high or down_only:
                order.append(low)
            if down_only:
                low = low + 1
            else:
                low, high = low + 1, high - 1
        self.order = order
        self.items = [(zz, k) for zz in order for k in range(pieces)]

    def _x(self, zz, k):
        i = zz * self.pieces + k
        return remote(self.part(zz, 1 - self.p.x, k), self.rx(zz, k), self.sx(i), self.cx(i), self.p.across)

    def _up(self, zz, k):
        i = zz * self.pieces + k
        return remote(self.rx(zz, k), self.rz(zz, k), self.sz(i), self.cu(i), self.p.up)

    def _down(self, zz, k, z):
        i = zz * self.pieces + k
        slot = self.p.depth if zz == z - 1 else zz
        return remote(self.rx(zz, k), self.rz(slot, k), self.sz(i), self.cd(i), self.p.down)

    def _live(self, zz, act):
        if self.down_only and zz > 0:
            pl.when(self.p.z >= zz)(act)
        else:
            act()

    def begin(self, t):
        if t < len(self.items):
            zz, k = self.items[t]
            self._live(zz, lambda: self._x(zz, k).start())

    def _pass(self, zz, k, more):
        p = self.p
        total = self.part(zz, p.x, k)[...].astype(jnp.float32) + self.rx(zz, k)[...].astype(jnp.float32)
        if more:
            total = total + self.rz(zz, k)[...].astype(jnp.float32)
        self.rx(zz, k)[...] = total.astype(jnp.bfloat16)

    def land(self, t):
        if t < 0 or t >= len(self.items):
            return
        p = self.p
        n = p.depth
        zz, k = self.items[t]
        self._live(zz, lambda: self._x(zz, k).wait_recv())

        def climb():
            self._pass(zz, k, False)
            self._up(zz, k).start()

        def sink():
            self._pass(zz, k, False)
            self._down(zz, k, n - 1).start()

        if zz > 0 and not self.down_only:
            pl.when(p.z == 0)(climb)
        if zz < n - 1:
            pl.when(p.z == n - 1)(sink)

    def chain(self, t, h):
        if t < 0 or t >= len(self.items):
            return
        p = self.p
        n = p.depth
        zz, k = self.items[t]
        low, high = h, n - 1 - h

        def from_low():
            self._up(zz, k).wait_recv()
            if zz > low:
                self._pass(zz, k, True)
                self._up(zz, k).start()

        def from_high():
            self._down(zz, k, high + 1).wait_recv()
            if zz < high:
                self._pass(zz, k, True)
                self._down(zz, k, high).start()

        if zz >= low and not self.down_only:
            pl.when(p.z == low)(from_low)
        if zz <= high:
            pl.when(p.z == high)(from_high)

    def step(self, t):
        self.land(t)
        for h in range(1, self.p.depth):
            self.chain(t - h, h)

    def steps(self):
        return len(self.items) + self.p.depth - 1

    def finish(self):
        p = self.p
        n = p.depth
        for zz, k in self.items:
            self._live(zz, lambda zz=zz, k=k: self._x(zz, k).wait_send())
            if not self.down_only:
                pl.when(p.z < zz)(lambda zz=zz, k=k: self._up(zz, k).wait_send())
            pl.when(p.z > zz)(lambda zz=zz, k=k: self._down(zz, k, zz + 1).wait_send())

            def store(zz=zz, k=k):
                total = self.part(zz, p.x, k)[...].astype(jnp.float32)
                total = total + self.rx(zz, k)[...].astype(jnp.float32)
                if zz > 0 and not self.down_only:
                    total = total + self.rz(zz, k)[...].astype(jnp.float32)
                if zz < n - 1:
                    total = total + self.rz(n, k)[...].astype(jnp.float32)
                self.out(k)[...] = total

            pl.when(p.z == zz)(store)


class CoreScatter:
    def __init__(self, place, wires, src, rc, out, rx, rz, down_only=False):
        self.p, self.src, self.rc = place, src, rc
        n = place.depth
        self.sc, self.cc = wires.take(2 * n), wires.take(2 * n)
        self.plane = Scatter(
            place, wires, lambda zz, xx, k: rc.at[zz * 2 + xx], lambda k: out,
            lambda zz, k: rx.at[zz], lambda slot, k: rz.at[slot], 1, down_only,
        )
        self.order = self.plane.order

    def _trade(self, zz, xx):
        p = self.p
        i = zz * 2 + xx
        return remote(self.src.at[p.slot(zz, xx, 1 - p.c)], self.rc.at[i], self.sc(i), self.cc(i), p.sibling)

    def trade(self, t):
        zz = self.order[t]
        self.plane._live(zz, lambda: each(lambda xx: self._trade(zz, xx).start(), (1 - self.p.x, self.p.x)))

    def join(self, t):
        p = self.p
        zz = self.order[t]

        def act():
            for xx in (1 - p.x, p.x):
                self._trade(zz, xx).wait_recv()
                at = zz * 2 + xx
                self.rc[at] = (
                    self.src[p.slot(zz, xx, p.c)].astype(jnp.float32) + self.rc[at].astype(jnp.float32)
                ).astype(jnp.bfloat16)

        self.plane._live(zz, act)
        self.plane.begin(t)

    def release(self):
        for zz in self.order:
            self.plane._live(zz, lambda zz=zz: each(lambda xx: self._trade(zz, xx).wait_send(), range(2)))

    def finish(self):
        self.plane.finish()


def scatter_kernel(depth, pieces, window, count, *refs):
    ins, outs = refs[:count], refs[count : 2 * count]
    rx, rz, sems = refs[2 * count :]
    p = Place(depth)
    p.greet()
    wires = Wires(sems)
    rows = outs[0].shape[0] // pieces

    def cut(ref, k):
        return ref.at[pl.ds(k * rows, rows)]

    jobs = []
    for a in range(count):
        jobs.append(
            Scatter(
                p, wires,
                lambda zz, xx, k, a=a: cut(ins[a].at[zz * 2 + xx], k),
                lambda k, a=a: cut(outs[a], k),
                lambda zz, k, a=a: cut(rx.at[a, zz], k),
                lambda slot, k, a=a: cut(rz.at[a, slot], k),
                pieces,
            )
        )
    for t in range(window):
        jobs[0].begin(t)
    for a, job in enumerate(jobs):
        total = len(job.items)
        for t in range(job.steps()):
            job.step(t)
            if t + window < total:
                job.begin(t + window)
            elif a + 1 < count and t + window - total < window:
                jobs[a + 1].begin(t + window - total)
    for job in jobs:
        job.finish()


def scatter_plane(arrays, depth, pieces, cid, window=3):
    count = len(arrays)
    block = arrays[0].shape[1:]
    bf = jnp.bfloat16
    return pl.pallas_call(
        functools.partial(scatter_kernel, depth, pieces, window, count),
        out_shape=tuple([jax.ShapeDtypeStruct(block, jnp.float32)] * count),
        in_specs=[pl.BlockSpec(memory_space=pltpu.VMEM)] * count,
        out_specs=tuple([pl.BlockSpec(memory_space=pltpu.VMEM)] * count),
        scratch_shapes=[
            pltpu.VMEM((count, depth) + block, bf),
            pltpu.VMEM((count, depth + 1) + block, bf),
            pltpu.SemaphoreType.DMA((count * 5 * depth * pieces,)),
        ],
        compiler_params=pltpu.CompilerParams(
            collective_id=cid, has_side_effects=True, vmem_limit_bytes=56 * 2**20
        ),
        name="scatter_%d" % cid,
    )(*arrays)


def mm(left, right):
    return jnp.dot(left, right, preferred_element_type=jnp.float32)


def flip(tile):
    return tile.astype(jnp.float32).T.astype(jnp.bfloat16)


def hidden_bias(first_key, first_query, begin, keys):
    queries = begin.shape[1]
    k_pos = first_key + lax.broadcasted_iota(jnp.int32, (keys, queries), 0)
    q_pos = first_query + lax.broadcasted_iota(jnp.int32, (keys, queries), 1)
    return jnp.where((k_pos >= begin) & (k_pos <= q_pos), 0.0, NEG)


def front_kernel(
    depth, scale, x, dy, gains, wq, wkv, wo, g_own, e0, e1, e2, begin, cosine, sine,
    b, hid, attn_sq, normed, q, o, kv, ot, lse, w_all, wo_all, gain_rows, dy_all, g_all, f0, f1, f2,
    wa_own, wo_own, x_all, raw, qt, top, total, acc, p_out, p_in, sems,
):
    f32, bf = jnp.float32, jnp.bfloat16
    p = Place(depth)
    p.greet(sibling=True, other=True)
    wires = Wires(sems)
    u, blk = p.u, p.blk
    tok, width = x.shape
    group, q_half = q.shape
    heads = q_half // HEAD_DIM
    kv_half = 2 * HEAD_DIM
    rows_dev = wq.shape[0]
    half, cols = e0.shape

    def rows_of(ref, z, xx, c, member):
        row = (p.slot(z, xx, c) * 2 + member) * rows_dev
        return ref.at[pl.ds(pl.multiple_of(row, 16), rows_dev)]

    wa_mine = Gather(p, wires, wa_own.at[u], lambda z, xx, c: rows_of(w_all, z, xx, c, u), True)
    wa_peer = Gather(p, wires, None, lambda z, xx, c: rows_of(w_all, z, xx, c, 1 - u), True)
    wo_mine = Gather(p, wires, wo_own.at[u], lambda z, xx, c: rows_of(wo_all, z, xx, c, u), True)
    wo_peer = Gather(p, wires, None, lambda z, xx, c: rows_of(wo_all, z, xx, c, 1 - u), True)
    kvs = Gather(p, wires, None, lambda z, xx, c: kv.at[p.slot(z, xx, c)], True, up_only=True)
    dys = Gather(p, wires, dy, lambda z, xx, c: dy_all.at[z * 2 + xx], False)
    gws = Gather(p, wires, g_own, lambda z, xx, c: g_all.at[z * 2 + xx], False)
    ws, wr = wires.take(2), wires.take(2)
    xs, xr, xl = wires.take(1)(0), wires.take(1)(0), wires.take(1)(0)
    es, er, el = wires.take(3), wires.take(3), wires.take(3)
    cs, cr = wires.take(6), wires.take(6)
    ps, pr = wires.take(3), wires.take(3)

    for h in range(2):
        wa_own[h, :, :q_half] = wq[:, h * q_half : (h + 1) * q_half]
        for part in range(2):
            wa_own[h, :, q_half + part * HEAD_DIM : q_half + (part + 1) * HEAD_DIM] = wkv[
                :, (part * 2 + h) * HEAD_DIM : (part * 2 + h + 1) * HEAD_DIM
            ]
        wo_own[h] = wo[:, h * q_half : (h + 1) * q_half]
    columns = gains[...].T[:rows_dev, :].astype(bf)
    for h in range(2):
        wa_own[h, :, q_half + kv_half :] = columns

    wa_swap = remote(wa_own.at[1 - u], rows_of(w_all, p.z, p.x, p.c, u), ws(0), wr(0), p.other)
    wo_swap = remote(wo_own.at[1 - u], rows_of(wo_all, p.z, p.x, p.c, u), ws(1), wr(1), p.other)
    x_swap = remote(x, x_all.at[u], xs, xr, p.other)
    x_keep = pltpu.make_async_copy(x, x_all.at[u], xl)

    def part(ref, row, core):
        return ref.at[
            pl.ds(pl.multiple_of(row * half, half), half), pl.ds(pl.multiple_of(core * cols, LANES), cols)
        ]

    experts = ((e0, f0), (e1, f1), (e2, f2))
    swaps = [remote(e, part(f, u, p.c), es(i), er(i), p.other) for i, (e, f) in enumerate(experts)]
    keeps = [pltpu.make_async_copy(e, part(f, u, p.c), el(i)) for i, (e, f) in enumerate(experts)]
    shares = [remote(e, part(f, u, p.c), cs(i), cr(i), p.sibling) for i, (e, f) in enumerate(experts)]
    passes = [
        remote(part(f, 1 - u, p.c), part(f, 1 - u, p.c), cs(3 + i), cr(3 + i), p.sibling)
        for i, (e, f) in enumerate(experts)
    ]

    wa_swap.start()
    wa_mine.start()
    x_swap.start()
    x_keep.start()
    wa_swap.wait_recv()
    wa_peer.start(in_place=True)
    wo_swap.start()
    gws.start()
    for i in range(3):
        swaps[i].start()
        keeps[i].start()
        shares[i].start()
    for d in range(1, depth):
        for g in (wa_mine, wa_peer):
            g.hop(d)
            g.cross(d - 1)
    wo_mine.start()
    wo_swap.wait_recv()
    wo_peer.start(in_place=True)
    x_keep.wait()
    x_swap.wait_recv()
    for g in (wa_mine, wa_peer):
        g.cross(depth - 1)
    for g in (wa_mine, wa_peer):
        g.finish()
    gain_rows[...] = w_all[:, q_half + kv_half :].astype(f32).T[:8, :]
    for m in range(2):
        xf = x_all[m].astype(f32)
        r1 = lax.rsqrt(jnp.mean(xf * xf, -1, keepdims=True) + EPS)
        normed[m * tok : (m + 1) * tok, :] = (xf * r1 * gain_rows[0:1, :]).astype(bf)
    raw[...] = mm(normed[...], w_all[:, : q_half + kv_half])

    def rope(values):
        return values * cosine[...] + pltpu.roll(values, HEAD_DIM // 2, 1) * sine[...]

    here = p.slot(p.z, p.x, p.c)
    kv[here, :, :HEAD_DIM] = rope(raw[:, q_half : q_half + HEAD_DIM]).astype(bf)
    kv[here, :, HEAD_DIM:] = raw[:, q_half + HEAD_DIM :].astype(bf)
    kvs.start(in_place=True)
    for h in range(heads):
        hs = slice(h * HEAD_DIM, (h + 1) * HEAD_DIM)
        turned = rope(raw[:, hs])
        q[:, hs] = turned.astype(bf)
        qt[:, h * group : (h + 1) * group] = turned.T.astype(bf)
    top[...] = jnp.full(top.shape, NEG, f32)
    total[...] = jnp.zeros(total.shape, f32)
    ot[...] = jnp.zeros(ot.shape, f32)

    background = {}

    def at_step(s, act):
        background.setdefault(s, []).append(act)

    at_step(1, lambda: kvs.cross(0))
    for d in range(1, depth):
        at_step(2 * d - 1, lambda d=d: kvs.hop(d))
        at_step(2 * d + 1 if d + 1 < depth else 2 * d + 2, lambda d=d: kvs.cross(d))
    at_step(1, dys.start)
    for d in range(1, depth):
        at_step(2 * d, lambda d=d: each(lambda g: (g.hop(d), g.cross(d - 1)) and None, (wo_mine, wo_peer)))
    at_step(8, lambda: each(lambda g: g.cross(depth - 1), (wo_mine, wo_peer)))
    at_step(9, lambda: gws.hop(1))
    at_step(10, lambda: (gws.hop(2), gws.cross(0)) and None)
    at_step(11, lambda: (gws.hop(3), gws.cross(1)) and None)
    at_step(12, lambda: dys.hop(1))
    at_step(12, lambda: dys.cross(0))
    at_step(15, lambda: dys.hop(2))

    def step(s, carry):
        d = s // 4
        i = s % 4
        zz = p.z - d
        xx = jnp.where(i < 2, p.x, 1 - p.x)
        cc = jnp.where(i % 2 == 0, p.c, 1 - p.c)
        j = p.slot(zz, xx, cc)

        pl.when((zz >= 0) & (i % 2 == 1))(lambda: kvs.core(zz, xx))

        def work():
            k = kv[j, :, :HEAD_DIM]
            vt = flip(kv[j, :, HEAD_DIM:])
            bias = hidden_bias(j * group, blk * group, begin[0:1, :], group)
            for h in range(heads):
                at = slice(h * group, (h + 1) * group)
                sc = mm(k, qt[:, at]) * (scale * LOG2E) + bias
                old = top[0:1, at]
                new = jnp.maximum(old, jnp.max(sc, axis=0, keepdims=True))
                w = jnp.exp2(sc - new)
                keep = jnp.exp2(old - new)
                total[0:1, at] = total[0:1, at] * keep + jnp.sum(w, axis=0, keepdims=True)
                ot[:, at] = ot[:, at] * keep + mm(vt, w.astype(bf))
                top[0:1, at] = new

        pl.when((zz >= 0) & (j <= blk))(work)
        for when, acts in background.items():
            pl.when(s == when)(lambda acts=acts: each(lambda act: act(), acts))
        return carry

    lax.fori_loop(0, 4 * depth, step, 0)

    for g in (wo_mine, wo_peer):
        g.finish()
    sums = total[0:1, :]
    lse[...] = jnp.broadcast_to(top[0:1, :] + jnp.log2(sums), lse.shape)
    for h in range(heads):
        at = slice(h * group, (h + 1) * group)
        mixed = ot[:, at] / sums[:, at]
        ot[:, at] = mixed
        o[:, h * HEAD_DIM : (h + 1) * HEAD_DIM] = mixed.T.astype(bf)

    wide = width // 3
    p_swaps = []
    for i in range(3):
        cb = i * wide
        acc[:, cb : cb + wide] = contract(o[...], wo_all[cb : cb + wide, :], 1, 1)
        theirs = pl.ds(pl.multiple_of((1 - u) * tok, tok), tok)
        p_out[i] = acc[theirs, cb : cb + wide].astype(bf)
        p_swaps.append(remote(p_out.at[i], p_in.at[i], ps(i), pr(i), p.other))
        p_swaps[i].start()
    dys.cross(1)
    dys.hop(3)
    gws.cross(2)
    gws.cross(3)
    for i in range(3):
        swaps[i].wait_recv()
        passes[i].start()
    mine = pl.ds(pl.multiple_of(u * tok, tok), tok)
    for i in range(3):
        p_swaps[i].wait_recv()
        acc[mine, i * wide : (i + 1) * wide] += p_in[i].astype(f32)
    branch = acc[mine, :]
    hidden = x[...].astype(f32) + branch
    hid[...] = hidden
    r2 = lax.rsqrt(jnp.mean(hidden * hidden, -1, keepdims=True) + EPS)
    b[...] = (hidden * r2 * gain_rows[1:2, :]).astype(bf)
    attn_sq[...] = jnp.broadcast_to(jnp.sum(branch * branch).reshape(1, 1), attn_sq.shape)
    dys.cross(2)
    dys.cross(3)
    kvs.finish(cores_taken=True)
    dys.finish()
    gws.finish()
    wa_swap.wait_send()
    wo_swap.wait_send()
    x_swap.wait_send()
    for i in range(3):
        swaps[i].wait_send()
        keeps[i].wait()
        shares[i].wait()
        passes[i].wait()
        p_swaps[i].wait_send()


def front(x, dy, gains, wq, wkv, wo, g_own, experts, begin, cosine, sine, depth, scale, cid):
    f32, bf = jnp.float32, jnp.bfloat16
    shape = jax.ShapeDtypeStruct
    vmem = pl.BlockSpec(memory_space=pltpu.VMEM)
    hbm = pl.BlockSpec(memory_space=pl.ANY)
    V = pltpu.VMEM
    tok, width = x.shape
    group = 2 * tok
    q_half = wq.shape[1] // 2
    kv_half = 2 * HEAD_DIM
    wide = q_half + kv_half + LANES
    rows = q_half // HEAD_DIM * group
    rows_dev = wq.shape[0]
    expert = shape((2 * experts[0].shape[0], 2 * experts[0].shape[1]), bf)
    return pl.pallas_call(
        functools.partial(front_kernel, depth, scale),
        out_shape=(
            shape((tok, width), bf),
            shape((tok, width), f32),
            shape((8, LANES), f32),
            shape((group, width), bf),
            shape((group, q_half), bf),
            shape((group, q_half), bf),
            shape((4 * depth, group, kv_half), bf),
            shape((HEAD_DIM, rows), f32),
            shape((8, rows), f32),
            shape((width, wide), bf),
            shape((width, q_half), bf),
            shape((8, width), f32),
            shape((2 * depth, tok, width), bf),
            shape((2 * depth,) + g_own.shape, f32),
            expert,
            expert,
            expert,
        ),
        in_specs=[vmem, hbm, vmem, vmem, vmem, vmem, vmem, hbm, hbm, hbm, vmem, vmem, vmem],
        out_specs=tuple([vmem] * 12 + [hbm] * 5),
        scratch_shapes=[
            V((2, rows_dev, wide), bf),
            V((2, rows_dev, q_half), bf),
            V((2, tok, width), bf),
            V((group, q_half + kv_half), f32),
            V((HEAD_DIM, rows), bf),
            V((8, rows), f32),
            V((8, rows), f32),
            V((group, width), f32),
            V((3, tok, width // 3), bf),
            V((3, tok, width // 3), bf),
            pltpu.SemaphoreType.DMA((7 * 16 * depth,)),
        ],
        compiler_params=pltpu.CompilerParams(
            collective_id=cid, has_side_effects=True, vmem_limit_bytes=56 * 2**20
        ),
        name="front",
    )(x, dy, gains, wq, wkv, wo, g_own, *experts, begin, cosine, sine)


def closing_kernel(
    depth, scale, attn_sq, dhr, dh, hid, x, gain, w, wo, a, q, o, kv, begin, ot, lse, cosine, sine, zp, gm, e0, e1, e2,
    out, gin, gq, go, gkv, gg, f0, f1, f2, sq,
    dhr_all, qt, dot_, dqt, delta, dkv, do, dq, at, acc,
    z_sum, z_rx, z_rz, go_p, go_rc, go_rx, go_rz, kv_sum, kv_rc, kv_rx, kv_rz,
    gq_rc, gq_rx, gq_rz, gk_p, gk_sum, gk_rc, gk_rx, gk_rz,
    e_own, e_core, e_low, e_peer, da_out, da_in, t_out, t_in, sq_own, sems,
):
    f32, bf = jnp.float32, jnp.bfloat16
    p = Place(depth)
    p.greet(sibling=True, other=True)
    wires = Wires(sems)
    u, blk = p.u, p.blk
    tok = x.shape[0]
    group, q_half = q.shape
    heads = q_half // HEAD_DIM
    kv_half = 2 * HEAD_DIM
    blocks = kv.shape[0]
    rows_blk = gq.shape[0]

    cols = f0.shape[1]
    rows_e = f0.shape[0]
    es, er, el, ps, pr = wires.take(3), wires.take(3), wires.take(3), wires.take(3), wires.take(3)

    def e_cols(ref, core):
        return ref.at[:, pl.ds(pl.multiple_of(core * cols, LANES), cols)]

    def e_rows(member):
        return pl.ds(pl.multiple_of(member * rows_e, rows_e), rows_e)

    experts = (e0, e1, e2)
    e_trade = [remote(e_cols(e, 1 - p.c), e_core.at[i], es(i), er(i), p.sibling) for i, e in enumerate(experts)]
    e_keep = [pltpu.make_async_copy(e_cols(e, p.c), e_own.at[i], el(i)) for i, e in enumerate(experts)]
    e_swap = [remote(e_low.at[i], e_peer.at[i], ps(i), pr(i), p.other) for i in range(3)]

    def e_join(i):
        e_trade[i].wait_recv()
        e_keep[i].wait()
        theirs = e_rows(1 - u)
        e_low[i] = (e_own[i, theirs, :].astype(f32) + e_core[i, theirs, :].astype(f32)).astype(bf)
        e_swap[i].start()

    def e_done(i):
        e_swap[i].wait_recv()
        mine = e_rows(u)
        total = e_own[i, mine, :].astype(f32) + e_core[i, mine, :].astype(f32)
        (f0, f1, f2)[i][...] = total + e_peer[i].astype(f32)

    ds, dr, dl = wires.take(1)(0), wires.take(1)(0), wires.take(1)(0)
    swap = remote(dhr, dhr_all.at[u], ds, dr, p.other)
    keep = pltpu.make_async_copy(dhr, dhr_all.at[u], dl)

    pieces = 2
    z_rows = tok // pieces

    def cut(ref, k):
        return ref.at[pl.ds(k * z_rows, z_rows)]

    zs = Scatter(
        p, wires,
        lambda zz, xx, k: cut(zp.at[zz * 2 + xx], k),
        lambda k: cut(z_sum, k),
        lambda zz, k: cut(z_rx.at[zz], k),
        lambda slot, k: cut(z_rz.at[slot], k),
        pieces,
    )
    gos = CoreScatter(p, wires, go_p, go_rc, go, go_rx, go_rz)
    kvs = CoreScatter(p, wires, dkv, kv_rc, kv_sum, kv_rx, kv_rz, down_only=True)
    gqs = CoreScatter(p, wires, go_p, gq_rc, gq, gq_rx, gq_rz)
    gks = CoreScatter(p, wires, gk_p, gk_rc, gk_sum, gk_rx, gk_rz)
    sqs = Gather(p, wires, sq_own, lambda z, xx, c: sq.at[p.slot(z, xx, c), u], True)
    qs, qr = wires.take(1)(0), wires.take(1)(0)
    sq_swap = remote(sq.at[:, u], sq.at[:, u], qs, qr, p.other)

    swap.start()
    keep.start()
    window = 3
    for t in range(window):
        zs.begin(t)
    for i in range(3):
        e_trade[i].start()
        e_keep[i].start()

    def z_step(t):
        zs.step(t)
        zs.begin(t + window)

    for h in range(heads):
        qt[:, h * group : (h + 1) * group] = flip(q[:, h * HEAD_DIM : (h + 1) * HEAD_DIM])
    dqt[...] = jnp.zeros(dqt.shape, f32)
    dkv[...] = jnp.zeros(dkv.shape, bf)
    for i in range(3):
        e_join(i)
    z_step(0)
    keep.wait()
    swap.wait_recv()

    for h in range(heads):
        cs = slice(h * HEAD_DIM, (h + 1) * HEAD_DIM)
        hs = slice(h * group, (h + 1) * group)
        part = jnp.concatenate([mm(dhr_all[m], wo[:, cs]) for m in range(2)], 0).astype(bf)
        do[:, cs] = part
        turned = part.astype(f32).T
        dot_[:, hs] = turned.astype(bf)
        delta[0:1, hs] = jnp.sum(turned * ot[:, hs], axis=0, keepdims=True)
    for m in range(2):
        at[:, m * tok : (m + 1) * tok] = flip(dhr_all[m])

    def out_rows(i, carry):
        rows = pl.ds(pl.multiple_of(i * rows_blk, rows_blk), rows_blk)
        go_p[i] = mm(at[rows, :], o[...]).astype(bf)
        return carry

    lax.fori_loop(0, blocks, out_rows, 0)
    for t in range(depth):
        gos.trade(t)

    background = {}

    def at_tile(j, act):
        background.setdefault(j, []).append(act)

    for t in range(1, zs.steps()):
        at_tile(min(t, blocks - 1), lambda t=t: z_step(t))
    for t in range(depth):
        at_tile(3 + t, lambda t=t: gos.join(t))
    for t in range(gos.plane.steps()):
        at_tile(8 + t, lambda t=t: gos.plane.step(t))

    def tile(j, carry):
        def work():
            k = kv[j, :, :HEAD_DIM]
            v = kv[j, :, HEAD_DIM:]
            kt = flip(k)
            bias = hidden_bias(j * group, blk * group, begin[0:1, :], group)
            dk = jnp.zeros((group, HEAD_DIM), f32)
            dv = jnp.zeros((group, HEAD_DIM), f32)
            for h in range(heads):
                hs = slice(h * group, (h + 1) * group)
                cs = slice(h * HEAD_DIM, (h + 1) * HEAD_DIM)
                s = mm(k, qt[:, hs]) * (scale * LOG2E) + bias
                e = jnp.exp2(s - lse[0:1, hs])
                g = (e * (mm(v, dot_[:, hs]) - delta[0:1, hs])).astype(bf)
                dqt[:, hs] += mm(kt, g)
                dk += mm(g, q[:, cs])
                dv += mm(e.astype(bf), do[:, cs])
            dkv[j, :, :HEAD_DIM] = (dk * scale).astype(bf)
            dkv[j, :, HEAD_DIM:] = dv.astype(bf)

        pl.when(j <= blk)(work)
        for when, acts in background.items():
            pl.when(j == when)(lambda acts=acts: each(lambda act: act(), acts))
        return carry

    lax.fori_loop(0, blocks, tile, 0)

    for t in range(depth):
        kvs.trade(t)
    gos.release()

    def back_turn(values):
        return values * cosine[...] - pltpu.roll(values, HEAD_DIM // 2, 1) * sine[...]

    for h in range(heads):
        hs = slice(h * group, (h + 1) * group)
        cs = slice(h * HEAD_DIM, (h + 1) * HEAD_DIM)
        dq[:, cs] = back_turn((dqt[:, hs] * scale).T.astype(bf).astype(f32)).astype(bf)
    for t in range(depth):
        kvs.join(t)
    kvs.plane.step(0)
    for j in range(0, D, 256):
        at[j : j + 256, :] = flip(a[:, j : j + 256])
    kvs.plane.step(1)

    def query_rows(i, carry):
        rows = pl.ds(pl.multiple_of(i * rows_blk, rows_blk), rows_blk)
        go_p[i] = mm(at[rows, :], dq[...]).astype(bf)
        return carry

    lax.fori_loop(0, blocks // 2, query_rows, 0)
    kvs.plane.step(2)
    lax.fori_loop(blocks // 2, blocks, query_rows, 0)
    kvs.plane.step(3)
    for m in range(2):
        for cb in range(0, D, 512):
            acc[m * tok : (m + 1) * tok, cb : cb + 512] = contract(
                dq[m * tok : (m + 1) * tok, :], w[cb : cb + 512, :q_half], 1, 1
            )
    for t in range(4, kvs.plane.steps()):
        kvs.plane.step(t)
    kvs.release()
    kvs.finish()
    kv_low = kv_sum[...].astype(bf).astype(f32)
    kv_pre = jnp.concatenate([back_turn(kv_low[:, :HEAD_DIM]).astype(bf), kv_low[:, HEAD_DIM:].astype(bf)], 1)

    da_s, da_r = wires.take(3), wires.take(3)
    wide = D // 3
    da_swaps = []
    for i in range(3):
        cb = i * wide
        part = contract(kv_pre, w[cb : cb + wide, q_half : q_half + kv_half], 1, 1)
        acc[:, cb : cb + wide] += part
        theirs = pl.ds(pl.multiple_of((1 - u) * tok, tok), tok)
        da_out[i] = acc[theirs, cb : cb + wide].astype(bf)
        da_swaps.append(remote(da_out.at[i], da_in.at[i], da_s(i), da_r(i), p.other))
        da_swaps[i].start()
    for t in range(depth):
        gqs.trade(t)

    def keyval_rows(i, carry):
        rows = pl.ds(pl.multiple_of(i * rows_blk, rows_blk), rows_blk)
        gk_p[i, :, :kv_half] = mm(at[rows, :], kv_pre).astype(bf)
        return carry

    lax.fori_loop(0, blocks, keyval_rows, 0)
    for t in range(depth):
        gqs.join(t)

    zs.finish()
    result = hid[...] + z_sum[...]
    out[...] = result.astype(bf)
    spread = lax.broadcasted_iota(jnp.int32, (8, LANES), 1)
    z_sq = jnp.sum(z_sum[...] * z_sum[...])
    r_sq = jnp.sum(result * result)
    sq_own[...] = jnp.where(
        spread == 0, attn_sq[...], jnp.where(spread == 1, z_sq, jnp.where(spread == 2, r_sq, 0.0))
    )
    sqs.start()
    gos.finish()
    for i in range(3):
        e_done(i)

    mine = pl.ds(pl.multiple_of(u * tok, tok), tok)
    for i in range(3):
        da_swaps[i].wait_recv()
        acc[mine, i * wide : (i + 1) * wide] += da_in[i].astype(f32)
    da = acc[mine, :]
    xf = x[...].astype(f32)
    r1 = lax.rsqrt(jnp.mean(xf * xf, -1, keepdims=True) + EPS)
    terms = (da * xf * r1).T
    weighted = da * gain[0:1, :]
    inner = jnp.mean(weighted * xf, -1, keepdims=True)
    gin[...] = dh[...] + r1 * weighted - xf * (r1 * r1 * r1 * inner)
    column = jnp.sum(terms, axis=1, keepdims=True)
    lane = lax.broadcasted_iota(jnp.int32, (D, LANES), 1)
    gain_cols = (jnp.where(lane == 0, column, 0.0) + gm[...].astype(f32)).astype(bf)
    for i in range(blocks):
        gk_p[i, :, kv_half:] = gain_cols[i * rows_blk : (i + 1) * rows_blk, :]
    for t in range(depth):
        gks.trade(t)
    sqs.hop(1)
    for t in range(depth):
        gks.join(t)
    steps = gqs.plane.steps()
    for t in range(steps):
        gqs.plane.step(t)
        gks.plane.step(t)
        if t + 2 < depth:
            sqs.hop(t + 2)
        if t < depth:
            sqs.cross(t)
    sqs.finish()
    sq_swap.start()
    gks.release()
    gks.finish()
    rows_dev = gkv.shape[0]
    theirs = pl.ds(pl.multiple_of((1 - u) * rows_dev, rows_dev), rows_dev)
    own = pl.ds(pl.multiple_of(u * rows_dev, rows_dev), rows_dev)
    t_out[...] = gk_sum[theirs, :]
    ts, tr = wires.take(1)(0), wires.take(1)(0)
    t_swap = remote(t_out, t_in, ts, tr, p.other)
    t_swap.start()
    gqs.release()
    gqs.finish()
    t_swap.wait_recv()
    for part in range(2):
        here = slice(part * HEAD_DIM, (part + 1) * HEAD_DIM)
        base = part * kv_half
        gkv[:, pl.ds(pl.multiple_of(base + u * HEAD_DIM, LANES), HEAD_DIM)] = gk_sum[own, here]
        gkv[:, pl.ds(pl.multiple_of(base + (1 - u) * HEAD_DIM, LANES), HEAD_DIM)] = t_in[:, here]
    gg[...] = gk_sum[own, kv_half:] + t_in[:, kv_half:]
    sq_swap.wait()
    t_swap.wait_send()
    swap.wait_send()
    for i in range(3):
        e_trade[i].wait_send()
        e_swap[i].wait_send()
        da_swaps[i].wait_send()


def closing(attn_sq, dhr, dh, hid, x, gain, w, wo, a, q, o, kv, begin, ot, lse, cosine, sine, zp, gm, grads, depth, scale, cid):
    f32, bf = jnp.float32, jnp.bfloat16
    tok, width = x.shape
    group, q_half = q.shape
    blocks = kv.shape[0]
    rows_blk = width // blocks
    rows_e, cols = grads[0].shape[0] // 2, grads[0].shape[1] // 2
    kv_half = 2 * HEAD_DIM
    shape = jax.ShapeDtypeStruct
    vmem = pl.BlockSpec(memory_space=pltpu.VMEM)
    hbm = pl.BlockSpec(memory_space=pl.ANY)
    V = pltpu.VMEM

    def buffers(block):
        return [
            V((blocks // 2,) + block, bf),
            V((depth,) + block, bf),
            V((depth + 1,) + block, bf),
        ]

    grad = shape((rows_e, cols), f32)
    rows = q_half // HEAD_DIM * group
    return pl.pallas_call(
        functools.partial(closing_kernel, depth, scale),
        out_shape=(
            shape((tok, width), bf),
            shape((tok, width), f32),
            shape((rows_blk, q_half), f32),
            shape((rows_blk, q_half), f32),
            shape((rows_blk // 2, 2 * kv_half), f32),
            shape((rows_blk // 2, LANES), f32),
            grad,
            grad,
            grad,
            shape((blocks, 2, 8, LANES), f32),
        ),
        in_specs=[vmem] * 19 + [hbm] * 3,
        out_specs=tuple([vmem] * 10),
        scratch_shapes=[
            V((2, tok, width), bf),
            V((HEAD_DIM, rows), bf),
            V((HEAD_DIM, rows), bf),
            V((HEAD_DIM, rows), f32),
            V((8, rows), f32),
            V(kv.shape, bf),
            V((group, q_half), bf),
            V((group, q_half), bf),
            V((width, group), bf),
            V((group, width), f32),
            V((tok, width), f32),
            V((depth, tok, width), bf),
            V((depth + 1, tok, width), bf),
            V((blocks, rows_blk, q_half), bf),
        ]
        + buffers((rows_blk, q_half))
        + [V((group, kv_half), f32)]
        + buffers((group, kv_half))
        + buffers((rows_blk, q_half))
        + [V((blocks, rows_blk, kv_half + LANES), bf), V((rows_blk, kv_half + LANES), f32)]
        + buffers((rows_blk, kv_half + LANES))
        + [
            V((3, 2 * rows_e, cols), bf),
            V((3, 2 * rows_e, cols), bf),
            V((3, rows_e, cols), bf),
            V((3, rows_e, cols), bf),
            V((3, tok, width // 3), bf),
            V((3, tok, width // 3), bf),
            V((rows_blk // 2, kv_half + LANES), f32),
            V((rows_blk // 2, kv_half + LANES), f32),
            V((8, LANES), f32),
            pltpu.SemaphoreType.DMA((320,)),
        ],
        compiler_params=pltpu.CompilerParams(
            collective_id=cid, has_side_effects=True, vmem_limit_bytes=60 * 2**20
        ),
        name="closing",
    )(attn_sq, dhr, dh, hid, x, gain, w, wo, a, q, o, kv, begin, ot, lse, cosine, sine, zp, gm, *grads)


def planned(
    layer_input,
    grad_output,
    gain_attn,
    gain_moe,
    w_query,
    w_keyval,
    w_out,
    w_gate,
    w_up,
    w_down,
    gate_weights,
    expert_ids,
    doc_starts,
):
    bf, f32 = jnp.bfloat16, jnp.float32
    n_blk = lax.axis_size("blk")
    n_uly = lax.axis_size("ulysses")
    depth = n_blk // 4
    tok = layer_input.shape[0]
    group = tok * n_uly
    rows_dev = w_query.shape[0]
    scale = 1.0 / math.sqrt(HEAD_DIM)
    blk = lax.axis_index("blk")
    u = lax.axis_index("ulysses")
    experts = n_blk // 2
    expert = blk // 2
    n_dev = n_blk * n_uly

    gains = jnp.zeros((LANES, LANES), f32).at[0, :rows_dev].set(gain_attn.astype(f32))
    gains = gains.at[1, :rows_dev].set(gain_moe.astype(f32))
    named = expert_ids[:, :, None] == jnp.arange(experts, dtype=jnp.int32)[None, None, :]
    g_own = jnp.sum(jnp.where(named, gate_weights[:, :, None], 0.0), 1).T
    positions = blk * group + jnp.arange(group, dtype=jnp.int32)
    begins = doc_begin(positions, doc_starts)
    half = HEAD_DIM // 2
    freq = ROPE_BASE ** (-jnp.arange(half, dtype=f32) * 2.0 / HEAD_DIM)
    angle = (positions - begins).astype(f32)[:, None] * freq[None, :]
    cosine = jnp.concatenate([jnp.cos(angle)] * 2, 1)
    sine = jnp.sin(angle)
    sine = jnp.concatenate([-sine, sine], 1)
    begin_rows = jnp.broadcast_to(begins[None, :], (8, group))
    (
        normed_m, hidden, attn_sq, normed_a, queries, mixed, kv_all, mixed_t, lse, w_all, out_w, gain_rows,
        dy_all, g_all, gate_w, up_w, down_w,
    ) = front(
        layer_input, grad_output, gains, w_query, w_keyval, w_out, g_own, (w_gate, w_up, w_down),
        begin_rows, cosine, sine, depth, scale, 1,
    )
    gain_m = gain_rows[1]
    factor_m = lax.rsqrt(jnp.mean(hidden * hidden, -1, keepdims=True) + EPS)

    rows_in = gather_plane(normed_m, depth, False, 3).reshape(2 * depth * tok, D)
    dy_in = dy_all.reshape(2 * depth * tok, D)
    weight = lax.dynamic_index_in_dim(g_all, expert, 1, keepdims=False).reshape(2 * depth * tok, 1)
    gate_pre = mm(rows_in, gate_w)
    up_pre = mm(rows_in, up_w)
    sig = jax.nn.sigmoid(gate_pre)
    act = (gate_pre * sig * up_pre).astype(bf)
    z_part = (weight * contract(act, down_w, 1, 1)).astype(bf)
    dyr = (weight * dy_in.astype(f32)).astype(bf)
    grad_act = mm(dyr, down_w)
    grad_gate_pre = (grad_act * up_pre * sig * (1.0 + gate_pre * (1.0 - sig))).astype(bf)
    grad_up_pre = (grad_act * gate_pre * sig).astype(bf)
    db_part = (contract(grad_gate_pre, gate_w, 1, 1) + contract(grad_up_pre, up_w, 1, 1)).astype(bf)
    block = (2 * depth, tok, D)
    (grad_normed_m,) = scatter_plane([db_part.reshape(block)], depth, 2, 4)
    grads_e = [
        contract(rows_in, grad_gate_pre, 0, 0).astype(bf),
        contract(rows_in, grad_up_pre, 0, 0).astype(bf),
        contract(dyr, act, 0, 0).astype(bf),
    ]
    grad_hidden = grad_output.astype(f32) + norm_back(hidden, factor_m, gain_m, grad_normed_m)
    spread = jnp.arange(LANES, dtype=jnp.int32)[None, :]
    pick_m = jnp.broadcast_to((spread == 1).astype(bf), (tok, LANES))
    gain_terms = contract((grad_normed_m * hidden * factor_m).astype(bf), pick_m, 0, 0).astype(bf)
    (
        layer_output, grad_input, part_query, part_out, part_keyval, gain_sums, grad_gate, grad_up, grad_down, squares
    ) = closing(
        attn_sq, grad_hidden.astype(bf), grad_hidden, hidden, layer_input, gain_rows, w_all, out_w, normed_a, queries,
        mixed, kv_all, begin_rows, mixed_t, lse, cosine, sine, z_part.reshape(block), gain_terms, grads_e,
        depth, scale, 5,
    )
    squares = jnp.sum(squares[:, :, 0, :3], (0, 1))
    branch_rms = jnp.sqrt(squares / (tok * n_dev * D))
    return (
        layer_output,
        grad_input,
        gain_sums[:, 0],
        gain_sums[:, 1],
        part_query,
        part_keyval,
        part_out,
        grad_gate,
        grad_up,
        grad_down,
        branch_rms,
    )


def solution(mesh):
    in_specs = (
        P(("blk", "ulysses"), None),
        P(("blk", "ulysses"), None),
        P(("blk", "ulysses")),
        P(("blk", "ulysses")),
        P(("blk", "ulysses"), None),
        P(("blk", "ulysses"), None),
        P(("blk", "ulysses"), None),
        P("ulysses", "blk"),
        P("ulysses", "blk"),
        P("ulysses", "blk"),
        P(("blk", "ulysses"), None),
        P(("blk", "ulysses"), None),
        P(),
    )
    out_specs = (
        P(("blk", "ulysses"), None),
        P(("blk", "ulysses"), None),
        P(("blk", "ulysses")),
        P(("blk", "ulysses")),
        P("blk", "ulysses"),
        P(("blk", "ulysses"), None),
        P("blk", "ulysses"),
        P("ulysses", "blk"),
        P("ulysses", "blk"),
        P("ulysses", "blk"),
        P(),
    )
    blocks, members = mesh.shape["blk"], mesh.shape["ulysses"]
    body = planned if blocks == 16 and members == KV_HEADS else local
    return jax.shard_map(body, mesh=mesh, in_specs=in_specs, out_specs=out_specs, check_vma=False)
```

```python
import functools
import math

import jax
import jax.numpy as jnp
from jax import lax
from jax.experimental import pallas as pl
from jax.experimental.pallas import tpu as pltpu
from jax.sharding import PartitionSpec as P

D = 1536
HEADS = 12
KV_HEADS = 2
HEAD_DIM = 128
TOP = 4


EPS = 1e-06
ROPE_BASE = 1000000.0
NEG = -1e30


def rotate(values, positions, sign):
    half = values.shape[-1] // 2
    freq = ROPE_BASE ** (-jnp.arange(half, dtype=jnp.float32) * 2.0 / values.shape[-1])
    angle = positions.astype(jnp.float32)[:, None] * freq[None, :]
    cosine = jnp.cos(angle)[:, None, :]
    sine = sign * jnp.sin(angle)[:, None, :]
    first = values[..., :half]
    second = values[..., half:]
    return jnp.concatenate([first * cosine - second * sine, second * cosine + first * sine], -1)


def doc_begin(positions, doc_starts):
    return jnp.max(
        jnp.where(doc_starts[None, :] <= positions[:, None], doc_starts[None, :], 0), axis=1
    )


def norm_back(values, factor, gain, grad):
    weighted = grad * gain
    inner = jnp.mean(weighted * values, -1, keepdims=True)
    return factor * weighted - values * factor * factor * factor * inner


def visible_mask(q_pos, q_begin, k_pos):
    return (k_pos[None, :] >= q_begin[:, None]) & (k_pos[None, :] <= q_pos[:, None])


def split_blocks(array):
    rows = array.shape[0]
    size = min(rows, 512)
    return (array.reshape((rows // size, size) + array.shape[1:]), size)


def contract(left, right, left_dim, right_dim):
    return lax.dot_general(
        left, right, (((left_dim,), (right_dim,)), ((), ())), preferred_element_type=jnp.float32
    )


def reorder_rows(array, outer, inner):
    rows = array.shape[0]
    shaped = array.reshape((outer, inner, rows // (outer * inner)) + array.shape[1:])
    return jnp.swapaxes(shaped, 0, 1).reshape(array.shape)


def route(payload):
    return lax.all_to_all(payload, "blk", split_axis=0, concat_axis=0, tiled=True)


def backward_block(queries, grads, lse, delta, q_pos, q_begin, keys, values, k_start, scale):
    k_pos = k_start + jnp.arange(keys.shape[0], dtype=jnp.int32)
    visible = visible_mask(q_pos, q_begin, k_pos)[None]
    scores = jnp.einsum("qhd,kd->hqk", queries, keys, preferred_element_type=jnp.float32) * scale
    probs = jnp.where(visible, jnp.exp(scores - lse[:, :, None]), 0.0)
    probs_low = probs.astype(jnp.bfloat16)
    grad_probs = jnp.einsum("qhd,kd->hqk", grads, values, preferred_element_type=jnp.float32)
    grad_scores = (probs * (grad_probs - delta[:, :, None])).astype(jnp.bfloat16)
    part_q = (
        jnp.einsum("hqk,kd->qhd", grad_scores, keys, preferred_element_type=jnp.float32) * scale
    )
    part_k = (
        jnp.einsum("hqk,qhd->kd", grad_scores, queries, preferred_element_type=jnp.float32) * scale
    )
    part_v = jnp.einsum("hqk,qhd->kd", probs_low, grads, preferred_element_type=jnp.float32)
    return (part_q, part_k, part_v)


def local(
    layer_input,
    grad_output,
    gain_attn,
    gain_moe,
    w_query,
    w_keyval,
    w_out,
    w_gate,
    w_up,
    w_down,
    gate_weights,
    expert_ids,
    doc_starts,
):
    n_blk = lax.axis_size("blk")
    n_uly = lax.axis_size("ulysses")
    tok = layer_input.shape[0]
    group = tok * n_uly
    heads_dev = HEADS // n_uly
    per_kv = HEADS // KV_HEADS
    which = [c * heads_dev // per_kv for c in range(n_uly)]
    kv_width = KV_HEADS * HEAD_DIM
    q_width = HEADS * HEAD_DIM
    scale = 1.0 / math.sqrt(HEAD_DIM)
    blk_index = lax.axis_index("blk")
    device = blk_index * n_uly + lax.axis_index("ulysses")
    tok_pos = device * tok + jnp.arange(tok, dtype=jnp.int32)
    places = tok_pos - doc_begin(tok_pos, doc_starts)
    gain_a, gain_m, query_w, keyval_w, out_w = (
        lax.all_gather(gain_attn, ("blk", "ulysses"), axis=0, tiled=True),
        lax.all_gather(gain_moe, ("blk", "ulysses"), axis=0, tiled=True),
        lax.all_gather(w_query, ("blk", "ulysses"), axis=0, tiled=True),
        lax.all_gather(w_keyval, ("blk", "ulysses"), axis=0, tiled=True),
        lax.all_gather(w_out, ("blk", "ulysses"), axis=0, tiled=True),
    )
    gate_w, up_w, down_w = (
        lax.all_gather(w_gate, "ulysses", axis=0, tiled=True),
        lax.all_gather(w_up, "ulysses", axis=0, tiled=True),
        lax.all_gather(w_down, "ulysses", axis=0, tiled=True),
    )
    gain_a = gain_a.astype(jnp.float32)
    gain_m = gain_m.astype(jnp.float32)
    inputs = layer_input.astype(jnp.float32)
    factor_a = lax.rsqrt(jnp.mean(inputs * inputs, -1, keepdims=True) + EPS)
    normed_a = (inputs * factor_a * gain_a).astype(jnp.bfloat16)
    query_raw = jnp.dot(normed_a, query_w, preferred_element_type=jnp.float32)
    keyval_raw = jnp.dot(normed_a, keyval_w, preferred_element_type=jnp.float32)
    queries = rotate(query_raw.reshape(tok, HEADS, HEAD_DIM), places, 1.0).astype(jnp.bfloat16)
    keys = rotate(keyval_raw[:, :kv_width].reshape(tok, KV_HEADS, HEAD_DIM), places, 1.0).astype(
        jnp.bfloat16
    )
    values = keyval_raw[:, kv_width:].reshape(tok, KV_HEADS, HEAD_DIM).astype(jnp.bfloat16)
    key_copies = jnp.stack([keys[:, j] for j in which], 1)
    value_copies = jnp.stack([values[:, j] for j in which], 1)
    spread_normed = jnp.broadcast_to(normed_a[:, None, :], (tok, n_uly, D))
    head_q, head_k, head_v, head_normed = (
        lax.all_to_all(queries, "ulysses", split_axis=1, concat_axis=0, tiled=True),
        lax.all_to_all(key_copies, "ulysses", split_axis=1, concat_axis=0, tiled=True),
        lax.all_to_all(value_copies, "ulysses", split_axis=1, concat_axis=0, tiled=True),
        lax.all_to_all(spread_normed, "ulysses", split_axis=1, concat_axis=0, tiled=True),
    )
    key_local = head_k[:, 0, :]
    value_local = head_v[:, 0, :]
    normed_group = head_normed[:, 0, :]
    q_pos = blk_index * group + jnp.arange(group, dtype=jnp.int32)
    q_begin = doc_begin(q_pos, doc_starts)
    start_state = (
        jnp.full((heads_dev, group), NEG, jnp.float32),
        jnp.zeros((heads_dev, group), jnp.float32),
        jnp.zeros((group, heads_dev, HEAD_DIM), jnp.float32),
    )
    state = start_state
    key_rows = lax.all_gather(key_local, "blk", axis=0, tiled=True)
    value_rows = lax.all_gather(value_local, "blk", axis=0, tiled=True)
    key_blocks, size = split_blocks(key_rows)
    value_blocks, _ = split_blocks(value_rows)

    def attend_step(inner, item):
        key_blk, value_blk, number = item
        k_start = number * size
        live = (k_start <= q_pos[-1]) & (k_start + size - 1 >= q_begin[0])

        def attend_work(current):
            top, total, acc = current
            k_pos = k_start + jnp.arange(size, dtype=jnp.int32)
            visible = visible_mask(q_pos, q_begin, k_pos)[None]
            scores = (
                jnp.einsum("qhd,kd->hqk", head_q, key_blk, preferred_element_type=jnp.float32)
                * scale
            )
            scores = jnp.where(visible, scores, NEG)
            new_top = jnp.maximum(top, jnp.max(scores, -1))
            weights = jnp.where(visible, jnp.exp(scores - new_top[:, :, None]), 0.0)
            keep = jnp.exp(top - new_top)
            total = total * keep + jnp.sum(weights, -1)
            acc = acc * jnp.transpose(keep)[:, :, None] + jnp.einsum(
                "hqk,kd->qhd",
                weights.astype(jnp.bfloat16),
                value_blk,
                preferred_element_type=jnp.float32,
            )
            return (new_top, total, acc)

        return (lax.cond(live, attend_work, lambda current: current, inner), None)

    state, _ = lax.scan(
        attend_step,
        state,
        (key_blocks, value_blocks, jnp.arange(key_blocks.shape[0], dtype=jnp.int32)),
    )
    top, total, acc = state
    mixed = acc / jnp.transpose(total)[:, :, None]
    mixed_low = mixed.astype(jnp.bfloat16)
    lse = top + jnp.log(total)
    attended = lax.all_to_all(
        mixed_low, "ulysses", split_axis=0, concat_axis=1, tiled=True
    ).reshape(tok, q_width)
    attn_branch = contract(attended, out_w, 1, 1)
    hidden = inputs + attn_branch
    factor_m = lax.rsqrt(jnp.mean(hidden * hidden, -1, keepdims=True) + EPS)
    normed_m = (hidden * factor_m * gain_m).astype(jnp.bfloat16)
    experts = n_blk // 2
    capacity = min(tok, 2 * tok * TOP // experts)
    flat_ids = expert_ids.reshape(-1)
    picks = (flat_ids[:, None] == jnp.arange(experts, dtype=jnp.int32)[None, :]).astype(jnp.int32)
    slots = jnp.sum((jnp.cumsum(picks, 0) - 1) * picks, -1)

    def dispatch(rows):
        buffer = jnp.zeros((experts, capacity, D), jnp.bfloat16).at[flat_ids, slots].set(rows)
        return route(jnp.repeat(buffer, 2, axis=0)).reshape(n_blk * capacity, D)

    def collect(rows):
        back = route(rows.astype(jnp.bfloat16).reshape(n_blk, capacity, D))
        return back[2 * flat_ids, slots].astype(jnp.float32) + back[2 * flat_ids + 1, slots].astype(
            jnp.float32
        )

    expert_in = dispatch(jnp.repeat(normed_m, TOP, axis=0))
    gate_pre = jnp.dot(expert_in, gate_w, preferred_element_type=jnp.float32)
    up_pre = jnp.dot(expert_in, up_w, preferred_element_type=jnp.float32)
    act = (jax.nn.silu(gate_pre) * up_pre).astype(jnp.bfloat16)
    expert_out = contract(act, down_w, 1, 1)
    returned = collect(expert_out).reshape(tok, TOP, D)
    moe_branch = jnp.sum(gate_weights[:, :, None] * returned, 1)
    result = hidden + moe_branch
    layer_output = result.astype(jnp.bfloat16)
    grad_res = grad_output.astype(jnp.float32)
    routed_grad = (
        (gate_weights[:, :, None] * grad_res[:, None, :]).reshape(tok * TOP, D).astype(jnp.bfloat16)
    )
    expert_grad = dispatch(routed_grad)
    grad_act = jnp.dot(expert_grad, down_w, preferred_element_type=jnp.float32)
    grad_down = contract(expert_grad, act, 0, 0)
    sig = jax.nn.sigmoid(gate_pre)
    grad_gate_pre = (grad_act * up_pre * sig * (1.0 + gate_pre * (1.0 - sig))).astype(jnp.bfloat16)
    grad_up_pre = (grad_act * gate_pre * sig).astype(jnp.bfloat16)
    grad_gate = contract(expert_in, grad_gate_pre, 0, 0)
    grad_up = contract(expert_in, grad_up_pre, 0, 0)
    grad_in = contract(grad_gate_pre, gate_w, 1, 1) + contract(grad_up_pre, up_w, 1, 1)
    grad_normed_m = jnp.sum(collect(grad_in).reshape(tok, TOP, D), 1)
    grad_gain_m = jnp.sum(grad_normed_m * hidden * factor_m, 0)
    grad_hidden = grad_res + norm_back(hidden, factor_m, gain_m, grad_normed_m)
    grad_hidden_low = grad_hidden.astype(jnp.bfloat16)
    grad_attended = jnp.dot(grad_hidden_low, out_w, preferred_element_type=jnp.float32).astype(
        jnp.bfloat16
    )
    spread_hidden = jnp.broadcast_to(grad_hidden_low[:, None, :], (tok, n_uly, D))
    head_grad, head_hidden = (
        lax.all_to_all(
            grad_attended.reshape(tok, HEADS, HEAD_DIM),
            "ulysses",
            split_axis=1,
            concat_axis=0,
            tiled=True,
        ),
        lax.all_to_all(spread_hidden, "ulysses", split_axis=1, concat_axis=0, tiled=True),
    )
    grad_out_slice = contract(
        head_hidden[:, 0, :], mixed_low.reshape(group, heads_dev * HEAD_DIM), 0, 0
    )
    delta = jnp.transpose(jnp.sum(head_grad.astype(jnp.float32) * mixed, -1))
    total_keys = group * n_blk
    zero_q = jnp.zeros((group, heads_dev, HEAD_DIM), jnp.float32)
    fold_start = (
        zero_q,
        jnp.zeros((total_keys, HEAD_DIM), jnp.float32),
        jnp.zeros((total_keys, HEAD_DIM), jnp.float32),
    )
    state = fold_start
    key_rows = lax.all_gather(key_local, "blk", axis=0, tiled=True)
    value_rows = lax.all_gather(value_local, "blk", axis=0, tiled=True)
    key_blocks, grads_size = split_blocks(key_rows)
    value_blocks, _ = split_blocks(value_rows)

    def grads_step(inner, item):
        key_blk, value_blk, number = item
        k_start = number * grads_size
        live = (k_start <= q_pos[-1]) & (k_start + grads_size - 1 >= q_begin[0])

        def grads_work(current):
            part_q, part_k, part_v = backward_block(
                head_q, head_grad, lse, delta, q_pos, q_begin, key_blk, value_blk, k_start, scale
            )
            grad_q, grad_keys, grad_values = current
            grad_keys = lax.dynamic_update_slice_in_dim(
                grad_keys,
                lax.dynamic_slice_in_dim(grad_keys, k_start, grads_size, 0) + part_k,
                k_start,
                0,
            )
            grad_values = lax.dynamic_update_slice_in_dim(
                grad_values,
                lax.dynamic_slice_in_dim(grad_values, k_start, grads_size, 0) + part_v,
                k_start,
                0,
            )
            return (grad_q + part_q, grad_keys, grad_values)

        return (lax.cond(live, grads_work, lambda current: current, inner), None)

    state, _ = lax.scan(
        grads_step,
        state,
        (key_blocks, value_blocks, jnp.arange(key_blocks.shape[0], dtype=jnp.int32)),
    )
    grad_q = state[0]
    grad_k, grad_v = (
        lax.psum_scatter(state[1], "blk", scatter_dimension=0, tiled=True),
        lax.psum_scatter(state[2], "blk", scatter_dimension=0, tiled=True),
    )
    group_places = q_pos - q_begin
    grad_q_pre = rotate(grad_q.astype(jnp.bfloat16).astype(jnp.float32), group_places, -1.0).astype(
        jnp.bfloat16
    )
    grad_query_slice = contract(normed_group, grad_q_pre.reshape(group, heads_dev * HEAD_DIM), 0, 0)
    token_q, token_k, token_v = (
        lax.all_to_all(grad_q_pre, "ulysses", split_axis=0, concat_axis=1, tiled=True),
        lax.all_to_all(
            grad_k.astype(jnp.bfloat16)[:, None, :],
            "ulysses",
            split_axis=0,
            concat_axis=1,
            tiled=True,
        ),
        lax.all_to_all(
            grad_v.astype(jnp.bfloat16)[:, None, :],
            "ulysses",
            split_axis=0,
            concat_axis=1,
            tiled=True,
        ),
    )
    summed_k = []
    summed_v = []
    for head in range(KV_HEADS):
        members = [c for c in range(n_uly) if which[c] == head]
        summed_k.append(sum((token_k[:, c].astype(jnp.float32) for c in members)))
        summed_v.append(sum((token_v[:, c].astype(jnp.float32) for c in members)))
    grad_key_heads = jnp.stack(summed_k, 1)
    grad_value_heads = jnp.stack(summed_v, 1)
    grad_query_pre = token_q.reshape(tok, q_width)
    grad_key_pre = rotate(grad_key_heads, places, -1.0).reshape(tok, kv_width)
    grad_keyval_pre = jnp.concatenate(
        [grad_key_pre, grad_value_heads.reshape(tok, kv_width)], 1
    ).astype(jnp.bfloat16)
    grad_normed_a = contract(grad_query_pre, query_w, 1, 1) + contract(
        grad_keyval_pre, keyval_w, 1, 1
    )
    grad_keyval_w = contract(normed_a, grad_keyval_pre, 0, 0)
    grad_gain_a = jnp.sum(grad_normed_a * inputs * factor_a, 0)
    grad_input = grad_hidden + norm_back(inputs, factor_a, gain_a, grad_normed_a)
    n_dev = n_blk * n_uly
    squares = jnp.stack(
        [
            jnp.sum(attn_branch * attn_branch),
            jnp.sum(moe_branch * moe_branch),
            jnp.sum(result * result),
        ]
    )
    square_rows = jnp.broadcast_to(squares[None, :], (n_dev, 3))
    part_gate, part_up, part_down, uly_gain_a, uly_gain_m, uly_keyval, uly_squares = (
        lax.psum_scatter(
            grad_gate.astype(jnp.bfloat16), "ulysses", scatter_dimension=0, tiled=True
        ).astype(jnp.float32),
        lax.psum_scatter(
            grad_up.astype(jnp.bfloat16), "ulysses", scatter_dimension=0, tiled=True
        ).astype(jnp.float32),
        lax.psum_scatter(
            grad_down.astype(jnp.bfloat16), "ulysses", scatter_dimension=0, tiled=True
        ).astype(jnp.float32),
        lax.psum_scatter(
            reorder_rows(grad_gain_a, n_blk, n_uly).astype(jnp.bfloat16),
            "ulysses",
            scatter_dimension=0,
            tiled=True,
        ).astype(jnp.float32),
        lax.psum_scatter(
            reorder_rows(grad_gain_m, n_blk, n_uly).astype(jnp.bfloat16),
            "ulysses",
            scatter_dimension=0,
            tiled=True,
        ).astype(jnp.float32),
        lax.psum_scatter(
            reorder_rows(grad_keyval_w, n_blk, n_uly).astype(jnp.bfloat16),
            "ulysses",
            scatter_dimension=0,
            tiled=True,
        ).astype(jnp.float32),
        lax.psum_scatter(
            square_rows.astype(jnp.bfloat16), "ulysses", scatter_dimension=0, tiled=True
        ).astype(jnp.float32),
    )
    part_outw, part_query, part_gain_a, part_gain_m, part_keyval, square_row = (
        lax.psum_scatter(grad_out_slice, "blk", scatter_dimension=0, tiled=True),
        lax.psum_scatter(grad_query_slice, "blk", scatter_dimension=0, tiled=True),
        lax.psum_scatter(uly_gain_a, "blk", scatter_dimension=0, tiled=True),
        lax.psum_scatter(uly_gain_m, "blk", scatter_dimension=0, tiled=True),
        lax.psum_scatter(uly_keyval, "blk", scatter_dimension=0, tiled=True),
        lax.psum_scatter(uly_squares, "blk", scatter_dimension=0, tiled=True),
    )
    branch_rms = jnp.sqrt(square_row[0] / (tok * n_dev * D))
    return (
        layer_output,
        grad_input,
        part_gain_a,
        part_gain_m,
        part_query,
        part_keyval,
        part_outw,
        part_gate,
        part_up,
        part_down,
        branch_rms,
    )


MESH = pl.DeviceIdType.MESH
LANES = 128
LOG2E = 1.4426950408889634


class Place:
    def __init__(self, depth):
        self.blk = lax.axis_index("blk")
        self.u = lax.axis_index("ulysses")
        self.depth = depth
        self.z = self.blk // 4
        self.x = (self.blk // 2) % 2
        self.c = self.blk % 2
        self.up = (self.blk + 4, self.u)
        self.down = (self.blk - 4, self.u)
        self.across = (self.blk + 2 - 4 * self.x, self.u)
        self.sibling = (self.blk + 1 - 2 * self.c, self.u)
        self.other = (self.blk, 1 - self.u)
        self.has_up = self.z < depth - 1
        self.has_down = self.z > 0

    def slot(self, z, x, c):
        return z * 4 + x * 2 + c

    def greet(self, sibling=False, other=False, plane=True):
        barrier = pltpu.get_barrier_semaphore()

        def hail(device):
            pl.semaphore_signal(barrier, inc=1, device_id=device, device_id_type=MESH)

        count = 0
        if plane:
            hail(self.across)
            pl.when(self.has_up)(lambda: hail(self.up))
            pl.when(self.has_down)(lambda: hail(self.down))
            count = 1 + self.has_up.astype(jnp.int32) + self.has_down.astype(jnp.int32)
        if sibling:
            hail(self.sibling)
            count = count + 1
        if other:
            hail(self.other)
            count = count + 1
        pl.semaphore_wait(barrier, count)


class Wires:
    def __init__(self, sems):
        self.sems = sems
        self.used = 0

    def take(self, count):
        base = self.used
        self.used += count
        return lambda index: self.sems.at[base + index]


def each(act, items):
    for item in items:
        act(item)


def remote(src, dst, send, recv, device):
    return pltpu.make_async_remote_copy(
        src_ref=src, dst_ref=dst, send_sem=send, recv_sem=recv, device_id=device, device_id_type=MESH
    )


class Gather:
    def __init__(self, place, wires, src, out, cores, up_only=False):
        self.p, self.src, self.out, self.cores, self.up_only = place, src, out, cores, up_only
        n = place.depth
        self.s_up, self.s_down, self.s_across = wires.take(n), wires.take(n), wires.take(n)
        self.r_z, self.r_x = wires.take(n), wires.take(n)
        if cores:
            self.s_core, self.r_core = wires.take(2 * n), wires.take(2 * n)
        self.own = wires.take(1)(0)

    def _send(self, zz, xx, kind, src=None):
        p = self.p
        dst = self.out(zz, xx, p.c)
        src = dst if src is None else src
        if kind == "up":
            return remote(src, dst, self.s_up(zz), self.r_z(zz), p.up)
        if kind == "down":
            return remote(src, dst, self.s_down(zz), self.r_z(zz), p.down)
        if kind == "across":
            return remote(src, dst, self.s_across(zz), self.r_x(zz), p.across)
        return remote(src, dst, self.s_core(zz * 2 + xx), self.r_core(zz * 2 + xx), p.sibling)

    def _keep(self):
        p = self.p
        return pltpu.make_async_copy(self.src, self.out(p.z, p.x, p.c), self.own)

    def start(self, in_place=False):
        p = self.p
        self.in_place = in_place
        src = None if in_place else self.src
        pl.when(p.has_up)(lambda: self._send(p.z, p.x, "up", src).start())
        if not self.up_only:
            pl.when(p.has_down)(lambda: self._send(p.z, p.x, "down", src).start())
        self._send(p.z, p.x, "across", src).start()
        if self.cores:
            self._send(p.z, p.x, "core", src).start()
        if not in_place:
            self._keep().start()

    def hop(self, d):
        p = self.p

        def low():
            zz = p.z - d
            self._send(zz, p.x, "up").wait_recv()
            pl.when(p.has_up)(lambda: self._send(zz, p.x, "up").start())
            self._send(zz, p.x, "across").start()
            if self.cores:
                self._send(zz, p.x, "core").start()

        def high():
            zz = p.z + d
            self._send(zz, p.x, "down").wait_recv()
            pl.when(p.has_down)(lambda: self._send(zz, p.x, "down").start())
            self._send(zz, p.x, "across").start()
            if self.cores:
                self._send(zz, p.x, "core").start()

        pl.when(p.z >= d)(low)
        if not self.up_only:
            pl.when(p.z + d < p.depth)(high)

    def cross(self, d):
        p = self.p

        def take(zz):
            self._send(zz, 1 - p.x, "across").wait_recv()
            if self.cores:
                self._send(zz, 1 - p.x, "core").start()

        if isinstance(d, int) and d == 0:
            take(p.z)
        else:
            pl.when(p.z >= d)(lambda: take(p.z - d))
            if not self.up_only:
                pl.when(p.z + d < p.depth)(lambda: take(p.z + d))

    def core(self, zz, xx):
        self._send(zz, xx, "core").wait_recv()

    def finish(self, cores_taken=False, kept=False):
        p = self.p
        for zz in range(p.depth):

            def ends(zz=zz):
                if self.cores:
                    for xx in range(2):
                        if not cores_taken:
                            self._send(zz, xx, "core").wait_recv()
                        self._send(zz, xx, "core").wait_send()
                self._send(zz, p.x, "across").wait_send()

            if self.up_only and zz > 0:
                pl.when(p.z >= zz)(ends)
            else:
                ends()
            pl.when(p.has_up & (p.z >= zz))(lambda zz=zz: self._send(zz, p.x, "up").wait_send())
            if not self.up_only:
                pl.when(p.has_down & (p.z <= zz))(lambda zz=zz: self._send(zz, p.x, "down").wait_send())
        if not self.in_place and not kept:
            self._keep().wait()


class Scatter:
    def __init__(self, place, wires, part, out, rx, rz, pieces, down_only=False):
        self.p, self.part, self.out, self.rx, self.rz = place, part, out, rx, rz
        n = place.depth
        total = n * pieces
        self.pieces, self.down_only = pieces, down_only
        self.sx, self.cx = wires.take(total), wires.take(total)
        self.sz, self.cu, self.cd = wires.take(total), wires.take(total), wires.take(total)
        order = []
        low, high = 0, n - 1
        while low <= high:
            if not down_only:
                order.append(high)
            if low != high or down_only:
                order.append(low)
            if down_only:
                low = low + 1
            else:
                low, high = low + 1, high - 1
        self.order = order
        self.items = [(zz, k) for zz in order for k in range(pieces)]

    def _x(self, zz, k):
        i = zz * self.pieces + k
        return remote(self.part(zz, 1 - self.p.x, k), self.rx(zz, k), self.sx(i), self.cx(i), self.p.across)

    def _up(self, zz, k):
        i = zz * self.pieces + k
        return remote(self.rx(zz, k), self.rz(zz, k), self.sz(i), self.cu(i), self.p.up)

    def _down(self, zz, k, z):
        i = zz * self.pieces + k
        if isinstance(zz, int) and isinstance(z, int):
            slot = self.p.depth if zz == z - 1 else zz
        else:
            slot = jnp.where(zz == z - 1, self.p.depth, zz)
        return remote(self.rx(zz, k), self.rz(slot, k), self.sz(i), self.cd(i), self.p.down)

    def _live(self, zz, act):
        if self.down_only and zz > 0:
            pl.when(self.p.z >= zz)(act)
        else:
            act()

    def begin(self, t):
        if t < len(self.items):
            zz, k = self.items[t]
            self._live(zz, lambda: self._x(zz, k).start())

    def _pass(self, zz, k, more):
        p = self.p
        total = self.part(zz, p.x, k)[...].astype(jnp.float32) + self.rx(zz, k)[...].astype(jnp.float32)
        if more:
            total = total + self.rz(zz, k)[...].astype(jnp.float32)
        self.rx(zz, k)[...] = total.astype(jnp.bfloat16)

    def land(self, t):
        if t < 0 or t >= len(self.items):
            return
        p = self.p
        n = p.depth
        zz, k = self.items[t]
        self._live(zz, lambda: self._x(zz, k).wait_recv())

        def climb():
            self._pass(zz, k, False)
            self._up(zz, k).start()

        def sink():
            self._pass(zz, k, False)
            self._down(zz, k, n - 1).start()

        if zz > 0 and not self.down_only:
            pl.when(p.z == 0)(climb)
        if zz < n - 1:
            pl.when(p.z == n - 1)(sink)

    def chain(self, t, h):
        if t < 0 or t >= len(self.items):
            return
        p = self.p
        n = p.depth
        zz, k = self.items[t]
        low, high = h, n - 1 - h

        def from_low():
            self._up(zz, k).wait_recv()
            if zz > low:
                self._pass(zz, k, True)
                self._up(zz, k).start()

        def from_high():
            self._down(zz, k, high + 1).wait_recv()
            if zz < high:
                self._pass(zz, k, True)
                self._down(zz, k, high).start()

        if zz >= low and not self.down_only:
            pl.when(p.z == low)(from_low)
        if zz <= high:
            pl.when(p.z == high)(from_high)

    def send(self, zz):
        for k in range(self.pieces):
            self._x(zz, k).start()

    def take(self, zz, k):
        p = self.p
        n = p.depth
        self._x(zz, k).wait_recv()

        def climb():
            self._pass(zz, k, False)
            self._up(zz, k).start()

        def sink():
            self._pass(zz, k, False)
            self._down(zz, k, p.z).start()

        pl.when((p.z == 0) & (zz > 0))(climb)
        pl.when((p.z == n - 1) & (zz < n - 1))(sink)

    def relay(self, zz, k):
        p = self.p

        def climb():
            self._pass(zz, k, True)
            self._up(zz, k).start()

        def sink():
            self._pass(zz, k, True)
            self._down(zz, k, p.z).start()

        pl.when((p.z > 0) & (zz >= p.z))(lambda: self._up(zz, k).wait_recv())
        pl.when((p.z > 0) & (zz > p.z))(climb)
        pl.when(p.has_up & (zz <= p.z))(lambda: self._down(zz, k, p.z + 1).wait_recv())
        pl.when(p.has_up & (zz < p.z))(sink)

    def step(self, t):
        self.land(t)
        for h in range(1, self.p.depth):
            self.chain(t - h, h)

    def steps(self):
        return len(self.items) + self.p.depth - 1

    def finish(self):
        p = self.p
        n = p.depth
        for zz, k in self.items:
            self._live(zz, lambda zz=zz, k=k: self._x(zz, k).wait_send())
            if not self.down_only:
                pl.when(p.z < zz)(lambda zz=zz, k=k: self._up(zz, k).wait_send())
            pl.when(p.z > zz)(lambda zz=zz, k=k: self._down(zz, k, zz + 1).wait_send())

            def store(zz=zz, k=k):
                total = self.part(zz, p.x, k)[...].astype(jnp.float32)
                total = total + self.rx(zz, k)[...].astype(jnp.float32)
                if zz > 0 and not self.down_only:
                    total = total + self.rz(zz, k)[...].astype(jnp.float32)
                if zz < n - 1:
                    total = total + self.rz(n, k)[...].astype(jnp.float32)
                self.out(k)[...] = total

            pl.when(p.z == zz)(store)


class CoreScatter:
    def __init__(self, place, wires, src, rc, out, rx, rz, down_only=False):
        self.p, self.src, self.rc = place, src, rc
        n = place.depth
        self.sc, self.cc = wires.take(2 * n), wires.take(2 * n)
        self.plane = Scatter(
            place, wires, lambda zz, xx, k: rc.at[zz * 2 + xx], lambda k: out,
            lambda zz, k: rx.at[zz], lambda slot, k: rz.at[slot], 1, down_only,
        )
        self.order = self.plane.order

    def _trade(self, zz, xx):
        p = self.p
        i = zz * 2 + xx
        return remote(self.src.at[p.slot(zz, xx, 1 - p.c)], self.rc.at[i], self.sc(i), self.cc(i), p.sibling)

    def trade(self, t):
        zz = self.order[t]
        self.plane._live(zz, lambda: each(lambda xx: self._trade(zz, xx).start(), (1 - self.p.x, self.p.x)))

    def join(self, t):
        p = self.p
        zz = self.order[t]

        def act():
            for xx in (1 - p.x, p.x):
                self._trade(zz, xx).wait_recv()
                at = zz * 2 + xx
                self.rc[at] = (
                    self.src[p.slot(zz, xx, p.c)].astype(jnp.float32) + self.rc[at].astype(jnp.float32)
                ).astype(jnp.bfloat16)

        self.plane._live(zz, act)
        self.plane.begin(t)

    def release(self):
        for zz in self.order:
            self.plane._live(zz, lambda zz=zz: each(lambda xx: self._trade(zz, xx).wait_send(), range(2)))

    def finish(self):
        self.plane.finish()


def mm(left, right):
    return jnp.dot(left, right, preferred_element_type=jnp.float32)


def flip(tile):
    return tile.astype(jnp.float32).T.astype(jnp.bfloat16)


def hidden_bias(first_key, first_query, begin, keys):
    queries = begin.shape[1]
    k_pos = first_key + lax.broadcasted_iota(jnp.int32, (keys, queries), 0)
    q_pos = first_query + lax.broadcasted_iota(jnp.int32, (keys, queries), 1)
    return jnp.where((k_pos >= begin) & (k_pos <= q_pos), 0.0, NEG)


def front_kernel(
    depth, scale, x, dy, gains, wq, wkv, wo, g_own, e0, e1, e2, begin, cosine, sine,
    b, hid, attn_sq, normed_t, q_rows, qt, o, kv, ot, lse, w_all, wo_all, gain_rows, dy_all, g_all, f0, f1, f2, x_all,
    wa_own, wo_own, normed, raw, top, total, acc, p_out, p_in, sems,
):
    f32, bf = jnp.float32, jnp.bfloat16
    p = Place(depth)
    p.greet(sibling=True, other=True)
    wires = Wires(sems)
    u, blk = p.u, p.blk
    tok, width = x.shape
    group, q_half = o.shape
    heads = q_half // HEAD_DIM
    kv_half = 2 * HEAD_DIM
    rows_dev = wq.shape[0]
    half, cols = e0.shape

    def rows_of(ref, z, xx, c, member):
        row = (p.slot(z, xx, c) * 2 + member) * rows_dev
        return ref.at[pl.ds(pl.multiple_of(row, 16), rows_dev)]

    wa_mine = Gather(p, wires, wa_own.at[u], lambda z, xx, c: rows_of(w_all, z, xx, c, u), True)
    wa_peer = Gather(p, wires, None, lambda z, xx, c: rows_of(w_all, z, xx, c, 1 - u), True)
    wo_mine = Gather(p, wires, wo_own.at[u], lambda z, xx, c: rows_of(wo_all, z, xx, c, u), True)
    wo_peer = Gather(p, wires, None, lambda z, xx, c: rows_of(wo_all, z, xx, c, 1 - u), True)
    kvs = Gather(p, wires, None, lambda z, xx, c: kv.at[p.slot(z, xx, c)], True, up_only=True)
    dys = Gather(p, wires, dy, lambda z, xx, c: dy_all.at[z * 2 + xx], False)
    gws = Gather(p, wires, g_own, lambda z, xx, c: g_all.at[z * 2 + xx], False)
    ws, wr = wires.take(2), wires.take(2)
    xs, xr, xl = wires.take(1)(0), wires.take(1)(0), wires.take(1)(0)
    es, er, el = wires.take(3), wires.take(3), wires.take(3)
    cs, cr = wires.take(6), wires.take(6)
    ps, pr = wires.take(3), wires.take(3)

    for h in range(2):
        wa_own[h, :, :q_half] = wq[:, h * q_half : (h + 1) * q_half]
        for part in range(2):
            wa_own[h, :, q_half + part * HEAD_DIM : q_half + (part + 1) * HEAD_DIM] = wkv[
                :, (part * 2 + h) * HEAD_DIM : (part * 2 + h + 1) * HEAD_DIM
            ]
        wo_own[h] = wo[:, h * q_half : (h + 1) * q_half]
    columns = gains[...].T[:rows_dev, :].astype(bf)
    for h in range(2):
        wa_own[h, :, q_half + kv_half :] = columns

    wa_swap = remote(wa_own.at[1 - u], rows_of(w_all, p.z, p.x, p.c, u), ws(0), wr(0), p.other)
    wo_swap = remote(wo_own.at[1 - u], rows_of(wo_all, p.z, p.x, p.c, u), ws(1), wr(1), p.other)
    x_swap = remote(x, x_all.at[u], xs, xr, p.other)
    x_keep = pltpu.make_async_copy(x, x_all.at[u], xl)

    def part(ref, row, core):
        return ref.at[
            pl.ds(pl.multiple_of(row * half, half), half), pl.ds(pl.multiple_of(core * cols, LANES), cols)
        ]

    experts = ((e0, f0), (e1, f1), (e2, f2))
    swaps = [remote(e, part(f, u, p.c), es(i), er(i), p.other) for i, (e, f) in enumerate(experts)]
    keeps = [pltpu.make_async_copy(e, part(f, u, p.c), el(i)) for i, (e, f) in enumerate(experts)]
    shares = [remote(e, part(f, u, p.c), cs(i), cr(i), p.sibling) for i, (e, f) in enumerate(experts)]
    passes = [
        remote(part(f, 1 - u, p.c), part(f, 1 - u, p.c), cs(3 + i), cr(3 + i), p.sibling)
        for i, (e, f) in enumerate(experts)
    ]

    wa_swap.start()
    wa_mine.start()
    x_swap.start()
    x_keep.start()
    wa_swap.wait_recv()
    wa_peer.start(in_place=True)
    wo_swap.start()
    gws.start()
    for i in range(3):
        swaps[i].start()
        keeps[i].start()
        shares[i].start()
    for d in range(1, depth):
        for g in (wa_mine, wa_peer):
            g.hop(d)
            g.cross(d - 1)
    wo_mine.start()
    wo_swap.wait_recv()
    wo_peer.start(in_place=True)
    x_keep.wait()
    x_swap.wait_recv()
    for g in (wa_mine, wa_peer):
        g.cross(depth - 1)
    for g in (wa_mine, wa_peer):
        g.finish()
    gain_rows[...] = w_all[:, q_half + kv_half :].astype(f32).T[:8, :]
    for m in range(2):
        xf = x_all[m].astype(f32)
        r1 = lax.rsqrt(jnp.mean(xf * xf, -1, keepdims=True) + EPS)
        normed[m * tok : (m + 1) * tok, :] = (xf * r1 * gain_rows[0:1, :]).astype(bf)
    raw[...] = mm(normed[...], w_all[:, : q_half + kv_half])

    def rope(values):
        return values * cosine[...] + pltpu.roll(values, HEAD_DIM // 2, 1) * sine[...]

    here = p.slot(p.z, p.x, p.c)
    kv[here, :, :HEAD_DIM] = rope(raw[:, q_half : q_half + HEAD_DIM]).astype(bf)
    kv[here, :, HEAD_DIM:] = raw[:, q_half + HEAD_DIM :].astype(bf)
    kvs.start(in_place=True)
    for h in range(heads):
        hs = slice(h * HEAD_DIM, (h + 1) * HEAD_DIM)
        turned = rope(raw[:, hs])
        q_rows[h * group : (h + 1) * group, :] = turned.astype(bf)
        qt[:, h * group : (h + 1) * group] = turned.T.astype(bf)
    for j in range(0, width, 256):
        normed_t[j : j + 256, :] = flip(normed[:, j : j + 256])
    top[...] = jnp.full(top.shape, NEG, f32)
    total[...] = jnp.zeros(total.shape, f32)
    ot[...] = jnp.zeros(ot.shape, f32)

    background = {}

    def at_step(s, act):
        background.setdefault(s, []).append(act)

    at_step(0, lambda: kvs.cross(0))
    for d in range(1, depth):
        at_step(2 * d - 2, lambda d=d: kvs.hop(d))
        at_step(2 * d, lambda d=d: kvs.cross(d))
    at_step(0, dys.start)
    for d in range(1, depth):
        at_step(2 * d - 1, lambda d=d: each(lambda g: (g.hop(d), g.cross(d - 1)) and None, (wo_mine, wo_peer)))
    at_step(6, lambda: each(lambda g: g.cross(depth - 1), (wo_mine, wo_peer)))
    at_step(5, lambda: gws.hop(1))
    at_step(6, lambda: (gws.hop(2), gws.cross(0)) and None)
    at_step(7, lambda: (gws.hop(3), gws.cross(1)) and None)
    at_step(7, lambda: dys.hop(1))
    at_step(7, lambda: dys.cross(0))

    def step(s, carry):
        d = s // 2
        zz = p.z - d
        xx = jnp.where(s % 2 == 0, p.x, 1 - p.x)
        j = p.slot(zz, xx, 0)

        pl.when(zz >= 0)(lambda: kvs.core(zz, xx))

        def work():
            pair = kv[pl.ds(j, 2)].reshape(2 * group, kv_half)
            k = pair[:, :HEAD_DIM]
            vt = flip(pair[:, HEAD_DIM:])
            bias = hidden_bias(j * group, blk * group, begin[0:1, :], 2 * group)
            at = [slice(h * group, (h + 1) * group) for h in range(heads)]
            sc = [mm(k, qt[:, hs]) * (scale * LOG2E) + bias for hs in at]
            old = [top[0:1, hs] for hs in at]
            new = [jnp.maximum(o_, jnp.max(s_, axis=0, keepdims=True)) for o_, s_ in zip(old, sc)]
            e = [jnp.exp2(s_ - n_) for s_, n_ in zip(sc, new)]
            part = [jnp.sum(e_, axis=0, keepdims=True) for e_ in e]
            mixed = [mm(vt, e_.astype(bf)) for e_ in e]
            for h, hs in enumerate(at):
                keep = jnp.exp2(old[h] - new[h])
                total[0:1, hs] = total[0:1, hs] * keep + part[h]
                ot[:, hs] = ot[:, hs] * keep + mixed[h]
                top[0:1, hs] = new[h]

        pl.when((zz >= 0) & (j <= blk))(work)
        for when, acts in background.items():
            pl.when(s == when)(lambda acts=acts: each(lambda act: act(), acts))
        return carry

    lax.fori_loop(0, 2 * depth, step, 0)

    for g in (wo_mine, wo_peer):
        g.finish()
    sums = total[0:1, :]
    lse[...] = jnp.broadcast_to(top[0:1, :] + jnp.log2(sums), lse.shape)
    for h in range(heads):
        at = slice(h * group, (h + 1) * group)
        mixed = ot[:, at] / sums[:, at]
        ot[:, at] = mixed
        o[:, h * HEAD_DIM : (h + 1) * HEAD_DIM] = mixed.T.astype(bf)

    wide = width // 3
    p_swaps = []
    for i in range(3):
        cb = i * wide
        acc[:, cb : cb + wide] = contract(o[...], wo_all[cb : cb + wide, :], 1, 1)
        theirs = pl.ds(pl.multiple_of((1 - u) * tok, tok), tok)
        p_out[i] = acc[theirs, cb : cb + wide].astype(bf)
        p_swaps.append(remote(p_out.at[i], p_in.at[i], ps(i), pr(i), p.other))
        p_swaps[i].start()
    dys.hop(2)
    dys.cross(1)
    dys.hop(3)
    gws.cross(2)
    gws.cross(3)
    for i in range(3):
        swaps[i].wait_recv()
        passes[i].start()
    mine = pl.ds(pl.multiple_of(u * tok, tok), tok)
    for i in range(3):
        p_swaps[i].wait_recv()
        acc[mine, i * wide : (i + 1) * wide] += p_in[i].astype(f32)
    branch = acc[mine, :]
    hidden = x[...].astype(f32) + branch
    hid[...] = hidden
    r2 = lax.rsqrt(jnp.mean(hidden * hidden, -1, keepdims=True) + EPS)
    b[...] = (hidden * r2 * gain_rows[1:2, :]).astype(bf)
    attn_sq[...] = jnp.broadcast_to(jnp.sum(branch * branch).reshape(1, 1), attn_sq.shape)
    dys.cross(2)
    dys.cross(3)
    kvs.finish(cores_taken=True)
    dys.finish()
    gws.finish()
    wa_swap.wait_send()
    wo_swap.wait_send()
    x_swap.wait_send()
    for i in range(3):
        swaps[i].wait_send()
        keeps[i].wait()
        shares[i].wait()
        passes[i].wait()
        p_swaps[i].wait_send()


def front(x, dy, gains, wq, wkv, wo, g_own, experts, begin, cosine, sine, depth, scale, cid):
    f32, bf = jnp.float32, jnp.bfloat16
    shape = jax.ShapeDtypeStruct
    vmem = pl.BlockSpec(memory_space=pltpu.VMEM)
    V = pltpu.VMEM
    tok, width = x.shape
    group = 2 * tok
    q_half = wq.shape[1] // 2
    kv_half = 2 * HEAD_DIM
    wide = q_half + kv_half + LANES
    rows = q_half // HEAD_DIM * group
    rows_dev = wq.shape[0]
    expert = shape((2 * experts[0].shape[0], 2 * experts[0].shape[1]), bf)
    return pl.pallas_call(
        functools.partial(front_kernel, depth, scale),
        out_shape=(
            shape((tok, width), bf),
            shape((tok, width), f32),
            shape((8, LANES), f32),
            shape((width, group), bf),
            shape((rows, HEAD_DIM), bf),
            shape((HEAD_DIM, rows), bf),
            shape((group, q_half), bf),
            shape((4 * depth, group, kv_half), bf),
            shape((HEAD_DIM, rows), f32),
            shape((8, rows), f32),
            shape((width, wide), bf),
            shape((width, q_half), bf),
            shape((8, width), f32),
            shape((2 * depth, tok, width), bf),
            shape((2 * depth,) + g_own.shape, f32),
            expert,
            expert,
            expert,
            shape((2, tok, width), bf),
        ),
        in_specs=[vmem] * 13,
        out_specs=tuple([vmem] * 19),
        scratch_shapes=[
            V((2, rows_dev, wide), bf),
            V((2, rows_dev, q_half), bf),
            V((group, width), bf),
            V((group, q_half + kv_half), f32),
            V((8, rows), f32),
            V((8, rows), f32),
            V((group, width), f32),
            V((3, tok, width // 3), bf),
            V((3, tok, width // 3), bf),
            pltpu.SemaphoreType.DMA((7 * 16 * depth,)),
        ],
        compiler_params=pltpu.CompilerParams(
            collective_id=cid, has_side_effects=True, vmem_limit_bytes=56 * 2**20
        ),
        name="front",
    )(x, dy, gains, wq, wkv, wo, g_own, *experts, begin, cosine, sine)


def experts_kernel(
    depth, b, dy_own, dy_all, g_all, wg, wu, wd, hid, gain_rows,
    z_p, e0, e1, e2, dh, dhr, gm,
    b_all, act, dgate, dup, dyr, db_p, rx, rz, db, turned, sems,
):
    f32, bf = jnp.float32, jnp.bfloat16
    p = Place(depth)
    p.greet()
    wires = Wires(sems)
    tok, width = b.shape
    hidden_units = wg.shape[1]
    expert = p.blk // 2
    pair = 2 * tok
    pieces = 2
    piece = tok // pieces

    rows = [
        Gather(
            p, wires, b.at[pl.ds(k * piece, piece)],
            lambda z, x, c, k=k: b_all.at[pl.ds(pl.multiple_of((z * 2 + x) * tok + k * piece, piece), piece)],
            False,
        )
        for k in range(pieces)
    ]

    def cut(ref, k):
        return ref.at[pl.ds(k * piece, piece)]

    sums = Scatter(
        p, wires,
        lambda zz, xx, k: cut(db_p.at[zz * 2 + xx], k),
        lambda k: cut(db, k),
        lambda zz, k: cut(rx.at[zz], k),
        lambda slot, k: cut(rz.at[slot], k),
        pieces,
    )
    each(lambda g: g.start(), rows)
    spread = lax.broadcasted_iota(jnp.int32, (tok, 8), 1)

    def weight(slot):
        return jnp.sum(jnp.where(spread == expert, g_all[slot].T, 0.0), axis=1, keepdims=True)

    def nth(i):
        inner = jnp.where(i == 0, 1, jnp.where(i == 1, 0, i))
        return jnp.where(
            p.z == 0, i, jnp.where(p.z == depth - 1, depth - 1 - i, jnp.where(p.z == 1, inner, depth - 1 - inner))
        )

    def block(i, carry):
        for d in range(depth):

            def arrive(d=d):
                for g in rows:
                    if d + 1 < depth:
                        g.hop(d + 1)
                    g.cross(d)

            pl.when(i == d)(arrive)
        pl.when(i == 0)(lambda: each(lambda g: g._keep().wait(), rows))
        zz = nth(i)
        at = pl.ds(pl.multiple_of(zz * pair, pair), pair)
        for xx in range(2):
            half = pl.ds(pl.multiple_of(zz * pair + xx * tok, tok), tok)
            dyr[half, :] = (weight(zz * 2 + xx) * dy_all[zz * 2 + xx].astype(f32)).astype(bf)
        for cb in range(0, hidden_units, 256):
            cs = slice(cb, cb + 256)
            gate = mm(b_all[at, :], wg[:, cs])
            up = mm(b_all[at, :], wu[:, cs])
            sig = jax.nn.sigmoid(gate)
            act[at, cs] = (gate * sig * up).astype(bf)
            dact = mm(dyr[at, :], wd[:, cs])
            dgate[at, cs] = (dact * up * sig * (1.0 + gate * (1.0 - sig))).astype(bf)
            dup[at, cs] = (dact * gate * sig).astype(bf)
        for cb in range(0, width, 512):
            cs = slice(cb, cb + 512)
            part = contract(dgate[at, :], wg[cs, :], 1, 1) + contract(dup[at, :], wu[cs, :], 1, 1)
            for xx in range(2):
                db_p[zz * 2 + xx, :, cs] = part[xx * tok : (xx + 1) * tok, :].astype(bf)
        pl.when(i == depth - 2)(lambda: sums.send(nth(1)))
        pl.when(i == depth - 1)(lambda: each(lambda n: sums.send(nth(n)), (3, 2, 0)))
        for cb in range(0, width, 512):
            cs = slice(cb, cb + 512)
            part = contract(act[at, :], wd[cs, :], 1, 1)
            for xx in range(2):
                z_p[zz * 2 + xx, :, cs] = (
                    weight(zz * 2 + xx) * part[xx * tok : (xx + 1) * tok, :]
                ).astype(bf)
        return carry

    lax.fori_loop(0, depth, block, 0)

    wide = 256

    def grads(n):
        cs = slice(n * wide, (n + 1) * wide)
        turned[...] = flip(b_all[:, cs])
        e0[cs, :] = mm(turned[...], dgate[...]).astype(bf)
        e1[cs, :] = mm(turned[...], dup[...]).astype(bf)

    def grads_down(n):
        cs = slice(n * wide, (n + 1) * wide)
        turned[...] = flip(dyr[:, cs])
        e2[cs, :] = mm(turned[...], act[...]).astype(bf)

    work = [lambda n=n: grads(n) for n in range(width // wide)]
    work += [lambda n=n: grads_down(n) for n in range(width // wide)]
    events = []
    for n in (1, 3):
        for k in range(pieces):
            events.append(lambda n=n, k=k: sums.take(nth(n), k))
    for k in range(pieces):
        for zz in (depth - 1, 0):
            events.append(lambda zz=zz, k=k: sums.relay(zz, k))
        events.append(lambda k=k: sums.take(nth(2), k))
    for k in range(pieces):
        for zz in (2, 1):
            events.append(lambda zz=zz, k=k: sums.relay(zz, k))
        events.append(lambda k=k: sums.take(nth(0), k))
    done = 0
    for t, event in enumerate(events):
        while done < len(work) and done * len(events) <= t * len(work):
            work[done]()
            done += 1
        event()
    for act_ in work[done:]:
        act_()
    sums.finish()
    each(lambda g: g.finish(kept=True), rows)

    h = hid[...]
    r2 = lax.rsqrt(jnp.mean(h * h, -1, keepdims=True) + EPS)
    weighted = db[...] * gain_rows[1:2, :]
    inner = jnp.mean(weighted * h, -1, keepdims=True)
    total = dy_own[...].astype(f32) + r2 * weighted - h * (r2 * r2 * r2 * inner)
    dh[...] = total
    dhr[...] = total.astype(bf)
    column = jnp.sum((db[...] * h * r2).T, axis=1, keepdims=True)
    lane = lax.broadcasted_iota(jnp.int32, (width, LANES), 1)
    gm[...] = jnp.where(lane == 1, column, 0.0)


def run_experts(b, dy_own, dy_all, g_all, weights, hid, gain_rows, depth, cid):
    f32, bf = jnp.float32, jnp.bfloat16
    shape = jax.ShapeDtypeStruct
    vmem = pl.BlockSpec(memory_space=pltpu.VMEM)
    V = pltpu.VMEM
    tok, width = b.shape
    units = weights[0].shape[1]
    rows = 2 * depth * tok
    grad = shape((width, units), bf)
    return pl.pallas_call(
        functools.partial(experts_kernel, depth),
        out_shape=(
            shape((2 * depth, tok, width), bf),
            grad,
            grad,
            grad,
            shape((tok, width), f32),
            shape((tok, width), bf),
            shape((width, LANES), f32),
        ),
        in_specs=[vmem] * 9,
        out_specs=tuple([vmem] * 7),
        scratch_shapes=[
            V((rows, width), bf),
            V((rows, units), bf),
            V((rows, units), bf),
            V((rows, units), bf),
            V((rows, width), bf),
            V((2 * depth, tok, width), bf),
            V((depth, tok, width), bf),
            V((depth + 1, tok, width), bf),
            V((tok, width), f32),
            V((256, rows), bf),
            pltpu.SemaphoreType.DMA((2 * (5 * depth + 1) + 10 * depth,)),
        ],
        compiler_params=pltpu.CompilerParams(
            collective_id=cid, has_side_effects=True, vmem_limit_bytes=58 * 2**20
        ),
        name="experts",
    )(b, dy_own, dy_all, g_all, *weights, hid, gain_rows)


def closing_kernel(
    depth, scale, attn_sq, dhr, dh, hid, x_all, gain, w, wo, at, q_rows, qt, o, kv, begin, ot, lse, cosine, sine, zp, gm, e0, e1, e2,
    out, gin, gq, go, gkv, gg, f0, f1, f2, sq,
    dhr_all, dot_, dqt, delta, dkv, do_rows, dq, att, acc,
    z_sum, z_rx, z_rz, go_p, go_rc, go_rx, go_rz, kv_sum, kv_rc, kv_rx, kv_rz,
    gq_rc, gq_rx, gq_rz, gk_p, gk_sum, gk_rc, gk_rx, gk_rz,
    e_own, e_core, e_low, e_peer, da_out, da_in, t_out, t_in, sq_own, sems,
):
    f32, bf = jnp.float32, jnp.bfloat16
    p = Place(depth)
    p.greet(sibling=True, other=True)
    wires = Wires(sems)
    u, blk = p.u, p.blk
    tok = dhr.shape[0]
    group, q_half = o.shape
    heads = q_half // HEAD_DIM
    kv_half = 2 * HEAD_DIM
    blocks = kv.shape[0]
    rows_blk = gq.shape[0]

    cols = f0.shape[1]
    rows_e = f0.shape[0]
    es, er, el, ps, pr = wires.take(3), wires.take(3), wires.take(3), wires.take(3), wires.take(3)

    def e_cols(ref, core):
        return ref.at[:, pl.ds(pl.multiple_of(core * cols, LANES), cols)]

    def e_rows(member):
        return pl.ds(pl.multiple_of(member * rows_e, rows_e), rows_e)

    experts = (e0, e1, e2)
    e_trade = [remote(e_cols(e, 1 - p.c), e_core.at[i], es(i), er(i), p.sibling) for i, e in enumerate(experts)]
    e_keep = [pltpu.make_async_copy(e_cols(e, p.c), e_own.at[i], el(i)) for i, e in enumerate(experts)]
    e_swap = [remote(e_low.at[i], e_peer.at[i], ps(i), pr(i), p.other) for i in range(3)]

    def e_join(i):
        e_trade[i].wait_recv()
        e_keep[i].wait()
        theirs = e_rows(1 - u)
        e_low[i] = (e_own[i, theirs, :].astype(f32) + e_core[i, theirs, :].astype(f32)).astype(bf)
        e_swap[i].start()

    def e_done(i):
        e_swap[i].wait_recv()
        mine = e_rows(u)
        total = e_own[i, mine, :].astype(f32) + e_core[i, mine, :].astype(f32)
        (f0, f1, f2)[i][...] = total + e_peer[i].astype(f32)

    ds, dr, dl = wires.take(1)(0), wires.take(1)(0), wires.take(1)(0)
    swap = remote(dhr, dhr_all.at[u], ds, dr, p.other)
    keep = pltpu.make_async_copy(dhr, dhr_all.at[u], dl)

    pieces = 2
    z_rows = tok // pieces

    def cut(ref, k):
        return ref.at[pl.ds(k * z_rows, z_rows)]

    zs = Scatter(
        p, wires,
        lambda zz, xx, k: cut(zp.at[zz * 2 + xx], k),
        lambda k: cut(z_sum, k),
        lambda zz, k: cut(z_rx.at[zz], k),
        lambda slot, k: cut(z_rz.at[slot], k),
        pieces,
    )
    gos = CoreScatter(p, wires, go_p, go_rc, go, go_rx, go_rz)
    kvs = CoreScatter(p, wires, dkv, kv_rc, kv_sum, kv_rx, kv_rz, down_only=True)
    gqs = CoreScatter(p, wires, go_p, gq_rc, gq, gq_rx, gq_rz)
    gks = CoreScatter(p, wires, gk_p, gk_rc, gk_sum, gk_rx, gk_rz)
    sqs = Gather(p, wires, sq_own, lambda z, xx, c: sq.at[p.slot(z, xx, c), u], True)
    qs, qr = wires.take(1)(0), wires.take(1)(0)
    sq_swap = remote(sq.at[:, u], sq.at[:, u], qs, qr, p.other)

    swap.start()
    keep.start()
    for i in range(3):
        e_trade[i].start()
        e_keep[i].start()
    ahead = 3
    for t in range(ahead):
        zs.begin(t)

    dqt[...] = jnp.zeros(dqt.shape, f32)
    dkv[...] = jnp.zeros(dkv.shape, bf)
    for i in range(3):
        e_join(i)
    keep.wait()
    swap.wait_recv()

    for m in range(2):
        part = mm(dhr_all[m], wo[...]).astype(bf)
        for h in range(heads):
            do_rows[h * group + m * tok : h * group + (m + 1) * tok, :] = part[:, h * HEAD_DIM : (h + 1) * HEAD_DIM]
    for h in range(heads):
        hs = slice(h * group, (h + 1) * group)
        part = do_rows[hs, :]
        turned = part.astype(f32).T
        dot_[:, hs] = turned.astype(bf)
        delta[0:1, hs] = jnp.sum(turned * ot[:, hs], axis=0, keepdims=True)

    background = {}
    later = []

    def at_tile(j, act):
        if j < blocks:
            background.setdefault(j, []).append(act)
        else:
            later.append((j, act))

    def out_rows(i, carry):
        rows = pl.ds(pl.multiple_of(i * rows_blk, rows_blk), rows_blk)
        go_p[i] = mm(att[rows, :], o[...]).astype(bf)
        return carry

    def out_grads():
        for m in range(2):
            att[:, m * tok : (m + 1) * tok] = flip(dhr_all[m])
        lax.fori_loop(0, blocks, out_rows, 0)
        for t in range(depth):
            gos.trade(t)

    def z_land(t):
        zs.land(t)
        zs.begin(t + ahead)

    for t in range(len(zs.items)):
        first = max(0, 2 * t - 4)
        at_tile(first, lambda t=t: z_land(t))
        for h in range(1, depth):
            at_tile(first + 4 * h, lambda t=t, h=h: zs.chain(t, h))
    for t in range(depth - 1):
        last = 4 * t + 3
        at_tile(last, lambda t=t: kvs.trade(t))
        at_tile(last + 1, lambda t=t: kvs.join(t))
        at_tile(last + 3, lambda t=t: kvs.plane.land(t))
        for h in range(1, depth):
            at_tile(last + 3 + 3 * h, lambda t=t, h=h: kvs.plane.chain(t, h))
    at_tile(8, out_grads)
    for t in range(depth):
        at_tile(9 + t, lambda t=t: gos.join(t))

    def tile(j, carry):
        def work():
            k = kv[j, :, :HEAD_DIM]
            v = kv[j, :, HEAD_DIM:]
            kt = flip(k)
            bias = hidden_bias(j * group, blk * group, begin[0:1, :], group)
            at_ = [slice(h * group, (h + 1) * group) for h in range(heads)]
            sc = [mm(k, qt[:, hs]) * (scale * LOG2E) + bias for hs in at_]
            dp = [mm(v, dot_[:, hs]) for hs in at_]
            e = [jnp.exp2(s_ - lse[0:1, hs]) for s_, hs in zip(sc, at_)]
            g = [(e_ * (d_ - delta[0:1, hs])).astype(bf) for e_, d_, hs in zip(e, dp, at_)]
            wide_g = jnp.concatenate(g, 1)
            dk = mm(wide_g, q_rows[...])
            dv = mm(jnp.concatenate([e_.astype(bf) for e_ in e], 1), do_rows[...])
            dqt[...] += mm(kt, wide_g)
            dkv[j, :, :HEAD_DIM] = (dk * scale).astype(bf)
            dkv[j, :, HEAD_DIM:] = dv.astype(bf)

        pl.when(j <= blk)(work)
        for when, acts in background.items():
            pl.when(j == when)(lambda acts=acts: each(lambda act: act(), acts))
        return carry

    lax.fori_loop(0, blocks, tile, 0)

    kvs.trade(depth - 1)
    gos.release()

    def back_turn(values):
        return values * cosine[...] - pltpu.roll(values, HEAD_DIM // 2, 1) * sine[...]

    for h in range(heads):
        hs = slice(h * group, (h + 1) * group)
        cs = slice(h * HEAD_DIM, (h + 1) * HEAD_DIM)
        dq[:, cs] = back_turn((dqt[:, hs] * scale).T.astype(bf).astype(f32)).astype(bf)
    kvs.join(depth - 1)

    def query_rows(i, carry):
        rows = pl.ds(pl.multiple_of(i * rows_blk, rows_blk), rows_blk)
        go_p[i] = mm(at[rows, :], dq[...]).astype(bf)
        return carry

    lax.fori_loop(0, blocks, query_rows, 0)
    for t in range(depth):
        gqs.trade(t)
    for m in range(2):
        for cb in range(0, D, 512):
            acc[m * tok : (m + 1) * tok, cb : cb + 512] = contract(
                dq[m * tok : (m + 1) * tok, :], w[cb : cb + 512, :q_half], 1, 1
            )
    kvs.plane.land(depth - 1)
    later.sort(key=lambda item: item[0])
    each(lambda item: item[1](), later)
    kvs.release()
    kvs.finish()
    for t in range(depth):
        gqs.join(t)
    kv_low = kv_sum[...].astype(bf).astype(f32)
    kv_pre = jnp.concatenate([back_turn(kv_low[:, :HEAD_DIM]).astype(bf), kv_low[:, HEAD_DIM:].astype(bf)], 1)

    da_s, da_r = wires.take(3), wires.take(3)
    wide = D // 3
    da_swaps = []
    for i in range(3):
        cb = i * wide
        part = contract(kv_pre, w[cb : cb + wide, q_half : q_half + kv_half], 1, 1)
        acc[:, cb : cb + wide] += part
        theirs = pl.ds(pl.multiple_of((1 - u) * tok, tok), tok)
        da_out[i] = acc[theirs, cb : cb + wide].astype(bf)
        da_swaps.append(remote(da_out.at[i], da_in.at[i], da_s(i), da_r(i), p.other))
        da_swaps[i].start()

    column = jnp.zeros((D, 1), f32)
    for m in range(2):
        xf = x_all[m].astype(f32)
        r1 = lax.rsqrt(jnp.mean(xf * xf, -1, keepdims=True) + EPS)
        terms = acc[m * tok : (m + 1) * tok, :] * xf * r1
        column = column + jnp.sum(terms.T, axis=1, keepdims=True)
    lane = lax.broadcasted_iota(jnp.int32, (D, LANES), 1)
    gain_cols = (jnp.where(lane == 0, column, 0.0) + gm[...]).astype(bf)
    for i in range(blocks):
        gk_p[i, :, kv_half:] = gain_cols[i * rows_blk : (i + 1) * rows_blk, :]

    def keyval_rows(i, carry):
        rows = pl.ds(pl.multiple_of(i * rows_blk, rows_blk), rows_blk)
        gk_p[i, :, :kv_half] = mm(at[rows, :], kv_pre).astype(bf)
        return carry

    lax.fori_loop(0, blocks, keyval_rows, 0)
    for t in range(depth):
        gks.trade(t)
    for t in range(depth):
        gks.join(t)

    zs.finish()
    result = hid[...] + z_sum[...]
    out[...] = result.astype(bf)
    spread = lax.broadcasted_iota(jnp.int32, (8, LANES), 1)
    z_sq = jnp.sum(z_sum[...] * z_sum[...])
    r_sq = jnp.sum(result * result)
    sq_own[...] = jnp.where(
        spread == 0, attn_sq[...], jnp.where(spread == 1, z_sq, jnp.where(spread == 2, r_sq, 0.0))
    )
    sqs.start()
    for t in range(gos.plane.steps()):
        gos.plane.step(t)
    gos.finish()
    for i in range(3):
        e_done(i)

    mine = pl.ds(pl.multiple_of(u * tok, tok), tok)
    for i in range(3):
        da_swaps[i].wait_recv()
        acc[mine, i * wide : (i + 1) * wide] += da_in[i].astype(f32)
    da = acc[mine, :]
    xf = x_all[u].astype(f32)
    r1 = lax.rsqrt(jnp.mean(xf * xf, -1, keepdims=True) + EPS)
    weighted = da * gain[0:1, :]
    inner = jnp.mean(weighted * xf, -1, keepdims=True)
    gin[...] = dh[...] + r1 * weighted - xf * (r1 * r1 * r1 * inner)
    steps = gqs.plane.steps()
    for t in range(steps):
        gqs.plane.step(t)
        gks.plane.step(t)
        if t + 1 < depth:
            sqs.hop(t + 1)
        if t < depth:
            sqs.cross(t)
    sqs.finish()
    sq_swap.start()
    gks.release()
    gks.finish()
    rows_dev = gkv.shape[0]
    theirs = pl.ds(pl.multiple_of((1 - u) * rows_dev, rows_dev), rows_dev)
    own = pl.ds(pl.multiple_of(u * rows_dev, rows_dev), rows_dev)
    t_out[...] = gk_sum[theirs, :]
    ts, tr = wires.take(1)(0), wires.take(1)(0)
    t_swap = remote(t_out, t_in, ts, tr, p.other)
    t_swap.start()
    gqs.release()
    gqs.finish()
    t_swap.wait_recv()
    for part in range(2):
        here = slice(part * HEAD_DIM, (part + 1) * HEAD_DIM)
        base = part * kv_half
        gkv[:, pl.ds(pl.multiple_of(base + u * HEAD_DIM, LANES), HEAD_DIM)] = gk_sum[own, here]
        gkv[:, pl.ds(pl.multiple_of(base + (1 - u) * HEAD_DIM, LANES), HEAD_DIM)] = t_in[:, here]
    gg[...] = gk_sum[own, kv_half:] + t_in[:, kv_half:]
    sq_swap.wait()
    t_swap.wait_send()
    swap.wait_send()
    for i in range(3):
        e_trade[i].wait_send()
        e_swap[i].wait_send()
        da_swaps[i].wait_send()


def closing(attn_sq, dhr, dh, hid, x_all, gain, w, wo, at, q_rows, qt, o, kv, begin, ot, lse, cosine, sine, zp, gm, grads, depth, scale, cid):
    f32, bf = jnp.float32, jnp.bfloat16
    tok, width = dhr.shape
    group, q_half = o.shape
    blocks = kv.shape[0]
    rows_blk = width // blocks
    rows_e, cols = grads[0].shape[0] // 2, grads[0].shape[1] // 2
    kv_half = 2 * HEAD_DIM
    shape = jax.ShapeDtypeStruct
    vmem = pl.BlockSpec(memory_space=pltpu.VMEM)
    hbm = pl.BlockSpec(memory_space=pl.ANY)
    V = pltpu.VMEM

    def buffers(block):
        return [
            V((blocks // 2,) + block, bf),
            V((depth,) + block, bf),
            V((depth + 1,) + block, bf),
        ]

    grad = shape((rows_e, cols), f32)
    rows = q_half // HEAD_DIM * group
    return pl.pallas_call(
        functools.partial(closing_kernel, depth, scale),
        out_shape=(
            shape((tok, width), bf),
            shape((tok, width), f32),
            shape((rows_blk, q_half), f32),
            shape((rows_blk, q_half), f32),
            shape((rows_blk // 2, 2 * kv_half), f32),
            shape((rows_blk // 2, LANES), f32),
            grad,
            grad,
            grad,
            shape((blocks, 2, 8, LANES), f32),
        ),
        in_specs=[vmem] * 20 + [hbm] * 3,
        out_specs=tuple([vmem] * 10),
        scratch_shapes=[
            V((2, tok, width), bf),
            V((HEAD_DIM, rows), bf),
            V((HEAD_DIM, rows), f32),
            V((8, rows), f32),
            V(kv.shape, bf),
            V((rows, HEAD_DIM), bf),
            V((group, q_half), bf),
            V((width, group), bf),
            V((group, width), f32),
            V((tok, width), f32),
            V((depth, tok, width), bf),
            V((depth + 1, tok, width), bf),
            V((blocks, rows_blk, q_half), bf),
        ]
        + buffers((rows_blk, q_half))
        + [V((group, kv_half), f32)]
        + buffers((group, kv_half))
        + buffers((rows_blk, q_half))
        + [V((blocks, rows_blk, kv_half + LANES), bf), V((rows_blk, kv_half + LANES), f32)]
        + buffers((rows_blk, kv_half + LANES))
        + [
            V((3, 2 * rows_e, cols), bf),
            V((3, 2 * rows_e, cols), bf),
            V((3, rows_e, cols), bf),
            V((3, rows_e, cols), bf),
            V((3, tok, width // 3), bf),
            V((3, tok, width // 3), bf),
            V((rows_blk // 2, kv_half + LANES), f32),
            V((rows_blk // 2, kv_half + LANES), f32),
            V((8, LANES), f32),
            pltpu.SemaphoreType.DMA((320,)),
        ],
        compiler_params=pltpu.CompilerParams(
            collective_id=cid, has_side_effects=True, vmem_limit_bytes=60 * 2**20
        ),
        name="closing",
    )(attn_sq, dhr, dh, hid, x_all, gain, w, wo, at, q_rows, qt, o, kv, begin, ot, lse, cosine, sine, zp, gm, *grads)


def planned(
    layer_input,
    grad_output,
    gain_attn,
    gain_moe,
    w_query,
    w_keyval,
    w_out,
    w_gate,
    w_up,
    w_down,
    gate_weights,
    expert_ids,
    doc_starts,
):
    bf, f32 = jnp.bfloat16, jnp.float32
    n_blk = lax.axis_size("blk")
    n_uly = lax.axis_size("ulysses")
    depth = n_blk // 4
    tok = layer_input.shape[0]
    group = tok * n_uly
    rows_dev = w_query.shape[0]
    scale = 1.0 / math.sqrt(HEAD_DIM)
    blk = lax.axis_index("blk")
    u = lax.axis_index("ulysses")
    experts = n_blk // 2
    n_dev = n_blk * n_uly

    gains = jnp.zeros((LANES, LANES), f32).at[0, :rows_dev].set(gain_attn.astype(f32))
    gains = gains.at[1, :rows_dev].set(gain_moe.astype(f32))
    named = expert_ids[:, :, None] == jnp.arange(experts, dtype=jnp.int32)[None, None, :]
    g_own = jnp.sum(jnp.where(named, gate_weights[:, :, None], 0.0), 1).T
    positions = blk * group + jnp.arange(group, dtype=jnp.int32)
    begins = doc_begin(positions, doc_starts)
    half = HEAD_DIM // 2
    freq = ROPE_BASE ** (-jnp.arange(half, dtype=f32) * 2.0 / HEAD_DIM)
    angle = (positions - begins).astype(f32)[:, None] * freq[None, :]
    cosine = jnp.concatenate([jnp.cos(angle)] * 2, 1)
    sine = jnp.sin(angle)
    sine = jnp.concatenate([-sine, sine], 1)
    begin_rows = jnp.broadcast_to(begins[None, :], (8, group))
    (
        normed_m, hidden, attn_sq, normed_t, query_rows, query_t, mixed, kv_all, mixed_t, lse, w_all, out_w, gain_rows,
        dy_all, g_all, gate_w, up_w, down_w, inputs,
    ) = front(
        layer_input, grad_output, gains, w_query, w_keyval, w_out, g_own, (w_gate, w_up, w_down),
        begin_rows, cosine, sine, depth, scale, 1,
    )
    z_part, grad_gate, grad_up, grad_down, grad_hidden, grad_hidden_low, gain_terms = run_experts(
        normed_m, grad_output, dy_all, g_all, (gate_w, up_w, down_w), hidden, gain_rows, depth, 2
    )
    (
        layer_output, grad_input, part_query, part_out, part_keyval, gain_sums, grad_gate, grad_up, grad_down, squares
    ) = closing(
        attn_sq, grad_hidden_low, grad_hidden, hidden, inputs, gain_rows, w_all, out_w, normed_t, query_rows, query_t,
        mixed, kv_all, begin_rows, mixed_t, lse, cosine, sine, z_part, gain_terms, (grad_gate, grad_up, grad_down),
        depth, scale, 3,
    )
    squares = jnp.sum(squares[:, :, 0, :3], (0, 1))
    branch_rms = jnp.sqrt(squares / (tok * n_dev * D))
    return (
        layer_output,
        grad_input,
        gain_sums[:, 0],
        gain_sums[:, 1],
        part_query,
        part_keyval,
        part_out,
        grad_gate,
        grad_up,
        grad_down,
        branch_rms,
    )


def solution(mesh):
    in_specs = (
        P(("blk", "ulysses"), None),
        P(("blk", "ulysses"), None),
        P(("blk", "ulysses")),
        P(("blk", "ulysses")),
        P(("blk", "ulysses"), None),
        P(("blk", "ulysses"), None),
        P(("blk", "ulysses"), None),
        P("ulysses", "blk"),
        P("ulysses", "blk"),
        P("ulysses", "blk"),
        P(("blk", "ulysses"), None),
        P(("blk", "ulysses"), None),
        P(),
    )
    out_specs = (
        P(("blk", "ulysses"), None),
        P(("blk", "ulysses"), None),
        P(("blk", "ulysses")),
        P(("blk", "ulysses")),
        P("blk", "ulysses"),
        P(("blk", "ulysses"), None),
        P("blk", "ulysses"),
        P("ulysses", "blk"),
        P("ulysses", "blk"),
        P("ulysses", "blk"),
        P(),
    )
    blocks, members = mesh.shape["blk"], mesh.shape["ulysses"]
    body = planned if blocks == 16 and members == KV_HEADS else local
    return jax.shard_map(body, mesh=mesh, in_specs=in_specs, out_specs=out_specs, check_vma=False)
```

```python
import functools
import math

import jax
import jax.numpy as jnp
import numpy as np
from jax import lax
from jax.experimental import pallas as pl
from jax.experimental.pallas import tpu as pltpu
from jax.sharding import PartitionSpec as P

D = 1536
HEADS = 12
KV_HEADS = 2
HEAD_DIM = 128
TOP = 4


EPS = 1e-06
ROPE_BASE = 1000000.0
NEG = -1e30


def rotate(values, positions, sign):
    half = values.shape[-1] // 2
    freq = ROPE_BASE ** (-jnp.arange(half, dtype=jnp.float32) * 2.0 / values.shape[-1])
    angle = positions.astype(jnp.float32)[:, None] * freq[None, :]
    cosine = jnp.cos(angle)[:, None, :]
    sine = sign * jnp.sin(angle)[:, None, :]
    first = values[..., :half]
    second = values[..., half:]
    return jnp.concatenate([first * cosine - second * sine, second * cosine + first * sine], -1)


def doc_begin(positions, doc_starts):
    return jnp.max(
        jnp.where(doc_starts[None, :] <= positions[:, None], doc_starts[None, :], 0), axis=1
    )


def norm_back(values, factor, gain, grad):
    weighted = grad * gain
    inner = jnp.mean(weighted * values, -1, keepdims=True)
    return factor * weighted - values * factor * factor * factor * inner


def visible_mask(q_pos, q_begin, k_pos):
    return (k_pos[None, :] >= q_begin[:, None]) & (k_pos[None, :] <= q_pos[:, None])


def split_blocks(array):
    rows = array.shape[0]
    size = min(rows, 512)
    return (array.reshape((rows // size, size) + array.shape[1:]), size)


def contract(left, right, left_dim, right_dim):
    return lax.dot_general(
        left, right, (((left_dim,), (right_dim,)), ((), ())), preferred_element_type=jnp.float32
    )


def reorder_rows(array, outer, inner):
    rows = array.shape[0]
    shaped = array.reshape((outer, inner, rows // (outer * inner)) + array.shape[1:])
    return jnp.swapaxes(shaped, 0, 1).reshape(array.shape)


def route(payload):
    return lax.all_to_all(payload, "blk", split_axis=0, concat_axis=0, tiled=True)


def backward_block(queries, grads, lse, delta, q_pos, q_begin, keys, values, k_start, scale):
    k_pos = k_start + jnp.arange(keys.shape[0], dtype=jnp.int32)
    visible = visible_mask(q_pos, q_begin, k_pos)[None]
    scores = jnp.einsum("qhd,kd->hqk", queries, keys, preferred_element_type=jnp.float32) * scale
    probs = jnp.where(visible, jnp.exp(scores - lse[:, :, None]), 0.0)
    probs_low = probs.astype(jnp.bfloat16)
    grad_probs = jnp.einsum("qhd,kd->hqk", grads, values, preferred_element_type=jnp.float32)
    grad_scores = (probs * (grad_probs - delta[:, :, None])).astype(jnp.bfloat16)
    part_q = (
        jnp.einsum("hqk,kd->qhd", grad_scores, keys, preferred_element_type=jnp.float32) * scale
    )
    part_k = (
        jnp.einsum("hqk,qhd->kd", grad_scores, queries, preferred_element_type=jnp.float32) * scale
    )
    part_v = jnp.einsum("hqk,qhd->kd", probs_low, grads, preferred_element_type=jnp.float32)
    return (part_q, part_k, part_v)


def local(
    layer_input,
    grad_output,
    gain_attn,
    gain_moe,
    w_query,
    w_keyval,
    w_out,
    w_gate,
    w_up,
    w_down,
    gate_weights,
    expert_ids,
    doc_starts,
):
    n_blk = lax.axis_size("blk")
    n_uly = lax.axis_size("ulysses")
    tok = layer_input.shape[0]
    group = tok * n_uly
    heads_dev = HEADS // n_uly
    per_kv = HEADS // KV_HEADS
    which = [c * heads_dev // per_kv for c in range(n_uly)]
    kv_width = KV_HEADS * HEAD_DIM
    q_width = HEADS * HEAD_DIM
    scale = 1.0 / math.sqrt(HEAD_DIM)
    blk_index = lax.axis_index("blk")
    device = blk_index * n_uly + lax.axis_index("ulysses")
    tok_pos = device * tok + jnp.arange(tok, dtype=jnp.int32)
    places = tok_pos - doc_begin(tok_pos, doc_starts)
    gain_a, gain_m, query_w, keyval_w, out_w = (
        lax.all_gather(gain_attn, ("blk", "ulysses"), axis=0, tiled=True),
        lax.all_gather(gain_moe, ("blk", "ulysses"), axis=0, tiled=True),
        lax.all_gather(w_query, ("blk", "ulysses"), axis=0, tiled=True),
        lax.all_gather(w_keyval, ("blk", "ulysses"), axis=0, tiled=True),
        lax.all_gather(w_out, ("blk", "ulysses"), axis=0, tiled=True),
    )
    gate_w, up_w, down_w = (
        lax.all_gather(w_gate, "ulysses", axis=0, tiled=True),
        lax.all_gather(w_up, "ulysses", axis=0, tiled=True),
        lax.all_gather(w_down, "ulysses", axis=0, tiled=True),
    )
    gain_a = gain_a.astype(jnp.float32)
    gain_m = gain_m.astype(jnp.float32)
    inputs = layer_input.astype(jnp.float32)
    factor_a = lax.rsqrt(jnp.mean(inputs * inputs, -1, keepdims=True) + EPS)
    normed_a = (inputs * factor_a * gain_a).astype(jnp.bfloat16)
    query_raw = jnp.dot(normed_a, query_w, preferred_element_type=jnp.float32)
    keyval_raw = jnp.dot(normed_a, keyval_w, preferred_element_type=jnp.float32)
    queries = rotate(query_raw.reshape(tok, HEADS, HEAD_DIM), places, 1.0).astype(jnp.bfloat16)
    keys = rotate(keyval_raw[:, :kv_width].reshape(tok, KV_HEADS, HEAD_DIM), places, 1.0).astype(
        jnp.bfloat16
    )
    values = keyval_raw[:, kv_width:].reshape(tok, KV_HEADS, HEAD_DIM).astype(jnp.bfloat16)
    key_copies = jnp.stack([keys[:, j] for j in which], 1)
    value_copies = jnp.stack([values[:, j] for j in which], 1)
    spread_normed = jnp.broadcast_to(normed_a[:, None, :], (tok, n_uly, D))
    head_q, head_k, head_v, head_normed = (
        lax.all_to_all(queries, "ulysses", split_axis=1, concat_axis=0, tiled=True),
        lax.all_to_all(key_copies, "ulysses", split_axis=1, concat_axis=0, tiled=True),
        lax.all_to_all(value_copies, "ulysses", split_axis=1, concat_axis=0, tiled=True),
        lax.all_to_all(spread_normed, "ulysses", split_axis=1, concat_axis=0, tiled=True),
    )
    key_local = head_k[:, 0, :]
    value_local = head_v[:, 0, :]
    normed_group = head_normed[:, 0, :]
    q_pos = blk_index * group + jnp.arange(group, dtype=jnp.int32)
    q_begin = doc_begin(q_pos, doc_starts)
    start_state = (
        jnp.full((heads_dev, group), NEG, jnp.float32),
        jnp.zeros((heads_dev, group), jnp.float32),
        jnp.zeros((group, heads_dev, HEAD_DIM), jnp.float32),
    )
    state = start_state
    key_rows = lax.all_gather(key_local, "blk", axis=0, tiled=True)
    value_rows = lax.all_gather(value_local, "blk", axis=0, tiled=True)
    key_blocks, size = split_blocks(key_rows)
    value_blocks, _ = split_blocks(value_rows)

    def attend_step(inner, item):
        key_blk, value_blk, number = item
        k_start = number * size
        live = (k_start <= q_pos[-1]) & (k_start + size - 1 >= q_begin[0])

        def attend_work(current):
            top, total, acc = current
            k_pos = k_start + jnp.arange(size, dtype=jnp.int32)
            visible = visible_mask(q_pos, q_begin, k_pos)[None]
            scores = (
                jnp.einsum("qhd,kd->hqk", head_q, key_blk, preferred_element_type=jnp.float32)
                * scale
            )
            scores = jnp.where(visible, scores, NEG)
            new_top = jnp.maximum(top, jnp.max(scores, -1))
            weights = jnp.where(visible, jnp.exp(scores - new_top[:, :, None]), 0.0)
            keep = jnp.exp(top - new_top)
            total = total * keep + jnp.sum(weights, -1)
            acc = acc * jnp.transpose(keep)[:, :, None] + jnp.einsum(
                "hqk,kd->qhd",
                weights.astype(jnp.bfloat16),
                value_blk,
                preferred_element_type=jnp.float32,
            )
            return (new_top, total, acc)

        return (lax.cond(live, attend_work, lambda current: current, inner), None)

    state, _ = lax.scan(
        attend_step,
        state,
        (key_blocks, value_blocks, jnp.arange(key_blocks.shape[0], dtype=jnp.int32)),
    )
    top, total, acc = state
    mixed = acc / jnp.transpose(total)[:, :, None]
    mixed_low = mixed.astype(jnp.bfloat16)
    lse = top + jnp.log(total)
    attended = lax.all_to_all(
        mixed_low, "ulysses", split_axis=0, concat_axis=1, tiled=True
    ).reshape(tok, q_width)
    attn_branch = contract(attended, out_w, 1, 1)
    hidden = inputs + attn_branch
    factor_m = lax.rsqrt(jnp.mean(hidden * hidden, -1, keepdims=True) + EPS)
    normed_m = (hidden * factor_m * gain_m).astype(jnp.bfloat16)
    experts = n_blk // 2
    capacity = min(tok, 2 * tok * TOP // experts)
    flat_ids = expert_ids.reshape(-1)
    picks = (flat_ids[:, None] == jnp.arange(experts, dtype=jnp.int32)[None, :]).astype(jnp.int32)
    slots = jnp.sum((jnp.cumsum(picks, 0) - 1) * picks, -1)

    def dispatch(rows):
        buffer = jnp.zeros((experts, capacity, D), jnp.bfloat16).at[flat_ids, slots].set(rows)
        return route(jnp.repeat(buffer, 2, axis=0)).reshape(n_blk * capacity, D)

    def collect(rows):
        back = route(rows.astype(jnp.bfloat16).reshape(n_blk, capacity, D))
        return back[2 * flat_ids, slots].astype(jnp.float32) + back[2 * flat_ids + 1, slots].astype(
            jnp.float32
        )

    expert_in = dispatch(jnp.repeat(normed_m, TOP, axis=0))
    gate_pre = jnp.dot(expert_in, gate_w, preferred_element_type=jnp.float32)
    up_pre = jnp.dot(expert_in, up_w, preferred_element_type=jnp.float32)
    act = (jax.nn.silu(gate_pre) * up_pre).astype(jnp.bfloat16)
    expert_out = contract(act, down_w, 1, 1)
    returned = collect(expert_out).reshape(tok, TOP, D)
    moe_branch = jnp.sum(gate_weights[:, :, None] * returned, 1)
    result = hidden + moe_branch
    layer_output = result.astype(jnp.bfloat16)
    grad_res = grad_output.astype(jnp.float32)
    routed_grad = (
        (gate_weights[:, :, None] * grad_res[:, None, :]).reshape(tok * TOP, D).astype(jnp.bfloat16)
    )
    expert_grad = dispatch(routed_grad)
    grad_act = jnp.dot(expert_grad, down_w, preferred_element_type=jnp.float32)
    grad_down = contract(expert_grad, act, 0, 0)
    sig = jax.nn.sigmoid(gate_pre)
    grad_gate_pre = (grad_act * up_pre * sig * (1.0 + gate_pre * (1.0 - sig))).astype(jnp.bfloat16)
    grad_up_pre = (grad_act * gate_pre * sig).astype(jnp.bfloat16)
    grad_gate = contract(expert_in, grad_gate_pre, 0, 0)
    grad_up = contract(expert_in, grad_up_pre, 0, 0)
    grad_in = contract(grad_gate_pre, gate_w, 1, 1) + contract(grad_up_pre, up_w, 1, 1)
    grad_normed_m = jnp.sum(collect(grad_in).reshape(tok, TOP, D), 1)
    grad_gain_m = jnp.sum(grad_normed_m * hidden * factor_m, 0)
    grad_hidden = grad_res + norm_back(hidden, factor_m, gain_m, grad_normed_m)
    grad_hidden_low = grad_hidden.astype(jnp.bfloat16)
    grad_attended = jnp.dot(grad_hidden_low, out_w, preferred_element_type=jnp.float32).astype(
        jnp.bfloat16
    )
    spread_hidden = jnp.broadcast_to(grad_hidden_low[:, None, :], (tok, n_uly, D))
    head_grad, head_hidden = (
        lax.all_to_all(
            grad_attended.reshape(tok, HEADS, HEAD_DIM),
            "ulysses",
            split_axis=1,
            concat_axis=0,
            tiled=True,
        ),
        lax.all_to_all(spread_hidden, "ulysses", split_axis=1, concat_axis=0, tiled=True),
    )
    grad_out_slice = contract(
        head_hidden[:, 0, :], mixed_low.reshape(group, heads_dev * HEAD_DIM), 0, 0
    )
    delta = jnp.transpose(jnp.sum(head_grad.astype(jnp.float32) * mixed, -1))
    total_keys = group * n_blk
    zero_q = jnp.zeros((group, heads_dev, HEAD_DIM), jnp.float32)
    fold_start = (
        zero_q,
        jnp.zeros((total_keys, HEAD_DIM), jnp.float32),
        jnp.zeros((total_keys, HEAD_DIM), jnp.float32),
    )
    state = fold_start
    key_rows = lax.all_gather(key_local, "blk", axis=0, tiled=True)
    value_rows = lax.all_gather(value_local, "blk", axis=0, tiled=True)
    key_blocks, grads_size = split_blocks(key_rows)
    value_blocks, _ = split_blocks(value_rows)

    def grads_step(inner, item):
        key_blk, value_blk, number = item
        k_start = number * grads_size
        live = (k_start <= q_pos[-1]) & (k_start + grads_size - 1 >= q_begin[0])

        def grads_work(current):
            part_q, part_k, part_v = backward_block(
                head_q, head_grad, lse, delta, q_pos, q_begin, key_blk, value_blk, k_start, scale
            )
            grad_q, grad_keys, grad_values = current
            grad_keys = lax.dynamic_update_slice_in_dim(
                grad_keys,
                lax.dynamic_slice_in_dim(grad_keys, k_start, grads_size, 0) + part_k,
                k_start,
                0,
            )
            grad_values = lax.dynamic_update_slice_in_dim(
                grad_values,
                lax.dynamic_slice_in_dim(grad_values, k_start, grads_size, 0) + part_v,
                k_start,
                0,
            )
            return (grad_q + part_q, grad_keys, grad_values)

        return (lax.cond(live, grads_work, lambda current: current, inner), None)

    state, _ = lax.scan(
        grads_step,
        state,
        (key_blocks, value_blocks, jnp.arange(key_blocks.shape[0], dtype=jnp.int32)),
    )
    grad_q = state[0]
    grad_k, grad_v = (
        lax.psum_scatter(state[1], "blk", scatter_dimension=0, tiled=True),
        lax.psum_scatter(state[2], "blk", scatter_dimension=0, tiled=True),
    )
    group_places = q_pos - q_begin
    grad_q_pre = rotate(grad_q.astype(jnp.bfloat16).astype(jnp.float32), group_places, -1.0).astype(
        jnp.bfloat16
    )
    grad_query_slice = contract(normed_group, grad_q_pre.reshape(group, heads_dev * HEAD_DIM), 0, 0)
    token_q, token_k, token_v = (
        lax.all_to_all(grad_q_pre, "ulysses", split_axis=0, concat_axis=1, tiled=True),
        lax.all_to_all(
            grad_k.astype(jnp.bfloat16)[:, None, :],
            "ulysses",
            split_axis=0,
            concat_axis=1,
            tiled=True,
        ),
        lax.all_to_all(
            grad_v.astype(jnp.bfloat16)[:, None, :],
            "ulysses",
            split_axis=0,
            concat_axis=1,
            tiled=True,
        ),
    )
    summed_k = []
    summed_v = []
    for head in range(KV_HEADS):
        members = [c for c in range(n_uly) if which[c] == head]
        summed_k.append(sum((token_k[:, c].astype(jnp.float32) for c in members)))
        summed_v.append(sum((token_v[:, c].astype(jnp.float32) for c in members)))
    grad_key_heads = jnp.stack(summed_k, 1)
    grad_value_heads = jnp.stack(summed_v, 1)
    grad_query_pre = token_q.reshape(tok, q_width)
    grad_key_pre = rotate(grad_key_heads, places, -1.0).reshape(tok, kv_width)
    grad_keyval_pre = jnp.concatenate(
        [grad_key_pre, grad_value_heads.reshape(tok, kv_width)], 1
    ).astype(jnp.bfloat16)
    grad_normed_a = contract(grad_query_pre, query_w, 1, 1) + contract(
        grad_keyval_pre, keyval_w, 1, 1
    )
    grad_keyval_w = contract(normed_a, grad_keyval_pre, 0, 0)
    grad_gain_a = jnp.sum(grad_normed_a * inputs * factor_a, 0)
    grad_input = grad_hidden + norm_back(inputs, factor_a, gain_a, grad_normed_a)
    n_dev = n_blk * n_uly
    squares = jnp.stack(
        [
            jnp.sum(attn_branch * attn_branch),
            jnp.sum(moe_branch * moe_branch),
            jnp.sum(result * result),
        ]
    )
    square_rows = jnp.broadcast_to(squares[None, :], (n_dev, 3))
    part_gate, part_up, part_down, uly_gain_a, uly_gain_m, uly_keyval, uly_squares = (
        lax.psum_scatter(
            grad_gate.astype(jnp.bfloat16), "ulysses", scatter_dimension=0, tiled=True
        ).astype(jnp.float32),
        lax.psum_scatter(
            grad_up.astype(jnp.bfloat16), "ulysses", scatter_dimension=0, tiled=True
        ).astype(jnp.float32),
        lax.psum_scatter(
            grad_down.astype(jnp.bfloat16), "ulysses", scatter_dimension=0, tiled=True
        ).astype(jnp.float32),
        lax.psum_scatter(
            reorder_rows(grad_gain_a, n_blk, n_uly).astype(jnp.bfloat16),
            "ulysses",
            scatter_dimension=0,
            tiled=True,
        ).astype(jnp.float32),
        lax.psum_scatter(
            reorder_rows(grad_gain_m, n_blk, n_uly).astype(jnp.bfloat16),
            "ulysses",
            scatter_dimension=0,
            tiled=True,
        ).astype(jnp.float32),
        lax.psum_scatter(
            reorder_rows(grad_keyval_w, n_blk, n_uly).astype(jnp.bfloat16),
            "ulysses",
            scatter_dimension=0,
            tiled=True,
        ).astype(jnp.float32),
        lax.psum_scatter(
            square_rows.astype(jnp.bfloat16), "ulysses", scatter_dimension=0, tiled=True
        ).astype(jnp.float32),
    )
    part_outw, part_query, part_gain_a, part_gain_m, part_keyval, square_row = (
        lax.psum_scatter(grad_out_slice, "blk", scatter_dimension=0, tiled=True),
        lax.psum_scatter(grad_query_slice, "blk", scatter_dimension=0, tiled=True),
        lax.psum_scatter(uly_gain_a, "blk", scatter_dimension=0, tiled=True),
        lax.psum_scatter(uly_gain_m, "blk", scatter_dimension=0, tiled=True),
        lax.psum_scatter(uly_keyval, "blk", scatter_dimension=0, tiled=True),
        lax.psum_scatter(uly_squares, "blk", scatter_dimension=0, tiled=True),
    )
    branch_rms = jnp.sqrt(square_row[0] / (tok * n_dev * D))
    return (
        layer_output,
        grad_input,
        part_gain_a,
        part_gain_m,
        part_query,
        part_keyval,
        part_outw,
        part_gate,
        part_up,
        part_down,
        branch_rms,
    )


MESH = pl.DeviceIdType.MESH
LANES = 128
LOG2E = 1.4426950408889634


class Place:
    def __init__(self, depth):
        self.blk = lax.axis_index("blk")
        self.u = lax.axis_index("ulysses")
        self.depth = depth
        self.z = self.blk // 4
        self.x = (self.blk // 2) % 2
        self.c = self.blk % 2
        self.up = (self.blk + 4, self.u)
        self.down = (self.blk - 4, self.u)
        self.across = (self.blk + 2 - 4 * self.x, self.u)
        self.sibling = (self.blk + 1 - 2 * self.c, self.u)
        self.other = (self.blk, 1 - self.u)
        self.has_up = self.z < depth - 1
        self.has_down = self.z > 0

    def along(self, z):
        return (self.blk + 4 * (z - self.z), self.u)

    def slot(self, z, x, c):
        return z * 4 + x * 2 + c

    def greet(self, sibling=False, other=False, plane=True):
        barrier = pltpu.get_barrier_semaphore()

        def hail(device):
            pl.semaphore_signal(barrier, inc=1, device_id=device, device_id_type=MESH)

        count = 0
        if plane:
            hail(self.across)
            for d in range(1, self.depth):
                pl.when(self.z >= d)(lambda d=d: hail(self.along(self.z - d)))
                pl.when(self.z + d < self.depth)(lambda d=d: hail(self.along(self.z + d)))
            count = self.depth
        if sibling:
            hail(self.sibling)
            count = count + 1
        if other:
            hail(self.other)
            count = count + 1
        pl.semaphore_wait(barrier, count)


class Wires:
    def __init__(self, sems):
        self.sems = sems
        self.used = 0

    def take(self, count):
        base = self.used
        self.used += count
        return lambda index: self.sems.at[base + index]


def each(act, items):
    for item in items:
        act(item)


def remote(src, dst, send, recv, device):
    return pltpu.make_async_remote_copy(
        src_ref=src, dst_ref=dst, send_sem=send, recv_sem=recv, device_id=device, device_id_type=MESH
    )


class Gather:
    def __init__(self, place, wires, src, out, cores, up_only=False, chain=False, far=False):
        self.p, self.src, self.out, self.cores, self.up_only, self.chain = place, src, out, cores, up_only, chain
        n = place.depth
        self.s_z = [wires.take(n) for _ in range(2 if chain else 1)]
        self.s_across = wires.take(n)
        self.r_z, self.r_x = wires.take(n), wires.take(n)
        if cores:
            self.s_core, self.r_core = wires.take(2 * n), wires.take(2 * n)
        self.far = wires.take(1)(0) if far else None

    def _across(self, zz, xx, src=None):
        dst = self.out(zz, xx, self.p.c)
        return remote(dst if src is None else src, dst, self.s_across(zz), self.r_x(zz), self.p.across)

    def _core(self, zz, xx, src=None):
        dst = self.out(zz, xx, self.p.c)
        at = zz * 2 + xx
        return remote(dst if src is None else src, dst, self.s_core(at), self.r_core(at), self.p.sibling)

    def _along(self, zz, to, src=None):
        p = self.p
        dst = self.out(zz, p.x, p.c)
        return remote(dst if src is None else src, dst, self.s_z[0](to), self.r_z(zz), p.along(to))

    def _next(self, zz, up, src=None):
        p = self.p
        dst = self.out(zz, p.x, p.c)
        return remote(
            dst if src is None else src, dst, self.s_z[up](zz), self.r_z(zz), p.along(p.z + (1 if up else -1))
        )

    def start_z(self, in_place=False):
        p = self.p
        src = None if in_place else self.src
        if self.chain:
            pl.when(p.has_up)(lambda: self._next(p.z, 1, src).start())
            pl.when(p.has_down)(lambda: self._next(p.z, 0, src).start())
            return
        for d in range(1, p.depth):
            pl.when(p.z + d < p.depth)(lambda d=d: self._along(p.z, p.z + d, src).start())
            if not self.up_only:
                pl.when(p.z >= d)(lambda d=d: self._along(p.z, p.z - d, src).start())

    def start_x(self, in_place=False):
        p = self.p
        src = None if in_place else self.src
        self._across(p.z, p.x, src).start()
        if self.cores:
            self._core(p.z, p.x, src).start()
        if self.far is not None:
            pltpu.make_async_copy(self.src, self.out(p.z, p.x, p.c), self.far).start()
        elif not in_place:
            self.out(p.z, p.x, p.c)[...] = self.src[...]

    def start(self, in_place=False):
        self.start_z(in_place)
        self.start_x(in_place)

    def hop(self, d):
        p = self.p

        def take(zz, up):
            remote(
                self.out(zz, p.x, p.c), self.out(zz, p.x, p.c), self.s_z[0](0), self.r_z(zz), p.across
            ).wait_recv()
            if self.chain:
                pl.when(p.has_up if up else p.has_down)(lambda: self._next(zz, up).start())
            self._across(zz, p.x).start()
            if self.cores:
                self._core(zz, p.x).start()

        pl.when(p.z >= d)(lambda: take(p.z - d, 1))
        if not self.up_only:
            pl.when(p.z + d < p.depth)(lambda: take(p.z + d, 0))

    def cross(self, d):
        p = self.p

        def take(zz):
            self._across(zz, 1 - p.x).wait_recv()
            if self.cores:
                self._core(zz, 1 - p.x).start()

        if isinstance(d, int) and d == 0:
            take(p.z)
        else:
            pl.when(p.z >= d)(lambda: take(p.z - d))
            if not self.up_only:
                pl.when(p.z + d < p.depth)(lambda: take(p.z + d))

    def core(self, zz, xx):
        self._core(zz, xx).wait_recv()

    def finish(self, cores_taken=False):
        p = self.p
        for zz in range(p.depth):

            def ends(zz=zz):
                if self.cores:
                    for xx in range(2):
                        if not cores_taken:
                            self._core(zz, xx).wait_recv()
                        self._core(zz, xx).wait_send()
                self._across(zz, p.x).wait_send()

            if self.up_only and zz > 0:
                pl.when(p.z >= zz)(ends)
            else:
                ends()
            if self.chain:
                pl.when(p.has_up & (p.z >= zz))(lambda zz=zz: self._next(zz, 1).wait_send())
                pl.when(p.has_down & (p.z <= zz))(lambda zz=zz: self._next(zz, 0).wait_send())
            else:
                away = (p.z < zz) if self.up_only else (p.z != zz)
                pl.when(away)(lambda zz=zz: self._along(p.z, zz).wait_send())
        if self.far is not None:
            pltpu.make_async_copy(self.src, self.out(p.z, p.x, p.c), self.far).wait()


class Scatter:
    def __init__(self, place, wires, part, out, rx, rz, pieces, down_only=False):
        self.p, self.part, self.out, self.rx, self.rz = place, part, out, rx, rz
        n = place.depth
        total = n * pieces
        self.pieces, self.down_only = pieces, down_only
        self.sx, self.cx = wires.take(total), wires.take(total)
        self.sz, self.cz = wires.take(total), wires.take(total)
        if down_only:
            self.order = list(range(n))
        else:
            self.order = [n - 1 - i // 2 if i % 2 == 0 else i // 2 for i in range(n)]
        self.items = [(zz, k) for zz in self.order for k in range(pieces)]

    def _x(self, zz, k):
        i = zz * self.pieces + k
        return remote(self.part(zz, 1 - self.p.x, k), self.rx(zz, k), self.sx(i), self.cx(i), self.p.across)

    def _z(self, zz, k, source=None):
        p = self.p
        source = p.z if source is None else source
        return remote(
            self.rx(zz, k),
            self.rz(source, k),
            self.sz(zz * self.pieces + k),
            self.cz(source * self.pieces + k),
            p.along(zz),
        )

    def _live(self, zz, act):
        if self.down_only and zz > 0:
            pl.when(self.p.z >= zz)(act)
        else:
            act()

    def begin(self, t):
        if t < len(self.items):
            zz, k = self.items[t]
            self._live(zz, lambda: self._x(zz, k).start())

    def send(self, zz):
        for k in range(self.pieces):
            self._x(zz, k).start()

    def take(self, zz, k):
        p = self.p

        def act():
            self._x(zz, k).wait_recv()

            def forward():
                total = self.part(zz, p.x, k)[...].astype(jnp.float32)
                total = total + self.rx(zz, k)[...].astype(jnp.float32)
                self.rx(zz, k)[...] = total.astype(jnp.bfloat16)
                self._z(zz, k).start()

            pl.when(p.z != zz)(forward)

        self._live(zz, act)

    def land(self, t):
        self.take(*self.items[t])

    def finish(self):
        p = self.p
        n = p.depth
        for zz, k in self.items:
            self._live(zz, lambda zz=zz, k=k: self._x(zz, k).wait_send())
            away = (p.z > zz) if self.down_only else (p.z != zz)
            pl.when(away)(lambda zz=zz, k=k: self._z(zz, k).wait_send())

            def store(zz=zz, k=k):
                total = self.part(zz, p.x, k)[...].astype(jnp.float32)
                total = total + self.rx(zz, k)[...].astype(jnp.float32)
                for source in range(zz + 1 if self.down_only else 0, n):
                    if source != zz:
                        self._z(zz, k, source).wait_recv()
                        total = total + self.rz(source, k)[...].astype(jnp.float32)
                self.out(k)[...] = total

            pl.when(p.z == zz)(store)


class CoreScatter:
    def __init__(self, place, wires, src, rc, out, rx, rz, down_only=False):
        self.p, self.src, self.rc, self.down_only = place, src, rc, down_only
        n = place.depth
        self.sc, self.cc = wires.take(n), wires.take(n)
        self.plane = Scatter(
            place, wires, lambda zz, xx, k: rc.at[zz * 2 + xx], lambda k: out,
            lambda zz, k: rx.at[zz], lambda source, k: rz.at[source], 1, down_only,
        )
        self.order = self.plane.order

    def _trade(self, zz):
        p = self.p
        if self.down_only:
            at = pl.ds(2 * zz, 2)
            return remote(self.src.at[at, 1 - p.c], self.rc.at[at], self.sc(zz), self.cc(zz), p.sibling)
        return remote(self.src.at[:, 1 - p.c], self.rc, self.sc(0), self.cc(0), p.sibling)

    def trade(self, t=0):
        zz = self.order[t]
        self.plane._live(zz, lambda: self._trade(zz).start())

    def join(self, t):
        p = self.p
        zz = self.order[t]

        def act():
            if self.down_only or t == 0:
                self._trade(zz).wait_recv()
            for xx in range(2):
                at = zz * 2 + xx
                self.rc[at] = (
                    self.src[at, p.c].astype(jnp.float32) + self.rc[at].astype(jnp.float32)
                ).astype(jnp.bfloat16)

        self.plane._live(zz, act)
        self.plane.begin(t)

    def land(self, t):
        self.plane.land(t)

    def release(self):
        for t, zz in enumerate(self.order):
            if self.down_only or t == 0:
                self.plane._live(zz, lambda zz=zz: self._trade(zz).wait_send())

    def finish(self):
        self.plane.finish()


def mm(left, right):
    return jnp.dot(left, right, preferred_element_type=jnp.float32)


def flip(tile):
    return tile.astype(jnp.float32).T.astype(jnp.bfloat16)


def hidden_bias(first_key, first_query, begin, keys):
    queries = begin.shape[1]
    k_pos = first_key + lax.broadcasted_iota(jnp.int32, (keys, queries), 0)
    q_pos = first_query + lax.broadcasted_iota(jnp.int32, (keys, queries), 1)
    return jnp.where((k_pos >= begin) & (k_pos <= q_pos), 0.0, NEG)


def front_kernel(
    depth, scale, docs, x, dy, gain_a, gain_m, wq, wkv, wo, ids, shares_of, freq, e0, e1, e2,
    b, hid, attn_sq, normed_t, q_rows, qt, o, ot, lse, gain_rows, g_all, x_all, begin, cosine, sine,
    kv_out, w_out, wo_out, dy_all, f0, f1, f2,
    kv, w_all, wo_all, own, square, g_own, wa_own, normed, raw, top, total, acc, p_out, p_in, sems,
):
    f32, bf = jnp.float32, jnp.bfloat16
    p = Place(depth)
    p.greet(sibling=True, other=True)
    wires = Wires(sems)
    u, blk = p.u, p.blk
    tok, width = x.shape
    group, q_half = o.shape
    heads = q_half // HEAD_DIM
    kv_half = 2 * HEAD_DIM
    rows_dev = wq.shape[0]
    half, cols = e0.shape
    experts = 2 * depth

    def rows_of(ref, z, xx, c, member):
        row = (p.slot(z, xx, c) * 2 + member) * rows_dev
        return ref.at[pl.ds(pl.multiple_of(row, 16), rows_dev)]

    wa_mine = Gather(p, wires, wa_own.at[u], lambda z, xx, c: rows_of(w_all, z, xx, c, u), True, chain=True)
    wa_peer = Gather(p, wires, None, lambda z, xx, c: rows_of(w_all, z, xx, c, 1 - u), True, chain=True)
    wos = Gather(
        p, wires, None,
        lambda z, xx, c: wo_all.at[pl.ds(pl.multiple_of(p.slot(z, xx, c) * 2 * rows_dev, 16), 2 * rows_dev)],
        True, chain=True,
    )
    kvs = Gather(p, wires, None, lambda z, xx, c: kv.at[p.slot(z, xx, c)], True, up_only=True)
    dys = Gather(p, wires, dy, lambda z, xx, c: dy_all.at[z * 2 + xx], False, chain=True, far=True)
    gws = Gather(p, wires, g_own, lambda z, xx, c: g_all.at[z * 2 + xx], False, chain=True)
    ws, wr = wires.take(2), wires.take(2)
    xs, xr = wires.take(1)(0), wires.take(1)(0)
    es, er = wires.take(3), wires.take(3)
    cs, cr = wires.take(6), wires.take(6)
    ps, pr = wires.take(3), wires.take(3)

    for h in range(2):
        wa_own[h, :, :q_half] = wq[:, h * q_half : (h + 1) * q_half]
        for part in range(2):
            wa_own[h, :, q_half + part * HEAD_DIM : q_half + (part + 1) * HEAD_DIM] = wkv[
                :, (part * 2 + h) * HEAD_DIM : (part * 2 + h + 1) * HEAD_DIM
            ]
    square[...] = jnp.zeros(square.shape, f32)
    square[0:1, :rows_dev] = gain_a[...].astype(f32)
    square[1:2, :rows_dev] = gain_m[...].astype(f32)
    columns = square[...].T[:rows_dev, :].astype(bf)
    for h in range(2):
        wa_own[h, :, q_half + kv_half :] = columns

    wa_swap = remote(wa_own.at[1 - u], rows_of(w_all, p.z, p.x, p.c, u), ws(0), wr(0), p.other)
    wo_swap = remote(
        wo.at[:, pl.ds(pl.multiple_of((1 - u) * q_half, LANES), q_half)],
        rows_of(wo_all, p.z, p.x, p.c, u), ws(1), wr(1), p.other,
    )
    x_swap = remote(x, x_all.at[u], xs, xr, p.other)

    def part(ref, row, core):
        return ref.at[
            pl.ds(pl.multiple_of(row * half, half), half), pl.ds(pl.multiple_of(core * cols, LANES), cols)
        ]

    halves = ((e0, f0), (e1, f1), (e2, f2))
    ls, ks = wires.take(3), wires.take(3)
    loads = [pltpu.make_async_copy(e, own.at[i], ls(i)) for i, (e, f) in enumerate(halves)]
    keeps = [pltpu.make_async_copy(own.at[i], part(f, u, p.c), ks(i)) for i, (e, f) in enumerate(halves)]
    swaps = [remote(own.at[i], part(f, u, p.c), es(i), er(i), p.other) for i, (e, f) in enumerate(halves)]
    shares = [remote(own.at[i], part(f, u, p.c), cs(i), cr(i), p.sibling) for i, (e, f) in enumerate(halves)]
    passes = [
        remote(part(f, 1 - u, p.c), part(f, 1 - u, p.c), cs(3 + i), cr(3 + i), p.sibling)
        for i, (e, f) in enumerate(halves)
    ]
    os_ = wires.take(3)
    stores = [
        pltpu.make_async_copy(v, r, os_(i)) for i, (v, r) in enumerate(((kv, kv_out), (w_all, w_out), (wo_all, wo_out)))
    ]

    def expert_out(i):
        swaps[i].start()
        shares[i].start()

    def expert_in(i):
        swaps[i].wait_recv()
        passes[i].start()

    wa_swap.start()
    wa_mine.start()
    wo_swap.start()
    x_swap.start()
    each(lambda load: load.start(), loads)

    def starts(places):
        first = jnp.zeros(places.shape, jnp.int32)
        for i in range(docs.shape[0]):
            first = jnp.where(docs[i] <= places, jnp.maximum(first, docs[i]), first)
        return first

    begin[...] = starts(blk * group + lax.broadcasted_iota(jnp.int32, begin.shape, 1))
    places = blk * group + lax.broadcasted_iota(jnp.int32, cosine.shape, 0)
    angle = (places - starts(places)).astype(f32) * freq[0:1, :]
    cosine[...] = jnp.cos(angle)
    sine[...] = jnp.where(lax.broadcasted_iota(jnp.int32, sine.shape, 1) < HEAD_DIM // 2, -1.0, 1.0) * jnp.sin(angle)
    for e in range(experts):
        g_own[e : e + 1, :] = jnp.sum(jnp.where(ids[...] == e, shares_of[...], 0.0), axis=0, keepdims=True)
    wa_swap.wait_recv()
    wa_peer.start(in_place=True)
    x_all[u] = x[...]
    rows_of(wo_all, p.z, p.x, p.c, u)[...] = wo[:, pl.ds(pl.multiple_of(u * q_half, LANES), q_half)]
    for i in range(3):
        loads[i].wait()
        keeps[i].start()
    gws.start()
    for d in range(1, depth):
        for g in (wa_mine, wa_peer):
            g.hop(d)
            g.cross(d - 1)
        gws.hop(d)
        gws.cross(d - 1)
        if d == 1:
            wo_swap.wait_recv()
            wos.start(in_place=True)
        else:
            wos.hop(d - 1)
    gws.cross(depth - 1)
    expert_out(0)
    x_swap.wait_recv()
    for g in (wa_mine, wa_peer):
        g.cross(depth - 1)
    for g in (wa_mine, wa_peer):
        g.finish()
    stores[1].start()
    gain_rows[...] = w_all[:, q_half + kv_half :].astype(f32).T[:8, :]
    for m in range(2):
        xf = x_all[m].astype(f32)
        r1 = lax.rsqrt(jnp.mean(xf * xf, -1, keepdims=True) + EPS)
        normed[m * tok : (m + 1) * tok, :] = (xf * r1 * gain_rows[0:1, :]).astype(bf)
    raw[...] = mm(normed[...], w_all[:, : q_half + kv_half])

    def rope(values):
        return values * cosine[...] + pltpu.roll(values, HEAD_DIM // 2, 1) * sine[...]

    here = p.slot(p.z, p.x, p.c)
    kv[here, :, :HEAD_DIM] = rope(raw[:, q_half : q_half + HEAD_DIM]).astype(bf)
    kv[here, :, HEAD_DIM:] = raw[:, q_half + HEAD_DIM :].astype(bf)
    kvs.start(in_place=True)
    for h in range(heads):
        hs = slice(h * HEAD_DIM, (h + 1) * HEAD_DIM)
        turned = rope(raw[:, hs])
        q_rows[h * group : (h + 1) * group, :] = turned.astype(bf)
        qt[:, h * group : (h + 1) * group] = turned.T.astype(bf)
    for j in range(0, width, 256):
        normed_t[j : j + 256, :] = flip(normed[:, j : j + 256])
    top[...] = jnp.full(top.shape, NEG, f32)
    total[...] = jnp.zeros(total.shape, f32)
    ot[...] = jnp.zeros(ot.shape, f32)

    background = {}

    def at_step(s, act):
        background.setdefault(s, []).append(act)

    at_step(0, lambda: kvs.cross(0))
    at_step(0, lambda: kvs.hop(1))
    at_step(0, dys.start_z)
    at_step(1, lambda: wos.hop(3))
    at_step(2, lambda: kvs.cross(1))
    at_step(2, lambda: kvs.hop(2))
    at_step(3, dys.start_x)
    at_step(3, lambda: wos.cross(0))
    at_step(4, lambda: kvs.cross(2))
    at_step(4, lambda: kvs.hop(3))
    at_step(5, lambda: wos.cross(1))
    at_step(5, lambda: expert_in(0))
    at_step(5, lambda: expert_out(1))
    at_step(6, lambda: kvs.cross(3))
    at_step(6, lambda: dys.hop(1))
    at_step(7, lambda: wos.cross(2))
    at_step(7, lambda: wos.cross(3))

    def step(s, carry):
        d = s // 2
        zz = p.z - d
        xx = jnp.where(s % 2 == 0, p.x, 1 - p.x)
        j = p.slot(zz, xx, 0)

        pl.when(zz >= 0)(lambda: kvs.core(zz, xx))

        def work():
            pair = kv[pl.ds(j, 2)].reshape(2 * group, kv_half)
            k = pair[:, :HEAD_DIM]
            vt = flip(pair[:, HEAD_DIM:])
            bias = hidden_bias(j * group, blk * group, begin[0:1, :], 2 * group)
            at = [slice(h * group, (h + 1) * group) for h in range(heads)]
            sc = [mm(k, qt[:, hs]) * (scale * LOG2E) + bias for hs in at]
            old = [top[0:1, hs] for hs in at]
            new = [jnp.maximum(o_, jnp.max(s_, axis=0, keepdims=True)) for o_, s_ in zip(old, sc)]
            e = [jnp.exp2(s_ - n_) for s_, n_ in zip(sc, new)]
            part = [jnp.sum(e_, axis=0, keepdims=True) for e_ in e]
            mixed = [mm(vt, e_.astype(bf)) for e_ in e]
            for h, hs in enumerate(at):
                keep = jnp.exp2(old[h] - new[h])
                total[0:1, hs] = total[0:1, hs] * keep + part[h]
                ot[:, hs] = ot[:, hs] * keep + mixed[h]
                top[0:1, hs] = new[h]

        pl.when((zz >= 0) & (j <= blk))(work)
        for when, acts in background.items():
            pl.when(s == when)(lambda acts=acts: each(lambda act: act(), acts))
        return carry

    lax.fori_loop(0, 2 * depth, step, 0)

    wos.finish()
    stores[2].start()
    sums = total[0:1, :]
    lse[...] = jnp.broadcast_to(top[0:1, :] + jnp.log2(sums), lse.shape)
    for h in range(heads):
        at = slice(h * group, (h + 1) * group)
        mixed = ot[:, at] / sums[:, at]
        ot[:, at] = mixed
        o[:, h * HEAD_DIM : (h + 1) * HEAD_DIM] = mixed.T.astype(bf)

    wide = width // 3
    p_swaps = []
    for i in range(3):
        cb = i * wide
        acc[:, cb : cb + wide] = contract(o[...], wo_all[cb : cb + wide, :], 1, 1)
        theirs = pl.ds(pl.multiple_of((1 - u) * tok, tok), tok)
        p_out[i] = acc[theirs, cb : cb + wide].astype(bf)
        p_swaps.append(remote(p_out.at[i], p_in.at[i], ps(i), pr(i), p.other))
        p_swaps[i].start()
    dys.hop(2)
    dys.cross(0)
    expert_in(1)
    expert_out(2)
    dys.hop(3)
    mine = pl.ds(pl.multiple_of(u * tok, tok), tok)
    for i in range(3):
        p_swaps[i].wait_recv()
        acc[mine, i * wide : (i + 1) * wide] += p_in[i].astype(f32)
    branch = acc[mine, :]
    hidden = x[...].astype(f32) + branch
    hid[...] = hidden
    r2 = lax.rsqrt(jnp.mean(hidden * hidden, -1, keepdims=True) + EPS)
    b[...] = (hidden * r2 * gain_rows[1:2, :]).astype(bf)
    attn_sq[...] = jnp.broadcast_to(jnp.sum(branch * branch).reshape(1, 1), attn_sq.shape)
    for d in range(1, depth):
        dys.cross(d)
    expert_in(2)
    kvs.finish(cores_taken=True)
    stores[0].start()
    dys.finish()
    gws.finish()
    wa_swap.wait_send()
    wo_swap.wait_send()
    x_swap.wait_send()
    for i in range(3):
        swaps[i].wait_send()
        keeps[i].wait()
        shares[i].wait()
        passes[i].wait()
        p_swaps[i].wait_send()
        stores[i].wait()


def front(docs, x, dy, gain_a, gain_m, wq, wkv, wo, ids, shares, experts, depth, scale, cid):
    f32, bf = jnp.float32, jnp.bfloat16
    shape = jax.ShapeDtypeStruct
    vmem = pl.BlockSpec(memory_space=pltpu.VMEM)
    hbm = pl.BlockSpec(memory_space=pl.ANY)
    V = pltpu.VMEM
    tok, width = x.shape
    group = 2 * tok
    q_half = wq.shape[1] // 2
    kv_half = 2 * HEAD_DIM
    wide = q_half + kv_half + LANES
    rows = q_half // HEAD_DIM * group
    rows_dev = wq.shape[0]
    expert = shape((2 * experts[0].shape[0], 2 * experts[0].shape[1]), bf)
    half = HEAD_DIM // 2
    freq = np.power(np.float32(ROPE_BASE), -np.arange(half, dtype=np.float32) * np.float32(2.0 / HEAD_DIM))
    freq = jnp.asarray(np.tile(freq.astype(np.float32), (8, 2)))
    return pl.pallas_call(
        functools.partial(front_kernel, depth, scale),
        out_shape=(
            shape((tok, width), bf),
            shape((tok, width), f32),
            shape((8, LANES), f32),
            shape((width, group), bf),
            shape((rows, HEAD_DIM), bf),
            shape((HEAD_DIM, rows), bf),
            shape((group, q_half), bf),
            shape((HEAD_DIM, rows), f32),
            shape((8, rows), f32),
            shape((8, width), f32),
            shape((2 * depth, 2 * depth, tok), f32),
            shape((2, tok, width), bf),
            shape((8, group), jnp.int32),
            shape((group, HEAD_DIM), f32),
            shape((group, HEAD_DIM), f32),
            shape((4 * depth, group, kv_half), bf),
            shape((width, wide), bf),
            shape((width, q_half), bf),
            shape((2 * depth, tok, width), bf),
            expert,
            expert,
            expert,
        ),
        in_specs=[pl.BlockSpec(memory_space=pltpu.SMEM)] + [vmem] * 10 + [hbm] * 3,
        out_specs=tuple([vmem] * 15 + [hbm] * 7),
        scratch_shapes=[
            V((4 * depth, group, kv_half), bf),
            V((width, wide), bf),
            V((width, q_half), bf),
            V((3,) + experts[0].shape, bf),
            V((LANES, LANES), f32),
            V((2 * depth, tok), f32),
            V((2, rows_dev, wide), bf),
            V((group, width), bf),
            V((group, q_half + kv_half), f32),
            V((8, rows), f32),
            V((8, rows), f32),
            V((group, width), f32),
            V((3, tok, width // 3), bf),
            V((3, tok, width // 3), bf),
            pltpu.SemaphoreType.DMA((7 * 16 * depth,)),
        ],
        compiler_params=pltpu.CompilerParams(
            collective_id=cid, has_side_effects=True, vmem_limit_bytes=56 * 2**20
        ),
        name="front",
    )(docs, x, dy, gain_a[None, :], gain_m[None, :], wq, wkv, wo, ids, shares, freq, *experts)


def experts_kernel(
    depth, b, dy_own, g_all, hid, gain_rows, dy_far, g_far, u_far, d_far,
    dh, dhr, gm, z_far, eg_far,
    dy_all, wg, wu, wd, z_p, eg, b_all, act, dgate, dup, dyr, db_p, rx, rz, db, turned, sems,
):
    f32, bf = jnp.float32, jnp.bfloat16
    p = Place(depth)
    p.greet()
    wires = Wires(sems)
    tok, width = b.shape
    hidden_units = wg.shape[1]
    expert = p.blk // 2
    pair = 2 * tok
    pieces = 2
    piece = tok // pieces

    rows = [
        Gather(
            p, wires, b.at[pl.ds(k * piece, piece)],
            lambda z, x, c, k=k: b_all.at[pl.ds(pl.multiple_of((z * 2 + x) * tok + k * piece, piece), piece)],
            False, chain=True,
        )
        for k in range(pieces)
    ]

    def cut(ref, k):
        return ref.at[pl.ds(k * piece, piece)]

    sums = Scatter(
        p, wires,
        lambda zz, xx, k: cut(db_p.at[zz * 2 + xx], k),
        lambda k: cut(db, k),
        lambda zz, k: cut(rx.at[zz], k),
        lambda slot, k: cut(rz.at[slot], k),
        pieces,
    )
    ls = wires.take(4)
    loads = [
        pltpu.make_async_copy(r, v, ls(i)) for i, (r, v) in enumerate(((dy_far, dy_all), (g_far, wg), (u_far, wu), (d_far, wd)))
    ]
    os_ = wires.take(3)
    stores = [
        pltpu.make_async_copy(v, r, os_(i))
        for i, (v, r) in enumerate(((z_p, z_far), (eg.at[pl.ds(0, 2)], eg_far.at[pl.ds(0, 2)]), (eg.at[2], eg_far.at[2])))
    ]
    each(lambda load: load.start(), loads)
    each(lambda g: g.start(), rows)
    spread = lax.broadcasted_iota(jnp.int32, (tok, 8), 1)

    def weight(slot):
        return jnp.sum(jnp.where(spread == expert, g_all[slot].T, 0.0), axis=1, keepdims=True)

    def nth(i):
        inner = jnp.where(i == 0, 1, jnp.where(i == 1, 0, i))
        return jnp.where(
            p.z == 0, i, jnp.where(p.z == depth - 1, depth - 1 - i, jnp.where(p.z == 1, inner, depth - 1 - inner))
        )

    def block(i, carry):
        for d in range(depth):

            def arrive(d=d):
                for g in rows:
                    if d + 1 < depth:
                        g.hop(d + 1)
                    g.cross(d)

            pl.when(i == d)(arrive)
        pl.when(i == 0)(lambda: each(lambda load: load.wait(), loads))
        zz = nth(i)
        at = pl.ds(pl.multiple_of(zz * pair, pair), pair)
        for xx in range(2):
            half = pl.ds(pl.multiple_of(zz * pair + xx * tok, tok), tok)
            dyr[half, :] = (weight(zz * 2 + xx) * dy_all[zz * 2 + xx].astype(f32)).astype(bf)
        for cb in range(0, hidden_units, 256):
            cs = slice(cb, cb + 256)
            gate = mm(b_all[at, :], wg[:, cs])
            up = mm(b_all[at, :], wu[:, cs])
            sig = jax.nn.sigmoid(gate)
            act[at, cs] = (gate * sig * up).astype(bf)
            dact = mm(dyr[at, :], wd[:, cs])
            dgate[at, cs] = (dact * up * sig * (1.0 + gate * (1.0 - sig))).astype(bf)
            dup[at, cs] = (dact * gate * sig).astype(bf)
        for cb in range(0, width, 512):
            cs = slice(cb, cb + 512)
            part = contract(dgate[at, :], wg[cs, :], 1, 1) + contract(dup[at, :], wu[cs, :], 1, 1)
            for xx in range(2):
                db_p[zz * 2 + xx, :, cs] = part[xx * tok : (xx + 1) * tok, :].astype(bf)
        pl.when(i == depth - 2)(lambda: sums.send(nth(1)))
        pl.when(i == depth - 1)(lambda: each(lambda n: sums.send(nth(n)), (3, 2)))
        for cb in range(0, width, 512):
            cs = slice(cb, cb + 512)
            part = contract(act[at, :], wd[cs, :], 1, 1)
            for xx in range(2):
                z_p[zz * 2 + xx, :, cs] = (
                    weight(zz * 2 + xx) * part[xx * tok : (xx + 1) * tok, :]
                ).astype(bf)
        return carry

    lax.fori_loop(0, depth, block, 0)

    stores[0].start()

    wide = 256

    def grads(n):
        cs = slice(n * wide, (n + 1) * wide)
        turned[...] = flip(b_all[:, cs])
        eg[0, cs, :] = mm(turned[...], dgate[...]).astype(bf)
        eg[1, cs, :] = mm(turned[...], dup[...]).astype(bf)

    def grads_down(n):
        cs = slice(n * wide, (n + 1) * wide)
        turned[...] = flip(dyr[:, cs])
        eg[2, cs, :] = mm(turned[...], act[...]).astype(bf)

    work = [lambda n=n: grads(n) for n in range(width // wide)]
    work += [lambda n=n: grads_down(n) for n in range(width // wide)]
    events = []
    for n in (1, 3, 2, 0):
        for k in range(pieces):
            events.append(lambda n=n, k=k: sums.take(nth(n), k))
        if n == 1:
            events.append(lambda: sums.send(nth(0)))
    done = 0
    for t, event in enumerate(events):
        while done < len(work) and done * len(events) <= t * len(work):
            work[done]()
            done += 1
        event()
    for act_ in work[done:]:
        act_()
    stores[1].start()
    stores[2].start()
    sums.finish()
    each(lambda g: g.finish(), rows)

    h = hid[...]
    r2 = lax.rsqrt(jnp.mean(h * h, -1, keepdims=True) + EPS)
    weighted = db[...] * gain_rows[1:2, :]
    inner = jnp.mean(weighted * h, -1, keepdims=True)
    total = dy_own[...].astype(f32) + r2 * weighted - h * (r2 * r2 * r2 * inner)
    dh[...] = total
    dhr[...] = total.astype(bf)
    column = jnp.sum((db[...] * h * r2).T, axis=1, keepdims=True)
    lane = lax.broadcasted_iota(jnp.int32, (width, LANES), 1)
    gm[...] = jnp.where(lane == 1, column, 0.0)
    each(lambda store: store.wait(), stores)


def run_experts(b, dy_own, dy_all, g_all, weights, hid, gain_rows, depth, cid):
    f32, bf = jnp.float32, jnp.bfloat16
    shape = jax.ShapeDtypeStruct
    vmem = pl.BlockSpec(memory_space=pltpu.VMEM)
    hbm = pl.BlockSpec(memory_space=pl.ANY)
    V = pltpu.VMEM
    tok, width = b.shape
    units = weights[0].shape[1]
    rows = 2 * depth * tok
    return pl.pallas_call(
        functools.partial(experts_kernel, depth),
        out_shape=(
            shape((tok, width), f32),
            shape((tok, width), bf),
            shape((width, LANES), f32),
            shape((2 * depth, tok, width), bf),
            shape((3, width, units), bf),
        ),
        in_specs=[vmem] * 5 + [hbm] * 4,
        out_specs=tuple([vmem] * 3 + [hbm] * 2),
        scratch_shapes=[
            V((2 * depth, tok, width), bf),
            V((width, units), bf),
            V((width, units), bf),
            V((width, units), bf),
            V((2 * depth, tok, width), bf),
            V((3, width, units), bf),
            V((rows, width), bf),
            V((rows, units), bf),
            V((rows, units), bf),
            V((rows, units), bf),
            V((rows, width), bf),
            V((2 * depth, tok, width), bf),
            V((depth, tok, width), bf),
            V((depth, tok, width), bf),
            V((tok, width), f32),
            V((256, rows), bf),
            pltpu.SemaphoreType.DMA((2 * 5 * depth + 8 * depth + 8,)),
        ],
        compiler_params=pltpu.CompilerParams(
            collective_id=cid, has_side_effects=True, vmem_limit_bytes=58 * 2**20
        ),
        name="experts",
    )(b, dy_own, g_all, hid, gain_rows, dy_all, *weights)


def closing_kernel(
    depth, scale, attn_sq, dhr, gain, begin, lse, cosine, sine,
    zp_far, wo_far, ot_far, o_far, q_far, qt_far, kv_far, w_far, at_far, x_far, hid_far, dh_far, gm_far, eg,
    out, gin, gq, go, gkv, gg, f0, f1, f2, rms,
    zp, wo, ot, o, q_rows, qt, kv, w, at, x_all, hid, dh, gm,
    dhr_all, dot_, dqt, delta, dkv, do_rows, dq, att, acc,
    z_sum, z_rx, z_rz, go_p, go_rc, go_rx, go_rz, kv_sum, kv_rc, kv_rx, kv_rz,
    gq_p, gq_rc, gq_rx, gq_rz, gk_p, gk_sum, gk_rc, gk_rx, gk_rz,
    e_own, e_core, e_low, e_peer, da_out, da_in, t_out, t_in, sq, square, sems,
):
    f32, bf = jnp.float32, jnp.bfloat16
    p = Place(depth)
    p.greet(sibling=True, other=True)
    wires = Wires(sems)
    u, blk = p.u, p.blk
    tok = dhr.shape[0]
    group, q_half = o.shape
    heads = q_half // HEAD_DIM
    kv_half = 2 * HEAD_DIM
    blocks = kv.shape[0]
    rows_blk = gq.shape[0]

    cols = f0.shape[1]
    rows_e = f0.shape[0]
    es, er, el, ps, pr = (wires.take(1)(0) for _ in range(5))

    def e_cols(core):
        return eg.at[:, :, pl.ds(pl.multiple_of(core * cols, LANES), cols)]

    def e_rows(member):
        return pl.ds(pl.multiple_of(member * rows_e, rows_e), rows_e)

    e_trade = remote(e_cols(1 - p.c), e_core, es, er, p.sibling)
    e_keep = [pltpu.make_async_copy(e_cols(p.c).at[i], e_own, el) for i in range(3)]
    e_swap = remote(e_low, e_peer, ps, pr, p.other)

    def e_join():
        e_trade.wait_recv()
        theirs, mine = e_rows(1 - u), e_rows(u)
        for i in range(3):
            e_keep[i].wait()
            e_low[i] = (e_own[theirs, :].astype(f32) + e_core[i, theirs, :].astype(f32)).astype(bf)
            (f0, f1, f2)[i][...] = e_own[mine, :].astype(f32) + e_core[i, mine, :].astype(f32)
            if i < 2:
                e_keep[i + 1].start()
        e_swap.start()

    def e_done():
        e_swap.wait_recv()
        for i in range(3):
            (f0, f1, f2)[i][...] += e_peer[i].astype(f32)

    ds, dr = wires.take(1)(0), wires.take(1)(0)
    swap = remote(dhr, dhr_all.at[u], ds, dr, p.other)

    pieces = 2
    z_rows = tok // pieces

    def cut(ref, k):
        return ref.at[pl.ds(k * z_rows, z_rows)]

    zs = Scatter(
        p, wires,
        lambda zz, xx, k: cut(zp.at[zz * 2 + xx], k),
        lambda k: cut(z_sum, k),
        lambda zz, k: cut(z_rx.at[zz], k),
        lambda slot, k: cut(z_rz.at[slot], k),
        pieces,
    )
    gos = CoreScatter(p, wires, go_p, go_rc, go, go_rx, go_rz)
    kvs = CoreScatter(p, wires, dkv, kv_rc, kv_sum, kv_rx, kv_rz, down_only=True)
    gqs = CoreScatter(p, wires, gq_p, gq_rc, gq, gq_rx, gq_rz)
    gks = CoreScatter(p, wires, gk_p, gk_rc, gk_sum, gk_rx, gk_rz)
    qs, qr = wires.take(3 + depth), wires.take(3 + depth)
    sq_here = sq.at[p.z, p.x, u, p.c]
    sq_core = remote(sq_here, sq_here, qs(0), qr(0), p.sibling)
    sq_other = remote(sq.at[p.z, p.x, u], sq.at[p.z, p.x, u], qs(1), qr(1), p.other)
    sq_across = remote(sq.at[p.z, p.x], sq.at[p.z, p.x], qs(2), qr(2), p.across)

    def sq_along(z, to):
        return remote(sq.at[z], sq.at[z], qs(3 + to), qr(3 + z), p.along(to))

    ls = wires.take(13)
    loads = [
        pltpu.make_async_copy(r, v, ls(i))
        for i, (r, v) in enumerate(
            (
                (zp_far, zp), (wo_far, wo), (ot_far, ot), (o_far, o), (q_far, q_rows), (qt_far, qt), (kv_far, kv),
                (w_far, w), (at_far, at), (x_far, x_all), (hid_far, hid), (dh_far, dh), (gm_far, gm),
            )
        )
    ]
    swap.start()
    each(lambda load: load.start(), loads)
    e_trade.start()
    e_keep[0].start()
    loads[0].wait()
    ahead = 3
    for t in range(ahead):
        zs.begin(t)

    dqt[...] = jnp.zeros(dqt.shape, f32)
    dkv[...] = jnp.zeros(dkv.shape, bf)
    dhr_all[u] = dhr[...]
    e_join()
    zs.land(0)
    zs.begin(ahead)
    each(lambda load: load.wait(), loads[1:])
    swap.wait_recv()

    for m in range(2):
        part = mm(dhr_all[m], wo[...]).astype(bf)
        for h in range(heads):
            do_rows[h * group + m * tok : h * group + (m + 1) * tok, :] = part[:, h * HEAD_DIM : (h + 1) * HEAD_DIM]
    for h in range(heads):
        hs = slice(h * group, (h + 1) * group)
        part = do_rows[hs, :]
        turned = part.astype(f32).T
        dot_[:, hs] = turned.astype(bf)
        delta[0:1, hs] = jnp.sum(turned * ot[:, hs], axis=0, keepdims=True)

    for m in range(2):
        att[:, m * tok : (m + 1) * tok] = flip(dhr_all[m])

    def out_rows(i, carry):
        rows = pl.ds(pl.multiple_of(i * rows_blk, rows_blk), rows_blk)
        go_p[i // 2, i % 2] = mm(att[rows, :], o[...]).astype(bf)
        return carry

    lax.fori_loop(0, blocks, out_rows, 0)
    gos.trade()

    background = {}

    def at_tile(j, act):
        background.setdefault(j, []).append(act)

    def z_step(t):
        zs.land(t)
        zs.begin(t + ahead)

    for t in range(1, len(zs.items)):
        at_tile((0, 0, 2, 4, 6, 9, 12, 15)[t], lambda t=t: z_step(t))
    for t in range(depth):
        at_tile((5, 8, 11, 14)[t], lambda t=t: gos.join(t))
    for t in range(depth - 1):
        last = 4 * t + 3
        at_tile(last, lambda t=t: kvs.trade(t))
        at_tile(last + 1, lambda t=t: kvs.join(t))
        if t < depth - 2:
            at_tile(last + 6, lambda t=t: kvs.land(t))

    def tile(j, carry):
        def work():
            k = kv[j, :, :HEAD_DIM]
            v = kv[j, :, HEAD_DIM:]
            kt = flip(k)
            bias = hidden_bias(j * group, blk * group, begin[0:1, :], group)
            at_ = [slice(h * group, (h + 1) * group) for h in range(heads)]
            sc = [mm(k, qt[:, hs]) * (scale * LOG2E) + bias for hs in at_]
            dp = [mm(v, dot_[:, hs]) for hs in at_]
            e = [jnp.exp2(s_ - lse[0:1, hs]) for s_, hs in zip(sc, at_)]
            g = [(e_ * (d_ - delta[0:1, hs])).astype(bf) for e_, d_, hs in zip(e, dp, at_)]
            wide_g = jnp.concatenate(g, 1)
            dk = mm(wide_g, q_rows[...])
            dv = mm(jnp.concatenate([e_.astype(bf) for e_ in e], 1), do_rows[...])
            dqt[...] += mm(kt, wide_g)
            dkv[j // 2, j % 2, :, :HEAD_DIM] = (dk * scale).astype(bf)
            dkv[j // 2, j % 2, :, HEAD_DIM:] = dv.astype(bf)

        pl.when(j <= blk)(work)
        for when, acts in background.items():
            pl.when(j == when)(lambda acts=acts: each(lambda act: act(), acts))
        return carry

    lax.fori_loop(0, blocks, tile, 0)

    kvs.trade(depth - 1)

    def back_turn(values):
        return values * cosine[...] - pltpu.roll(values, HEAD_DIM // 2, 1) * sine[...]

    for h in range(heads):
        hs = slice(h * group, (h + 1) * group)
        cs = slice(h * HEAD_DIM, (h + 1) * HEAD_DIM)
        dq[:, cs] = back_turn((dqt[:, hs] * scale).T.astype(bf).astype(f32)).astype(bf)
    kvs.join(depth - 1)

    def query_rows(i, carry):
        rows = pl.ds(pl.multiple_of(i * rows_blk, rows_blk), rows_blk)
        gq_p[i // 2, i % 2] = mm(at[rows, :], dq[...]).astype(bf)
        return carry

    lax.fori_loop(0, blocks, query_rows, 0)
    gqs.trade()
    kvs.land(depth - 2)
    gqs.join(0)
    gqs.join(1)
    for m in range(2):
        for cb in range(0, D, 512):
            acc[m * tok : (m + 1) * tok, cb : cb + 512] = contract(
                dq[m * tok : (m + 1) * tok, :], w[cb : cb + 512, :q_half], 1, 1
            )
    kvs.land(depth - 1)
    kvs.release()
    kvs.finish()
    kv_low = kv_sum[...].astype(bf).astype(f32)
    kv_pre = jnp.concatenate([back_turn(kv_low[:, :HEAD_DIM]).astype(bf), kv_low[:, HEAD_DIM:].astype(bf)], 1)

    da_s, da_r = wires.take(3), wires.take(3)
    wide = D // 3
    da_swaps = []
    for i in range(3):
        cb = i * wide
        part = contract(kv_pre, w[cb : cb + wide, q_half : q_half + kv_half], 1, 1)
        acc[:, cb : cb + wide] += part
        theirs = pl.ds(pl.multiple_of((1 - u) * tok, tok), tok)
        da_out[i] = acc[theirs, cb : cb + wide].astype(bf)
        da_swaps.append(remote(da_out.at[i], da_in.at[i], da_s(i), da_r(i), p.other))
        da_swaps[i].start()

    column = jnp.zeros((D, 1), f32)
    for m in range(2):
        xf = x_all[m].astype(f32)
        r1 = lax.rsqrt(jnp.mean(xf * xf, -1, keepdims=True) + EPS)
        terms = acc[m * tok : (m + 1) * tok, :] * xf * r1
        column = column + jnp.sum(terms.T, axis=1, keepdims=True)
    lane = lax.broadcasted_iota(jnp.int32, (D, LANES), 1)
    gain_cols = (jnp.where(lane == 0, column, 0.0) + gm[...]).astype(bf)
    for i in range(blocks):
        gk_p[i // 2, i % 2, :, kv_half:] = gain_cols[i * rows_blk : (i + 1) * rows_blk, :]

    def keyval_rows(i, carry):
        rows = pl.ds(pl.multiple_of(i * rows_blk, rows_blk), rows_blk)
        gk_p[i // 2, i % 2, :, :kv_half] = mm(at[rows, :], kv_pre).astype(bf)
        return carry

    lax.fori_loop(0, blocks, keyval_rows, 0)
    gks.trade()
    for t in range(depth):
        gks.join(t)
    for t in range(2, depth):
        gqs.join(t)
    gqs.release()

    for t in range(depth):
        gos.land(t)
    zs.finish()
    result = hid[...] + z_sum[...]
    out[...] = result.astype(bf)
    spread = lax.broadcasted_iota(jnp.int32, (8, LANES), 1)
    z_sq = jnp.sum(z_sum[...] * z_sum[...])
    r_sq = jnp.sum(result * result)
    sq_here[...] = jnp.where(
        spread == 0, attn_sq[...], jnp.where(spread == 1, z_sq, jnp.where(spread == 2, r_sq, 0.0))
    )
    sq_core.start()
    for t in range(depth):
        gks.land(t)
    sq_core.wait_recv()
    sq_other.start()
    for t in range(2):
        gqs.land(t)

    mine = pl.ds(pl.multiple_of(u * tok, tok), tok)
    for i in range(3):
        da_swaps[i].wait_recv()
        acc[mine, i * wide : (i + 1) * wide] += da_in[i].astype(f32)
    da = acc[mine, :]
    xf = x_all[u].astype(f32)
    r1 = lax.rsqrt(jnp.mean(xf * xf, -1, keepdims=True) + EPS)
    weighted = da * gain[0:1, :]
    inner = jnp.mean(weighted * xf, -1, keepdims=True)
    gin[...] = dh[...] + r1 * weighted - xf * (r1 * r1 * r1 * inner)
    sq_other.wait_recv()
    sq_across.start()
    gks.release()
    gks.finish()
    rows_dev = gkv.shape[0]
    theirs = pl.ds(pl.multiple_of((1 - u) * rows_dev, rows_dev), rows_dev)
    own = pl.ds(pl.multiple_of(u * rows_dev, rows_dev), rows_dev)
    t_out[...] = gk_sum[theirs, :]
    ts, tr = wires.take(1)(0), wires.take(1)(0)
    t_swap = remote(t_out, t_in, ts, tr, p.other)
    t_swap.start()
    sq_across.wait_recv()
    for d in range(1, depth):
        pl.when(p.z >= d)(lambda d=d: sq_along(p.z, p.z - d).start())
        pl.when(p.z + d < depth)(lambda d=d: sq_along(p.z, p.z + d).start())
    for t in range(2, depth):
        gqs.land(t)
    e_done()
    gos.release()
    gos.finish()
    gqs.finish()
    t_swap.wait_recv()
    for part in range(2):
        here = slice(part * HEAD_DIM, (part + 1) * HEAD_DIM)
        base = part * kv_half
        gkv[:, pl.ds(pl.multiple_of(base + u * HEAD_DIM, LANES), HEAD_DIM)] = gk_sum[own, here]
        gkv[:, pl.ds(pl.multiple_of(base + (1 - u) * HEAD_DIM, LANES), HEAD_DIM)] = t_in[:, here]
    square[...] = jnp.zeros(square.shape, f32)
    square[:rows_dev, :] = gk_sum[own, kv_half:] + t_in[:, kv_half:]
    gg[...] = square[...].T[:8, :]
    sq_core.wait_send()
    sq_other.wait_send()
    sq_across.wait_send()
    for z in range(depth):
        pl.when(p.z != z)(lambda z=z: sq_along(z, z).wait_recv())
        pl.when(p.z != z)(lambda z=z: sq_along(p.z, z).wait_send())
    squares = jnp.zeros((8, LANES), f32)
    for z in range(depth):
        for n in range(8):
            squares = squares + sq[z, n // 4, n // 2 % 2, n % 2]
    rms[...] = jnp.sqrt(squares / (8 * depth * tok * D))
    t_swap.wait_send()
    swap.wait_send()
    e_trade.wait_send()
    e_swap.wait_send()
    for i in range(3):
        da_swaps[i].wait_send()


def closing(attn_sq, dhr, gain, begin, lse, cosine, sine, large, eg, depth, scale, cid):
    f32, bf = jnp.float32, jnp.bfloat16
    tok, width = dhr.shape
    group, q_half = large[3].shape
    blocks = large[6].shape[0]
    kv_block = large[6].shape[1:]
    rows_blk = width // blocks
    rows_e, cols = eg.shape[1] // 2, eg.shape[2] // 2
    kv_half = 2 * HEAD_DIM
    shape = jax.ShapeDtypeStruct
    vmem = pl.BlockSpec(memory_space=pltpu.VMEM)
    hbm = pl.BlockSpec(memory_space=pl.ANY)
    V = pltpu.VMEM

    def buffers(block):
        return [
            V((blocks // 2,) + block, bf),
            V((depth,) + block, bf),
            V((depth,) + block, bf),
        ]

    grad = shape((rows_e, cols), f32)
    rows = q_half // HEAD_DIM * group
    return pl.pallas_call(
        functools.partial(closing_kernel, depth, scale),
        out_shape=(
            shape((tok, width), bf),
            shape((tok, width), f32),
            shape((rows_blk, q_half), f32),
            shape((rows_blk, q_half), f32),
            shape((rows_blk // 2, 2 * kv_half), f32),
            shape((8, LANES), f32),
            grad,
            grad,
            grad,
            shape((8, LANES), f32),
        ),
        in_specs=[vmem] * 7 + [hbm] * 14,
        out_specs=tuple([vmem] * 10),
        scratch_shapes=[V(array.shape, array.dtype) for array in large]
        + [
            V((2, tok, width), bf),
            V((HEAD_DIM, rows), bf),
            V((HEAD_DIM, rows), f32),
            V((8, rows), f32),
            V((blocks // 2, 2) + kv_block, bf),
            V((rows, HEAD_DIM), bf),
            V((group, q_half), bf),
            V((width, group), bf),
            V((group, width), f32),
            V((tok, width), f32),
            V((depth, tok, width), bf),
            V((depth, tok, width), bf),
            V((blocks // 2, 2, rows_blk, q_half), bf),
        ]
        + buffers((rows_blk, q_half))
        + [V((group, kv_half), f32)]
        + buffers((group, kv_half))
        + [V((blocks // 2, 2, rows_blk, q_half), bf)]
        + buffers((rows_blk, q_half))
        + [V((blocks // 2, 2, rows_blk, kv_half + LANES), bf), V((rows_blk, kv_half + LANES), f32)]
        + buffers((rows_blk, kv_half + LANES))
        + [
            V((2 * rows_e, cols), bf),
            V((3, 2 * rows_e, cols), bf),
            V((3, rows_e, cols), bf),
            V((3, rows_e, cols), bf),
            V((3, tok, width // 3), bf),
            V((3, tok, width // 3), bf),
            V((rows_blk // 2, kv_half + LANES), f32),
            V((rows_blk // 2, kv_half + LANES), f32),
            V((depth, 2, 2, 2, 8, LANES), f32),
            V((LANES, LANES), f32),
            pltpu.SemaphoreType.DMA((320,)),
        ],
        compiler_params=pltpu.CompilerParams(
            collective_id=cid, has_side_effects=True, vmem_limit_bytes=60 * 2**20
        ),
        name="closing",
    )(attn_sq, dhr, gain, begin, lse, cosine, sine, *large, eg)


def deliver_kernel(count, gains, rms, *refs):
    ins, (gain_a, gain_m, rms_out) = refs[:count], refs[count : count + 3]
    outs, held, sems = refs[count + 3 : 2 * count + 3], refs[2 * count + 3 : 3 * count + 3], refs[3 * count + 3]
    loads = [pltpu.make_async_copy(ins[i], held[i], sems.at[i]) for i in range(count)]
    stores = [pltpu.make_async_copy(held[i], outs[i], sems.at[count + i]) for i in range(count)]
    each(lambda load: load.start(), loads)
    gain_a[...] = gains[0:1, : gain_a.shape[1]]
    gain_m[...] = gains[1:2, : gain_m.shape[1]]
    rms_out[...] = rms[0:1, : rms_out.shape[1]]
    for load, store in zip(loads, stores):
        load.wait()
        store.start()
    each(lambda store: store.wait(), stores)


def deliver(gains, rms, arrays, rows):
    count = len(arrays)
    hbm = pl.BlockSpec(memory_space=pl.ANY)
    vmem = pl.BlockSpec(memory_space=pltpu.VMEM)
    small = [jax.ShapeDtypeStruct((1, n), jnp.float32) for n in (rows, rows, 3)]
    return pl.pallas_call(
        functools.partial(deliver_kernel, count),
        out_shape=tuple(small + [jax.ShapeDtypeStruct(a.shape, a.dtype) for a in arrays]),
        in_specs=[vmem] * 2 + [hbm] * count,
        out_specs=tuple([vmem] * 3 + [hbm] * count),
        scratch_shapes=[pltpu.VMEM(a.shape, a.dtype) for a in arrays] + [pltpu.SemaphoreType.DMA((2 * count,))],
        compiler_params=pltpu.CompilerParams(vmem_limit_bytes=60 * 2**20),
        name="deliver",
    )(gains, rms, *arrays)


def planned(
    layer_input,
    grad_output,
    gain_attn,
    gain_moe,
    w_query,
    w_keyval,
    w_out,
    w_gate,
    w_up,
    w_down,
    gate_weights,
    expert_ids,
    doc_starts,
):
    depth = lax.axis_size("blk") // 4
    scale = 1.0 / math.sqrt(HEAD_DIM)
    (
        normed_m, hidden, attn_sq, normed_t, query_rows, query_t, mixed, mixed_t, lse, gain_rows, g_all, inputs,
        begin_rows, cosine, sine, kv_all, w_all, out_w, dy_all, gate_w, up_w, down_w,
    ) = front(
        doc_starts, layer_input, grad_output, gain_attn, gain_moe, w_query, w_keyval, w_out, expert_ids.T, gate_weights.T,
        (w_gate, w_up, w_down), depth, scale, 1,
    )
    grad_hidden, grad_hidden_low, gain_terms, z_part, expert_grads = run_experts(
        normed_m, grad_output, dy_all, g_all, (gate_w, up_w, down_w), hidden, gain_rows, depth, 2
    )
    large = (
        z_part, out_w, mixed_t, mixed, query_rows, query_t, kv_all, w_all, normed_t, inputs, hidden, grad_hidden, gain_terms
    )
    results = closing(
        attn_sq, grad_hidden_low, gain_rows, begin_rows, lse, cosine, sine, large, expert_grads, depth, scale, 3
    )
    (
        gain_a, gain_m, rms, layer_output, grad_input, part_query, part_out, part_keyval, grad_gate, grad_up, grad_down
    ) = deliver(results[5], results[9], results[:5] + results[6:9], gain_attn.shape[0])
    return (
        layer_output,
        grad_input,
        gain_a.reshape(-1),
        gain_m.reshape(-1),
        part_query,
        part_keyval,
        part_out,
        grad_gate,
        grad_up,
        grad_down,
        rms.reshape(-1),
    )


def solution(mesh):
    in_specs = (
        P(("blk", "ulysses"), None),
        P(("blk", "ulysses"), None),
        P(("blk", "ulysses")),
        P(("blk", "ulysses")),
        P(("blk", "ulysses"), None),
        P(("blk", "ulysses"), None),
        P(("blk", "ulysses"), None),
        P("ulysses", "blk"),
        P("ulysses", "blk"),
        P("ulysses", "blk"),
        P(("blk", "ulysses"), None),
        P(("blk", "ulysses"), None),
        P(),
    )
    out_specs = (
        P(("blk", "ulysses"), None),
        P(("blk", "ulysses"), None),
        P(("blk", "ulysses")),
        P(("blk", "ulysses")),
        P("blk", "ulysses"),
        P(("blk", "ulysses"), None),
        P("blk", "ulysses"),
        P("ulysses", "blk"),
        P("ulysses", "blk"),
        P("ulysses", "blk"),
        P(),
    )
    blocks, members = mesh.shape["blk"], mesh.shape["ulysses"]
    body = planned if blocks == 16 and members == KV_HEADS else local
    return jax.shard_map(body, mesh=mesh, in_specs=in_specs, out_specs=out_specs, check_vma=False)
```

```python
import functools
import math

import jax
import jax.numpy as jnp
import numpy as np
from jax import lax
from jax.experimental import pallas as pl
from jax.experimental.pallas import tpu as pltpu
from jax.sharding import PartitionSpec as P

D = 1536
HEADS = 12
KV_HEADS = 2
HEAD_DIM = 128
TOP = 4


EPS = 1e-06
ROPE_BASE = 1000000.0
NEG = -1e30
EARLY = (3,)


def rotate(values, positions, sign):
    half = values.shape[-1] // 2
    freq = ROPE_BASE ** (-jnp.arange(half, dtype=jnp.float32) * 2.0 / values.shape[-1])
    angle = positions.astype(jnp.float32)[:, None] * freq[None, :]
    cosine = jnp.cos(angle)[:, None, :]
    sine = sign * jnp.sin(angle)[:, None, :]
    first = values[..., :half]
    second = values[..., half:]
    return jnp.concatenate([first * cosine - second * sine, second * cosine + first * sine], -1)


def doc_begin(positions, doc_starts):
    return jnp.max(
        jnp.where(doc_starts[None, :] <= positions[:, None], doc_starts[None, :], 0), axis=1
    )


def norm_back(values, factor, gain, grad):
    weighted = grad * gain
    inner = jnp.mean(weighted * values, -1, keepdims=True)
    return factor * weighted - values * factor * factor * factor * inner


def visible_mask(q_pos, q_begin, k_pos):
    return (k_pos[None, :] >= q_begin[:, None]) & (k_pos[None, :] <= q_pos[:, None])


def split_blocks(array):
    rows = array.shape[0]
    size = min(rows, 512)
    return (array.reshape((rows // size, size) + array.shape[1:]), size)


def contract(left, right, left_dim, right_dim):
    return lax.dot_general(
        left, right, (((left_dim,), (right_dim,)), ((), ())), preferred_element_type=jnp.float32
    )


def reorder_rows(array, outer, inner):
    rows = array.shape[0]
    shaped = array.reshape((outer, inner, rows // (outer * inner)) + array.shape[1:])
    return jnp.swapaxes(shaped, 0, 1).reshape(array.shape)


def route(payload):
    return lax.all_to_all(payload, "blk", split_axis=0, concat_axis=0, tiled=True)


def backward_block(queries, grads, lse, delta, q_pos, q_begin, keys, values, k_start, scale):
    k_pos = k_start + jnp.arange(keys.shape[0], dtype=jnp.int32)
    visible = visible_mask(q_pos, q_begin, k_pos)[None]
    scores = jnp.einsum("qhd,kd->hqk", queries, keys, preferred_element_type=jnp.float32) * scale
    probs = jnp.where(visible, jnp.exp(scores - lse[:, :, None]), 0.0)
    probs_low = probs.astype(jnp.bfloat16)
    grad_probs = jnp.einsum("qhd,kd->hqk", grads, values, preferred_element_type=jnp.float32)
    grad_scores = (probs * (grad_probs - delta[:, :, None])).astype(jnp.bfloat16)
    part_q = (
        jnp.einsum("hqk,kd->qhd", grad_scores, keys, preferred_element_type=jnp.float32) * scale
    )
    part_k = (
        jnp.einsum("hqk,qhd->kd", grad_scores, queries, preferred_element_type=jnp.float32) * scale
    )
    part_v = jnp.einsum("hqk,qhd->kd", probs_low, grads, preferred_element_type=jnp.float32)
    return (part_q, part_k, part_v)


def local(
    layer_input,
    grad_output,
    gain_attn,
    gain_moe,
    w_query,
    w_keyval,
    w_out,
    w_gate,
    w_up,
    w_down,
    gate_weights,
    expert_ids,
    doc_starts,
):
    n_blk = lax.axis_size("blk")
    n_uly = lax.axis_size("ulysses")
    tok = layer_input.shape[0]
    group = tok * n_uly
    heads_dev = HEADS // n_uly
    per_kv = HEADS // KV_HEADS
    which = [c * heads_dev // per_kv for c in range(n_uly)]
    kv_width = KV_HEADS * HEAD_DIM
    q_width = HEADS * HEAD_DIM
    scale = 1.0 / math.sqrt(HEAD_DIM)
    blk_index = lax.axis_index("blk")
    device = blk_index * n_uly + lax.axis_index("ulysses")
    tok_pos = device * tok + jnp.arange(tok, dtype=jnp.int32)
    places = tok_pos - doc_begin(tok_pos, doc_starts)
    gain_a, gain_m, query_w, keyval_w, out_w = (
        lax.all_gather(gain_attn, ("blk", "ulysses"), axis=0, tiled=True),
        lax.all_gather(gain_moe, ("blk", "ulysses"), axis=0, tiled=True),
        lax.all_gather(w_query, ("blk", "ulysses"), axis=0, tiled=True),
        lax.all_gather(w_keyval, ("blk", "ulysses"), axis=0, tiled=True),
        lax.all_gather(w_out, ("blk", "ulysses"), axis=0, tiled=True),
    )
    gate_w, up_w, down_w = (
        lax.all_gather(w_gate, "ulysses", axis=0, tiled=True),
        lax.all_gather(w_up, "ulysses", axis=0, tiled=True),
        lax.all_gather(w_down, "ulysses", axis=0, tiled=True),
    )
    gain_a = gain_a.astype(jnp.float32)
    gain_m = gain_m.astype(jnp.float32)
    inputs = layer_input.astype(jnp.float32)
    factor_a = lax.rsqrt(jnp.mean(inputs * inputs, -1, keepdims=True) + EPS)
    normed_a = (inputs * factor_a * gain_a).astype(jnp.bfloat16)
    query_raw = jnp.dot(normed_a, query_w, preferred_element_type=jnp.float32)
    keyval_raw = jnp.dot(normed_a, keyval_w, preferred_element_type=jnp.float32)
    queries = rotate(query_raw.reshape(tok, HEADS, HEAD_DIM), places, 1.0).astype(jnp.bfloat16)
    keys = rotate(keyval_raw[:, :kv_width].reshape(tok, KV_HEADS, HEAD_DIM), places, 1.0).astype(
        jnp.bfloat16
    )
    values = keyval_raw[:, kv_width:].reshape(tok, KV_HEADS, HEAD_DIM).astype(jnp.bfloat16)
    key_copies = jnp.stack([keys[:, j] for j in which], 1)
    value_copies = jnp.stack([values[:, j] for j in which], 1)
    spread_normed = jnp.broadcast_to(normed_a[:, None, :], (tok, n_uly, D))
    head_q, head_k, head_v, head_normed = (
        lax.all_to_all(queries, "ulysses", split_axis=1, concat_axis=0, tiled=True),
        lax.all_to_all(key_copies, "ulysses", split_axis=1, concat_axis=0, tiled=True),
        lax.all_to_all(value_copies, "ulysses", split_axis=1, concat_axis=0, tiled=True),
        lax.all_to_all(spread_normed, "ulysses", split_axis=1, concat_axis=0, tiled=True),
    )
    key_local = head_k[:, 0, :]
    value_local = head_v[:, 0, :]
    normed_group = head_normed[:, 0, :]
    q_pos = blk_index * group + jnp.arange(group, dtype=jnp.int32)
    q_begin = doc_begin(q_pos, doc_starts)
    start_state = (
        jnp.full((heads_dev, group), NEG, jnp.float32),
        jnp.zeros((heads_dev, group), jnp.float32),
        jnp.zeros((group, heads_dev, HEAD_DIM), jnp.float32),
    )
    state = start_state
    key_rows = lax.all_gather(key_local, "blk", axis=0, tiled=True)
    value_rows = lax.all_gather(value_local, "blk", axis=0, tiled=True)
    key_blocks, size = split_blocks(key_rows)
    value_blocks, _ = split_blocks(value_rows)

    def attend_step(inner, item):
        key_blk, value_blk, number = item
        k_start = number * size
        live = (k_start <= q_pos[-1]) & (k_start + size - 1 >= q_begin[0])

        def attend_work(current):
            top, total, acc = current
            k_pos = k_start + jnp.arange(size, dtype=jnp.int32)
            visible = visible_mask(q_pos, q_begin, k_pos)[None]
            scores = (
                jnp.einsum("qhd,kd->hqk", head_q, key_blk, preferred_element_type=jnp.float32)
                * scale
            )
            scores = jnp.where(visible, scores, NEG)
            new_top = jnp.maximum(top, jnp.max(scores, -1))
            weights = jnp.where(visible, jnp.exp(scores - new_top[:, :, None]), 0.0)
            keep = jnp.exp(top - new_top)
            total = total * keep + jnp.sum(weights, -1)
            acc = acc * jnp.transpose(keep)[:, :, None] + jnp.einsum(
                "hqk,kd->qhd",
                weights.astype(jnp.bfloat16),
                value_blk,
                preferred_element_type=jnp.float32,
            )
            return (new_top, total, acc)

        return (lax.cond(live, attend_work, lambda current: current, inner), None)

    state, _ = lax.scan(
        attend_step,
        state,
        (key_blocks, value_blocks, jnp.arange(key_blocks.shape[0], dtype=jnp.int32)),
    )
    top, total, acc = state
    mixed = acc / jnp.transpose(total)[:, :, None]
    mixed_low = mixed.astype(jnp.bfloat16)
    lse = top + jnp.log(total)
    attended = lax.all_to_all(
        mixed_low, "ulysses", split_axis=0, concat_axis=1, tiled=True
    ).reshape(tok, q_width)
    attn_branch = contract(attended, out_w, 1, 1)
    hidden = inputs + attn_branch
    factor_m = lax.rsqrt(jnp.mean(hidden * hidden, -1, keepdims=True) + EPS)
    normed_m = (hidden * factor_m * gain_m).astype(jnp.bfloat16)
    experts = n_blk // 2
    capacity = min(tok, 2 * tok * TOP // experts)
    flat_ids = expert_ids.reshape(-1)
    picks = (flat_ids[:, None] == jnp.arange(experts, dtype=jnp.int32)[None, :]).astype(jnp.int32)
    slots = jnp.sum((jnp.cumsum(picks, 0) - 1) * picks, -1)

    def dispatch(rows):
        buffer = jnp.zeros((experts, capacity, D), jnp.bfloat16).at[flat_ids, slots].set(rows)
        return route(jnp.repeat(buffer, 2, axis=0)).reshape(n_blk * capacity, D)

    def collect(rows):
        back = route(rows.astype(jnp.bfloat16).reshape(n_blk, capacity, D))
        return back[2 * flat_ids, slots].astype(jnp.float32) + back[2 * flat_ids + 1, slots].astype(
            jnp.float32
        )

    expert_in = dispatch(jnp.repeat(normed_m, TOP, axis=0))
    gate_pre = jnp.dot(expert_in, gate_w, preferred_element_type=jnp.float32)
    up_pre = jnp.dot(expert_in, up_w, preferred_element_type=jnp.float32)
    act = (jax.nn.silu(gate_pre) * up_pre).astype(jnp.bfloat16)
    expert_out = contract(act, down_w, 1, 1)
    returned = collect(expert_out).reshape(tok, TOP, D)
    moe_branch = jnp.sum(gate_weights[:, :, None] * returned, 1)
    result = hidden + moe_branch
    layer_output = result.astype(jnp.bfloat16)
    grad_res = grad_output.astype(jnp.float32)
    routed_grad = (
        (gate_weights[:, :, None] * grad_res[:, None, :]).reshape(tok * TOP, D).astype(jnp.bfloat16)
    )
    expert_grad = dispatch(routed_grad)
    grad_act = jnp.dot(expert_grad, down_w, preferred_element_type=jnp.float32)
    grad_down = contract(expert_grad, act, 0, 0)
    sig = jax.nn.sigmoid(gate_pre)
    grad_gate_pre = (grad_act * up_pre * sig * (1.0 + gate_pre * (1.0 - sig))).astype(jnp.bfloat16)
    grad_up_pre = (grad_act * gate_pre * sig).astype(jnp.bfloat16)
    grad_gate = contract(expert_in, grad_gate_pre, 0, 0)
    grad_up = contract(expert_in, grad_up_pre, 0, 0)
    grad_in = contract(grad_gate_pre, gate_w, 1, 1) + contract(grad_up_pre, up_w, 1, 1)
    grad_normed_m = jnp.sum(collect(grad_in).reshape(tok, TOP, D), 1)
    grad_gain_m = jnp.sum(grad_normed_m * hidden * factor_m, 0)
    grad_hidden = grad_res + norm_back(hidden, factor_m, gain_m, grad_normed_m)
    grad_hidden_low = grad_hidden.astype(jnp.bfloat16)
    grad_attended = jnp.dot(grad_hidden_low, out_w, preferred_element_type=jnp.float32).astype(
        jnp.bfloat16
    )
    spread_hidden = jnp.broadcast_to(grad_hidden_low[:, None, :], (tok, n_uly, D))
    head_grad, head_hidden = (
        lax.all_to_all(
            grad_attended.reshape(tok, HEADS, HEAD_DIM),
            "ulysses",
            split_axis=1,
            concat_axis=0,
            tiled=True,
        ),
        lax.all_to_all(spread_hidden, "ulysses", split_axis=1, concat_axis=0, tiled=True),
    )
    grad_out_slice = contract(
        head_hidden[:, 0, :], mixed_low.reshape(group, heads_dev * HEAD_DIM), 0, 0
    )
    delta = jnp.transpose(jnp.sum(head_grad.astype(jnp.float32) * mixed, -1))
    total_keys = group * n_blk
    zero_q = jnp.zeros((group, heads_dev, HEAD_DIM), jnp.float32)
    fold_start = (
        zero_q,
        jnp.zeros((total_keys, HEAD_DIM), jnp.float32),
        jnp.zeros((total_keys, HEAD_DIM), jnp.float32),
    )
    state = fold_start
    key_rows = lax.all_gather(key_local, "blk", axis=0, tiled=True)
    value_rows = lax.all_gather(value_local, "blk", axis=0, tiled=True)
    key_blocks, grads_size = split_blocks(key_rows)
    value_blocks, _ = split_blocks(value_rows)

    def grads_step(inner, item):
        key_blk, value_blk, number = item
        k_start = number * grads_size
        live = (k_start <= q_pos[-1]) & (k_start + grads_size - 1 >= q_begin[0])

        def grads_work(current):
            part_q, part_k, part_v = backward_block(
                head_q, head_grad, lse, delta, q_pos, q_begin, key_blk, value_blk, k_start, scale
            )
            grad_q, grad_keys, grad_values = current
            grad_keys = lax.dynamic_update_slice_in_dim(
                grad_keys,
                lax.dynamic_slice_in_dim(grad_keys, k_start, grads_size, 0) + part_k,
                k_start,
                0,
            )
            grad_values = lax.dynamic_update_slice_in_dim(
                grad_values,
                lax.dynamic_slice_in_dim(grad_values, k_start, grads_size, 0) + part_v,
                k_start,
                0,
            )
            return (grad_q + part_q, grad_keys, grad_values)

        return (lax.cond(live, grads_work, lambda current: current, inner), None)

    state, _ = lax.scan(
        grads_step,
        state,
        (key_blocks, value_blocks, jnp.arange(key_blocks.shape[0], dtype=jnp.int32)),
    )
    grad_q = state[0]
    grad_k, grad_v = (
        lax.psum_scatter(state[1], "blk", scatter_dimension=0, tiled=True),
        lax.psum_scatter(state[2], "blk", scatter_dimension=0, tiled=True),
    )
    group_places = q_pos - q_begin
    grad_q_pre = rotate(grad_q.astype(jnp.bfloat16).astype(jnp.float32), group_places, -1.0).astype(
        jnp.bfloat16
    )
    grad_query_slice = contract(normed_group, grad_q_pre.reshape(group, heads_dev * HEAD_DIM), 0, 0)
    token_q, token_k, token_v = (
        lax.all_to_all(grad_q_pre, "ulysses", split_axis=0, concat_axis=1, tiled=True),
        lax.all_to_all(
            grad_k.astype(jnp.bfloat16)[:, None, :],
            "ulysses",
            split_axis=0,
            concat_axis=1,
            tiled=True,
        ),
        lax.all_to_all(
            grad_v.astype(jnp.bfloat16)[:, None, :],
            "ulysses",
            split_axis=0,
            concat_axis=1,
            tiled=True,
        ),
    )
    summed_k = []
    summed_v = []
    for head in range(KV_HEADS):
        members = [c for c in range(n_uly) if which[c] == head]
        summed_k.append(sum((token_k[:, c].astype(jnp.float32) for c in members)))
        summed_v.append(sum((token_v[:, c].astype(jnp.float32) for c in members)))
    grad_key_heads = jnp.stack(summed_k, 1)
    grad_value_heads = jnp.stack(summed_v, 1)
    grad_query_pre = token_q.reshape(tok, q_width)
    grad_key_pre = rotate(grad_key_heads, places, -1.0).reshape(tok, kv_width)
    grad_keyval_pre = jnp.concatenate(
        [grad_key_pre, grad_value_heads.reshape(tok, kv_width)], 1
    ).astype(jnp.bfloat16)
    grad_normed_a = contract(grad_query_pre, query_w, 1, 1) + contract(
        grad_keyval_pre, keyval_w, 1, 1
    )
    grad_keyval_w = contract(normed_a, grad_keyval_pre, 0, 0)
    grad_gain_a = jnp.sum(grad_normed_a * inputs * factor_a, 0)
    grad_input = grad_hidden + norm_back(inputs, factor_a, gain_a, grad_normed_a)
    n_dev = n_blk * n_uly
    squares = jnp.stack(
        [
            jnp.sum(attn_branch * attn_branch),
            jnp.sum(moe_branch * moe_branch),
            jnp.sum(result * result),
        ]
    )
    square_rows = jnp.broadcast_to(squares[None, :], (n_dev, 3))
    part_gate, part_up, part_down, uly_gain_a, uly_gain_m, uly_keyval, uly_squares = (
        lax.psum_scatter(
            grad_gate.astype(jnp.bfloat16), "ulysses", scatter_dimension=0, tiled=True
        ).astype(jnp.float32),
        lax.psum_scatter(
            grad_up.astype(jnp.bfloat16), "ulysses", scatter_dimension=0, tiled=True
        ).astype(jnp.float32),
        lax.psum_scatter(
            grad_down.astype(jnp.bfloat16), "ulysses", scatter_dimension=0, tiled=True
        ).astype(jnp.float32),
        lax.psum_scatter(
            reorder_rows(grad_gain_a, n_blk, n_uly).astype(jnp.bfloat16),
            "ulysses",
            scatter_dimension=0,
            tiled=True,
        ).astype(jnp.float32),
        lax.psum_scatter(
            reorder_rows(grad_gain_m, n_blk, n_uly).astype(jnp.bfloat16),
            "ulysses",
            scatter_dimension=0,
            tiled=True,
        ).astype(jnp.float32),
        lax.psum_scatter(
            reorder_rows(grad_keyval_w, n_blk, n_uly).astype(jnp.bfloat16),
            "ulysses",
            scatter_dimension=0,
            tiled=True,
        ).astype(jnp.float32),
        lax.psum_scatter(
            square_rows.astype(jnp.bfloat16), "ulysses", scatter_dimension=0, tiled=True
        ).astype(jnp.float32),
    )
    part_outw, part_query, part_gain_a, part_gain_m, part_keyval, square_row = (
        lax.psum_scatter(grad_out_slice, "blk", scatter_dimension=0, tiled=True),
        lax.psum_scatter(grad_query_slice, "blk", scatter_dimension=0, tiled=True),
        lax.psum_scatter(uly_gain_a, "blk", scatter_dimension=0, tiled=True),
        lax.psum_scatter(uly_gain_m, "blk", scatter_dimension=0, tiled=True),
        lax.psum_scatter(uly_keyval, "blk", scatter_dimension=0, tiled=True),
        lax.psum_scatter(uly_squares, "blk", scatter_dimension=0, tiled=True),
    )
    branch_rms = jnp.sqrt(square_row[0] / (tok * n_dev * D))
    return (
        layer_output,
        grad_input,
        part_gain_a,
        part_gain_m,
        part_query,
        part_keyval,
        part_outw,
        part_gate,
        part_up,
        part_down,
        branch_rms,
    )


MESH = pl.DeviceIdType.MESH
LANES = 128
LOG2E = 1.4426950408889634


class Place:
    def __init__(self, depth):
        self.blk = lax.axis_index("blk")
        self.u = lax.axis_index("ulysses")
        self.depth = depth
        self.z = self.blk // 4
        self.x = (self.blk // 2) % 2
        self.c = self.blk % 2
        self.up = (self.blk + 4, self.u)
        self.down = (self.blk - 4, self.u)
        self.across = (self.blk + 2 - 4 * self.x, self.u)
        self.sibling = (self.blk + 1 - 2 * self.c, self.u)
        self.other = (self.blk, 1 - self.u)
        self.has_up = self.z < depth - 1
        self.has_down = self.z > 0

    def along(self, z):
        return (self.blk + 4 * (z - self.z), self.u)

    def slot(self, z, x, c):
        return z * 4 + x * 2 + c

    def greet(self, sibling=False, other=False, plane=True):
        barrier = pltpu.get_barrier_semaphore()

        def hail(device):
            pl.semaphore_signal(barrier, inc=1, device_id=device, device_id_type=MESH)

        count = 0
        if plane:
            hail(self.across)
            for d in range(1, self.depth):
                pl.when(self.z >= d)(lambda d=d: hail(self.along(self.z - d)))
                pl.when(self.z + d < self.depth)(lambda d=d: hail(self.along(self.z + d)))
            count = self.depth
        if sibling:
            hail(self.sibling)
            count = count + 1
        if other:
            hail(self.other)
            count = count + 1
        pl.semaphore_wait(barrier, count)


class Wires:
    def __init__(self, sems):
        self.sems = sems
        self.used = 0

    def take(self, count):
        base = self.used
        self.used += count
        return lambda index: self.sems.at[base + index]


def each(act, items):
    for item in items:
        act(item)


def remote(src, dst, send, recv, device):
    return pltpu.make_async_remote_copy(
        src_ref=src, dst_ref=dst, send_sem=send, recv_sem=recv, device_id=device, device_id_type=MESH
    )


class Gather:
    def __init__(self, place, wires, src, out, cores, up_only=False, chain=False, far=False):
        self.p, self.src, self.out, self.cores, self.up_only, self.chain = place, src, out, cores, up_only, chain
        n = place.depth
        self.s_z = [wires.take(n) for _ in range(2 if chain else 1)]
        self.s_across = wires.take(n)
        self.r_z, self.r_x = wires.take(n), wires.take(n)
        if cores:
            self.s_core, self.r_core = wires.take(2 * n), wires.take(2 * n)
        self.far = wires.take(1)(0) if far else None

    def _across(self, zz, xx, src=None):
        dst = self.out(zz, xx, self.p.c)
        return remote(dst if src is None else src, dst, self.s_across(zz), self.r_x(zz), self.p.across)

    def _core(self, zz, xx, src=None):
        dst = self.out(zz, xx, self.p.c)
        at = zz * 2 + xx
        return remote(dst if src is None else src, dst, self.s_core(at), self.r_core(at), self.p.sibling)

    def _along(self, zz, to, src=None):
        p = self.p
        dst = self.out(zz, p.x, p.c)
        return remote(dst if src is None else src, dst, self.s_z[0](to), self.r_z(zz), p.along(to))

    def _next(self, zz, up, src=None):
        p = self.p
        dst = self.out(zz, p.x, p.c)
        return remote(
            dst if src is None else src, dst, self.s_z[up](zz), self.r_z(zz), p.along(p.z + (1 if up else -1))
        )

    def start_z(self, in_place=False):
        p = self.p
        src = None if in_place else self.src
        if self.chain:
            pl.when(p.has_up)(lambda: self._next(p.z, 1, src).start())
            pl.when(p.has_down)(lambda: self._next(p.z, 0, src).start())
            return
        for d in range(1, p.depth):
            pl.when(p.z + d < p.depth)(lambda d=d: self._along(p.z, p.z + d, src).start())
            if not self.up_only:
                pl.when(p.z >= d)(lambda d=d: self._along(p.z, p.z - d, src).start())

    def start_x(self, in_place=False):
        p = self.p
        src = None if in_place else self.src
        self._across(p.z, p.x, src).start()
        if self.cores:
            self._core(p.z, p.x, src).start()
        if self.far is not None:
            pltpu.make_async_copy(self.src, self.out(p.z, p.x, p.c), self.far).start()
        elif not in_place:
            self.out(p.z, p.x, p.c)[...] = self.src[...]

    def start(self, in_place=False):
        self.start_z(in_place)
        self.start_x(in_place)

    def hop(self, d):
        p = self.p

        def take(zz, up):
            remote(
                self.out(zz, p.x, p.c), self.out(zz, p.x, p.c), self.s_z[0](0), self.r_z(zz), p.across
            ).wait_recv()
            if self.chain:
                pl.when(p.has_up if up else p.has_down)(lambda: self._next(zz, up).start())
            self._across(zz, p.x).start()
            if self.cores:
                self._core(zz, p.x).start()

        pl.when(p.z >= d)(lambda: take(p.z - d, 1))
        if not self.up_only:
            pl.when(p.z + d < p.depth)(lambda: take(p.z + d, 0))

    def cross(self, d):
        p = self.p

        def take(zz):
            self._across(zz, 1 - p.x).wait_recv()
            if self.cores:
                self._core(zz, 1 - p.x).start()

        if isinstance(d, int) and d == 0:
            take(p.z)
        else:
            pl.when(p.z >= d)(lambda: take(p.z - d))
            if not self.up_only:
                pl.when(p.z + d < p.depth)(lambda: take(p.z + d))

    def crossed(self, zz):
        self._across(zz, 1 - self.p.x).wait_recv()

    def core(self, zz, xx):
        self._core(zz, xx).wait_recv()

    def finish(self, cores_taken=False):
        p = self.p
        for zz in range(p.depth):

            def ends(zz=zz):
                if self.cores:
                    for xx in range(2):
                        if not cores_taken:
                            self._core(zz, xx).wait_recv()
                        self._core(zz, xx).wait_send()
                self._across(zz, p.x).wait_send()

            if self.up_only and zz > 0:
                pl.when(p.z >= zz)(ends)
            else:
                ends()
            if self.chain:
                pl.when(p.has_up & (p.z >= zz))(lambda zz=zz: self._next(zz, 1).wait_send())
                pl.when(p.has_down & (p.z <= zz))(lambda zz=zz: self._next(zz, 0).wait_send())
            else:
                away = (p.z < zz) if self.up_only else (p.z != zz)
                pl.when(away)(lambda zz=zz: self._along(p.z, zz).wait_send())
        if self.far is not None:
            pltpu.make_async_copy(self.src, self.out(p.z, p.x, p.c), self.far).wait()


class Scatter:
    def __init__(self, place, wires, part, out, rx, rz, pieces, down_only=False, ready=()):
        self.ready = ready
        self.p, self.part, self.out, self.rx, self.rz = place, part, out, rx, rz
        n = place.depth
        total = n * pieces
        self.pieces, self.down_only = pieces, down_only
        self.sx, self.cx = wires.take(total), wires.take(total)
        self.sz, self.cz = wires.take(total), wires.take(total)
        if down_only:
            self.order = list(range(n))
        else:
            self.order = [n - 1 - i // 2 if i % 2 == 0 else i // 2 for i in range(n)]
        self.items = [(zz, k) for zz in self.order if zz not in ready for k in range(pieces)]

    def _x(self, zz, k):
        i = zz * self.pieces + k
        return remote(self.part(zz, 1 - self.p.x, k), self.rx(zz, k), self.sx(i), self.cx(i), self.p.across)

    def _z(self, zz, k, source=None):
        p = self.p
        source = p.z if source is None else source
        return remote(
            self.rx(zz, k),
            self.rz(source, k),
            self.sz(zz * self.pieces + k),
            self.cz(source * self.pieces + k),
            p.along(zz),
        )

    def _live(self, zz, act):
        if self.down_only and zz > 0:
            pl.when(self.p.z >= zz)(act)
        else:
            act()

    def begin(self, t):
        if t < len(self.items):
            zz, k = self.items[t]
            self._live(zz, lambda: self._x(zz, k).start())

    def send(self, zz):
        for k in range(self.pieces):
            self._x(zz, k).start()

    def take(self, zz, k):
        p = self.p

        def act():
            self._x(zz, k).wait_recv()

            def forward():
                total = self.part(zz, p.x, k)[...].astype(jnp.float32)
                total = total + self.rx(zz, k)[...].astype(jnp.float32)
                self.rx(zz, k)[...] = total.astype(jnp.bfloat16)
                self._z(zz, k).start()

            pl.when(p.z != zz)(forward)

        self._live(zz, act)

    def land(self, t):
        self.take(*self.items[t])

    def forward(self):
        for zz in self.ready:
            for k in range(self.pieces):
                pl.when(self.p.z != zz)(lambda zz=zz, k=k: self._z(zz, k).start())

    def finish(self):
        p = self.p
        n = p.depth
        for zz, k in [(zz, k) for zz in self.order for k in range(self.pieces)]:
            if zz not in self.ready:
                self._live(zz, lambda zz=zz, k=k: self._x(zz, k).wait_send())
            away = (p.z > zz) if self.down_only else (p.z != zz)
            pl.when(away)(lambda zz=zz, k=k: self._z(zz, k).wait_send())

            def store(zz=zz, k=k):
                total = self.rx(zz, k)[...].astype(jnp.float32)
                if zz not in self.ready:
                    total = total + self.part(zz, p.x, k)[...].astype(jnp.float32)
                for source in range(zz + 1 if self.down_only else 0, n):
                    if source != zz:
                        self._z(zz, k, source).wait_recv()
                        total = total + self.rz(source, k)[...].astype(jnp.float32)
                self.out(k)[...] = total

            pl.when(p.z == zz)(store)


class CoreScatter:
    def __init__(self, place, wires, src, rc, out, rx, rz, down_only=False):
        self.p, self.src, self.rc, self.down_only = place, src, rc, down_only
        n = place.depth
        self.sc, self.cc = wires.take(n), wires.take(n)
        self.plane = Scatter(
            place, wires, lambda zz, xx, k: rc.at[zz * 2 + xx], lambda k: out,
            lambda zz, k: rx.at[zz], lambda source, k: rz.at[source], 1, down_only,
        )
        self.order = self.plane.order

    def _trade(self, zz):
        p = self.p
        if self.down_only:
            at = pl.ds(2 * zz, 2)
            return remote(self.src.at[at, 1 - p.c], self.rc.at[at], self.sc(zz), self.cc(zz), p.sibling)
        return remote(self.src.at[:, 1 - p.c], self.rc, self.sc(0), self.cc(0), p.sibling)

    def trade(self, t=0):
        zz = self.order[t]
        self.plane._live(zz, lambda: self._trade(zz).start())

    def join(self, t):
        p = self.p
        zz = self.order[t]

        def act():
            if self.down_only or t == 0:
                self._trade(zz).wait_recv()
            for xx in range(2):
                at = zz * 2 + xx
                self.rc[at] = (
                    self.src[at, p.c].astype(jnp.float32) + self.rc[at].astype(jnp.float32)
                ).astype(jnp.bfloat16)

        self.plane._live(zz, act)
        self.plane.begin(t)

    def land(self, t):
        self.plane.land(t)

    def release(self):
        for t, zz in enumerate(self.order):
            if self.down_only or t == 0:
                self.plane._live(zz, lambda zz=zz: self._trade(zz).wait_send())

    def finish(self):
        self.plane.finish()


def mm(left, right):
    return jnp.dot(left, right, preferred_element_type=jnp.float32)


def flip(tile):
    return tile.astype(jnp.float32).T.astype(jnp.bfloat16)


def hidden_bias(first_key, first_query, begin, keys):
    queries = begin.shape[1]
    k_pos = first_key + lax.broadcasted_iota(jnp.int32, (keys, queries), 0)
    q_pos = first_query + lax.broadcasted_iota(jnp.int32, (keys, queries), 1)
    return jnp.where((k_pos >= begin) & (k_pos <= q_pos), 0.0, NEG)


def front_kernel(
    depth, scale, docs, x, dy, gain_a, gain_m, wq, wkv, wo, ids, shares_of, freq, e0, e1, e2,
    b, hid, attn_sq, normed_t, q_rows, qt, o, ot, lse, gain_rows, g_all, x_all, begin, cosine, sine,
    kv_out, w_out, wo_out, dy_all, f0, f1, f2,
    kv, w_all, wo_all, own, square, g_own, wa_own, normed, raw, top, total, acc, p_out, p_in, sems,
):
    f32, bf = jnp.float32, jnp.bfloat16
    p = Place(depth)
    p.greet(sibling=True, other=True)
    wires = Wires(sems)
    u, blk = p.u, p.blk
    tok, width = x.shape
    group, q_half = o.shape
    heads = q_half // HEAD_DIM
    kv_half = 2 * HEAD_DIM
    rows_dev = wq.shape[0]
    half, cols = e0.shape
    experts = 2 * depth

    def rows_of(ref, z, xx, c, member):
        row = (p.slot(z, xx, c) * 2 + member) * rows_dev
        return ref.at[pl.ds(pl.multiple_of(row, 16), rows_dev)]

    wa_mine = Gather(p, wires, wa_own.at[u], lambda z, xx, c: rows_of(w_all, z, xx, c, u), True, chain=True)
    wa_peer = Gather(p, wires, None, lambda z, xx, c: rows_of(w_all, z, xx, c, 1 - u), True, chain=True)
    wos = Gather(
        p, wires, None,
        lambda z, xx, c: wo_all.at[pl.ds(pl.multiple_of(p.slot(z, xx, c) * 2 * rows_dev, 16), 2 * rows_dev)],
        True, chain=True,
    )
    kvs = Gather(p, wires, None, lambda z, xx, c: kv.at[p.slot(z, xx, c)], True, up_only=True)
    piece = tok // 2
    dys = [
        Gather(
            p, wires, dy.at[pl.ds(k * piece, piece)],
            lambda z, xx, c, k=k: dy_all.at[z * 2 + xx, pl.ds(k * piece, piece)], False, chain=True, far=True,
        )
        for k in range(2)
    ]
    gws = Gather(p, wires, g_own, lambda z, xx, c: g_all.at[z * 2 + xx], False, chain=True)
    ws, wr = wires.take(2), wires.take(2)
    xs, xr = wires.take(1)(0), wires.take(1)(0)
    es, er = wires.take(3), wires.take(3)
    cs, cr = wires.take(6), wires.take(6)
    ps, pr = wires.take(3), wires.take(3)

    for h in range(2):
        wa_own[h, :, :q_half] = wq[:, h * q_half : (h + 1) * q_half]
        for part in range(2):
            wa_own[h, :, q_half + part * HEAD_DIM : q_half + (part + 1) * HEAD_DIM] = wkv[
                :, (part * 2 + h) * HEAD_DIM : (part * 2 + h + 1) * HEAD_DIM
            ]
    square[...] = jnp.zeros(square.shape, f32)
    square[0:1, :rows_dev] = gain_a[...].astype(f32)
    square[1:2, :rows_dev] = gain_m[...].astype(f32)
    columns = square[...].T[:rows_dev, :].astype(bf)
    for h in range(2):
        wa_own[h, :, q_half + kv_half :] = columns

    wa_swap = remote(wa_own.at[1 - u], rows_of(w_all, p.z, p.x, p.c, u), ws(0), wr(0), p.other)
    wo_swap = remote(
        wo.at[:, pl.ds(pl.multiple_of((1 - u) * q_half, LANES), q_half)],
        rows_of(wo_all, p.z, p.x, p.c, u), ws(1), wr(1), p.other,
    )
    x_swap = remote(x, x_all.at[u], xs, xr, p.other)

    def part(ref, row, core):
        return ref.at[
            pl.ds(pl.multiple_of(row * half, half), half), pl.ds(pl.multiple_of(core * cols, LANES), cols)
        ]

    halves = ((e0, f0), (e1, f1), (e2, f2))
    ls, ks = wires.take(3), wires.take(3)
    loads = [pltpu.make_async_copy(e, own.at[i], ls(i)) for i, (e, f) in enumerate(halves)]
    keeps = [pltpu.make_async_copy(own.at[i], part(f, u, p.c), ks(i)) for i, (e, f) in enumerate(halves)]
    swaps = [remote(own.at[i], part(f, u, p.c), es(i), er(i), p.other) for i, (e, f) in enumerate(halves)]
    shares = [remote(own.at[i], part(f, u, p.c), cs(i), cr(i), p.sibling) for i, (e, f) in enumerate(halves)]
    passes = [
        remote(part(f, 1 - u, p.c), part(f, 1 - u, p.c), cs(3 + i), cr(3 + i), p.sibling)
        for i, (e, f) in enumerate(halves)
    ]
    os_ = wires.take(3)
    stores = [
        pltpu.make_async_copy(v, r, os_(i)) for i, (v, r) in enumerate(((kv, kv_out), (w_all, w_out), (wo_all, wo_out)))
    ]

    def expert_out(i):
        swaps[i].start()
        shares[i].start()

    def expert_in(i):
        swaps[i].wait_recv()
        passes[i].start()

    wa_swap.start()
    wa_mine.start()
    wo_swap.start()
    x_swap.start()
    each(lambda load: load.start(), loads)

    def starts(places):
        first = jnp.zeros(places.shape, jnp.int32)
        for i in range(docs.shape[0]):
            first = jnp.where(docs[i] <= places, jnp.maximum(first, docs[i]), first)
        return first

    begin[...] = starts(blk * group + lax.broadcasted_iota(jnp.int32, begin.shape, 1))
    places = blk * group + lax.broadcasted_iota(jnp.int32, cosine.shape, 0)
    angle = (places - starts(places)).astype(f32) * freq[0:1, :]
    cosine[...] = jnp.cos(angle)
    sine[...] = jnp.where(lax.broadcasted_iota(jnp.int32, sine.shape, 1) < HEAD_DIM // 2, -1.0, 1.0) * jnp.sin(angle)
    for e in range(experts):
        g_own[e : e + 1, :] = jnp.sum(jnp.where(ids[...] == e, shares_of[...], 0.0), axis=0, keepdims=True)
    wa_swap.wait_recv()
    wa_peer.start(in_place=True)
    x_all[u] = x[...]
    rows_of(wo_all, p.z, p.x, p.c, u)[...] = wo[:, pl.ds(pl.multiple_of(u * q_half, LANES), q_half)]
    for i in range(3):
        loads[i].wait()
        keeps[i].start()
    gws.start()
    for d in range(1, depth):
        for g in (wa_mine, wa_peer):
            g.hop(d)
            g.cross(d - 1)
        gws.hop(d)
        gws.cross(d - 1)
        if d == 1:
            wo_swap.wait_recv()
            wos.start(in_place=True)
            expert_out(0)
        else:
            wos.hop(d - 1)
    gws.cross(depth - 1)
    dys[0].start()
    expert_out(1)
    x_swap.wait_recv()
    for g in (wa_mine, wa_peer):
        g.cross(depth - 1)
    for g in (wa_mine, wa_peer):
        g.finish()
    stores[1].start()
    gain_rows[...] = w_all[:, q_half + kv_half :].astype(f32).T[:8, :]
    for m in range(2):
        xf = x_all[m].astype(f32)
        r1 = lax.rsqrt(jnp.mean(xf * xf, -1, keepdims=True) + EPS)
        normed[m * tok : (m + 1) * tok, :] = (xf * r1 * gain_rows[0:1, :]).astype(bf)
    raw[...] = mm(normed[...], w_all[:, : q_half + kv_half])

    def rope(values):
        return values * cosine[...] + pltpu.roll(values, HEAD_DIM // 2, 1) * sine[...]

    here = p.slot(p.z, p.x, p.c)
    kv[here, :, :HEAD_DIM] = rope(raw[:, q_half : q_half + HEAD_DIM]).astype(bf)
    kv[here, :, HEAD_DIM:] = raw[:, q_half + HEAD_DIM :].astype(bf)
    kvs.start(in_place=True)
    for h in range(heads):
        hs = slice(h * HEAD_DIM, (h + 1) * HEAD_DIM)
        turned = rope(raw[:, hs])
        q_rows[h * group : (h + 1) * group, :] = turned.astype(bf)
        qt[:, h * group : (h + 1) * group] = turned.T.astype(bf)
    for j in range(0, width, 256):
        normed_t[j : j + 256, :] = flip(normed[:, j : j + 256])
    top[...] = jnp.full(top.shape, NEG, f32)
    total[...] = jnp.zeros(total.shape, f32)
    ot[...] = jnp.zeros(ot.shape, f32)

    background = {}

    def at_step(s, act):
        background.setdefault(s, []).append(act)

    at_step(0, lambda: kvs.cross(0))
    at_step(0, lambda: kvs.hop(1))
    at_step(0, dys[1].start_z)
    at_step(1, lambda: wos.hop(3))
    at_step(1, lambda: dys[0].hop(1))
    at_step(2, lambda: kvs.cross(1))
    at_step(2, lambda: kvs.hop(2))
    at_step(2, dys[1].start_x)
    at_step(3, lambda: wos.cross(0))
    at_step(3, lambda: dys[1].hop(1))
    at_step(4, lambda: kvs.cross(2))
    at_step(4, lambda: kvs.hop(3))
    at_step(5, lambda: wos.cross(1))
    at_step(2, lambda: expert_in(0))
    at_step(2, lambda: expert_out(2))
    at_step(5, lambda: dys[0].hop(2))
    at_step(6, lambda: kvs.cross(3))
    at_step(6, lambda: dys[1].hop(2))
    at_step(7, lambda: wos.cross(2))
    at_step(7, lambda: wos.cross(3))

    def step(s, carry):
        d = s // 2
        zz = p.z - d
        xx = jnp.where(s % 2 == 0, p.x, 1 - p.x)
        j = p.slot(zz, xx, 0)

        pl.when(zz >= 0)(lambda: kvs.core(zz, xx))

        def work():
            pair = kv[pl.ds(j, 2)].reshape(2 * group, kv_half)
            k = pair[:, :HEAD_DIM]
            vt = flip(pair[:, HEAD_DIM:])
            bias = hidden_bias(j * group, blk * group, begin[0:1, :], 2 * group)
            at = [slice(h * group, (h + 1) * group) for h in range(heads)]
            sc = [mm(k, qt[:, hs]) * (scale * LOG2E) + bias for hs in at]
            old = [top[0:1, hs] for hs in at]
            new = [jnp.maximum(o_, jnp.max(s_, axis=0, keepdims=True)) for o_, s_ in zip(old, sc)]
            e = [jnp.exp2(s_ - n_) for s_, n_ in zip(sc, new)]
            part = [jnp.sum(e_, axis=0, keepdims=True) for e_ in e]
            mixed = [mm(vt, e_.astype(bf)) for e_ in e]
            for h, hs in enumerate(at):
                keep = jnp.exp2(old[h] - new[h])
                total[0:1, hs] = total[0:1, hs] * keep + part[h]
                ot[:, hs] = ot[:, hs] * keep + mixed[h]
                top[0:1, hs] = new[h]

        pl.when((zz >= 0) & (j <= blk))(work)
        for when, acts in background.items():
            pl.when(s == when)(lambda acts=acts: each(lambda act: act(), acts))
        return carry

    lax.fori_loop(0, 2 * depth, step, 0)

    wos.finish()
    stores[2].start()
    sums = total[0:1, :]
    lse[...] = jnp.broadcast_to(top[0:1, :] + jnp.log2(sums), lse.shape)
    for h in range(heads):
        at = slice(h * group, (h + 1) * group)
        mixed = ot[:, at] / sums[:, at]
        ot[:, at] = mixed
        o[:, h * HEAD_DIM : (h + 1) * HEAD_DIM] = mixed.T.astype(bf)

    wide = width // 3
    p_swaps = []
    for i in range(3):
        cb = i * wide
        acc[:, cb : cb + wide] = contract(o[...], wo_all[cb : cb + wide, :], 1, 1)
        theirs = pl.ds(pl.multiple_of((1 - u) * tok, tok), tok)
        p_out[i] = acc[theirs, cb : cb + wide].astype(bf)
        p_swaps.append(remote(p_out.at[i], p_in.at[i], ps(i), pr(i), p.other))
        p_swaps[i].start()
    each(lambda g: g.hop(3), dys)
    expert_in(1)
    for d in range(2):
        each(lambda g: g.cross(d), dys)
    mine = pl.ds(pl.multiple_of(u * tok, tok), tok)
    for i in range(3):
        p_swaps[i].wait_recv()
        acc[mine, i * wide : (i + 1) * wide] += p_in[i].astype(f32)
    branch = acc[mine, :]
    hidden = x[...].astype(f32) + branch
    hid[...] = hidden
    r2 = lax.rsqrt(jnp.mean(hidden * hidden, -1, keepdims=True) + EPS)
    b[...] = (hidden * r2 * gain_rows[1:2, :]).astype(bf)
    attn_sq[...] = jnp.broadcast_to(jnp.sum(branch * branch).reshape(1, 1), attn_sq.shape)
    for d in range(2, depth):
        each(lambda g: g.cross(d), dys)
    expert_in(2)
    kvs.finish(cores_taken=True)
    stores[0].start()
    each(lambda g: g.finish(), dys)
    gws.finish()
    wa_swap.wait_send()
    wo_swap.wait_send()
    x_swap.wait_send()
    for i in range(3):
        swaps[i].wait_send()
        keeps[i].wait()
        shares[i].wait()
        passes[i].wait()
        p_swaps[i].wait_send()
        stores[i].wait()


def front(docs, x, dy, gain_a, gain_m, wq, wkv, wo, ids, shares, experts, depth, scale, cid):
    f32, bf = jnp.float32, jnp.bfloat16
    shape = jax.ShapeDtypeStruct
    vmem = pl.BlockSpec(memory_space=pltpu.VMEM)
    hbm = pl.BlockSpec(memory_space=pl.ANY)
    V = pltpu.VMEM
    tok, width = x.shape
    group = 2 * tok
    q_half = wq.shape[1] // 2
    kv_half = 2 * HEAD_DIM
    wide = q_half + kv_half + LANES
    rows = q_half // HEAD_DIM * group
    rows_dev = wq.shape[0]
    expert = shape((2 * experts[0].shape[0], 2 * experts[0].shape[1]), bf)
    half = HEAD_DIM // 2
    freq = np.power(np.float32(ROPE_BASE), -np.arange(half, dtype=np.float32) * np.float32(2.0 / HEAD_DIM))
    freq = jnp.asarray(np.tile(freq.astype(np.float32), (8, 2)))
    return pl.pallas_call(
        functools.partial(front_kernel, depth, scale),
        out_shape=(
            shape((tok, width), bf),
            shape((tok, width), f32),
            shape((8, LANES), f32),
            shape((width, group), bf),
            shape((rows, HEAD_DIM), bf),
            shape((HEAD_DIM, rows), bf),
            shape((group, q_half), bf),
            shape((HEAD_DIM, rows), f32),
            shape((8, rows), f32),
            shape((8, width), f32),
            shape((2 * depth, 2 * depth, tok), f32),
            shape((2, tok, width), bf),
            shape((8, group), jnp.int32),
            shape((group, HEAD_DIM), f32),
            shape((group, HEAD_DIM), f32),
            shape((4 * depth, group, kv_half), bf),
            shape((width, wide), bf),
            shape((width, q_half), bf),
            shape((2 * depth, tok, width), bf),
            expert,
            expert,
            expert,
        ),
        in_specs=[pl.BlockSpec(memory_space=pltpu.SMEM)] + [vmem] * 10 + [hbm] * 3,
        out_specs=tuple([vmem] * 15 + [hbm] * 7),
        scratch_shapes=[
            V((4 * depth, group, kv_half), bf),
            V((width, wide), bf),
            V((width, q_half), bf),
            V((3,) + experts[0].shape, bf),
            V((LANES, LANES), f32),
            V((2 * depth, tok), f32),
            V((2, rows_dev, wide), bf),
            V((group, width), bf),
            V((group, q_half + kv_half), f32),
            V((8, rows), f32),
            V((8, rows), f32),
            V((group, width), f32),
            V((3, tok, width // 3), bf),
            V((3, tok, width // 3), bf),
            pltpu.SemaphoreType.DMA((8 * 16 * depth,)),
        ],
        compiler_params=pltpu.CompilerParams(
            collective_id=cid, has_side_effects=True, vmem_limit_bytes=56 * 2**20
        ),
        name="front",
    )(docs, x, dy, gain_a[None, :], gain_m[None, :], wq, wkv, wo, ids, shares, freq, *experts)


def experts_kernel(
    depth, b, dy_own, g_all, hid, gain_rows, dy_far, g_far, u_far, d_far,
    dh, dhr, gm, z_sums, z_far, eg_far,
    dy_all, wg, wu, wd, z_p, eg, z_rx, b_all, act, dgate, dup, dyr, db_p, rx, rz, db, turned, sems,
):
    f32, bf = jnp.float32, jnp.bfloat16
    p = Place(depth)
    p.greet()
    wires = Wires(sems)
    tok, width = b.shape
    hidden_units = wg.shape[1]
    expert = p.blk // 2
    pair = 2 * tok
    pieces = 2
    piece = tok // pieces

    rows = [
        Gather(
            p, wires, b.at[pl.ds(k * piece, piece)],
            lambda z, x, c, k=k: b_all.at[pl.ds(pl.multiple_of((z * 2 + x) * tok + k * piece, piece), piece)],
            False, chain=True,
        )
        for k in range(pieces)
    ]

    def cut(ref, k):
        return ref.at[pl.ds(k * piece, piece)]

    sums = Scatter(
        p, wires,
        lambda zz, xx, k: cut(db_p.at[zz * 2 + xx], k),
        lambda k: cut(db, k),
        lambda zz, k: cut(rx.at[zz], k),
        lambda slot, k: cut(rz.at[slot], k),
        pieces,
    )
    ls = wires.take(4)
    loads = [
        pltpu.make_async_copy(r, v, ls(i)) for i, (r, v) in enumerate(((dy_far, dy_all), (g_far, wg), (u_far, wu), (d_far, wd)))
    ]
    os_ = wires.take(3)
    stores = [
        pltpu.make_async_copy(v, r, os_(i))
        for i, (v, r) in enumerate(((z_p, z_far), (eg.at[pl.ds(0, 2)], eg_far.at[pl.ds(0, 2)]), (eg.at[2], eg_far.at[2])))
    ]
    each(lambda load: load.start(), loads)
    each(lambda g: g.start(), rows)
    spread = lax.broadcasted_iota(jnp.int32, (tok, 8), 1)

    def weight(slot):
        return jnp.sum(jnp.where(spread == expert, g_all[slot].T, 0.0), axis=1, keepdims=True)

    def nth(i):
        inner = jnp.where(i == 0, 1, jnp.where(i == 1, 0, i))
        other = jnp.where(i == 0, 2, jnp.where(i == 1, 1, jnp.where(i == 2, 3, 0)))
        return jnp.where(p.z == 0, i, jnp.where(p.z == depth - 1, depth - 1 - i, jnp.where(p.z == 1, inner, other)))

    def block(i, carry):
        for d in range(1, depth):
            pl.when(i == d - 1)(lambda d=d: each(lambda g: g.hop(d), rows))
        each(lambda g: g.crossed(nth(i)), rows)
        pl.when(i == 0)(lambda: each(lambda load: load.wait(), loads))
        zz = nth(i)
        at = pl.ds(pl.multiple_of(zz * pair, pair), pair)
        for xx in range(2):
            half = pl.ds(pl.multiple_of(zz * pair + xx * tok, tok), tok)
            dyr[half, :] = (weight(zz * 2 + xx) * dy_all[zz * 2 + xx].astype(f32)).astype(bf)
        for cb in range(0, hidden_units, 256):
            cs = slice(cb, cb + 256)
            gate = mm(b_all[at, :], wg[:, cs])
            up = mm(b_all[at, :], wu[:, cs])
            sig = jax.nn.sigmoid(gate)
            act[at, cs] = (gate * sig * up).astype(bf)
            dact = mm(dyr[at, :], wd[:, cs])
            dgate[at, cs] = (dact * up * sig * (1.0 + gate * (1.0 - sig))).astype(bf)
            dup[at, cs] = (dact * gate * sig).astype(bf)
        for cb in range(0, width, 512):
            cs = slice(cb, cb + 512)
            part = contract(dgate[at, :], wg[cs, :], 1, 1) + contract(dup[at, :], wu[cs, :], 1, 1)
            for xx in range(2):
                db_p[zz * 2 + xx, :, cs] = part[xx * tok : (xx + 1) * tok, :].astype(bf)
        pl.when(i == depth - 2)(lambda: sums.send(nth(2)))
        pl.when(i == depth - 1)(lambda: each(lambda n: sums.send(nth(n)), (3, 1)))
        for cb in range(0, width, 512):
            cs = slice(cb, cb + 512)
            part = contract(act[at, :], wd[cs, :], 1, 1)
            for xx in range(2):
                z_p[zz * 2 + xx, :, cs] = (
                    weight(zz * 2 + xx) * part[xx * tok : (xx + 1) * tok, :]
                ).astype(bf)
        return carry

    lax.fori_loop(0, depth, block, 0)

    stores[0].start()
    zs_, zr_ = wires.take(2 * len(EARLY)), wires.take(2 * len(EARLY))

    def z_send(n, k):
        return remote(
            cut(z_p.at[EARLY[n] * 2 + 1 - p.x], k), cut(z_rx.at[n], k), zs_(2 * n + k), zr_(2 * n + k), p.across
        )

    z_pieces = [(n, k) for n in range(len(EARLY)) for k in range(pieces)]

    wide = 256

    def grads(n):
        cs = slice(n * wide, (n + 1) * wide)
        turned[...] = flip(b_all[:, cs])
        eg[0, cs, :] = mm(turned[...], dgate[...]).astype(bf)
        eg[1, cs, :] = mm(turned[...], dup[...]).astype(bf)

    def grads_down(n):
        cs = slice(n * wide, (n + 1) * wide)
        turned[...] = flip(dyr[:, cs])
        eg[2, cs, :] = mm(turned[...], act[...]).astype(bf)

    work = [lambda n=n: grads(n) for n in range(width // wide)]
    work += [lambda n=n: grads_down(n) for n in range(width // wide)]
    events = []
    for n in (2, 3, 1, 0):
        for k in range(pieces):
            events.append(lambda n=n, k=k: sums.take(nth(n), k))
        if n == 2:
            events.append(lambda: sums.send(nth(0)))
        if n == 1:
            events.append(lambda: each(lambda piece_: z_send(*piece_).start(), z_pieces[:2]))
    done = 0
    for t, event in enumerate(events):
        while done < len(work) and done * len(events) <= t * len(work):
            work[done]()
            done += 1
        event()
    for act_ in work[done:]:
        act_()
    stores[1].start()
    stores[2].start()
    each(lambda piece_: z_send(*piece_).start(), z_pieces[2:])
    sums.finish()
    each(lambda g: g.finish(), rows)

    h = hid[...]
    r2 = lax.rsqrt(jnp.mean(h * h, -1, keepdims=True) + EPS)
    weighted = db[...] * gain_rows[1:2, :]
    inner = jnp.mean(weighted * h, -1, keepdims=True)
    total = dy_own[...].astype(f32) + r2 * weighted - h * (r2 * r2 * r2 * inner)
    dh[...] = total
    dhr[...] = total.astype(bf)
    column = jnp.sum((db[...] * h * r2).T, axis=1, keepdims=True)
    lane = lax.broadcasted_iota(jnp.int32, (width, LANES), 1)
    gm[...] = jnp.where(lane == 1, column, 0.0)
    for n, zz in enumerate(EARLY):
        for k in range(pieces):
            z_send(n, k).wait()
        z_sums[n] = (z_p[zz * 2 + p.x].astype(f32) + z_rx[n].astype(f32)).astype(bf)
    each(lambda store: store.wait(), stores)


def run_experts(b, dy_own, dy_all, g_all, weights, hid, gain_rows, depth, cid):
    f32, bf = jnp.float32, jnp.bfloat16
    shape = jax.ShapeDtypeStruct
    vmem = pl.BlockSpec(memory_space=pltpu.VMEM)
    hbm = pl.BlockSpec(memory_space=pl.ANY)
    V = pltpu.VMEM
    tok, width = b.shape
    units = weights[0].shape[1]
    rows = 2 * depth * tok
    return pl.pallas_call(
        functools.partial(experts_kernel, depth),
        out_shape=(
            shape((tok, width), f32),
            shape((tok, width), bf),
            shape((width, LANES), f32),
            shape((len(EARLY), tok, width), bf),
            shape((2 * depth, tok, width), bf),
            shape((3, width, units), bf),
        ),
        in_specs=[vmem] * 5 + [hbm] * 4,
        out_specs=tuple([vmem] * 4 + [hbm] * 2),
        scratch_shapes=[
            V((2 * depth, tok, width), bf),
            V((width, units), bf),
            V((width, units), bf),
            V((width, units), bf),
            V((2 * depth, tok, width), bf),
            V((3, width, units), bf),
            V((len(EARLY), tok, width), bf),
            V((rows, width), bf),
            V((rows, units), bf),
            V((rows, units), bf),
            V((rows, units), bf),
            V((rows, width), bf),
            V((2 * depth, tok, width), bf),
            V((depth, tok, width), bf),
            V((depth, tok, width), bf),
            V((tok, width), f32),
            V((256, rows), bf),
            pltpu.SemaphoreType.DMA((2 * 5 * depth + 8 * depth + 8 + 4 * len(EARLY),)),
        ],
        compiler_params=pltpu.CompilerParams(
            collective_id=cid, has_side_effects=True, vmem_limit_bytes=58 * 2**20
        ),
        name="experts",
    )(b, dy_own, g_all, hid, gain_rows, dy_all, *weights)


def closing_kernel(
    depth, scale, attn_sq, dhr, gain, begin, lse, cosine, sine,
    z_sums, zp_far, wo_far, ot_far, o_far, q_far, qt_far, kv_far, w_far, at_far, x_far, hid_far, dh_far, gm_far, eg,
    out, gin, gq, go, gkv, gg, f0, f1, f2, rms,
    zp, wo, ot, o, q_rows, qt, kv, w, at, x_all, hid, dh, gm,
    dhr_all, dot_, dqt, delta, dkv, do_rows, dq, att, acc,
    z_sum, z_rx, z_rz, go_p, go_rc, go_rx, go_rz, kv_sum, kv_rc, kv_rx, kv_rz,
    gq_p, gq_rc, gq_rx, gq_rz, gk_p, gk_sum, gk_rc, gk_rx, gk_rz,
    e_own, e_core, e_low, e_peer, da_out, da_in, t_out, t_in, sq, square, sems,
):
    f32, bf = jnp.float32, jnp.bfloat16
    p = Place(depth)
    p.greet(sibling=True, other=True)
    wires = Wires(sems)
    u, blk = p.u, p.blk
    tok = dhr.shape[0]
    group, q_half = o.shape
    heads = q_half // HEAD_DIM
    kv_half = 2 * HEAD_DIM
    blocks = kv.shape[0]
    rows_blk = gq.shape[0]

    cols = f0.shape[1]
    rows_e = f0.shape[0]
    es, er, el, ps, pr = (wires.take(1)(0) for _ in range(5))

    def e_cols(core):
        return eg.at[:, :, pl.ds(pl.multiple_of(core * cols, LANES), cols)]

    def e_rows(member):
        return pl.ds(pl.multiple_of(member * rows_e, rows_e), rows_e)

    e_trade = remote(e_cols(1 - p.c), e_core, es, er, p.sibling)
    e_keep = [pltpu.make_async_copy(e_cols(p.c).at[i], e_own, el) for i in range(3)]
    e_swap = remote(e_low, e_peer, ps, pr, p.other)

    def e_join():
        e_trade.wait_recv()
        theirs, mine = e_rows(1 - u), e_rows(u)
        for i in range(3):
            e_keep[i].wait()
            e_low[i] = (e_own[theirs, :].astype(f32) + e_core[i, theirs, :].astype(f32)).astype(bf)
            (f0, f1, f2)[i][...] = e_own[mine, :].astype(f32) + e_core[i, mine, :].astype(f32)
            if i < 2:
                e_keep[i + 1].start()
        e_swap.start()

    def e_done():
        e_swap.wait_recv()
        for i in range(3):
            (f0, f1, f2)[i][...] += e_peer[i].astype(f32)

    ds, dr = wires.take(1)(0), wires.take(1)(0)
    swap = remote(dhr, dhr_all.at[u], ds, dr, p.other)

    pieces = 2
    z_rows = tok // pieces

    def cut(ref, k):
        return ref.at[pl.ds(k * z_rows, z_rows)]

    zs = Scatter(
        p, wires,
        lambda zz, xx, k: cut(zp.at[zz * 2 + xx], k),
        lambda k: cut(z_sum, k),
        lambda zz, k: cut(z_rx.at[zz], k),
        lambda slot, k: cut(z_rz.at[slot], k),
        pieces, ready=EARLY,
    )
    gos = CoreScatter(p, wires, go_p, go_rc, go, go_rx, go_rz)
    kvs = CoreScatter(p, wires, dkv, kv_rc, kv_sum, kv_rx, kv_rz, down_only=True)
    gqs = CoreScatter(p, wires, gq_p, gq_rc, gq, gq_rx, gq_rz)
    gks = CoreScatter(p, wires, gk_p, gk_rc, gk_sum, gk_rx, gk_rz)
    qs, qr = wires.take(3 + depth), wires.take(3 + depth)
    sq_here = sq.at[p.z, p.x, u, p.c]
    sq_core = remote(sq_here, sq_here, qs(0), qr(0), p.sibling)
    sq_other = remote(sq.at[p.z, p.x, u], sq.at[p.z, p.x, u], qs(1), qr(1), p.other)
    sq_across = remote(sq.at[p.z, p.x], sq.at[p.z, p.x], qs(2), qr(2), p.across)

    def sq_along(z, to):
        return remote(sq.at[z], sq.at[z], qs(3 + to), qr(3 + z), p.along(to))

    ls = wires.take(13)
    loads = [
        pltpu.make_async_copy(r, v, ls(i))
        for i, (r, v) in enumerate(
            (
                (zp_far, zp), (wo_far, wo), (ot_far, ot), (o_far, o), (q_far, q_rows), (qt_far, qt), (kv_far, kv),
                (w_far, w), (at_far, at), (x_far, x_all), (hid_far, hid), (dh_far, dh), (gm_far, gm),
            )
        )
    ]
    zl = wires.take(len(EARLY))
    z_loads = [pltpu.make_async_copy(z_sums.at[n], z_rx.at[zz], zl(n)) for n, zz in enumerate(EARLY)]
    swap.start()
    each(lambda load: load.start(), z_loads)
    each(lambda load: load.start(), loads)
    e_trade.start()
    e_keep[0].start()
    loads[0].wait()
    ahead = 2
    for t in range(ahead):
        zs.begin(t)

    each(lambda load: load.wait(), z_loads)
    zs.forward()
    dqt[...] = jnp.zeros(dqt.shape, f32)
    dkv[...] = jnp.zeros(dkv.shape, bf)
    dhr_all[u] = dhr[...]
    e_join()
    zs.land(0)
    zs.begin(ahead)
    each(lambda load: load.wait(), loads[1:])
    swap.wait_recv()

    for m in range(2):
        part = mm(dhr_all[m], wo[...]).astype(bf)
        for h in range(heads):
            do_rows[h * group + m * tok : h * group + (m + 1) * tok, :] = part[:, h * HEAD_DIM : (h + 1) * HEAD_DIM]
    for h in range(heads):
        hs = slice(h * group, (h + 1) * group)
        part = do_rows[hs, :]
        turned = part.astype(f32).T
        dot_[:, hs] = turned.astype(bf)
        delta[0:1, hs] = jnp.sum(turned * ot[:, hs], axis=0, keepdims=True)

    def spread_rows(payload, turned, right, cols=None):
        some = 4

        def rows(i, carry):
            at_rows = pl.ds(pl.multiple_of(i * some * rows_blk, some * rows_blk), some * rows_blk)
            part = mm(turned[at_rows, :], right).astype(bf)
            for n in range(some):
                piece = part[n * rows_blk : (n + 1) * rows_blk, :]
                if cols is None:
                    payload[i * 2 + n // 2, n % 2] = piece
                else:
                    payload[i * 2 + n // 2, n % 2, :, :cols] = piece
            return carry

        lax.fori_loop(0, blocks // some, rows, 0)

    for m in range(2):
        att[:, m * tok : (m + 1) * tok] = flip(dhr_all[m])

    spread_rows(go_p, att, o[...])
    gos.trade()

    background = {}

    def at_tile(j, act):
        background.setdefault(j, []).append(act)

    def z_step(t):
        zs.land(t)
        zs.begin(t + ahead)

    for t in range(1, len(zs.items)):
        at_tile((0, 0, 2, 4, 6, 9, 12, 15)[t], lambda t=t: z_step(t))
    for t in range(depth):
        at_tile((5, 8, 11, 14)[t], lambda t=t: gos.join(t))
    for t in range(depth - 1):
        last = 4 * t + 3
        at_tile(last, lambda t=t: kvs.trade(t))
        at_tile(last + 1, lambda t=t: kvs.join(t))
        if t < depth - 2:
            at_tile(last + 6, lambda t=t: kvs.land(t))

    def tile(j, carry):
        def work():
            k = kv[j, :, :HEAD_DIM]
            v = kv[j, :, HEAD_DIM:]
            kt = flip(k)
            bias = hidden_bias(j * group, blk * group, begin[0:1, :], group)
            at_ = [slice(h * group, (h + 1) * group) for h in range(heads)]
            sc = [mm(k, qt[:, hs]) * (scale * LOG2E) + bias for hs in at_]
            dp = [mm(v, dot_[:, hs]) for hs in at_]
            e = [jnp.exp2(s_ - lse[0:1, hs]) for s_, hs in zip(sc, at_)]
            g = [(e_ * (d_ - delta[0:1, hs])).astype(bf) for e_, d_, hs in zip(e, dp, at_)]
            wide_g = jnp.concatenate(g, 1)
            dk = mm(wide_g, q_rows[...])
            dv = mm(jnp.concatenate([e_.astype(bf) for e_ in e], 1), do_rows[...])
            dqt[...] += mm(kt, wide_g)
            dkv[j // 2, j % 2, :, :HEAD_DIM] = (dk * scale).astype(bf)
            dkv[j // 2, j % 2, :, HEAD_DIM:] = dv.astype(bf)

        pl.when(j <= blk)(work)
        for when, acts in background.items():
            pl.when(j == when)(lambda acts=acts: each(lambda act: act(), acts))
        return carry

    lax.fori_loop(0, blocks, tile, 0)

    kvs.trade(depth - 1)

    def back_turn(values):
        return values * cosine[...] - pltpu.roll(values, HEAD_DIM // 2, 1) * sine[...]

    for h in range(heads):
        hs = slice(h * group, (h + 1) * group)
        cs = slice(h * HEAD_DIM, (h + 1) * HEAD_DIM)
        dq[:, cs] = back_turn((dqt[:, hs] * scale).T.astype(bf).astype(f32)).astype(bf)
    kvs.join(depth - 1)

    spread_rows(gq_p, at, dq[...])
    gqs.trade()
    kvs.land(depth - 2)
    gqs.join(0)
    gqs.join(1)
    for m in range(2):
        for cb in range(0, D, 512):
            acc[m * tok : (m + 1) * tok, cb : cb + 512] = contract(
                dq[m * tok : (m + 1) * tok, :], w[cb : cb + 512, :q_half], 1, 1
            )
    kvs.land(depth - 1)
    kvs.release()
    kvs.finish()
    kv_low = kv_sum[...].astype(bf).astype(f32)
    kv_pre = jnp.concatenate([back_turn(kv_low[:, :HEAD_DIM]).astype(bf), kv_low[:, HEAD_DIM:].astype(bf)], 1)

    da_s, da_r = wires.take(3), wires.take(3)
    wide = D // 3
    da_swaps = []
    for i in range(3):
        cb = i * wide
        part = contract(kv_pre, w[cb : cb + wide, q_half : q_half + kv_half], 1, 1)
        acc[:, cb : cb + wide] += part
        theirs = pl.ds(pl.multiple_of((1 - u) * tok, tok), tok)
        da_out[i] = acc[theirs, cb : cb + wide].astype(bf)
        da_swaps.append(remote(da_out.at[i], da_in.at[i], da_s(i), da_r(i), p.other))
        da_swaps[i].start()

    column = jnp.zeros((D, 1), f32)
    for m in range(2):
        xf = x_all[m].astype(f32)
        r1 = lax.rsqrt(jnp.mean(xf * xf, -1, keepdims=True) + EPS)
        terms = acc[m * tok : (m + 1) * tok, :] * xf * r1
        column = column + jnp.sum(terms.T, axis=1, keepdims=True)
    lane = lax.broadcasted_iota(jnp.int32, (D, LANES), 1)
    gain_cols = (jnp.where(lane == 0, column, 0.0) + gm[...]).astype(bf)
    for i in range(blocks):
        gk_p[i // 2, i % 2, :, kv_half:] = gain_cols[i * rows_blk : (i + 1) * rows_blk, :]

    spread_rows(gk_p, at, kv_pre, kv_half)
    gks.trade()
    for t in range(depth):
        gks.join(t)
    for t in range(2, depth):
        gqs.join(t)
    gqs.release()

    for t in range(depth):
        gos.land(t)
    zs.finish()
    result = hid[...] + z_sum[...]
    out[...] = result.astype(bf)
    spread = lax.broadcasted_iota(jnp.int32, (8, LANES), 1)
    z_sq = jnp.sum(z_sum[...] * z_sum[...])
    r_sq = jnp.sum(result * result)
    sq_here[...] = jnp.where(
        spread == 0, attn_sq[...], jnp.where(spread == 1, z_sq, jnp.where(spread == 2, r_sq, 0.0))
    )
    sq_core.start()
    gks.land(0)
    sq_core.wait_recv()
    sq_other.start()
    gks.land(1)
    gks.land(2)
    sq_other.wait_recv()
    sq_across.start()
    gks.land(3)
    for t in range(2):
        gqs.land(t)
    sq_across.wait_recv()
    for d in range(1, depth):
        pl.when(p.z >= d)(lambda d=d: sq_along(p.z, p.z - d).start())
        pl.when(p.z + d < depth)(lambda d=d: sq_along(p.z, p.z + d).start())

    mine = pl.ds(pl.multiple_of(u * tok, tok), tok)
    for i in range(3):
        da_swaps[i].wait_recv()
        acc[mine, i * wide : (i + 1) * wide] += da_in[i].astype(f32)
    da = acc[mine, :]
    xf = x_all[u].astype(f32)
    r1 = lax.rsqrt(jnp.mean(xf * xf, -1, keepdims=True) + EPS)
    weighted = da * gain[0:1, :]
    inner = jnp.mean(weighted * xf, -1, keepdims=True)
    gin[...] = dh[...] + r1 * weighted - xf * (r1 * r1 * r1 * inner)
    gks.release()
    gks.finish()
    rows_dev = gkv.shape[0]
    theirs = pl.ds(pl.multiple_of((1 - u) * rows_dev, rows_dev), rows_dev)
    own = pl.ds(pl.multiple_of(u * rows_dev, rows_dev), rows_dev)
    t_out[...] = gk_sum[theirs, :]
    ts, tr = wires.take(1)(0), wires.take(1)(0)
    t_swap = remote(t_out, t_in, ts, tr, p.other)
    t_swap.start()
    for t in range(2, depth):
        gqs.land(t)
    e_done()
    gos.release()
    gos.finish()
    gqs.finish()
    t_swap.wait_recv()
    for part in range(2):
        here = slice(part * HEAD_DIM, (part + 1) * HEAD_DIM)
        base = part * kv_half
        gkv[:, pl.ds(pl.multiple_of(base + u * HEAD_DIM, LANES), HEAD_DIM)] = gk_sum[own, here]
        gkv[:, pl.ds(pl.multiple_of(base + (1 - u) * HEAD_DIM, LANES), HEAD_DIM)] = t_in[:, here]
    square[...] = jnp.zeros(square.shape, f32)
    square[:rows_dev, :] = gk_sum[own, kv_half:] + t_in[:, kv_half:]
    gg[...] = square[...].T[:8, :]
    sq_core.wait_send()
    sq_other.wait_send()
    sq_across.wait_send()
    for z in range(depth):
        pl.when(p.z != z)(lambda z=z: sq_along(z, z).wait_recv())
        pl.when(p.z != z)(lambda z=z: sq_along(p.z, z).wait_send())
    squares = jnp.zeros((8, LANES), f32)
    for z in range(depth):
        for n in range(8):
            squares = squares + sq[z, n // 4, n // 2 % 2, n % 2]
    rms[...] = jnp.sqrt(squares / (8 * depth * tok * D))
    t_swap.wait_send()
    swap.wait_send()
    e_trade.wait_send()
    e_swap.wait_send()
    for i in range(3):
        da_swaps[i].wait_send()


def closing(attn_sq, dhr, gain, begin, lse, cosine, sine, z_sums, large, eg, depth, scale, cid):
    f32, bf = jnp.float32, jnp.bfloat16
    tok, width = dhr.shape
    group, q_half = large[3].shape
    blocks = large[6].shape[0]
    kv_block = large[6].shape[1:]
    rows_blk = width // blocks
    rows_e, cols = eg.shape[1] // 2, eg.shape[2] // 2
    kv_half = 2 * HEAD_DIM
    shape = jax.ShapeDtypeStruct
    vmem = pl.BlockSpec(memory_space=pltpu.VMEM)
    hbm = pl.BlockSpec(memory_space=pl.ANY)
    V = pltpu.VMEM

    def buffers(block):
        return [
            V((blocks // 2,) + block, bf),
            V((depth,) + block, bf),
            V((depth,) + block, bf),
        ]

    grad = shape((rows_e, cols), f32)
    rows = q_half // HEAD_DIM * group
    return pl.pallas_call(
        functools.partial(closing_kernel, depth, scale),
        out_shape=(
            shape((tok, width), bf),
            shape((tok, width), f32),
            shape((rows_blk, q_half), f32),
            shape((rows_blk, q_half), f32),
            shape((rows_blk // 2, 2 * kv_half), f32),
            shape((8, LANES), f32),
            grad,
            grad,
            grad,
            shape((8, LANES), f32),
        ),
        in_specs=[vmem] * 7 + [hbm] * 15,
        out_specs=tuple([vmem] * 10),
        scratch_shapes=[V(array.shape, array.dtype) for array in large]
        + [
            V((2, tok, width), bf),
            V((HEAD_DIM, rows), bf),
            V((HEAD_DIM, rows), f32),
            V((8, rows), f32),
            V((blocks // 2, 2) + kv_block, bf),
            V((rows, HEAD_DIM), bf),
            V((group, q_half), bf),
            V((width, group), bf),
            V((group, width), f32),
            V((tok, width), f32),
            V((depth, tok, width), bf),
            V((depth, tok, width), bf),
            V((blocks // 2, 2, rows_blk, q_half), bf),
        ]
        + buffers((rows_blk, q_half))
        + [V((group, kv_half), f32)]
        + buffers((group, kv_half))
        + [V((blocks // 2, 2, rows_blk, q_half), bf)]
        + buffers((rows_blk, q_half))
        + [V((blocks // 2, 2, rows_blk, kv_half + LANES), bf), V((rows_blk, kv_half + LANES), f32)]
        + buffers((rows_blk, kv_half + LANES))
        + [
            V((2 * rows_e, cols), bf),
            V((3, 2 * rows_e, cols), bf),
            V((3, rows_e, cols), bf),
            V((3, rows_e, cols), bf),
            V((3, tok, width // 3), bf),
            V((3, tok, width // 3), bf),
            V((rows_blk // 2, kv_half + LANES), f32),
            V((rows_blk // 2, kv_half + LANES), f32),
            V((depth, 2, 2, 2, 8, LANES), f32),
            V((LANES, LANES), f32),
            pltpu.SemaphoreType.DMA((320,)),
        ],
        compiler_params=pltpu.CompilerParams(
            collective_id=cid, has_side_effects=True, vmem_limit_bytes=60 * 2**20
        ),
        name="closing",
    )(attn_sq, dhr, gain, begin, lse, cosine, sine, z_sums, *large, eg)


def deliver_kernel(count, gains, rms, *refs):
    ins, (gain_a, gain_m, rms_out) = refs[:count], refs[count : count + 3]
    outs, held, sems = refs[count + 3 : 2 * count + 3], refs[2 * count + 3 : 3 * count + 3], refs[3 * count + 3]
    loads = [pltpu.make_async_copy(ins[i], held[i], sems.at[i]) for i in range(count)]
    stores = [pltpu.make_async_copy(held[i], outs[i], sems.at[count + i]) for i in range(count)]
    each(lambda load: load.start(), loads)
    gain_a[...] = gains[0:1, : gain_a.shape[1]]
    gain_m[...] = gains[1:2, : gain_m.shape[1]]
    rms_out[...] = rms[0:1, : rms_out.shape[1]]
    for load, store in zip(loads, stores):
        load.wait()
        store.start()
    each(lambda store: store.wait(), stores)


def deliver(gains, rms, arrays, rows):
    count = len(arrays)
    hbm = pl.BlockSpec(memory_space=pl.ANY)
    vmem = pl.BlockSpec(memory_space=pltpu.VMEM)
    small = [jax.ShapeDtypeStruct((1, n), jnp.float32) for n in (rows, rows, 3)]
    return pl.pallas_call(
        functools.partial(deliver_kernel, count),
        out_shape=tuple(small + [jax.ShapeDtypeStruct(a.shape, a.dtype) for a in arrays]),
        in_specs=[vmem] * 2 + [hbm] * count,
        out_specs=tuple([vmem] * 3 + [hbm] * count),
        scratch_shapes=[pltpu.VMEM(a.shape, a.dtype) for a in arrays] + [pltpu.SemaphoreType.DMA((2 * count,))],
        compiler_params=pltpu.CompilerParams(vmem_limit_bytes=60 * 2**20),
        name="deliver",
    )(gains, rms, *arrays)


def planned(
    layer_input,
    grad_output,
    gain_attn,
    gain_moe,
    w_query,
    w_keyval,
    w_out,
    w_gate,
    w_up,
    w_down,
    gate_weights,
    expert_ids,
    doc_starts,
):
    depth = lax.axis_size("blk") // 4
    scale = 1.0 / math.sqrt(HEAD_DIM)
    (
        normed_m, hidden, attn_sq, normed_t, query_rows, query_t, mixed, mixed_t, lse, gain_rows, g_all, inputs,
        begin_rows, cosine, sine, kv_all, w_all, out_w, dy_all, gate_w, up_w, down_w,
    ) = front(
        doc_starts, layer_input, grad_output, gain_attn, gain_moe, w_query, w_keyval, w_out, expert_ids.T, gate_weights.T,
        (w_gate, w_up, w_down), depth, scale, 1,
    )
    grad_hidden, grad_hidden_low, gain_terms, z_sums, z_part, expert_grads = run_experts(
        normed_m, grad_output, dy_all, g_all, (gate_w, up_w, down_w), hidden, gain_rows, depth, 2
    )
    large = (
        z_part, out_w, mixed_t, mixed, query_rows, query_t, kv_all, w_all, normed_t, inputs, hidden, grad_hidden, gain_terms
    )
    results = closing(
        attn_sq, grad_hidden_low, gain_rows, begin_rows, lse, cosine, sine, z_sums, large, expert_grads, depth, scale, 3
    )
    (
        gain_a, gain_m, rms, layer_output, grad_input, part_query, part_out, part_keyval, grad_gate, grad_up, grad_down
    ) = deliver(results[5], results[9], results[:5] + results[6:9], gain_attn.shape[0])
    return (
        layer_output,
        grad_input,
        gain_a.reshape(-1),
        gain_m.reshape(-1),
        part_query,
        part_keyval,
        part_out,
        grad_gate,
        grad_up,
        grad_down,
        rms.reshape(-1),
    )


def solution(mesh):
    in_specs = (
        P(("blk", "ulysses"), None),
        P(("blk", "ulysses"), None),
        P(("blk", "ulysses")),
        P(("blk", "ulysses")),
        P(("blk", "ulysses"), None),
        P(("blk", "ulysses"), None),
        P(("blk", "ulysses"), None),
        P("ulysses", "blk"),
        P("ulysses", "blk"),
        P("ulysses", "blk"),
        P(("blk", "ulysses"), None),
        P(("blk", "ulysses"), None),
        P(),
    )
    out_specs = (
        P(("blk", "ulysses"), None),
        P(("blk", "ulysses"), None),
        P(("blk", "ulysses")),
        P(("blk", "ulysses")),
        P("blk", "ulysses"),
        P(("blk", "ulysses"), None),
        P("blk", "ulysses"),
        P("ulysses", "blk"),
        P("ulysses", "blk"),
        P("ulysses", "blk"),
        P(),
    )
    blocks, members = mesh.shape["blk"], mesh.shape["ulysses"]
    body = planned if blocks == 16 and members == KV_HEADS else local
    return jax.shard_map(body, mesh=mesh, in_specs=in_specs, out_specs=out_specs, check_vma=False)
```

```python
import functools
import math

import jax
import jax.numpy as jnp
import numpy as np
from jax import lax
from jax.experimental import pallas as pl
from jax.experimental.pallas import tpu as pltpu
from jax.sharding import PartitionSpec as P

D = 1536
HEADS = 12
KV_HEADS = 2
HEAD_DIM = 128
TOP = 4


EPS = 1e-06
ROPE_BASE = 1000000.0
NEG = -1e30
EARLY = (0,)


def rotate(values, positions, sign):
    half = values.shape[-1] // 2
    freq = ROPE_BASE ** (-jnp.arange(half, dtype=jnp.float32) * 2.0 / values.shape[-1])
    angle = positions.astype(jnp.float32)[:, None] * freq[None, :]
    cosine = jnp.cos(angle)[:, None, :]
    sine = sign * jnp.sin(angle)[:, None, :]
    first = values[..., :half]
    second = values[..., half:]
    return jnp.concatenate([first * cosine - second * sine, second * cosine + first * sine], -1)


def doc_begin(positions, doc_starts):
    return jnp.max(
        jnp.where(doc_starts[None, :] <= positions[:, None], doc_starts[None, :], 0), axis=1
    )


def norm_back(values, factor, gain, grad):
    weighted = grad * gain
    inner = jnp.mean(weighted * values, -1, keepdims=True)
    return factor * weighted - values * factor * factor * factor * inner


def visible_mask(q_pos, q_begin, k_pos):
    return (k_pos[None, :] >= q_begin[:, None]) & (k_pos[None, :] <= q_pos[:, None])


def split_blocks(array):
    rows = array.shape[0]
    size = min(rows, 512)
    return (array.reshape((rows // size, size) + array.shape[1:]), size)


def contract(left, right, left_dim, right_dim):
    return lax.dot_general(
        left, right, (((left_dim,), (right_dim,)), ((), ())), preferred_element_type=jnp.float32
    )


def reorder_rows(array, outer, inner):
    rows = array.shape[0]
    shaped = array.reshape((outer, inner, rows // (outer * inner)) + array.shape[1:])
    return jnp.swapaxes(shaped, 0, 1).reshape(array.shape)


def route(payload):
    return lax.all_to_all(payload, "blk", split_axis=0, concat_axis=0, tiled=True)


def backward_block(queries, grads, lse, delta, q_pos, q_begin, keys, values, k_start, scale):
    k_pos = k_start + jnp.arange(keys.shape[0], dtype=jnp.int32)
    visible = visible_mask(q_pos, q_begin, k_pos)[None]
    scores = jnp.einsum("qhd,kd->hqk", queries, keys, preferred_element_type=jnp.float32) * scale
    probs = jnp.where(visible, jnp.exp(scores - lse[:, :, None]), 0.0)
    probs_low = probs.astype(jnp.bfloat16)
    grad_probs = jnp.einsum("qhd,kd->hqk", grads, values, preferred_element_type=jnp.float32)
    grad_scores = (probs * (grad_probs - delta[:, :, None])).astype(jnp.bfloat16)
    part_q = (
        jnp.einsum("hqk,kd->qhd", grad_scores, keys, preferred_element_type=jnp.float32) * scale
    )
    part_k = (
        jnp.einsum("hqk,qhd->kd", grad_scores, queries, preferred_element_type=jnp.float32) * scale
    )
    part_v = jnp.einsum("hqk,qhd->kd", probs_low, grads, preferred_element_type=jnp.float32)
    return (part_q, part_k, part_v)


def local(
    layer_input,
    grad_output,
    gain_attn,
    gain_moe,
    w_query,
    w_keyval,
    w_out,
    w_gate,
    w_up,
    w_down,
    gate_weights,
    expert_ids,
    doc_starts,
):
    n_blk = lax.axis_size("blk")
    n_uly = lax.axis_size("ulysses")
    tok = layer_input.shape[0]
    group = tok * n_uly
    heads_dev = HEADS // n_uly
    per_kv = HEADS // KV_HEADS
    which = [c * heads_dev // per_kv for c in range(n_uly)]
    kv_width = KV_HEADS * HEAD_DIM
    q_width = HEADS * HEAD_DIM
    scale = 1.0 / math.sqrt(HEAD_DIM)
    blk_index = lax.axis_index("blk")
    device = blk_index * n_uly + lax.axis_index("ulysses")
    tok_pos = device * tok + jnp.arange(tok, dtype=jnp.int32)
    places = tok_pos - doc_begin(tok_pos, doc_starts)
    gain_a, gain_m, query_w, keyval_w, out_w = (
        lax.all_gather(gain_attn, ("blk", "ulysses"), axis=0, tiled=True),
        lax.all_gather(gain_moe, ("blk", "ulysses"), axis=0, tiled=True),
        lax.all_gather(w_query, ("blk", "ulysses"), axis=0, tiled=True),
        lax.all_gather(w_keyval, ("blk", "ulysses"), axis=0, tiled=True),
        lax.all_gather(w_out, ("blk", "ulysses"), axis=0, tiled=True),
    )
    gate_w, up_w, down_w = (
        lax.all_gather(w_gate, "ulysses", axis=0, tiled=True),
        lax.all_gather(w_up, "ulysses", axis=0, tiled=True),
        lax.all_gather(w_down, "ulysses", axis=0, tiled=True),
    )
    gain_a = gain_a.astype(jnp.float32)
    gain_m = gain_m.astype(jnp.float32)
    inputs = layer_input.astype(jnp.float32)
    factor_a = lax.rsqrt(jnp.mean(inputs * inputs, -1, keepdims=True) + EPS)
    normed_a = (inputs * factor_a * gain_a).astype(jnp.bfloat16)
    query_raw = jnp.dot(normed_a, query_w, preferred_element_type=jnp.float32)
    keyval_raw = jnp.dot(normed_a, keyval_w, preferred_element_type=jnp.float32)
    queries = rotate(query_raw.reshape(tok, HEADS, HEAD_DIM), places, 1.0).astype(jnp.bfloat16)
    keys = rotate(keyval_raw[:, :kv_width].reshape(tok, KV_HEADS, HEAD_DIM), places, 1.0).astype(
        jnp.bfloat16
    )
    values = keyval_raw[:, kv_width:].reshape(tok, KV_HEADS, HEAD_DIM).astype(jnp.bfloat16)
    key_copies = jnp.stack([keys[:, j] for j in which], 1)
    value_copies = jnp.stack([values[:, j] for j in which], 1)
    spread_normed = jnp.broadcast_to(normed_a[:, None, :], (tok, n_uly, D))
    head_q, head_k, head_v, head_normed = (
        lax.all_to_all(queries, "ulysses", split_axis=1, concat_axis=0, tiled=True),
        lax.all_to_all(key_copies, "ulysses", split_axis=1, concat_axis=0, tiled=True),
        lax.all_to_all(value_copies, "ulysses", split_axis=1, concat_axis=0, tiled=True),
        lax.all_to_all(spread_normed, "ulysses", split_axis=1, concat_axis=0, tiled=True),
    )
    key_local = head_k[:, 0, :]
    value_local = head_v[:, 0, :]
    normed_group = head_normed[:, 0, :]
    q_pos = blk_index * group + jnp.arange(group, dtype=jnp.int32)
    q_begin = doc_begin(q_pos, doc_starts)
    start_state = (
        jnp.full((heads_dev, group), NEG, jnp.float32),
        jnp.zeros((heads_dev, group), jnp.float32),
        jnp.zeros((group, heads_dev, HEAD_DIM), jnp.float32),
    )
    state = start_state
    key_rows = lax.all_gather(key_local, "blk", axis=0, tiled=True)
    value_rows = lax.all_gather(value_local, "blk", axis=0, tiled=True)
    key_blocks, size = split_blocks(key_rows)
    value_blocks, _ = split_blocks(value_rows)

    def attend_step(inner, item):
        key_blk, value_blk, number = item
        k_start = number * size
        live = (k_start <= q_pos[-1]) & (k_start + size - 1 >= q_begin[0])

        def attend_work(current):
            top, total, acc = current
            k_pos = k_start + jnp.arange(size, dtype=jnp.int32)
            visible = visible_mask(q_pos, q_begin, k_pos)[None]
            scores = (
                jnp.einsum("qhd,kd->hqk", head_q, key_blk, preferred_element_type=jnp.float32)
                * scale
            )
            scores = jnp.where(visible, scores, NEG)
            new_top = jnp.maximum(top, jnp.max(scores, -1))
            weights = jnp.where(visible, jnp.exp(scores - new_top[:, :, None]), 0.0)
            keep = jnp.exp(top - new_top)
            total = total * keep + jnp.sum(weights, -1)
            acc = acc * jnp.transpose(keep)[:, :, None] + jnp.einsum(
                "hqk,kd->qhd",
                weights.astype(jnp.bfloat16),
                value_blk,
                preferred_element_type=jnp.float32,
            )
            return (new_top, total, acc)

        return (lax.cond(live, attend_work, lambda current: current, inner), None)

    state, _ = lax.scan(
        attend_step,
        state,
        (key_blocks, value_blocks, jnp.arange(key_blocks.shape[0], dtype=jnp.int32)),
    )
    top, total, acc = state
    mixed = acc / jnp.transpose(total)[:, :, None]
    mixed_low = mixed.astype(jnp.bfloat16)
    lse = top + jnp.log(total)
    attended = lax.all_to_all(
        mixed_low, "ulysses", split_axis=0, concat_axis=1, tiled=True
    ).reshape(tok, q_width)
    attn_branch = contract(attended, out_w, 1, 1)
    hidden = inputs + attn_branch
    factor_m = lax.rsqrt(jnp.mean(hidden * hidden, -1, keepdims=True) + EPS)
    normed_m = (hidden * factor_m * gain_m).astype(jnp.bfloat16)
    experts = n_blk // 2
    capacity = min(tok, 2 * tok * TOP // experts)
    flat_ids = expert_ids.reshape(-1)
    picks = (flat_ids[:, None] == jnp.arange(experts, dtype=jnp.int32)[None, :]).astype(jnp.int32)
    slots = jnp.sum((jnp.cumsum(picks, 0) - 1) * picks, -1)

    def dispatch(rows):
        buffer = jnp.zeros((experts, capacity, D), jnp.bfloat16).at[flat_ids, slots].set(rows)
        return route(jnp.repeat(buffer, 2, axis=0)).reshape(n_blk * capacity, D)

    def collect(rows):
        back = route(rows.astype(jnp.bfloat16).reshape(n_blk, capacity, D))
        return back[2 * flat_ids, slots].astype(jnp.float32) + back[2 * flat_ids + 1, slots].astype(
            jnp.float32
        )

    expert_in = dispatch(jnp.repeat(normed_m, TOP, axis=0))
    gate_pre = jnp.dot(expert_in, gate_w, preferred_element_type=jnp.float32)
    up_pre = jnp.dot(expert_in, up_w, preferred_element_type=jnp.float32)
    act = (jax.nn.silu(gate_pre) * up_pre).astype(jnp.bfloat16)
    expert_out = contract(act, down_w, 1, 1)
    returned = collect(expert_out).reshape(tok, TOP, D)
    moe_branch = jnp.sum(gate_weights[:, :, None] * returned, 1)
    result = hidden + moe_branch
    layer_output = result.astype(jnp.bfloat16)
    grad_res = grad_output.astype(jnp.float32)
    routed_grad = (
        (gate_weights[:, :, None] * grad_res[:, None, :]).reshape(tok * TOP, D).astype(jnp.bfloat16)
    )
    expert_grad = dispatch(routed_grad)
    grad_act = jnp.dot(expert_grad, down_w, preferred_element_type=jnp.float32)
    grad_down = contract(expert_grad, act, 0, 0)
    sig = jax.nn.sigmoid(gate_pre)
    grad_gate_pre = (grad_act * up_pre * sig * (1.0 + gate_pre * (1.0 - sig))).astype(jnp.bfloat16)
    grad_up_pre = (grad_act * gate_pre * sig).astype(jnp.bfloat16)
    grad_gate = contract(expert_in, grad_gate_pre, 0, 0)
    grad_up = contract(expert_in, grad_up_pre, 0, 0)
    grad_in = contract(grad_gate_pre, gate_w, 1, 1) + contract(grad_up_pre, up_w, 1, 1)
    grad_normed_m = jnp.sum(collect(grad_in).reshape(tok, TOP, D), 1)
    grad_gain_m = jnp.sum(grad_normed_m * hidden * factor_m, 0)
    grad_hidden = grad_res + norm_back(hidden, factor_m, gain_m, grad_normed_m)
    grad_hidden_low = grad_hidden.astype(jnp.bfloat16)
    grad_attended = jnp.dot(grad_hidden_low, out_w, preferred_element_type=jnp.float32).astype(
        jnp.bfloat16
    )
    spread_hidden = jnp.broadcast_to(grad_hidden_low[:, None, :], (tok, n_uly, D))
    head_grad, head_hidden = (
        lax.all_to_all(
            grad_attended.reshape(tok, HEADS, HEAD_DIM),
            "ulysses",
            split_axis=1,
            concat_axis=0,
            tiled=True,
        ),
        lax.all_to_all(spread_hidden, "ulysses", split_axis=1, concat_axis=0, tiled=True),
    )
    grad_out_slice = contract(
        head_hidden[:, 0, :], mixed_low.reshape(group, heads_dev * HEAD_DIM), 0, 0
    )
    delta = jnp.transpose(jnp.sum(head_grad.astype(jnp.float32) * mixed, -1))
    total_keys = group * n_blk
    zero_q = jnp.zeros((group, heads_dev, HEAD_DIM), jnp.float32)
    fold_start = (
        zero_q,
        jnp.zeros((total_keys, HEAD_DIM), jnp.float32),
        jnp.zeros((total_keys, HEAD_DIM), jnp.float32),
    )
    state = fold_start
    key_rows = lax.all_gather(key_local, "blk", axis=0, tiled=True)
    value_rows = lax.all_gather(value_local, "blk", axis=0, tiled=True)
    key_blocks, grads_size = split_blocks(key_rows)
    value_blocks, _ = split_blocks(value_rows)

    def grads_step(inner, item):
        key_blk, value_blk, number = item
        k_start = number * grads_size
        live = (k_start <= q_pos[-1]) & (k_start + grads_size - 1 >= q_begin[0])

        def grads_work(current):
            part_q, part_k, part_v = backward_block(
                head_q, head_grad, lse, delta, q_pos, q_begin, key_blk, value_blk, k_start, scale
            )
            grad_q, grad_keys, grad_values = current
            grad_keys = lax.dynamic_update_slice_in_dim(
                grad_keys,
                lax.dynamic_slice_in_dim(grad_keys, k_start, grads_size, 0) + part_k,
                k_start,
                0,
            )
            grad_values = lax.dynamic_update_slice_in_dim(
                grad_values,
                lax.dynamic_slice_in_dim(grad_values, k_start, grads_size, 0) + part_v,
                k_start,
                0,
            )
            return (grad_q + part_q, grad_keys, grad_values)

        return (lax.cond(live, grads_work, lambda current: current, inner), None)

    state, _ = lax.scan(
        grads_step,
        state,
        (key_blocks, value_blocks, jnp.arange(key_blocks.shape[0], dtype=jnp.int32)),
    )
    grad_q = state[0]
    grad_k, grad_v = (
        lax.psum_scatter(state[1], "blk", scatter_dimension=0, tiled=True),
        lax.psum_scatter(state[2], "blk", scatter_dimension=0, tiled=True),
    )
    group_places = q_pos - q_begin
    grad_q_pre = rotate(grad_q.astype(jnp.bfloat16).astype(jnp.float32), group_places, -1.0).astype(
        jnp.bfloat16
    )
    grad_query_slice = contract(normed_group, grad_q_pre.reshape(group, heads_dev * HEAD_DIM), 0, 0)
    token_q, token_k, token_v = (
        lax.all_to_all(grad_q_pre, "ulysses", split_axis=0, concat_axis=1, tiled=True),
        lax.all_to_all(
            grad_k.astype(jnp.bfloat16)[:, None, :],
            "ulysses",
            split_axis=0,
            concat_axis=1,
            tiled=True,
        ),
        lax.all_to_all(
            grad_v.astype(jnp.bfloat16)[:, None, :],
            "ulysses",
            split_axis=0,
            concat_axis=1,
            tiled=True,
        ),
    )
    summed_k = []
    summed_v = []
    for head in range(KV_HEADS):
        members = [c for c in range(n_uly) if which[c] == head]
        summed_k.append(sum((token_k[:, c].astype(jnp.float32) for c in members)))
        summed_v.append(sum((token_v[:, c].astype(jnp.float32) for c in members)))
    grad_key_heads = jnp.stack(summed_k, 1)
    grad_value_heads = jnp.stack(summed_v, 1)
    grad_query_pre = token_q.reshape(tok, q_width)
    grad_key_pre = rotate(grad_key_heads, places, -1.0).reshape(tok, kv_width)
    grad_keyval_pre = jnp.concatenate(
        [grad_key_pre, grad_value_heads.reshape(tok, kv_width)], 1
    ).astype(jnp.bfloat16)
    grad_normed_a = contract(grad_query_pre, query_w, 1, 1) + contract(
        grad_keyval_pre, keyval_w, 1, 1
    )
    grad_keyval_w = contract(normed_a, grad_keyval_pre, 0, 0)
    grad_gain_a = jnp.sum(grad_normed_a * inputs * factor_a, 0)
    grad_input = grad_hidden + norm_back(inputs, factor_a, gain_a, grad_normed_a)
    n_dev = n_blk * n_uly
    squares = jnp.stack(
        [
            jnp.sum(attn_branch * attn_branch),
            jnp.sum(moe_branch * moe_branch),
            jnp.sum(result * result),
        ]
    )
    square_rows = jnp.broadcast_to(squares[None, :], (n_dev, 3))
    part_gate, part_up, part_down, uly_gain_a, uly_gain_m, uly_keyval, uly_squares = (
        lax.psum_scatter(
            grad_gate.astype(jnp.bfloat16), "ulysses", scatter_dimension=0, tiled=True
        ).astype(jnp.float32),
        lax.psum_scatter(
            grad_up.astype(jnp.bfloat16), "ulysses", scatter_dimension=0, tiled=True
        ).astype(jnp.float32),
        lax.psum_scatter(
            grad_down.astype(jnp.bfloat16), "ulysses", scatter_dimension=0, tiled=True
        ).astype(jnp.float32),
        lax.psum_scatter(
            reorder_rows(grad_gain_a, n_blk, n_uly).astype(jnp.bfloat16),
            "ulysses",
            scatter_dimension=0,
            tiled=True,
        ).astype(jnp.float32),
        lax.psum_scatter(
            reorder_rows(grad_gain_m, n_blk, n_uly).astype(jnp.bfloat16),
            "ulysses",
            scatter_dimension=0,
            tiled=True,
        ).astype(jnp.float32),
        lax.psum_scatter(
            reorder_rows(grad_keyval_w, n_blk, n_uly).astype(jnp.bfloat16),
            "ulysses",
            scatter_dimension=0,
            tiled=True,
        ).astype(jnp.float32),
        lax.psum_scatter(
            square_rows.astype(jnp.bfloat16), "ulysses", scatter_dimension=0, tiled=True
        ).astype(jnp.float32),
    )
    part_outw, part_query, part_gain_a, part_gain_m, part_keyval, square_row = (
        lax.psum_scatter(grad_out_slice, "blk", scatter_dimension=0, tiled=True),
        lax.psum_scatter(grad_query_slice, "blk", scatter_dimension=0, tiled=True),
        lax.psum_scatter(uly_gain_a, "blk", scatter_dimension=0, tiled=True),
        lax.psum_scatter(uly_gain_m, "blk", scatter_dimension=0, tiled=True),
        lax.psum_scatter(uly_keyval, "blk", scatter_dimension=0, tiled=True),
        lax.psum_scatter(uly_squares, "blk", scatter_dimension=0, tiled=True),
    )
    branch_rms = jnp.sqrt(square_row[0] / (tok * n_dev * D))
    return (
        layer_output,
        grad_input,
        part_gain_a,
        part_gain_m,
        part_query,
        part_keyval,
        part_outw,
        part_gate,
        part_up,
        part_down,
        branch_rms,
    )


MESH = pl.DeviceIdType.MESH
LANES = 128
LOG2E = 1.4426950408889634


class Place:
    def __init__(self, depth):
        self.blk = lax.axis_index("blk")
        self.u = lax.axis_index("ulysses")
        self.depth = depth
        self.z = self.blk // 4
        self.x = (self.blk // 2) % 2
        self.c = self.blk % 2
        self.up = (self.blk + 4, self.u)
        self.down = (self.blk - 4, self.u)
        self.across = (self.blk + 2 - 4 * self.x, self.u)
        self.sibling = (self.blk + 1 - 2 * self.c, self.u)
        self.other = (self.blk, 1 - self.u)
        self.has_up = self.z < depth - 1
        self.has_down = self.z > 0

    def along(self, z):
        return (self.blk + 4 * (z - self.z), self.u)

    def slot(self, z, x, c):
        return z * 4 + x * 2 + c

    def greet(self, sibling=False, other=False, plane=True):
        barrier = pltpu.get_barrier_semaphore()

        def hail(device):
            pl.semaphore_signal(barrier, inc=1, device_id=device, device_id_type=MESH)

        count = 0
        if plane:
            hail(self.across)
            for d in range(1, self.depth):
                pl.when(self.z >= d)(lambda d=d: hail(self.along(self.z - d)))
                pl.when(self.z + d < self.depth)(lambda d=d: hail(self.along(self.z + d)))
            count = self.depth
        if sibling:
            hail(self.sibling)
            count = count + 1
        if other:
            hail(self.other)
            count = count + 1
        pl.semaphore_wait(barrier, count)


class Wires:
    def __init__(self, sems):
        self.sems = sems
        self.used = 0

    def take(self, count):
        base = self.used
        self.used += count
        return lambda index: self.sems.at[base + index]


def each(act, items):
    for item in items:
        act(item)


def remote(src, dst, send, recv, device):
    return pltpu.make_async_remote_copy(
        src_ref=src, dst_ref=dst, send_sem=send, recv_sem=recv, device_id=device, device_id_type=MESH
    )


class Gather:
    def __init__(self, place, wires, src, out, cores, up_only=False, chain=False, far=False):
        self.p, self.src, self.out, self.cores, self.up_only, self.chain = place, src, out, cores, up_only, chain
        n = place.depth
        self.s_z = [wires.take(n) for _ in range(2 if chain else 1)]
        self.s_across = wires.take(n)
        self.r_z, self.r_x = wires.take(n), wires.take(n)
        if cores:
            self.s_core, self.r_core = wires.take(2 * n), wires.take(2 * n)
        self.far = wires.take(1)(0) if far else None

    def _across(self, zz, xx, src=None):
        dst = self.out(zz, xx, self.p.c)
        return remote(dst if src is None else src, dst, self.s_across(zz), self.r_x(zz), self.p.across)

    def _core(self, zz, xx, src=None):
        dst = self.out(zz, xx, self.p.c)
        at = zz * 2 + xx
        return remote(dst if src is None else src, dst, self.s_core(at), self.r_core(at), self.p.sibling)

    def _along(self, zz, to, src=None):
        p = self.p
        dst = self.out(zz, p.x, p.c)
        return remote(dst if src is None else src, dst, self.s_z[0](to), self.r_z(zz), p.along(to))

    def _next(self, zz, up, src=None):
        p = self.p
        dst = self.out(zz, p.x, p.c)
        return remote(
            dst if src is None else src, dst, self.s_z[up](zz), self.r_z(zz), p.along(p.z + (1 if up else -1))
        )

    def start_z(self, in_place=False):
        p = self.p
        src = None if in_place else self.src
        if self.chain:
            pl.when(p.has_up)(lambda: self._next(p.z, 1, src).start())
            pl.when(p.has_down)(lambda: self._next(p.z, 0, src).start())
            return
        for d in range(1, p.depth):
            pl.when(p.z + d < p.depth)(lambda d=d: self._along(p.z, p.z + d, src).start())
            if not self.up_only:
                pl.when(p.z >= d)(lambda d=d: self._along(p.z, p.z - d, src).start())

    def start_x(self, in_place=False):
        p = self.p
        src = None if in_place else self.src
        self._across(p.z, p.x, src).start()
        if self.cores:
            self._core(p.z, p.x, src).start()
        if self.far is not None:
            pltpu.make_async_copy(self.src, self.out(p.z, p.x, p.c), self.far).start()
        elif not in_place:
            self.out(p.z, p.x, p.c)[...] = self.src[...]

    def start(self, in_place=False):
        self.start_z(in_place)
        self.start_x(in_place)

    def hop(self, d):
        p = self.p

        def take(zz, up):
            remote(
                self.out(zz, p.x, p.c), self.out(zz, p.x, p.c), self.s_z[0](0), self.r_z(zz), p.across
            ).wait_recv()
            if self.chain:
                pl.when(p.has_up if up else p.has_down)(lambda: self._next(zz, up).start())
            self._across(zz, p.x).start()
            if self.cores:
                self._core(zz, p.x).start()

        pl.when(p.z >= d)(lambda: take(p.z - d, 1))
        if not self.up_only:
            pl.when(p.z + d < p.depth)(lambda: take(p.z + d, 0))

    def cross(self, d):
        p = self.p

        def take(zz):
            self._across(zz, 1 - p.x).wait_recv()
            if self.cores:
                self._core(zz, 1 - p.x).start()

        if isinstance(d, int) and d == 0:
            take(p.z)
        else:
            pl.when(p.z >= d)(lambda: take(p.z - d))
            if not self.up_only:
                pl.when(p.z + d < p.depth)(lambda: take(p.z + d))

    def crossed(self, zz):
        self._across(zz, 1 - self.p.x).wait_recv()

    def core(self, zz, xx):
        self._core(zz, xx).wait_recv()

    def finish(self, cores_taken=False):
        p = self.p
        for zz in range(p.depth):

            def ends(zz=zz):
                if self.cores:
                    for xx in range(2):
                        if not cores_taken:
                            self._core(zz, xx).wait_recv()
                        self._core(zz, xx).wait_send()
                self._across(zz, p.x).wait_send()

            if self.up_only and zz > 0:
                pl.when(p.z >= zz)(ends)
            else:
                ends()
            if self.chain:
                pl.when(p.has_up & (p.z >= zz))(lambda zz=zz: self._next(zz, 1).wait_send())
                pl.when(p.has_down & (p.z <= zz))(lambda zz=zz: self._next(zz, 0).wait_send())
            else:
                away = (p.z < zz) if self.up_only else (p.z != zz)
                pl.when(away)(lambda zz=zz: self._along(p.z, zz).wait_send())
        if self.far is not None:
            pltpu.make_async_copy(self.src, self.out(p.z, p.x, p.c), self.far).wait()


class Scatter:
    def __init__(self, place, wires, part, out, rx, rz, pieces, down_only=False, ready=()):
        self.ready = ready
        self.p, self.part, self.out, self.rx, self.rz = place, part, out, rx, rz
        n = place.depth
        total = n * pieces
        self.pieces, self.down_only = pieces, down_only
        self.sx, self.cx = wires.take(total), wires.take(total)
        self.sz, self.cz = wires.take(total), wires.take(total)
        if down_only:
            self.order = list(range(n))
        else:
            self.order = [n - 1] + list(range(n - 1))
        self.items = [(zz, k) for zz in self.order if zz not in ready for k in range(pieces)]

    def _x(self, zz, k):
        i = zz * self.pieces + k
        return remote(self.part(zz, 1 - self.p.x, k), self.rx(zz, k), self.sx(i), self.cx(i), self.p.across)

    def _z(self, zz, k, source=None):
        p = self.p
        source = p.z if source is None else source
        return remote(
            self.rx(zz, k),
            self.rz(source, k),
            self.sz(zz * self.pieces + k),
            self.cz(source * self.pieces + k),
            p.along(zz),
        )

    def _live(self, zz, act):
        if self.down_only and zz > 0:
            pl.when(self.p.z >= zz)(act)
        else:
            act()

    def begin(self, t):
        if t < len(self.items):
            zz, k = self.items[t]
            self._live(zz, lambda: self._x(zz, k).start())

    def send(self, zz):
        for k in range(self.pieces):
            self._x(zz, k).start()

    def take(self, zz, k):
        p = self.p

        def act():
            self._x(zz, k).wait_recv()

            def forward():
                total = self.part(zz, p.x, k)[...].astype(jnp.float32)
                total = total + self.rx(zz, k)[...].astype(jnp.float32)
                self.rx(zz, k)[...] = total.astype(jnp.bfloat16)
                self._z(zz, k).start()

            pl.when(p.z != zz)(forward)

        self._live(zz, act)

    def land(self, t):
        self.take(*self.items[t])

    def forward(self):
        for zz in self.ready:
            for k in range(self.pieces):
                pl.when(self.p.z != zz)(lambda zz=zz, k=k: self._z(zz, k).start())

    def finish(self):
        p = self.p
        n = p.depth
        for zz, k in [(zz, k) for zz in self.order for k in range(self.pieces)]:
            if zz not in self.ready:
                self._live(zz, lambda zz=zz, k=k: self._x(zz, k).wait_send())
            away = (p.z > zz) if self.down_only else (p.z != zz)
            pl.when(away)(lambda zz=zz, k=k: self._z(zz, k).wait_send())

            def store(zz=zz, k=k):
                total = self.rx(zz, k)[...].astype(jnp.float32)
                if zz not in self.ready:
                    total = total + self.part(zz, p.x, k)[...].astype(jnp.float32)
                for source in range(zz + 1 if self.down_only else 0, n):
                    if source != zz:
                        self._z(zz, k, source).wait_recv()
                        total = total + self.rz(source, k)[...].astype(jnp.float32)
                self.out(k)[...] = total

            pl.when(p.z == zz)(store)


class CoreScatter:
    def __init__(self, place, wires, src, rc, out, rx, rz, down_only=False):
        self.p, self.src, self.rc, self.down_only = place, src, rc, down_only
        n = place.depth
        self.sc, self.cc = wires.take(n), wires.take(n)
        self.plane = Scatter(
            place, wires, lambda zz, xx, k: rc.at[zz * 2 + xx], lambda k: out,
            lambda zz, k: rx.at[zz], lambda source, k: rz.at[source], 1, down_only,
        )
        self.order = self.plane.order

    def _trade(self, zz):
        p = self.p
        if self.down_only:
            at = pl.ds(2 * zz, 2)
            return remote(self.src.at[at, 1 - p.c], self.rc.at[at], self.sc(zz), self.cc(zz), p.sibling)
        return remote(self.src.at[:, 1 - p.c], self.rc, self.sc(0), self.cc(0), p.sibling)

    def trade(self, t=0):
        zz = self.order[t]
        self.plane._live(zz, lambda: self._trade(zz).start())

    def join(self, t):
        p = self.p
        zz = self.order[t]

        def act():
            if self.down_only or t == 0:
                self._trade(zz).wait_recv()
            for xx in range(2):
                at = zz * 2 + xx
                self.rc[at] = (
                    self.src[at, p.c].astype(jnp.float32) + self.rc[at].astype(jnp.float32)
                ).astype(jnp.bfloat16)

        self.plane._live(zz, act)
        self.plane.begin(t)

    def land(self, t):
        self.plane.land(t)

    def release(self):
        for t, zz in enumerate(self.order):
            if self.down_only or t == 0:
                self.plane._live(zz, lambda zz=zz: self._trade(zz).wait_send())

    def finish(self):
        self.plane.finish()


def mm(left, right):
    return jnp.dot(left, right, preferred_element_type=jnp.float32)


def flip(tile):
    return tile.astype(jnp.float32).T.astype(jnp.bfloat16)


def hidden_bias(first_key, first_query, begin, keys):
    queries = begin.shape[1]
    k_pos = first_key + lax.broadcasted_iota(jnp.int32, (keys, queries), 0)
    q_pos = first_query + lax.broadcasted_iota(jnp.int32, (keys, queries), 1)
    return jnp.where((k_pos >= begin) & (k_pos <= q_pos), 0.0, NEG)


def front_kernel(
    depth, scale, docs, x, dy, gain_a, gain_m, wq, wkv, wo, ids, shares_of, freq, e0, e1, e2,
    b, hid, attn_sq, normed_t, q_rows, qt, o, ot, lse, gain_rows, g_all, x_all, begin, cosine, sine,
    kv_out, w_out, wo_out, dy_all, f0, f1, f2,
    kv, w_all, wo_all, own, square, g_own, wa_own, normed, raw, top, total, acc, p_out, p_in, sems,
):
    f32, bf = jnp.float32, jnp.bfloat16
    p = Place(depth)
    p.greet(sibling=True, other=True)
    wires = Wires(sems)
    u, blk = p.u, p.blk
    tok, width = x.shape
    group, q_half = o.shape
    heads = q_half // HEAD_DIM
    kv_half = 2 * HEAD_DIM
    rows_dev = wq.shape[0]
    half, cols = e0.shape
    experts = 2 * depth

    def rows_of(ref, z, xx, c, member):
        row = (p.slot(z, xx, c) * 2 + member) * rows_dev
        return ref.at[pl.ds(pl.multiple_of(row, 16), rows_dev)]

    wa_mine = Gather(p, wires, wa_own.at[u], lambda z, xx, c: rows_of(w_all, z, xx, c, u), True, chain=True)
    wa_peer = Gather(p, wires, None, lambda z, xx, c: rows_of(w_all, z, xx, c, 1 - u), True, chain=True)
    wos = Gather(
        p, wires, None,
        lambda z, xx, c: wo_all.at[pl.ds(pl.multiple_of(p.slot(z, xx, c) * 2 * rows_dev, 16), 2 * rows_dev)],
        True, chain=True,
    )
    kvs = Gather(p, wires, None, lambda z, xx, c: kv.at[p.slot(z, xx, c)], True, up_only=True)
    piece = tok // 2
    dys = [
        Gather(
            p, wires, dy.at[pl.ds(k * piece, piece)],
            lambda z, xx, c, k=k: dy_all.at[z * 2 + xx, pl.ds(k * piece, piece)], False, chain=True, far=True,
        )
        for k in range(2)
    ]
    gws = Gather(p, wires, g_own, lambda z, xx, c: g_all.at[z * 2 + xx], False, chain=True)
    ws, wr = wires.take(2), wires.take(2)
    xs, xr = wires.take(1)(0), wires.take(1)(0)
    es, er = wires.take(3), wires.take(3)
    cs, cr = wires.take(6), wires.take(6)
    ps, pr = wires.take(3), wires.take(3)

    for h in range(2):
        wa_own[h, :, :q_half] = wq[:, h * q_half : (h + 1) * q_half]
        for part in range(2):
            wa_own[h, :, q_half + part * HEAD_DIM : q_half + (part + 1) * HEAD_DIM] = wkv[
                :, (part * 2 + h) * HEAD_DIM : (part * 2 + h + 1) * HEAD_DIM
            ]
    square[...] = jnp.zeros(square.shape, f32)
    square[0:1, :rows_dev] = gain_a[...].astype(f32)
    square[1:2, :rows_dev] = gain_m[...].astype(f32)
    columns = square[...].T[:rows_dev, :].astype(bf)
    for h in range(2):
        wa_own[h, :, q_half + kv_half :] = columns

    wa_swap = remote(wa_own.at[1 - u], rows_of(w_all, p.z, p.x, p.c, u), ws(0), wr(0), p.other)
    wo_swap = remote(
        wo.at[:, pl.ds(pl.multiple_of((1 - u) * q_half, LANES), q_half)],
        rows_of(wo_all, p.z, p.x, p.c, u), ws(1), wr(1), p.other,
    )
    x_swap = remote(x, x_all.at[u], xs, xr, p.other)

    def part(ref, row, core):
        return ref.at[
            pl.ds(pl.multiple_of(row * half, half), half), pl.ds(pl.multiple_of(core * cols, LANES), cols)
        ]

    halves = ((e0, f0), (e1, f1), (e2, f2))
    ls, ks = wires.take(3), wires.take(3)
    loads = [pltpu.make_async_copy(e, own.at[i], ls(i)) for i, (e, f) in enumerate(halves)]
    keeps = [pltpu.make_async_copy(own.at[i], part(f, u, p.c), ks(i)) for i, (e, f) in enumerate(halves)]
    swaps = [remote(own.at[i], part(f, u, p.c), es(i), er(i), p.other) for i, (e, f) in enumerate(halves)]
    shares = [remote(own.at[i], part(f, u, p.c), cs(i), cr(i), p.sibling) for i, (e, f) in enumerate(halves)]
    passes = [
        remote(part(f, 1 - u, p.c), part(f, 1 - u, p.c), cs(3 + i), cr(3 + i), p.sibling)
        for i, (e, f) in enumerate(halves)
    ]
    os_ = wires.take(3)
    stores = [
        pltpu.make_async_copy(v, r, os_(i)) for i, (v, r) in enumerate(((kv, kv_out), (w_all, w_out), (wo_all, wo_out)))
    ]

    def expert_out(i):
        swaps[i].start()
        shares[i].start()

    def expert_in(i):
        swaps[i].wait_recv()
        passes[i].start()

    wa_swap.start()
    wa_mine.start()
    wo_swap.start()
    x_swap.start()
    each(lambda load: load.start(), loads)

    def starts(places):
        first = jnp.zeros(places.shape, jnp.int32)
        for i in range(docs.shape[0]):
            first = jnp.where(docs[i] <= places, jnp.maximum(first, docs[i]), first)
        return first

    begin[...] = starts(blk * group + lax.broadcasted_iota(jnp.int32, begin.shape, 1))
    places = blk * group + lax.broadcasted_iota(jnp.int32, cosine.shape, 0)
    angle = (places - starts(places)).astype(f32) * freq[0:1, :]
    cosine[...] = jnp.cos(angle)
    sine[...] = jnp.where(lax.broadcasted_iota(jnp.int32, sine.shape, 1) < HEAD_DIM // 2, -1.0, 1.0) * jnp.sin(angle)
    for e in range(experts):
        g_own[e : e + 1, :] = jnp.sum(jnp.where(ids[...] == e, shares_of[...], 0.0), axis=0, keepdims=True)
    wa_swap.wait_recv()
    wa_peer.start(in_place=True)
    x_all[u] = x[...]
    rows_of(wo_all, p.z, p.x, p.c, u)[...] = wo[:, pl.ds(pl.multiple_of(u * q_half, LANES), q_half)]
    for i in range(3):
        loads[i].wait()
        keeps[i].start()
    gws.start()
    for d in range(1, depth):
        for g in (wa_mine, wa_peer):
            g.hop(d)
            g.cross(d - 1)
        gws.hop(d)
        gws.cross(d - 1)
        if d == 1:
            wo_swap.wait_recv()
            wos.start(in_place=True)
            expert_out(0)
        else:
            wos.hop(d - 1)
    gws.cross(depth - 1)
    dys[0].start()
    expert_out(1)
    x_swap.wait_recv()
    for g in (wa_mine, wa_peer):
        g.cross(depth - 1)
    for g in (wa_mine, wa_peer):
        g.finish()
    stores[1].start()
    gain_rows[...] = w_all[:, q_half + kv_half :].astype(f32).T[:8, :]
    for m in range(2):
        xf = x_all[m].astype(f32)
        r1 = lax.rsqrt(jnp.mean(xf * xf, -1, keepdims=True) + EPS)
        normed[m * tok : (m + 1) * tok, :] = (xf * r1 * gain_rows[0:1, :]).astype(bf)
    raw[...] = mm(normed[...], w_all[:, : q_half + kv_half])

    def rope(values):
        return values * cosine[...] + pltpu.roll(values, HEAD_DIM // 2, 1) * sine[...]

    here = p.slot(p.z, p.x, p.c)
    kv[here, :, :HEAD_DIM] = rope(raw[:, q_half : q_half + HEAD_DIM]).astype(bf)
    kv[here, :, HEAD_DIM:] = raw[:, q_half + HEAD_DIM :].astype(bf)
    kvs.start(in_place=True)
    for h in range(heads):
        hs = slice(h * HEAD_DIM, (h + 1) * HEAD_DIM)
        turned = rope(raw[:, hs])
        q_rows[h * group : (h + 1) * group, :] = turned.astype(bf)
        qt[:, h * group : (h + 1) * group] = turned.T.astype(bf)
    for j in range(0, width, 256):
        normed_t[j : j + 256, :] = flip(normed[:, j : j + 256])
    top[...] = jnp.full(top.shape, NEG, f32)
    total[...] = jnp.zeros(total.shape, f32)
    ot[...] = jnp.zeros(ot.shape, f32)

    background = {}

    def at_step(s, act):
        background.setdefault(s, []).append(act)

    at_step(0, lambda: kvs.cross(0))
    at_step(0, lambda: kvs.hop(1))
    at_step(0, dys[1].start_z)
    at_step(1, lambda: wos.hop(3))
    at_step(1, lambda: dys[0].hop(1))
    at_step(2, lambda: kvs.cross(1))
    at_step(2, lambda: kvs.hop(2))
    at_step(2, dys[1].start_x)
    at_step(3, lambda: wos.cross(0))
    at_step(3, lambda: dys[1].hop(1))
    at_step(4, lambda: kvs.cross(2))
    at_step(4, lambda: kvs.hop(3))
    at_step(5, lambda: wos.cross(1))
    at_step(2, lambda: expert_in(0))
    at_step(2, lambda: expert_out(2))
    at_step(5, lambda: dys[0].hop(2))
    at_step(6, lambda: kvs.cross(3))
    at_step(6, lambda: dys[1].hop(2))
    at_step(7, lambda: wos.cross(2))
    at_step(7, lambda: wos.cross(3))

    def step(s, carry):
        d = s // 2
        zz = p.z - d
        xx = jnp.where(s % 2 == 0, p.x, 1 - p.x)
        j = p.slot(zz, xx, 0)

        pl.when(zz >= 0)(lambda: kvs.core(zz, xx))

        def work():
            pair = kv[pl.ds(j, 2)].reshape(2 * group, kv_half)
            k = pair[:, :HEAD_DIM]
            vt = flip(pair[:, HEAD_DIM:])
            bias = hidden_bias(j * group, blk * group, begin[0:1, :], 2 * group)
            at = [slice(h * group, (h + 1) * group) for h in range(heads)]
            sc = [mm(k, qt[:, hs]) * (scale * LOG2E) + bias for hs in at]
            old = [top[0:1, hs] for hs in at]
            new = [jnp.maximum(o_, jnp.max(s_, axis=0, keepdims=True)) for o_, s_ in zip(old, sc)]
            e = [jnp.exp2(s_ - n_) for s_, n_ in zip(sc, new)]
            part = [jnp.sum(e_, axis=0, keepdims=True) for e_ in e]
            mixed = [mm(vt, e_.astype(bf)) for e_ in e]
            for h, hs in enumerate(at):
                keep = jnp.exp2(old[h] - new[h])
                total[0:1, hs] = total[0:1, hs] * keep + part[h]
                ot[:, hs] = ot[:, hs] * keep + mixed[h]
                top[0:1, hs] = new[h]

        pl.when((zz >= 0) & (j <= blk))(work)
        for when, acts in background.items():
            pl.when(s == when)(lambda acts=acts: each(lambda act: act(), acts))
        return carry

    lax.fori_loop(0, 2 * depth, step, 0)

    wos.finish()
    stores[2].start()
    sums = total[0:1, :]
    lse[...] = jnp.broadcast_to(top[0:1, :] + jnp.log2(sums), lse.shape)
    for h in range(heads):
        at = slice(h * group, (h + 1) * group)
        mixed = ot[:, at] / sums[:, at]
        ot[:, at] = mixed
        o[:, h * HEAD_DIM : (h + 1) * HEAD_DIM] = mixed.T.astype(bf)

    wide = width // 3
    p_swaps = []
    for i in range(3):
        cb = i * wide
        acc[:, cb : cb + wide] = contract(o[...], wo_all[cb : cb + wide, :], 1, 1)
        theirs = pl.ds(pl.multiple_of((1 - u) * tok, tok), tok)
        p_out[i] = acc[theirs, cb : cb + wide].astype(bf)
        p_swaps.append(remote(p_out.at[i], p_in.at[i], ps(i), pr(i), p.other))
        p_swaps[i].start()
    each(lambda g: g.hop(3), dys)
    expert_in(1)
    for d in range(2):
        each(lambda g: g.cross(d), dys)
    mine = pl.ds(pl.multiple_of(u * tok, tok), tok)
    for i in range(3):
        p_swaps[i].wait_recv()
        acc[mine, i * wide : (i + 1) * wide] += p_in[i].astype(f32)
    branch = acc[mine, :]
    hidden = x[...].astype(f32) + branch
    hid[...] = hidden
    r2 = lax.rsqrt(jnp.mean(hidden * hidden, -1, keepdims=True) + EPS)
    b[...] = (hidden * r2 * gain_rows[1:2, :]).astype(bf)
    attn_sq[...] = jnp.broadcast_to(jnp.sum(branch * branch).reshape(1, 1), attn_sq.shape)
    for d in range(2, depth):
        each(lambda g: g.cross(d), dys)
    expert_in(2)
    kvs.finish(cores_taken=True)
    stores[0].start()
    each(lambda g: g.finish(), dys)
    gws.finish()
    wa_swap.wait_send()
    wo_swap.wait_send()
    x_swap.wait_send()
    for i in range(3):
        swaps[i].wait_send()
        keeps[i].wait()
        shares[i].wait()
        passes[i].wait()
        p_swaps[i].wait_send()
        stores[i].wait()


def front(docs, x, dy, gain_a, gain_m, wq, wkv, wo, ids, shares, experts, depth, scale, cid):
    f32, bf = jnp.float32, jnp.bfloat16
    shape = jax.ShapeDtypeStruct
    vmem = pl.BlockSpec(memory_space=pltpu.VMEM)
    hbm = pl.BlockSpec(memory_space=pl.ANY)
    V = pltpu.VMEM
    tok, width = x.shape
    group = 2 * tok
    q_half = wq.shape[1] // 2
    kv_half = 2 * HEAD_DIM
    wide = q_half + kv_half + LANES
    rows = q_half // HEAD_DIM * group
    rows_dev = wq.shape[0]
    expert = shape((2 * experts[0].shape[0], 2 * experts[0].shape[1]), bf)
    half = HEAD_DIM // 2
    freq = np.power(np.float32(ROPE_BASE), -np.arange(half, dtype=np.float32) * np.float32(2.0 / HEAD_DIM))
    freq = jnp.asarray(np.tile(freq.astype(np.float32), (8, 2)))
    return pl.pallas_call(
        functools.partial(front_kernel, depth, scale),
        out_shape=(
            shape((tok, width), bf),
            shape((tok, width), f32),
            shape((8, LANES), f32),
            shape((width, group), bf),
            shape((rows, HEAD_DIM), bf),
            shape((HEAD_DIM, rows), bf),
            shape((group, q_half), bf),
            shape((HEAD_DIM, rows), f32),
            shape((8, rows), f32),
            shape((8, width), f32),
            shape((2 * depth, 2 * depth, tok), f32),
            shape((2, tok, width), bf),
            shape((8, group), jnp.int32),
            shape((group, HEAD_DIM), f32),
            shape((group, HEAD_DIM), f32),
            shape((4 * depth, group, kv_half), bf),
            shape((width, wide), bf),
            shape((width, q_half), bf),
            shape((2 * depth, tok, width), bf),
            expert,
            expert,
            expert,
        ),
        in_specs=[pl.BlockSpec(memory_space=pltpu.SMEM)] + [vmem] * 10 + [hbm] * 3,
        out_specs=tuple([vmem] * 15 + [hbm] * 7),
        scratch_shapes=[
            V((4 * depth, group, kv_half), bf),
            V((width, wide), bf),
            V((width, q_half), bf),
            V((3,) + experts[0].shape, bf),
            V((LANES, LANES), f32),
            V((2 * depth, tok), f32),
            V((2, rows_dev, wide), bf),
            V((group, width), bf),
            V((group, q_half + kv_half), f32),
            V((8, rows), f32),
            V((8, rows), f32),
            V((group, width), f32),
            V((3, tok, width // 3), bf),
            V((3, tok, width // 3), bf),
            pltpu.SemaphoreType.DMA((8 * 16 * depth,)),
        ],
        compiler_params=pltpu.CompilerParams(
            collective_id=cid, has_side_effects=True, vmem_limit_bytes=56 * 2**20
        ),
        name="front",
    )(docs, x, dy, gain_a[None, :], gain_m[None, :], wq, wkv, wo, ids, shares, freq, *experts)


def experts_kernel(
    depth, b, dy_own, g_all, hid, gain_rows, dy_far, g_far, u_far, d_far,
    dh, dhr, gm, z_sums, z_far, eg_far,
    dy_all, wg, wu, wd, z_p, eg, z_rx, b_all, act, dgate, dup, dyr, db_p, rx, rz, db, turned, sems,
):
    f32, bf = jnp.float32, jnp.bfloat16
    p = Place(depth)
    p.greet()
    wires = Wires(sems)
    tok, width = b.shape
    hidden_units = wg.shape[1]
    expert = p.blk // 2
    pair = 2 * tok
    pieces = 2
    piece = tok // pieces

    rows = [
        Gather(
            p, wires, b.at[pl.ds(k * piece, piece)],
            lambda z, x, c, k=k: b_all.at[pl.ds(pl.multiple_of((z * 2 + x) * tok + k * piece, piece), piece)],
            False, chain=True,
        )
        for k in range(pieces)
    ]

    def cut(ref, k):
        return ref.at[pl.ds(k * piece, piece)]

    sums = Scatter(
        p, wires,
        lambda zz, xx, k: cut(db_p.at[zz * 2 + xx], k),
        lambda k: cut(db, k),
        lambda zz, k: cut(rx.at[zz], k),
        lambda slot, k: cut(rz.at[slot], k),
        pieces,
    )
    ls = wires.take(4)
    loads = [
        pltpu.make_async_copy(r, v, ls(i)) for i, (r, v) in enumerate(((dy_far, dy_all), (g_far, wg), (u_far, wu), (d_far, wd)))
    ]
    os_ = wires.take(3)
    stores = [
        pltpu.make_async_copy(v, r, os_(i))
        for i, (v, r) in enumerate(((z_p, z_far), (eg.at[pl.ds(0, 2)], eg_far.at[pl.ds(0, 2)]), (eg.at[2], eg_far.at[2])))
    ]
    each(lambda load: load.start(), loads)
    each(lambda g: g.start(), rows)
    spread = lax.broadcasted_iota(jnp.int32, (tok, 8), 1)

    def weight(slot):
        return jnp.sum(jnp.where(spread == expert, g_all[slot].T, 0.0), axis=1, keepdims=True)

    def nth(i):
        inner = jnp.where(i == 0, 1, jnp.where(i == 1, 0, i))
        other = jnp.where(i == 0, 2, jnp.where(i == 1, 1, jnp.where(i == 2, 3, 0)))
        return jnp.where(p.z == 0, i, jnp.where(p.z == depth - 1, depth - 1 - i, jnp.where(p.z == 1, inner, other)))

    def block(i, carry):
        for d in range(1, depth):
            pl.when(i == d - 1)(lambda d=d: each(lambda g: g.hop(d), rows))
        each(lambda g: g.crossed(nth(i)), rows)
        pl.when(i == 0)(lambda: each(lambda load: load.wait(), loads))
        zz = nth(i)
        at = pl.ds(pl.multiple_of(zz * pair, pair), pair)
        for xx in range(2):
            half = pl.ds(pl.multiple_of(zz * pair + xx * tok, tok), tok)
            dyr[half, :] = (weight(zz * 2 + xx) * dy_all[zz * 2 + xx].astype(f32)).astype(bf)
        for cb in range(0, hidden_units, 256):
            cs = slice(cb, cb + 256)
            gate = mm(b_all[at, :], wg[:, cs])
            up = mm(b_all[at, :], wu[:, cs])
            sig = jax.nn.sigmoid(gate)
            act[at, cs] = (gate * sig * up).astype(bf)
            dact = mm(dyr[at, :], wd[:, cs])
            dgate[at, cs] = (dact * up * sig * (1.0 + gate * (1.0 - sig))).astype(bf)
            dup[at, cs] = (dact * gate * sig).astype(bf)
        for cb in range(0, width, 512):
            cs = slice(cb, cb + 512)
            part = contract(dgate[at, :], wg[cs, :], 1, 1) + contract(dup[at, :], wu[cs, :], 1, 1)
            for xx in range(2):
                db_p[zz * 2 + xx, :, cs] = part[xx * tok : (xx + 1) * tok, :].astype(bf)
        pl.when(i == depth - 2)(lambda: sums.send(nth(2)))
        pl.when(i == depth - 1)(lambda: each(lambda n: sums.send(nth(n)), (3, 1)))
        for cb in range(0, width, 512):
            cs = slice(cb, cb + 512)
            part = contract(act[at, :], wd[cs, :], 1, 1)
            for xx in range(2):
                z_p[zz * 2 + xx, :, cs] = (
                    weight(zz * 2 + xx) * part[xx * tok : (xx + 1) * tok, :]
                ).astype(bf)
        return carry

    lax.fori_loop(0, depth, block, 0)

    stores[0].start()
    zs_, zr_ = wires.take(2 * len(EARLY)), wires.take(2 * len(EARLY))

    def z_send(n, k):
        return remote(
            cut(z_p.at[EARLY[n] * 2 + 1 - p.x], k), cut(z_rx.at[n], k), zs_(2 * n + k), zr_(2 * n + k), p.across
        )

    z_pieces = [(n, k) for n in range(len(EARLY)) for k in range(pieces)]

    wide = 256

    def grads(n):
        cs = slice(n * wide, (n + 1) * wide)
        turned[...] = flip(b_all[:, cs])
        eg[0, cs, :] = mm(turned[...], dgate[...]).astype(bf)
        eg[1, cs, :] = mm(turned[...], dup[...]).astype(bf)

    def grads_down(n):
        cs = slice(n * wide, (n + 1) * wide)
        turned[...] = flip(dyr[:, cs])
        eg[2, cs, :] = mm(turned[...], act[...]).astype(bf)

    work = [lambda n=n: grads(n) for n in range(width // wide)]
    work += [lambda n=n: grads_down(n) for n in range(width // wide)]
    events = []
    for n in (2, 3, 1, 0):
        for k in range(pieces):
            events.append(lambda n=n, k=k: sums.take(nth(n), k))
        if n == 2:
            events.append(lambda: sums.send(nth(0)))
        if n == 1:
            events.append(lambda: each(lambda piece_: z_send(*piece_).start(), z_pieces[:2]))
    done = 0
    for t, event in enumerate(events):
        while done < len(work) and done * len(events) <= t * len(work):
            work[done]()
            done += 1
        event()
    for act_ in work[done:]:
        act_()
    stores[1].start()
    stores[2].start()
    each(lambda piece_: z_send(*piece_).start(), z_pieces[2:])
    sums.finish()
    each(lambda g: g.finish(), rows)

    h = hid[...]
    r2 = lax.rsqrt(jnp.mean(h * h, -1, keepdims=True) + EPS)
    weighted = db[...] * gain_rows[1:2, :]
    inner = jnp.mean(weighted * h, -1, keepdims=True)
    total = dy_own[...].astype(f32) + r2 * weighted - h * (r2 * r2 * r2 * inner)
    dh[...] = total
    dhr[...] = total.astype(bf)
    column = jnp.sum((db[...] * h * r2).T, axis=1, keepdims=True)
    lane = lax.broadcasted_iota(jnp.int32, (width, LANES), 1)
    gm[...] = jnp.where(lane == 1, column, 0.0)
    for n, zz in enumerate(EARLY):
        for k in range(pieces):
            z_send(n, k).wait()
        z_sums[n] = (z_p[zz * 2 + p.x].astype(f32) + z_rx[n].astype(f32)).astype(bf)
    each(lambda store: store.wait(), stores)


def run_experts(b, dy_own, dy_all, g_all, weights, hid, gain_rows, depth, cid):
    f32, bf = jnp.float32, jnp.bfloat16
    shape = jax.ShapeDtypeStruct
    vmem = pl.BlockSpec(memory_space=pltpu.VMEM)
    hbm = pl.BlockSpec(memory_space=pl.ANY)
    V = pltpu.VMEM
    tok, width = b.shape
    units = weights[0].shape[1]
    rows = 2 * depth * tok
    return pl.pallas_call(
        functools.partial(experts_kernel, depth),
        out_shape=(
            shape((tok, width), f32),
            shape((tok, width), bf),
            shape((width, LANES), f32),
            shape((len(EARLY), tok, width), bf),
            shape((2 * depth, tok, width), bf),
            shape((3, width, units), bf),
        ),
        in_specs=[vmem] * 5 + [hbm] * 4,
        out_specs=tuple([vmem] * 4 + [hbm] * 2),
        scratch_shapes=[
            V((2 * depth, tok, width), bf),
            V((width, units), bf),
            V((width, units), bf),
            V((width, units), bf),
            V((2 * depth, tok, width), bf),
            V((3, width, units), bf),
            V((len(EARLY), tok, width), bf),
            V((rows, width), bf),
            V((rows, units), bf),
            V((rows, units), bf),
            V((rows, units), bf),
            V((rows, width), bf),
            V((2 * depth, tok, width), bf),
            V((depth, tok, width), bf),
            V((depth, tok, width), bf),
            V((tok, width), f32),
            V((256, rows), bf),
            pltpu.SemaphoreType.DMA((2 * 5 * depth + 8 * depth + 8 + 4 * len(EARLY),)),
        ],
        compiler_params=pltpu.CompilerParams(
            collective_id=cid, has_side_effects=True, vmem_limit_bytes=58 * 2**20
        ),
        name="experts",
    )(b, dy_own, g_all, hid, gain_rows, dy_all, *weights)


def closing_kernel(
    depth, scale, attn_sq, dhr, gain, begin, lse, cosine, sine,
    z_sums, zp_far, wo_far, ot_far, o_far, q_far, qt_far, kv_far, w_far, at_far, x_far, hid_far, dh_far, gm_far, eg,
    out, gin, gq, go, gkv, gg, f0, f1, f2, rms,
    zp, wo, ot, o, q_rows, qt, kv, w, at, x_all, hid, dh, gm,
    dhr_all, dot_, dqt, delta, dkv, do_rows, dq, att, acc,
    z_sum, z_rx, z_rz, go_p, go_rc, go_rx, go_rz, kv_sum, kv_rc, kv_rx, kv_rz,
    gq_p, gq_rc, gq_rx, gq_rz, gk_p, gk_sum, gk_rc, gk_rx, gk_rz,
    e_own, e_core, e_low, e_peer, da_out, da_in, t_out, t_in, sq, square, sems,
):
    f32, bf = jnp.float32, jnp.bfloat16
    p = Place(depth)
    p.greet(sibling=True, other=True)
    wires = Wires(sems)
    u, blk = p.u, p.blk
    tok = dhr.shape[0]
    group, q_half = o.shape
    heads = q_half // HEAD_DIM
    kv_half = 2 * HEAD_DIM
    blocks = kv.shape[0]
    rows_blk = gq.shape[0]

    cols = f0.shape[1]
    rows_e = f0.shape[0]
    es, er, el, ps, pr = (wires.take(1)(0) for _ in range(5))

    def e_cols(core):
        return eg.at[:, :, pl.ds(pl.multiple_of(core * cols, LANES), cols)]

    def e_rows(member):
        return pl.ds(pl.multiple_of(member * rows_e, rows_e), rows_e)

    e_trade = remote(e_cols(1 - p.c), e_core, es, er, p.sibling)
    e_keep = [pltpu.make_async_copy(e_cols(p.c).at[i], e_own, el) for i in range(3)]
    e_swap = remote(e_low, e_peer, ps, pr, p.other)

    def e_join():
        e_trade.wait_recv()
        theirs, mine = e_rows(1 - u), e_rows(u)
        for i in range(3):
            e_keep[i].wait()
            e_low[i] = (e_own[theirs, :].astype(f32) + e_core[i, theirs, :].astype(f32)).astype(bf)
            (f0, f1, f2)[i][...] = e_own[mine, :].astype(f32) + e_core[i, mine, :].astype(f32)
            if i < 2:
                e_keep[i + 1].start()
        e_swap.start()

    def e_done():
        e_swap.wait_recv()
        for i in range(3):
            (f0, f1, f2)[i][...] += e_peer[i].astype(f32)

    ds, dr = wires.take(1)(0), wires.take(1)(0)
    swap = remote(dhr, dhr_all.at[u], ds, dr, p.other)

    pieces = 2
    z_rows = tok // pieces

    def cut(ref, k):
        return ref.at[pl.ds(k * z_rows, z_rows)]

    zs = Scatter(
        p, wires,
        lambda zz, xx, k: cut(zp.at[zz * 2 + xx], k),
        lambda k: cut(z_sum, k),
        lambda zz, k: cut(z_rx.at[zz], k),
        lambda slot, k: cut(z_rz.at[slot], k),
        pieces, ready=EARLY,
    )
    gos = CoreScatter(p, wires, go_p, go_rc, go, go_rx, go_rz)
    kvs = CoreScatter(p, wires, dkv, kv_rc, kv_sum, kv_rx, kv_rz, down_only=True)
    gqs = CoreScatter(p, wires, gq_p, gq_rc, gq, gq_rx, gq_rz)
    gks = CoreScatter(p, wires, gk_p, gk_rc, gk_sum, gk_rx, gk_rz)
    qs, qr = wires.take(3 + depth), wires.take(3 + depth)
    sq_here = sq.at[p.z, p.x, u, p.c]
    sq_core = remote(sq_here, sq_here, qs(0), qr(0), p.sibling)
    sq_other = remote(sq.at[p.z, p.x, u], sq.at[p.z, p.x, u], qs(1), qr(1), p.other)
    sq_across = remote(sq.at[p.z, p.x], sq.at[p.z, p.x], qs(2), qr(2), p.across)

    def sq_along(z, to):
        return remote(sq.at[z], sq.at[z], qs(3 + to), qr(3 + z), p.along(to))

    ls = wires.take(13)
    loads = [
        pltpu.make_async_copy(r, v, ls(i))
        for i, (r, v) in enumerate(
            (
                (zp_far, zp), (wo_far, wo), (ot_far, ot), (o_far, o), (q_far, q_rows), (qt_far, qt), (kv_far, kv),
                (w_far, w), (at_far, at), (x_far, x_all), (hid_far, hid), (dh_far, dh), (gm_far, gm),
            )
        )
    ]
    zl = wires.take(len(EARLY))
    z_loads = [pltpu.make_async_copy(z_sums.at[n], z_rx.at[zz], zl(n)) for n, zz in enumerate(EARLY)]
    swap.start()
    each(lambda load: load.start(), z_loads)
    each(lambda load: load.start(), loads)
    e_trade.start()
    e_keep[0].start()
    loads[0].wait()
    ahead = 2
    for t in range(ahead):
        zs.begin(t)

    each(lambda load: load.wait(), z_loads)
    zs.forward()
    dqt[...] = jnp.zeros(dqt.shape, f32)
    dkv[...] = jnp.zeros(dkv.shape, bf)
    dhr_all[u] = dhr[...]
    e_join()
    zs.land(0)
    zs.begin(ahead)
    each(lambda load: load.wait(), loads[1:])
    swap.wait_recv()

    for m in range(2):
        part = mm(dhr_all[m], wo[...]).astype(bf)
        for h in range(heads):
            do_rows[h * group + m * tok : h * group + (m + 1) * tok, :] = part[:, h * HEAD_DIM : (h + 1) * HEAD_DIM]
    for h in range(heads):
        hs = slice(h * group, (h + 1) * group)
        part = do_rows[hs, :]
        turned = part.astype(f32).T
        dot_[:, hs] = turned.astype(bf)
        delta[0:1, hs] = jnp.sum(turned * ot[:, hs], axis=0, keepdims=True)

    def spread_rows(payload, turned, right, cols=None):
        some = 4

        def rows(i, carry):
            at_rows = pl.ds(pl.multiple_of(i * some * rows_blk, some * rows_blk), some * rows_blk)
            part = mm(turned[at_rows, :], right).astype(bf)
            for n in range(some):
                piece = part[n * rows_blk : (n + 1) * rows_blk, :]
                if cols is None:
                    payload[i * 2 + n // 2, n % 2] = piece
                else:
                    payload[i * 2 + n // 2, n % 2, :, :cols] = piece
            return carry

        lax.fori_loop(0, blocks // some, rows, 0)

    for m in range(2):
        att[:, m * tok : (m + 1) * tok] = flip(dhr_all[m])

    spread_rows(go_p, att, o[...])
    gos.trade()

    background = {}

    def at_tile(j, act):
        background.setdefault(j, []).append(act)

    def z_step(t):
        zs.land(t)
        zs.begin(t + ahead)

    for t in range(1, len(zs.items)):
        at_tile((0, 0, 2, 4, 6, 9, 12, 15)[t], lambda t=t: z_step(t))
    for t in range(depth):
        at_tile((5, 8, 11, 14)[t], lambda t=t: gos.join(t))
    for t in range(3):
        at_tile((11, 14, 15)[t], lambda t=t: gos.land(t))
    for t in range(depth - 1):
        last = 4 * t + 3
        at_tile(last, lambda t=t: kvs.trade(t))
        at_tile(last + 1, lambda t=t: kvs.join(t))
        if t < depth - 2:
            at_tile(last + 6, lambda t=t: kvs.land(t))

    def tile(j, carry):
        def work():
            k = kv[j, :, :HEAD_DIM]
            v = kv[j, :, HEAD_DIM:]
            kt = flip(k)
            bias = hidden_bias(j * group, blk * group, begin[0:1, :], group)
            at_ = [slice(h * group, (h + 1) * group) for h in range(heads)]
            sc = [mm(k, qt[:, hs]) * (scale * LOG2E) + bias for hs in at_]
            dp = [mm(v, dot_[:, hs]) for hs in at_]
            e = [jnp.exp2(s_ - lse[0:1, hs]) for s_, hs in zip(sc, at_)]
            g = [(e_ * (d_ - delta[0:1, hs])).astype(bf) for e_, d_, hs in zip(e, dp, at_)]
            wide_g = jnp.concatenate(g, 1)
            dk = mm(wide_g, q_rows[...])
            dv = mm(jnp.concatenate([e_.astype(bf) for e_ in e], 1), do_rows[...])
            dqt[...] += mm(kt, wide_g)
            dkv[j // 2, j % 2, :, :HEAD_DIM] = (dk * scale).astype(bf)
            dkv[j // 2, j % 2, :, HEAD_DIM:] = dv.astype(bf)

        pl.when(j <= blk)(work)
        for when, acts in background.items():
            pl.when(j == when)(lambda acts=acts: each(lambda act: act(), acts))
        return carry

    lax.fori_loop(0, blocks, tile, 0)

    kvs.trade(depth - 1)

    def back_turn(values):
        return values * cosine[...] - pltpu.roll(values, HEAD_DIM // 2, 1) * sine[...]

    for h in range(heads):
        hs = slice(h * group, (h + 1) * group)
        cs = slice(h * HEAD_DIM, (h + 1) * HEAD_DIM)
        dq[:, cs] = back_turn((dqt[:, hs] * scale).T.astype(bf).astype(f32)).astype(bf)
    kvs.join(depth - 1)

    spread_rows(gq_p, at, dq[...])
    gqs.trade()
    kvs.land(depth - 2)
    gqs.join(0)
    gqs.join(1)
    for m in range(2):
        for cb in range(0, D, 512):
            acc[m * tok : (m + 1) * tok, cb : cb + 512] = contract(
                dq[m * tok : (m + 1) * tok, :], w[cb : cb + 512, :q_half], 1, 1
            )
    kvs.land(depth - 1)
    kvs.release()
    kvs.finish()
    kv_low = kv_sum[...].astype(bf).astype(f32)
    kv_pre = jnp.concatenate([back_turn(kv_low[:, :HEAD_DIM]).astype(bf), kv_low[:, HEAD_DIM:].astype(bf)], 1)

    da_s, da_r = wires.take(3), wires.take(3)
    wide = D // 3
    da_swaps = []
    for i in range(3):
        cb = i * wide
        part = contract(kv_pre, w[cb : cb + wide, q_half : q_half + kv_half], 1, 1)
        acc[:, cb : cb + wide] += part
        theirs = pl.ds(pl.multiple_of((1 - u) * tok, tok), tok)
        da_out[i] = acc[theirs, cb : cb + wide].astype(bf)
        da_swaps.append(remote(da_out.at[i], da_in.at[i], da_s(i), da_r(i), p.other))
        da_swaps[i].start()

    column = jnp.zeros((D, 1), f32)
    for m in range(2):
        xf = x_all[m].astype(f32)
        r1 = lax.rsqrt(jnp.mean(xf * xf, -1, keepdims=True) + EPS)
        terms = acc[m * tok : (m + 1) * tok, :] * xf * r1
        column = column + jnp.sum(terms.T, axis=1, keepdims=True)
    lane = lax.broadcasted_iota(jnp.int32, (D, LANES), 1)
    gain_cols = (jnp.where(lane == 0, column, 0.0) + gm[...]).astype(bf)
    for i in range(blocks):
        gk_p[i // 2, i % 2, :, kv_half:] = gain_cols[i * rows_blk : (i + 1) * rows_blk, :]

    spread_rows(gk_p, at, kv_pre, kv_half)
    gqs.land(0)
    gqs.land(1)
    gks.trade()
    for t in range(depth):
        gks.join(t)
    for t in range(2, depth):
        gqs.join(t)
    gqs.release()

    gos.land(3)
    zs.finish()
    result = hid[...] + z_sum[...]
    out[...] = result.astype(bf)
    spread = lax.broadcasted_iota(jnp.int32, (8, LANES), 1)
    z_sq = jnp.sum(z_sum[...] * z_sum[...])
    r_sq = jnp.sum(result * result)
    sq_here[...] = jnp.where(
        spread == 0, attn_sq[...], jnp.where(spread == 1, z_sq, jnp.where(spread == 2, r_sq, 0.0))
    )
    sq_core.start()
    gks.land(0)
    sq_core.wait_recv()
    sq_other.start()
    gks.land(1)
    gks.land(2)
    sq_other.wait_recv()
    sq_across.start()
    gks.land(3)
    sq_across.wait_recv()
    for d in range(1, depth):
        pl.when(p.z >= d)(lambda d=d: sq_along(p.z, p.z - d).start())
        pl.when(p.z + d < depth)(lambda d=d: sq_along(p.z, p.z + d).start())

    mine = pl.ds(pl.multiple_of(u * tok, tok), tok)
    for i in range(3):
        da_swaps[i].wait_recv()
        acc[mine, i * wide : (i + 1) * wide] += da_in[i].astype(f32)
    da = acc[mine, :]
    xf = x_all[u].astype(f32)
    r1 = lax.rsqrt(jnp.mean(xf * xf, -1, keepdims=True) + EPS)
    weighted = da * gain[0:1, :]
    inner = jnp.mean(weighted * xf, -1, keepdims=True)
    gin[...] = dh[...] + r1 * weighted - xf * (r1 * r1 * r1 * inner)
    for t in range(2, depth):
        gqs.land(t)
    gks.release()
    gks.finish()
    rows_dev = gkv.shape[0]
    theirs = pl.ds(pl.multiple_of((1 - u) * rows_dev, rows_dev), rows_dev)
    own = pl.ds(pl.multiple_of(u * rows_dev, rows_dev), rows_dev)
    t_out[...] = gk_sum[theirs, :]
    ts, tr = wires.take(1)(0), wires.take(1)(0)
    t_swap = remote(t_out, t_in, ts, tr, p.other)
    t_swap.start()
    e_done()
    gos.release()
    gos.finish()
    gqs.finish()
    t_swap.wait_recv()
    for part in range(2):
        here = slice(part * HEAD_DIM, (part + 1) * HEAD_DIM)
        base = part * kv_half
        gkv[:, pl.ds(pl.multiple_of(base + u * HEAD_DIM, LANES), HEAD_DIM)] = gk_sum[own, here]
        gkv[:, pl.ds(pl.multiple_of(base + (1 - u) * HEAD_DIM, LANES), HEAD_DIM)] = t_in[:, here]
    square[...] = jnp.zeros(square.shape, f32)
    square[:rows_dev, :] = gk_sum[own, kv_half:] + t_in[:, kv_half:]
    gg[...] = square[...].T[:8, :]
    sq_core.wait_send()
    sq_other.wait_send()
    sq_across.wait_send()
    for z in range(depth):
        pl.when(p.z != z)(lambda z=z: sq_along(z, z).wait_recv())
        pl.when(p.z != z)(lambda z=z: sq_along(p.z, z).wait_send())
    squares = jnp.zeros((8, LANES), f32)
    for z in range(depth):
        for n in range(8):
            squares = squares + sq[z, n // 4, n // 2 % 2, n % 2]
    rms[...] = jnp.sqrt(squares / (8 * depth * tok * D))
    t_swap.wait_send()
    swap.wait_send()
    e_trade.wait_send()
    e_swap.wait_send()
    for i in range(3):
        da_swaps[i].wait_send()


def closing(attn_sq, dhr, gain, begin, lse, cosine, sine, z_sums, large, eg, depth, scale, cid):
    f32, bf = jnp.float32, jnp.bfloat16
    tok, width = dhr.shape
    group, q_half = large[3].shape
    blocks = large[6].shape[0]
    kv_block = large[6].shape[1:]
    rows_blk = width // blocks
    rows_e, cols = eg.shape[1] // 2, eg.shape[2] // 2
    kv_half = 2 * HEAD_DIM
    shape = jax.ShapeDtypeStruct
    vmem = pl.BlockSpec(memory_space=pltpu.VMEM)
    hbm = pl.BlockSpec(memory_space=pl.ANY)
    V = pltpu.VMEM

    def buffers(block):
        return [
            V((blocks // 2,) + block, bf),
            V((depth,) + block, bf),
            V((depth,) + block, bf),
        ]

    grad = shape((rows_e, cols), f32)
    rows = q_half // HEAD_DIM * group
    return pl.pallas_call(
        functools.partial(closing_kernel, depth, scale),
        out_shape=(
            shape((tok, width), bf),
            shape((tok, width), f32),
            shape((rows_blk, q_half), f32),
            shape((rows_blk, q_half), f32),
            shape((rows_blk // 2, 2 * kv_half), f32),
            shape((8, LANES), f32),
            grad,
            grad,
            grad,
            shape((8, LANES), f32),
        ),
        in_specs=[vmem] * 7 + [hbm] * 15,
        out_specs=tuple([vmem] * 10),
        scratch_shapes=[V(array.shape, array.dtype) for array in large]
        + [
            V((2, tok, width), bf),
            V((HEAD_DIM, rows), bf),
            V((HEAD_DIM, rows), f32),
            V((8, rows), f32),
            V((blocks // 2, 2) + kv_block, bf),
            V((rows, HEAD_DIM), bf),
            V((group, q_half), bf),
            V((width, group), bf),
            V((group, width), f32),
            V((tok, width), f32),
            V((depth, tok, width), bf),
            V((depth, tok, width), bf),
            V((blocks // 2, 2, rows_blk, q_half), bf),
        ]
        + buffers((rows_blk, q_half))
        + [V((group, kv_half), f32)]
        + buffers((group, kv_half))
        + [V((blocks // 2, 2, rows_blk, q_half), bf)]
        + buffers((rows_blk, q_half))
        + [V((blocks // 2, 2, rows_blk, kv_half + LANES), bf), V((rows_blk, kv_half + LANES), f32)]
        + buffers((rows_blk, kv_half + LANES))
        + [
            V((2 * rows_e, cols), bf),
            V((3, 2 * rows_e, cols), bf),
            V((3, rows_e, cols), bf),
            V((3, rows_e, cols), bf),
            V((3, tok, width // 3), bf),
            V((3, tok, width // 3), bf),
            V((rows_blk // 2, kv_half + LANES), f32),
            V((rows_blk // 2, kv_half + LANES), f32),
            V((depth, 2, 2, 2, 8, LANES), f32),
            V((LANES, LANES), f32),
            pltpu.SemaphoreType.DMA((320,)),
        ],
        compiler_params=pltpu.CompilerParams(
            collective_id=cid, has_side_effects=True, vmem_limit_bytes=60 * 2**20
        ),
        name="closing",
    )(attn_sq, dhr, gain, begin, lse, cosine, sine, z_sums, *large, eg)


def deliver_kernel(count, gains, rms, *refs):
    ins, (gain_a, gain_m, rms_out) = refs[:count], refs[count : count + 3]
    outs, held, sems = refs[count + 3 : 2 * count + 3], refs[2 * count + 3 : 3 * count + 3], refs[3 * count + 3]
    loads = [pltpu.make_async_copy(ins[i], held[i], sems.at[i]) for i in range(count)]
    stores = [pltpu.make_async_copy(held[i], outs[i], sems.at[count + i]) for i in range(count)]
    each(lambda load: load.start(), loads)
    gain_a[...] = gains[0:1, : gain_a.shape[1]]
    gain_m[...] = gains[1:2, : gain_m.shape[1]]
    rms_out[...] = rms[0:1, : rms_out.shape[1]]
    for load, store in zip(loads, stores):
        load.wait()
        store.start()
    each(lambda store: store.wait(), stores)


def deliver(gains, rms, arrays, rows):
    count = len(arrays)
    hbm = pl.BlockSpec(memory_space=pl.ANY)
    vmem = pl.BlockSpec(memory_space=pltpu.VMEM)
    small = [jax.ShapeDtypeStruct((1, n), jnp.float32) for n in (rows, rows, 3)]
    return pl.pallas_call(
        functools.partial(deliver_kernel, count),
        out_shape=tuple(small + [jax.ShapeDtypeStruct(a.shape, a.dtype) for a in arrays]),
        in_specs=[vmem] * 2 + [hbm] * count,
        out_specs=tuple([vmem] * 3 + [hbm] * count),
        scratch_shapes=[pltpu.VMEM(a.shape, a.dtype) for a in arrays] + [pltpu.SemaphoreType.DMA((2 * count,))],
        compiler_params=pltpu.CompilerParams(vmem_limit_bytes=60 * 2**20),
        name="deliver",
    )(gains, rms, *arrays)


def planned(
    layer_input,
    grad_output,
    gain_attn,
    gain_moe,
    w_query,
    w_keyval,
    w_out,
    w_gate,
    w_up,
    w_down,
    gate_weights,
    expert_ids,
    doc_starts,
):
    depth = lax.axis_size("blk") // 4
    scale = 1.0 / math.sqrt(HEAD_DIM)
    (
        normed_m, hidden, attn_sq, normed_t, query_rows, query_t, mixed, mixed_t, lse, gain_rows, g_all, inputs,
        begin_rows, cosine, sine, kv_all, w_all, out_w, dy_all, gate_w, up_w, down_w,
    ) = front(
        doc_starts, layer_input, grad_output, gain_attn, gain_moe, w_query, w_keyval, w_out, expert_ids.T, gate_weights.T,
        (w_gate, w_up, w_down), depth, scale, 1,
    )
    grad_hidden, grad_hidden_low, gain_terms, z_sums, z_part, expert_grads = run_experts(
        normed_m, grad_output, dy_all, g_all, (gate_w, up_w, down_w), hidden, gain_rows, depth, 2
    )
    large = (
        z_part, out_w, mixed_t, mixed, query_rows, query_t, kv_all, w_all, normed_t, inputs, hidden, grad_hidden, gain_terms
    )
    results = closing(
        attn_sq, grad_hidden_low, gain_rows, begin_rows, lse, cosine, sine, z_sums, large, expert_grads, depth, scale, 3
    )
    (
        gain_a, gain_m, rms, layer_output, grad_input, part_query, part_out, part_keyval, grad_gate, grad_up, grad_down
    ) = deliver(results[5], results[9], results[:5] + results[6:9], gain_attn.shape[0])
    return (
        layer_output,
        grad_input,
        gain_a.reshape(-1),
        gain_m.reshape(-1),
        part_query,
        part_keyval,
        part_out,
        grad_gate,
        grad_up,
        grad_down,
        rms.reshape(-1),
    )


def solution(mesh):
    in_specs = (
        P(("blk", "ulysses"), None),
        P(("blk", "ulysses"), None),
        P(("blk", "ulysses")),
        P(("blk", "ulysses")),
        P(("blk", "ulysses"), None),
        P(("blk", "ulysses"), None),
        P(("blk", "ulysses"), None),
        P("ulysses", "blk"),
        P("ulysses", "blk"),
        P("ulysses", "blk"),
        P(("blk", "ulysses"), None),
        P(("blk", "ulysses"), None),
        P(),
    )
    out_specs = (
        P(("blk", "ulysses"), None),
        P(("blk", "ulysses"), None),
        P(("blk", "ulysses")),
        P(("blk", "ulysses")),
        P("blk", "ulysses"),
        P(("blk", "ulysses"), None),
        P("blk", "ulysses"),
        P("ulysses", "blk"),
        P("ulysses", "blk"),
        P("ulysses", "blk"),
        P(),
    )
    blocks, members = mesh.shape["blk"], mesh.shape["ulysses"]
    body = planned if blocks == 16 and members == KV_HEADS else local
    return jax.shard_map(body, mesh=mesh, in_specs=in_specs, out_specs=out_specs, check_vma=False)
```

```python
import functools
import math

import jax
import jax.numpy as jnp
import numpy as np
from jax import lax
from jax.experimental import pallas as pl
from jax.experimental.pallas import tpu as pltpu
from jax.sharding import PartitionSpec as P

D = 1536
HEADS = 12
KV_HEADS = 2
HEAD_DIM = 128
TOP = 4


EPS = 1e-06
ROPE_BASE = 1000000.0
NEG = -1e30
EARLY = (0,)


def rotate(values, positions, sign):
    half = values.shape[-1] // 2
    freq = ROPE_BASE ** (-jnp.arange(half, dtype=jnp.float32) * 2.0 / values.shape[-1])
    angle = positions.astype(jnp.float32)[:, None] * freq[None, :]
    cosine = jnp.cos(angle)[:, None, :]
    sine = sign * jnp.sin(angle)[:, None, :]
    first = values[..., :half]
    second = values[..., half:]
    return jnp.concatenate([first * cosine - second * sine, second * cosine + first * sine], -1)


def doc_begin(positions, doc_starts):
    return jnp.max(
        jnp.where(doc_starts[None, :] <= positions[:, None], doc_starts[None, :], 0), axis=1
    )


def norm_back(values, factor, gain, grad):
    weighted = grad * gain
    inner = jnp.mean(weighted * values, -1, keepdims=True)
    return factor * weighted - values * factor * factor * factor * inner


def visible_mask(q_pos, q_begin, k_pos):
    return (k_pos[None, :] >= q_begin[:, None]) & (k_pos[None, :] <= q_pos[:, None])


def split_blocks(array):
    rows = array.shape[0]
    size = min(rows, 512)
    return (array.reshape((rows // size, size) + array.shape[1:]), size)


def contract(left, right, left_dim, right_dim):
    return lax.dot_general(
        left, right, (((left_dim,), (right_dim,)), ((), ())), preferred_element_type=jnp.float32
    )


def reorder_rows(array, outer, inner):
    rows = array.shape[0]
    shaped = array.reshape((outer, inner, rows // (outer * inner)) + array.shape[1:])
    return jnp.swapaxes(shaped, 0, 1).reshape(array.shape)


def route(payload):
    return lax.all_to_all(payload, "blk", split_axis=0, concat_axis=0, tiled=True)


def backward_block(queries, grads, lse, delta, q_pos, q_begin, keys, values, k_start, scale):
    k_pos = k_start + jnp.arange(keys.shape[0], dtype=jnp.int32)
    visible = visible_mask(q_pos, q_begin, k_pos)[None]
    scores = jnp.einsum("qhd,kd->hqk", queries, keys, preferred_element_type=jnp.float32) * scale
    probs = jnp.where(visible, jnp.exp(scores - lse[:, :, None]), 0.0)
    probs_low = probs.astype(jnp.bfloat16)
    grad_probs = jnp.einsum("qhd,kd->hqk", grads, values, preferred_element_type=jnp.float32)
    grad_scores = (probs * (grad_probs - delta[:, :, None])).astype(jnp.bfloat16)
    part_q = (
        jnp.einsum("hqk,kd->qhd", grad_scores, keys, preferred_element_type=jnp.float32) * scale
    )
    part_k = (
        jnp.einsum("hqk,qhd->kd", grad_scores, queries, preferred_element_type=jnp.float32) * scale
    )
    part_v = jnp.einsum("hqk,qhd->kd", probs_low, grads, preferred_element_type=jnp.float32)
    return (part_q, part_k, part_v)


def local(
    layer_input,
    grad_output,
    gain_attn,
    gain_moe,
    w_query,
    w_keyval,
    w_out,
    w_gate,
    w_up,
    w_down,
    gate_weights,
    expert_ids,
    doc_starts,
):
    n_blk = lax.axis_size("blk")
    n_uly = lax.axis_size("ulysses")
    tok = layer_input.shape[0]
    group = tok * n_uly
    heads_dev = HEADS // n_uly
    per_kv = HEADS // KV_HEADS
    which = [c * heads_dev // per_kv for c in range(n_uly)]
    kv_width = KV_HEADS * HEAD_DIM
    q_width = HEADS * HEAD_DIM
    scale = 1.0 / math.sqrt(HEAD_DIM)
    blk_index = lax.axis_index("blk")
    device = blk_index * n_uly + lax.axis_index("ulysses")
    tok_pos = device * tok + jnp.arange(tok, dtype=jnp.int32)
    places = tok_pos - doc_begin(tok_pos, doc_starts)
    gain_a, gain_m, query_w, keyval_w, out_w = (
        lax.all_gather(gain_attn, ("blk", "ulysses"), axis=0, tiled=True),
        lax.all_gather(gain_moe, ("blk", "ulysses"), axis=0, tiled=True),
        lax.all_gather(w_query, ("blk", "ulysses"), axis=0, tiled=True),
        lax.all_gather(w_keyval, ("blk", "ulysses"), axis=0, tiled=True),
        lax.all_gather(w_out, ("blk", "ulysses"), axis=0, tiled=True),
    )
    gate_w, up_w, down_w = (
        lax.all_gather(w_gate, "ulysses", axis=0, tiled=True),
        lax.all_gather(w_up, "ulysses", axis=0, tiled=True),
        lax.all_gather(w_down, "ulysses", axis=0, tiled=True),
    )
    gain_a = gain_a.astype(jnp.float32)
    gain_m = gain_m.astype(jnp.float32)
    inputs = layer_input.astype(jnp.float32)
    factor_a = lax.rsqrt(jnp.mean(inputs * inputs, -1, keepdims=True) + EPS)
    normed_a = (inputs * factor_a * gain_a).astype(jnp.bfloat16)
    query_raw = jnp.dot(normed_a, query_w, preferred_element_type=jnp.float32)
    keyval_raw = jnp.dot(normed_a, keyval_w, preferred_element_type=jnp.float32)
    queries = rotate(query_raw.reshape(tok, HEADS, HEAD_DIM), places, 1.0).astype(jnp.bfloat16)
    keys = rotate(keyval_raw[:, :kv_width].reshape(tok, KV_HEADS, HEAD_DIM), places, 1.0).astype(
        jnp.bfloat16
    )
    values = keyval_raw[:, kv_width:].reshape(tok, KV_HEADS, HEAD_DIM).astype(jnp.bfloat16)
    key_copies = jnp.stack([keys[:, j] for j in which], 1)
    value_copies = jnp.stack([values[:, j] for j in which], 1)
    spread_normed = jnp.broadcast_to(normed_a[:, None, :], (tok, n_uly, D))
    head_q, head_k, head_v, head_normed = (
        lax.all_to_all(queries, "ulysses", split_axis=1, concat_axis=0, tiled=True),
        lax.all_to_all(key_copies, "ulysses", split_axis=1, concat_axis=0, tiled=True),
        lax.all_to_all(value_copies, "ulysses", split_axis=1, concat_axis=0, tiled=True),
        lax.all_to_all(spread_normed, "ulysses", split_axis=1, concat_axis=0, tiled=True),
    )
    key_local = head_k[:, 0, :]
    value_local = head_v[:, 0, :]
    normed_group = head_normed[:, 0, :]
    q_pos = blk_index * group + jnp.arange(group, dtype=jnp.int32)
    q_begin = doc_begin(q_pos, doc_starts)
    start_state = (
        jnp.full((heads_dev, group), NEG, jnp.float32),
        jnp.zeros((heads_dev, group), jnp.float32),
        jnp.zeros((group, heads_dev, HEAD_DIM), jnp.float32),
    )
    state = start_state
    key_rows = lax.all_gather(key_local, "blk", axis=0, tiled=True)
    value_rows = lax.all_gather(value_local, "blk", axis=0, tiled=True)
    key_blocks, size = split_blocks(key_rows)
    value_blocks, _ = split_blocks(value_rows)

    def attend_step(inner, item):
        key_blk, value_blk, number = item
        k_start = number * size
        live = (k_start <= q_pos[-1]) & (k_start + size - 1 >= q_begin[0])

        def attend_work(current):
            top, total, acc = current
            k_pos = k_start + jnp.arange(size, dtype=jnp.int32)
            visible = visible_mask(q_pos, q_begin, k_pos)[None]
            scores = (
                jnp.einsum("qhd,kd->hqk", head_q, key_blk, preferred_element_type=jnp.float32)
                * scale
            )
            scores = jnp.where(visible, scores, NEG)
            new_top = jnp.maximum(top, jnp.max(scores, -1))
            weights = jnp.where(visible, jnp.exp(scores - new_top[:, :, None]), 0.0)
            keep = jnp.exp(top - new_top)
            total = total * keep + jnp.sum(weights, -1)
            acc = acc * jnp.transpose(keep)[:, :, None] + jnp.einsum(
                "hqk,kd->qhd",
                weights.astype(jnp.bfloat16),
                value_blk,
                preferred_element_type=jnp.float32,
            )
            return (new_top, total, acc)

        return (lax.cond(live, attend_work, lambda current: current, inner), None)

    state, _ = lax.scan(
        attend_step,
        state,
        (key_blocks, value_blocks, jnp.arange(key_blocks.shape[0], dtype=jnp.int32)),
    )
    top, total, acc = state
    mixed = acc / jnp.transpose(total)[:, :, None]
    mixed_low = mixed.astype(jnp.bfloat16)
    lse = top + jnp.log(total)
    attended = lax.all_to_all(
        mixed_low, "ulysses", split_axis=0, concat_axis=1, tiled=True
    ).reshape(tok, q_width)
    attn_branch = contract(attended, out_w, 1, 1)
    hidden = inputs + attn_branch
    factor_m = lax.rsqrt(jnp.mean(hidden * hidden, -1, keepdims=True) + EPS)
    normed_m = (hidden * factor_m * gain_m).astype(jnp.bfloat16)
    experts = n_blk // 2
    capacity = min(tok, 2 * tok * TOP // experts)
    flat_ids = expert_ids.reshape(-1)
    picks = (flat_ids[:, None] == jnp.arange(experts, dtype=jnp.int32)[None, :]).astype(jnp.int32)
    slots = jnp.sum((jnp.cumsum(picks, 0) - 1) * picks, -1)

    def dispatch(rows):
        buffer = jnp.zeros((experts, capacity, D), jnp.bfloat16).at[flat_ids, slots].set(rows)
        return route(jnp.repeat(buffer, 2, axis=0)).reshape(n_blk * capacity, D)

    def collect(rows):
        back = route(rows.astype(jnp.bfloat16).reshape(n_blk, capacity, D))
        return back[2 * flat_ids, slots].astype(jnp.float32) + back[2 * flat_ids + 1, slots].astype(
            jnp.float32
        )

    expert_in = dispatch(jnp.repeat(normed_m, TOP, axis=0))
    gate_pre = jnp.dot(expert_in, gate_w, preferred_element_type=jnp.float32)
    up_pre = jnp.dot(expert_in, up_w, preferred_element_type=jnp.float32)
    act = (jax.nn.silu(gate_pre) * up_pre).astype(jnp.bfloat16)
    expert_out = contract(act, down_w, 1, 1)
    returned = collect(expert_out).reshape(tok, TOP, D)
    moe_branch = jnp.sum(gate_weights[:, :, None] * returned, 1)
    result = hidden + moe_branch
    layer_output = result.astype(jnp.bfloat16)
    grad_res = grad_output.astype(jnp.float32)
    routed_grad = (
        (gate_weights[:, :, None] * grad_res[:, None, :]).reshape(tok * TOP, D).astype(jnp.bfloat16)
    )
    expert_grad = dispatch(routed_grad)
    grad_act = jnp.dot(expert_grad, down_w, preferred_element_type=jnp.float32)
    grad_down = contract(expert_grad, act, 0, 0)
    sig = jax.nn.sigmoid(gate_pre)
    grad_gate_pre = (grad_act * up_pre * sig * (1.0 + gate_pre * (1.0 - sig))).astype(jnp.bfloat16)
    grad_up_pre = (grad_act * gate_pre * sig).astype(jnp.bfloat16)
    grad_gate = contract(expert_in, grad_gate_pre, 0, 0)
    grad_up = contract(expert_in, grad_up_pre, 0, 0)
    grad_in = contract(grad_gate_pre, gate_w, 1, 1) + contract(grad_up_pre, up_w, 1, 1)
    grad_normed_m = jnp.sum(collect(grad_in).reshape(tok, TOP, D), 1)
    grad_gain_m = jnp.sum(grad_normed_m * hidden * factor_m, 0)
    grad_hidden = grad_res + norm_back(hidden, factor_m, gain_m, grad_normed_m)
    grad_hidden_low = grad_hidden.astype(jnp.bfloat16)
    grad_attended = jnp.dot(grad_hidden_low, out_w, preferred_element_type=jnp.float32).astype(
        jnp.bfloat16
    )
    spread_hidden = jnp.broadcast_to(grad_hidden_low[:, None, :], (tok, n_uly, D))
    head_grad, head_hidden = (
        lax.all_to_all(
            grad_attended.reshape(tok, HEADS, HEAD_DIM),
            "ulysses",
            split_axis=1,
            concat_axis=0,
            tiled=True,
        ),
        lax.all_to_all(spread_hidden, "ulysses", split_axis=1, concat_axis=0, tiled=True),
    )
    grad_out_slice = contract(
        head_hidden[:, 0, :], mixed_low.reshape(group, heads_dev * HEAD_DIM), 0, 0
    )
    delta = jnp.transpose(jnp.sum(head_grad.astype(jnp.float32) * mixed, -1))
    total_keys = group * n_blk
    zero_q = jnp.zeros((group, heads_dev, HEAD_DIM), jnp.float32)
    fold_start = (
        zero_q,
        jnp.zeros((total_keys, HEAD_DIM), jnp.float32),
        jnp.zeros((total_keys, HEAD_DIM), jnp.float32),
    )
    state = fold_start
    key_rows = lax.all_gather(key_local, "blk", axis=0, tiled=True)
    value_rows = lax.all_gather(value_local, "blk", axis=0, tiled=True)
    key_blocks, grads_size = split_blocks(key_rows)
    value_blocks, _ = split_blocks(value_rows)

    def grads_step(inner, item):
        key_blk, value_blk, number = item
        k_start = number * grads_size
        live = (k_start <= q_pos[-1]) & (k_start + grads_size - 1 >= q_begin[0])

        def grads_work(current):
            part_q, part_k, part_v = backward_block(
                head_q, head_grad, lse, delta, q_pos, q_begin, key_blk, value_blk, k_start, scale
            )
            grad_q, grad_keys, grad_values = current
            grad_keys = lax.dynamic_update_slice_in_dim(
                grad_keys,
                lax.dynamic_slice_in_dim(grad_keys, k_start, grads_size, 0) + part_k,
                k_start,
                0,
            )
            grad_values = lax.dynamic_update_slice_in_dim(
                grad_values,
                lax.dynamic_slice_in_dim(grad_values, k_start, grads_size, 0) + part_v,
                k_start,
                0,
            )
            return (grad_q + part_q, grad_keys, grad_values)

        return (lax.cond(live, grads_work, lambda current: current, inner), None)

    state, _ = lax.scan(
        grads_step,
        state,
        (key_blocks, value_blocks, jnp.arange(key_blocks.shape[0], dtype=jnp.int32)),
    )
    grad_q = state[0]
    grad_k, grad_v = (
        lax.psum_scatter(state[1], "blk", scatter_dimension=0, tiled=True),
        lax.psum_scatter(state[2], "blk", scatter_dimension=0, tiled=True),
    )
    group_places = q_pos - q_begin
    grad_q_pre = rotate(grad_q.astype(jnp.bfloat16).astype(jnp.float32), group_places, -1.0).astype(
        jnp.bfloat16
    )
    grad_query_slice = contract(normed_group, grad_q_pre.reshape(group, heads_dev * HEAD_DIM), 0, 0)
    token_q, token_k, token_v = (
        lax.all_to_all(grad_q_pre, "ulysses", split_axis=0, concat_axis=1, tiled=True),
        lax.all_to_all(
            grad_k.astype(jnp.bfloat16)[:, None, :],
            "ulysses",
            split_axis=0,
            concat_axis=1,
            tiled=True,
        ),
        lax.all_to_all(
            grad_v.astype(jnp.bfloat16)[:, None, :],
            "ulysses",
            split_axis=0,
            concat_axis=1,
            tiled=True,
        ),
    )
    summed_k = []
    summed_v = []
    for head in range(KV_HEADS):
        members = [c for c in range(n_uly) if which[c] == head]
        summed_k.append(sum((token_k[:, c].astype(jnp.float32) for c in members)))
        summed_v.append(sum((token_v[:, c].astype(jnp.float32) for c in members)))
    grad_key_heads = jnp.stack(summed_k, 1)
    grad_value_heads = jnp.stack(summed_v, 1)
    grad_query_pre = token_q.reshape(tok, q_width)
    grad_key_pre = rotate(grad_key_heads, places, -1.0).reshape(tok, kv_width)
    grad_keyval_pre = jnp.concatenate(
        [grad_key_pre, grad_value_heads.reshape(tok, kv_width)], 1
    ).astype(jnp.bfloat16)
    grad_normed_a = contract(grad_query_pre, query_w, 1, 1) + contract(
        grad_keyval_pre, keyval_w, 1, 1
    )
    grad_keyval_w = contract(normed_a, grad_keyval_pre, 0, 0)
    grad_gain_a = jnp.sum(grad_normed_a * inputs * factor_a, 0)
    grad_input = grad_hidden + norm_back(inputs, factor_a, gain_a, grad_normed_a)
    n_dev = n_blk * n_uly
    squares = jnp.stack(
        [
            jnp.sum(attn_branch * attn_branch),
            jnp.sum(moe_branch * moe_branch),
            jnp.sum(result * result),
        ]
    )
    square_rows = jnp.broadcast_to(squares[None, :], (n_dev, 3))
    part_gate, part_up, part_down, uly_gain_a, uly_gain_m, uly_keyval, uly_squares = (
        lax.psum_scatter(
            grad_gate.astype(jnp.bfloat16), "ulysses", scatter_dimension=0, tiled=True
        ).astype(jnp.float32),
        lax.psum_scatter(
            grad_up.astype(jnp.bfloat16), "ulysses", scatter_dimension=0, tiled=True
        ).astype(jnp.float32),
        lax.psum_scatter(
            grad_down.astype(jnp.bfloat16), "ulysses", scatter_dimension=0, tiled=True
        ).astype(jnp.float32),
        lax.psum_scatter(
            reorder_rows(grad_gain_a, n_blk, n_uly).astype(jnp.bfloat16),
            "ulysses",
            scatter_dimension=0,
            tiled=True,
        ).astype(jnp.float32),
        lax.psum_scatter(
            reorder_rows(grad_gain_m, n_blk, n_uly).astype(jnp.bfloat16),
            "ulysses",
            scatter_dimension=0,
            tiled=True,
        ).astype(jnp.float32),
        lax.psum_scatter(
            reorder_rows(grad_keyval_w, n_blk, n_uly).astype(jnp.bfloat16),
            "ulysses",
            scatter_dimension=0,
            tiled=True,
        ).astype(jnp.float32),
        lax.psum_scatter(
            square_rows.astype(jnp.bfloat16), "ulysses", scatter_dimension=0, tiled=True
        ).astype(jnp.float32),
    )
    part_outw, part_query, part_gain_a, part_gain_m, part_keyval, square_row = (
        lax.psum_scatter(grad_out_slice, "blk", scatter_dimension=0, tiled=True),
        lax.psum_scatter(grad_query_slice, "blk", scatter_dimension=0, tiled=True),
        lax.psum_scatter(uly_gain_a, "blk", scatter_dimension=0, tiled=True),
        lax.psum_scatter(uly_gain_m, "blk", scatter_dimension=0, tiled=True),
        lax.psum_scatter(uly_keyval, "blk", scatter_dimension=0, tiled=True),
        lax.psum_scatter(uly_squares, "blk", scatter_dimension=0, tiled=True),
    )
    branch_rms = jnp.sqrt(square_row[0] / (tok * n_dev * D))
    return (
        layer_output,
        grad_input,
        part_gain_a,
        part_gain_m,
        part_query,
        part_keyval,
        part_outw,
        part_gate,
        part_up,
        part_down,
        branch_rms,
    )


MESH = pl.DeviceIdType.MESH
LANES = 128
LOG2E = 1.4426950408889634


class Place:
    def __init__(self, depth):
        self.blk = lax.axis_index("blk")
        self.u = lax.axis_index("ulysses")
        self.depth = depth
        self.z = self.blk // 4
        self.x = (self.blk // 2) % 2
        self.c = self.blk % 2
        self.up = (self.blk + 4, self.u)
        self.down = (self.blk - 4, self.u)
        self.across = (self.blk + 2 - 4 * self.x, self.u)
        self.sibling = (self.blk + 1 - 2 * self.c, self.u)
        self.other = (self.blk, 1 - self.u)
        self.has_up = self.z < depth - 1
        self.has_down = self.z > 0

    def along(self, z):
        return (self.blk + 4 * (z - self.z), self.u)

    def slot(self, z, x, c):
        return z * 4 + x * 2 + c

    def greet(self, sibling=False, other=False, plane=True):
        barrier = pltpu.get_barrier_semaphore()

        def hail(device):
            pl.semaphore_signal(barrier, inc=1, device_id=device, device_id_type=MESH)

        count = 0
        if plane:
            hail(self.across)
            for d in range(1, self.depth):
                pl.when(self.z >= d)(lambda d=d: hail(self.along(self.z - d)))
                pl.when(self.z + d < self.depth)(lambda d=d: hail(self.along(self.z + d)))
            count = self.depth
        if sibling:
            hail(self.sibling)
            count = count + 1
        if other:
            hail(self.other)
            count = count + 1
        pl.semaphore_wait(barrier, count)


class Wires:
    def __init__(self, sems):
        self.sems = sems
        self.used = 0

    def take(self, count):
        base = self.used
        self.used += count
        return lambda index: self.sems.at[base + index]


def each(act, items):
    for item in items:
        act(item)


def remote(src, dst, send, recv, device):
    return pltpu.make_async_remote_copy(
        src_ref=src, dst_ref=dst, send_sem=send, recv_sem=recv, device_id=device, device_id_type=MESH
    )


class Gather:
    def __init__(self, place, wires, src, out, cores, up_only=False, chain=False, far=False):
        self.p, self.src, self.out, self.cores, self.up_only, self.chain = place, src, out, cores, up_only, chain
        n = place.depth
        self.s_z = [wires.take(n) for _ in range(2 if chain else 1)]
        self.s_across = wires.take(n)
        self.r_z, self.r_x = wires.take(n), wires.take(n)
        if cores:
            self.s_core, self.r_core = wires.take(2 * n), wires.take(2 * n)
        self.far = wires.take(1)(0) if far else None

    def _across(self, zz, xx, src=None):
        dst = self.out(zz, xx, self.p.c)
        return remote(dst if src is None else src, dst, self.s_across(zz), self.r_x(zz), self.p.across)

    def _core(self, zz, xx, src=None):
        dst = self.out(zz, xx, self.p.c)
        at = zz * 2 + xx
        return remote(dst if src is None else src, dst, self.s_core(at), self.r_core(at), self.p.sibling)

    def _along(self, zz, to, src=None):
        p = self.p
        dst = self.out(zz, p.x, p.c)
        return remote(dst if src is None else src, dst, self.s_z[0](to), self.r_z(zz), p.along(to))

    def _next(self, zz, up, src=None):
        p = self.p
        dst = self.out(zz, p.x, p.c)
        return remote(
            dst if src is None else src, dst, self.s_z[up](zz), self.r_z(zz), p.along(p.z + (1 if up else -1))
        )

    def start_z(self, in_place=False):
        p = self.p
        src = None if in_place else self.src
        if self.chain:
            pl.when(p.has_up)(lambda: self._next(p.z, 1, src).start())
            pl.when(p.has_down)(lambda: self._next(p.z, 0, src).start())
            return
        for d in range(1, p.depth):
            pl.when(p.z + d < p.depth)(lambda d=d: self._along(p.z, p.z + d, src).start())
            if not self.up_only:
                pl.when(p.z >= d)(lambda d=d: self._along(p.z, p.z - d, src).start())

    def start_x(self, in_place=False):
        p = self.p
        src = None if in_place else self.src
        self._across(p.z, p.x, src).start()
        if self.cores:
            self._core(p.z, p.x, src).start()
        if self.far is not None:
            pltpu.make_async_copy(self.src, self.out(p.z, p.x, p.c), self.far).start()
        elif not in_place:
            self.out(p.z, p.x, p.c)[...] = self.src[...]

    def start(self, in_place=False):
        self.start_z(in_place)
        self.start_x(in_place)

    def hop(self, d):
        p = self.p

        def take(zz, up):
            remote(
                self.out(zz, p.x, p.c), self.out(zz, p.x, p.c), self.s_z[0](0), self.r_z(zz), p.across
            ).wait_recv()
            if self.chain:
                pl.when(p.has_up if up else p.has_down)(lambda: self._next(zz, up).start())
            self._across(zz, p.x).start()
            if self.cores:
                self._core(zz, p.x).start()

        pl.when(p.z >= d)(lambda: take(p.z - d, 1))
        if not self.up_only:
            pl.when(p.z + d < p.depth)(lambda: take(p.z + d, 0))

    def cross(self, d):
        p = self.p

        def take(zz):
            self._across(zz, 1 - p.x).wait_recv()
            if self.cores:
                self._core(zz, 1 - p.x).start()

        if isinstance(d, int) and d == 0:
            take(p.z)
        else:
            pl.when(p.z >= d)(lambda: take(p.z - d))
            if not self.up_only:
                pl.when(p.z + d < p.depth)(lambda: take(p.z + d))

    def crossed(self, zz):
        self._across(zz, 1 - self.p.x).wait_recv()

    def core(self, zz, xx):
        self._core(zz, xx).wait_recv()

    def finish(self, cores_taken=False):
        p = self.p
        for zz in range(p.depth):

            def ends(zz=zz):
                if self.cores:
                    for xx in range(2):
                        if not cores_taken:
                            self._core(zz, xx).wait_recv()
                        self._core(zz, xx).wait_send()
                self._across(zz, p.x).wait_send()

            if self.up_only and zz > 0:
                pl.when(p.z >= zz)(ends)
            else:
                ends()
            if self.chain:
                pl.when(p.has_up & (p.z >= zz))(lambda zz=zz: self._next(zz, 1).wait_send())
                pl.when(p.has_down & (p.z <= zz))(lambda zz=zz: self._next(zz, 0).wait_send())
            else:
                away = (p.z < zz) if self.up_only else (p.z != zz)
                pl.when(away)(lambda zz=zz: self._along(p.z, zz).wait_send())
        if self.far is not None:
            pltpu.make_async_copy(self.src, self.out(p.z, p.x, p.c), self.far).wait()


class Scatter:
    def __init__(self, place, wires, part, out, rx, rz, pieces, down_only=False, ready=()):
        self.ready = ready
        self.p, self.part, self.out, self.rx, self.rz = place, part, out, rx, rz
        n = place.depth
        total = n * pieces
        self.pieces, self.down_only = pieces, down_only
        self.sx, self.cx = wires.take(total), wires.take(total)
        self.sz, self.cz = wires.take(total), wires.take(total)
        if down_only:
            self.order = list(range(n))
        else:
            self.order = [n - 1] + list(range(n - 1))
        self.items = [(zz, k) for zz in self.order if zz not in ready for k in range(pieces)]

    def _x(self, zz, k):
        i = zz * self.pieces + k
        return remote(self.part(zz, 1 - self.p.x, k), self.rx(zz, k), self.sx(i), self.cx(i), self.p.across)

    def _z(self, zz, k, source=None):
        p = self.p
        source = p.z if source is None else source
        return remote(
            self.rx(zz, k),
            self.rz(source, k),
            self.sz(zz * self.pieces + k),
            self.cz(source * self.pieces + k),
            p.along(zz),
        )

    def _live(self, zz, act):
        if self.down_only and zz > 0:
            pl.when(self.p.z >= zz)(act)
        else:
            act()

    def begin(self, t):
        if t < len(self.items):
            zz, k = self.items[t]
            self._live(zz, lambda: self._x(zz, k).start())

    def send(self, zz):
        for k in range(self.pieces):
            self._x(zz, k).start()

    def take(self, zz, k):
        p = self.p

        def act():
            self._x(zz, k).wait_recv()

            def forward():
                total = self.part(zz, p.x, k)[...].astype(jnp.float32)
                total = total + self.rx(zz, k)[...].astype(jnp.float32)
                self.rx(zz, k)[...] = total.astype(jnp.bfloat16)
                self._z(zz, k).start()

            pl.when(p.z != zz)(forward)

        self._live(zz, act)

    def land(self, t):
        self.take(*self.items[t])

    def forward(self):
        for zz in self.ready:
            for k in range(self.pieces):
                pl.when(self.p.z != zz)(lambda zz=zz, k=k: self._z(zz, k).start())

    def finish(self):
        p = self.p
        n = p.depth
        for zz, k in [(zz, k) for zz in self.order for k in range(self.pieces)]:
            if zz not in self.ready:
                self._live(zz, lambda zz=zz, k=k: self._x(zz, k).wait_send())
            away = (p.z > zz) if self.down_only else (p.z != zz)
            pl.when(away)(lambda zz=zz, k=k: self._z(zz, k).wait_send())

            def store(zz=zz, k=k):
                total = self.rx(zz, k)[...].astype(jnp.float32)
                if zz not in self.ready:
                    total = total + self.part(zz, p.x, k)[...].astype(jnp.float32)
                for source in range(zz + 1 if self.down_only else 0, n):
                    if source != zz:
                        self._z(zz, k, source).wait_recv()
                        total = total + self.rz(source, k)[...].astype(jnp.float32)
                self.out(k)[...] = total

            pl.when(p.z == zz)(store)


class CoreScatter:
    def __init__(self, place, wires, src, rc, out, rx, rz, down_only=False):
        self.p, self.src, self.rc, self.down_only = place, src, rc, down_only
        n = place.depth
        self.sc, self.cc = wires.take(n), wires.take(n)
        self.plane = Scatter(
            place, wires, lambda zz, xx, k: rc.at[zz * 2 + xx], lambda k: out,
            lambda zz, k: rx.at[zz], lambda source, k: rz.at[source], 1, down_only,
        )
        self.order = self.plane.order

    def _trade(self, zz):
        p = self.p
        if self.down_only:
            at = pl.ds(2 * zz, 2)
            return remote(self.src.at[at, 1 - p.c], self.rc.at[at], self.sc(zz), self.cc(zz), p.sibling)
        return remote(self.src.at[:, 1 - p.c], self.rc, self.sc(0), self.cc(0), p.sibling)

    def trade(self, t=0):
        zz = self.order[t]
        self.plane._live(zz, lambda: self._trade(zz).start())

    def join(self, t):
        p = self.p
        zz = self.order[t]

        def act():
            if self.down_only or t == 0:
                self._trade(zz).wait_recv()
            for xx in range(2):
                at = zz * 2 + xx
                self.rc[at] = (
                    self.src[at, p.c].astype(jnp.float32) + self.rc[at].astype(jnp.float32)
                ).astype(jnp.bfloat16)

        self.plane._live(zz, act)
        self.plane.begin(t)

    def land(self, t):
        self.plane.land(t)

    def release(self):
        for t, zz in enumerate(self.order):
            if self.down_only or t == 0:
                self.plane._live(zz, lambda zz=zz: self._trade(zz).wait_send())

    def finish(self):
        self.plane.finish()


def mm(left, right):
    return jnp.dot(left, right, preferred_element_type=jnp.float32)


def flip(tile):
    return tile.astype(jnp.float32).T.astype(jnp.bfloat16)


def hidden_bias(first_key, first_query, begin, keys):
    queries = begin.shape[1]
    k_pos = first_key + lax.broadcasted_iota(jnp.int32, (keys, queries), 0)
    q_pos = first_query + lax.broadcasted_iota(jnp.int32, (keys, queries), 1)
    return jnp.where((k_pos >= begin) & (k_pos <= q_pos), 0.0, NEG)


def front_kernel(
    depth, scale, docs, x, dy, gain_a, gain_m, wq, wkv, wo, ids, shares_of, freq, e0, e1, e2,
    b, hid, attn_sq, normed_t, q_rows, qt, o, ot, lse, gain_rows, g_all, x_all, begin, cosine, sine,
    kv_out, w_out, wo_out, dy_all, f0, f1, f2,
    kv, w_all, wo_all, own, square, g_own, wa_own, normed, raw, top, total, acc, p_out, p_in, sems,
):
    f32, bf = jnp.float32, jnp.bfloat16
    p = Place(depth)
    p.greet(sibling=True, other=True)
    wires = Wires(sems)
    u, blk = p.u, p.blk
    tok, width = x.shape
    group, q_half = o.shape
    heads = q_half // HEAD_DIM
    kv_half = 2 * HEAD_DIM
    rows_dev = wq.shape[0]
    half, cols = e0.shape
    experts = 2 * depth

    def rows_of(ref, z, xx, c, member):
        row = (p.slot(z, xx, c) * 2 + member) * rows_dev
        return ref.at[pl.ds(pl.multiple_of(row, 16), rows_dev)]

    wa_mine = Gather(p, wires, wa_own.at[u], lambda z, xx, c: rows_of(w_all, z, xx, c, u), True, chain=True)
    wa_peer = Gather(p, wires, None, lambda z, xx, c: rows_of(w_all, z, xx, c, 1 - u), True, chain=True)
    wos = Gather(
        p, wires, None,
        lambda z, xx, c: wo_all.at[pl.ds(pl.multiple_of(p.slot(z, xx, c) * 2 * rows_dev, 16), 2 * rows_dev)],
        True, chain=True,
    )
    kvs = Gather(p, wires, None, lambda z, xx, c: kv.at[p.slot(z, xx, c)], True, up_only=True)
    piece = tok // 2
    dys = [
        Gather(
            p, wires, dy.at[pl.ds(k * piece, piece)],
            lambda z, xx, c, k=k: dy_all.at[z * 2 + xx, pl.ds(k * piece, piece)], False, chain=True, far=True,
        )
        for k in range(2)
    ]
    gws = Gather(p, wires, g_own, lambda z, xx, c: g_all.at[z * 2 + xx], False, chain=True)
    ws, wr = wires.take(2), wires.take(2)
    xs, xr = wires.take(1)(0), wires.take(1)(0)
    es, er = wires.take(3), wires.take(3)
    cs, cr = wires.take(6), wires.take(6)
    ps, pr = wires.take(3), wires.take(3)

    for h in range(2):
        wa_own[h, :, :q_half] = wq[:, h * q_half : (h + 1) * q_half]
        for part in range(2):
            wa_own[h, :, q_half + part * HEAD_DIM : q_half + (part + 1) * HEAD_DIM] = wkv[
                :, (part * 2 + h) * HEAD_DIM : (part * 2 + h + 1) * HEAD_DIM
            ]
    square[...] = jnp.zeros(square.shape, f32)
    square[0:1, :rows_dev] = gain_a[...].astype(f32)
    square[1:2, :rows_dev] = gain_m[...].astype(f32)
    columns = square[...].T[:rows_dev, :].astype(bf)
    for h in range(2):
        wa_own[h, :, q_half + kv_half :] = columns

    wa_swap = remote(wa_own.at[1 - u], rows_of(w_all, p.z, p.x, p.c, u), ws(0), wr(0), p.other)
    wo_swap = remote(
        wo.at[:, pl.ds(pl.multiple_of((1 - u) * q_half, LANES), q_half)],
        rows_of(wo_all, p.z, p.x, p.c, u), ws(1), wr(1), p.other,
    )
    x_swap = remote(x, x_all.at[u], xs, xr, p.other)

    def part(ref, row, core):
        return ref.at[
            pl.ds(pl.multiple_of(row * half, half), half), pl.ds(pl.multiple_of(core * cols, LANES), cols)
        ]

    halves = ((e0, f0), (e1, f1), (e2, f2))
    ls, ks = wires.take(3), wires.take(3)
    loads = [pltpu.make_async_copy(e, own.at[i], ls(i)) for i, (e, f) in enumerate(halves)]
    keeps = [pltpu.make_async_copy(own.at[i], part(f, u, p.c), ks(i)) for i, (e, f) in enumerate(halves)]
    swaps = [remote(own.at[i], part(f, u, p.c), es(i), er(i), p.other) for i, (e, f) in enumerate(halves)]
    shares = [remote(own.at[i], part(f, u, p.c), cs(i), cr(i), p.sibling) for i, (e, f) in enumerate(halves)]
    passes = [
        remote(part(f, 1 - u, p.c), part(f, 1 - u, p.c), cs(3 + i), cr(3 + i), p.sibling)
        for i, (e, f) in enumerate(halves)
    ]
    os_ = wires.take(3)
    stores = [
        pltpu.make_async_copy(v, r, os_(i)) for i, (v, r) in enumerate(((kv, kv_out), (w_all, w_out), (wo_all, wo_out)))
    ]

    def expert_out(i):
        swaps[i].start()
        shares[i].start()

    def expert_in(i):
        swaps[i].wait_recv()
        passes[i].start()

    wa_swap.start()
    wa_mine.start()
    wo_swap.start()
    x_swap.start()
    each(lambda load: load.start(), loads)

    def starts(places):
        first = jnp.zeros(places.shape, jnp.int32)
        for i in range(docs.shape[0]):
            first = jnp.where(docs[i] <= places, jnp.maximum(first, docs[i]), first)
        return first

    begin[...] = starts(blk * group + lax.broadcasted_iota(jnp.int32, begin.shape, 1))
    places = blk * group + lax.broadcasted_iota(jnp.int32, cosine.shape, 0)
    angle = (places - starts(places)).astype(f32) * freq[0:1, :]
    cosine[...] = jnp.cos(angle)
    sine[...] = jnp.where(lax.broadcasted_iota(jnp.int32, sine.shape, 1) < HEAD_DIM // 2, -1.0, 1.0) * jnp.sin(angle)
    for e in range(experts):
        g_own[e : e + 1, :] = jnp.sum(jnp.where(ids[...] == e, shares_of[...], 0.0), axis=0, keepdims=True)
    wa_swap.wait_recv()
    wa_peer.start(in_place=True)
    x_all[u] = x[...]
    rows_of(wo_all, p.z, p.x, p.c, u)[...] = wo[:, pl.ds(pl.multiple_of(u * q_half, LANES), q_half)]
    for i in range(3):
        loads[i].wait()
        keeps[i].start()
    gws.start()
    for d in range(1, depth):
        for g in (wa_mine, wa_peer):
            g.hop(d)
            g.cross(d - 1)
        gws.hop(d)
        gws.cross(d - 1)
        if d == 1:
            wo_swap.wait_recv()
            wos.start(in_place=True)
            expert_out(0)
        else:
            wos.hop(d - 1)
    gws.cross(depth - 1)
    dys[0].start()
    expert_out(1)
    x_swap.wait_recv()
    for g in (wa_mine, wa_peer):
        g.cross(depth - 1)
    for g in (wa_mine, wa_peer):
        g.finish()
    stores[1].start()
    gain_rows[...] = w_all[:, q_half + kv_half :].astype(f32).T[:8, :]
    for m in range(2):
        xf = x_all[m].astype(f32)
        r1 = lax.rsqrt(jnp.mean(xf * xf, -1, keepdims=True) + EPS)
        normed[m * tok : (m + 1) * tok, :] = (xf * r1 * gain_rows[0:1, :]).astype(bf)
    raw[...] = mm(normed[...], w_all[:, : q_half + kv_half])

    def rope(values):
        return values * cosine[...] + pltpu.roll(values, HEAD_DIM // 2, 1) * sine[...]

    here = p.slot(p.z, p.x, p.c)
    kv[here, :, :HEAD_DIM] = rope(raw[:, q_half : q_half + HEAD_DIM]).astype(bf)
    kv[here, :, HEAD_DIM:] = raw[:, q_half + HEAD_DIM :].astype(bf)
    kvs.start(in_place=True)
    for h in range(heads):
        hs = slice(h * HEAD_DIM, (h + 1) * HEAD_DIM)
        turned = rope(raw[:, hs])
        q_rows[h * group : (h + 1) * group, :] = turned.astype(bf)
        qt[:, h * group : (h + 1) * group] = turned.T.astype(bf)
    for j in range(0, width, 256):
        normed_t[j : j + 256, :] = flip(normed[:, j : j + 256])
    top[...] = jnp.full(top.shape, NEG, f32)
    total[...] = jnp.zeros(total.shape, f32)
    ot[...] = jnp.zeros(ot.shape, f32)

    background = {}

    def at_step(s, act):
        background.setdefault(s, []).append(act)

    at_step(0, lambda: kvs.cross(0))
    at_step(0, lambda: kvs.hop(1))
    at_step(0, dys[1].start_z)
    at_step(1, lambda: wos.hop(3))
    at_step(1, lambda: dys[0].hop(1))
    at_step(2, lambda: kvs.hop(2))
    at_step(3, lambda: kvs.cross(1))
    at_step(2, dys[1].start_x)
    at_step(3, lambda: wos.cross(0))
    at_step(3, lambda: dys[1].hop(1))
    at_step(4, lambda: kvs.hop(3))
    at_step(5, lambda: kvs.cross(2))
    at_step(5, lambda: wos.cross(1))
    at_step(2, lambda: expert_in(0))
    at_step(2, lambda: expert_out(2))
    at_step(5, lambda: dys[0].hop(2))
    at_step(6, lambda: kvs.cross(3))
    at_step(6, lambda: dys[1].hop(2))
    at_step(7, lambda: wos.cross(2))
    at_step(7, lambda: wos.cross(3))

    def step(s, carry):
        d = jnp.where(s < 3, s // 2, jnp.where(s % 2 == 1, (s + 1) // 2, (s - 2) // 2))
        d = jnp.where(s == 7, 3, d)
        crossed = (s == 1) | (s == 4) | (s == 6) | (s == 7)
        zz = p.z - d
        xx = jnp.where(crossed, 1 - p.x, p.x)
        j = p.slot(zz, xx, 0)

        pl.when(zz >= 0)(lambda: kvs.core(zz, xx))

        def work():
            pair = kv[pl.ds(j, 2)].reshape(2 * group, kv_half)
            k = pair[:, :HEAD_DIM]
            vt = flip(pair[:, HEAD_DIM:])
            bias = hidden_bias(j * group, blk * group, begin[0:1, :], 2 * group)
            at = [slice(h * group, (h + 1) * group) for h in range(heads)]
            sc = [mm(k, qt[:, hs]) * (scale * LOG2E) + bias for hs in at]
            old = [top[0:1, hs] for hs in at]
            new = [jnp.maximum(o_, jnp.max(s_, axis=0, keepdims=True)) for o_, s_ in zip(old, sc)]
            e = [jnp.exp2(s_ - n_) for s_, n_ in zip(sc, new)]
            part = [jnp.sum(e_, axis=0, keepdims=True) for e_ in e]
            mixed = [mm(vt, e_.astype(bf)) for e_ in e]
            for h, hs in enumerate(at):
                keep = jnp.exp2(old[h] - new[h])
                total[0:1, hs] = total[0:1, hs] * keep + part[h]
                ot[:, hs] = ot[:, hs] * keep + mixed[h]
                top[0:1, hs] = new[h]

        pl.when((zz >= 0) & (j <= blk))(work)
        for when, acts in background.items():
            pl.when(s == when)(lambda acts=acts: each(lambda act: act(), acts))
        return carry

    lax.fori_loop(0, 2 * depth, step, 0)

    wos.finish()
    stores[2].start()
    sums = total[0:1, :]
    lse[...] = jnp.broadcast_to(top[0:1, :] + jnp.log2(sums), lse.shape)
    for h in range(heads):
        at = slice(h * group, (h + 1) * group)
        mixed = ot[:, at] / sums[:, at]
        ot[:, at] = mixed
        o[:, h * HEAD_DIM : (h + 1) * HEAD_DIM] = mixed.T.astype(bf)

    wide = width // 3
    p_swaps = []
    for i in range(3):
        cb = i * wide
        acc[:, cb : cb + wide] = contract(o[...], wo_all[cb : cb + wide, :], 1, 1)
        theirs = pl.ds(pl.multiple_of((1 - u) * tok, tok), tok)
        p_out[i] = acc[theirs, cb : cb + wide].astype(bf)
        p_swaps.append(remote(p_out.at[i], p_in.at[i], ps(i), pr(i), p.other))
        p_swaps[i].start()
    each(lambda g: g.hop(3), dys)
    expert_in(1)
    for d in range(2):
        each(lambda g: g.cross(d), dys)
    mine = pl.ds(pl.multiple_of(u * tok, tok), tok)
    for i in range(3):
        p_swaps[i].wait_recv()
        acc[mine, i * wide : (i + 1) * wide] += p_in[i].astype(f32)
    branch = acc[mine, :]
    hidden = x[...].astype(f32) + branch
    hid[...] = hidden
    r2 = lax.rsqrt(jnp.mean(hidden * hidden, -1, keepdims=True) + EPS)
    b[...] = (hidden * r2 * gain_rows[1:2, :]).astype(bf)
    attn_sq[...] = jnp.broadcast_to(jnp.sum(branch * branch).reshape(1, 1), attn_sq.shape)
    for d in range(2, depth):
        each(lambda g: g.cross(d), dys)
    expert_in(2)
    kvs.finish(cores_taken=True)
    stores[0].start()
    each(lambda g: g.finish(), dys)
    gws.finish()
    wa_swap.wait_send()
    wo_swap.wait_send()
    x_swap.wait_send()
    for i in range(3):
        swaps[i].wait_send()
        keeps[i].wait()
        shares[i].wait()
        passes[i].wait()
        p_swaps[i].wait_send()
        stores[i].wait()


def front(docs, x, dy, gain_a, gain_m, wq, wkv, wo, ids, shares, experts, depth, scale, cid):
    f32, bf = jnp.float32, jnp.bfloat16
    shape = jax.ShapeDtypeStruct
    vmem = pl.BlockSpec(memory_space=pltpu.VMEM)
    hbm = pl.BlockSpec(memory_space=pl.ANY)
    V = pltpu.VMEM
    tok, width = x.shape
    group = 2 * tok
    q_half = wq.shape[1] // 2
    kv_half = 2 * HEAD_DIM
    wide = q_half + kv_half + LANES
    rows = q_half // HEAD_DIM * group
    rows_dev = wq.shape[0]
    expert = shape((2 * experts[0].shape[0], 2 * experts[0].shape[1]), bf)
    half = HEAD_DIM // 2
    freq = np.power(np.float32(ROPE_BASE), -np.arange(half, dtype=np.float32) * np.float32(2.0 / HEAD_DIM))
    freq = jnp.asarray(np.tile(freq.astype(np.float32), (8, 2)))
    return pl.pallas_call(
        functools.partial(front_kernel, depth, scale),
        out_shape=(
            shape((tok, width), bf),
            shape((tok, width), f32),
            shape((8, LANES), f32),
            shape((width, group), bf),
            shape((rows, HEAD_DIM), bf),
            shape((HEAD_DIM, rows), bf),
            shape((group, q_half), bf),
            shape((HEAD_DIM, rows), f32),
            shape((8, rows), f32),
            shape((8, width), f32),
            shape((2 * depth, 2 * depth, tok), f32),
            shape((2, tok, width), bf),
            shape((8, group), jnp.int32),
            shape((group, HEAD_DIM), f32),
            shape((group, HEAD_DIM), f32),
            shape((4 * depth, group, kv_half), bf),
            shape((width, wide), bf),
            shape((width, q_half), bf),
            shape((2 * depth, tok, width), bf),
            expert,
            expert,
            expert,
        ),
        in_specs=[pl.BlockSpec(memory_space=pltpu.SMEM)] + [vmem] * 10 + [hbm] * 3,
        out_specs=tuple([vmem] * 15 + [hbm] * 7),
        scratch_shapes=[
            V((4 * depth, group, kv_half), bf),
            V((width, wide), bf),
            V((width, q_half), bf),
            V((3,) + experts[0].shape, bf),
            V((LANES, LANES), f32),
            V((2 * depth, tok), f32),
            V((2, rows_dev, wide), bf),
            V((group, width), bf),
            V((group, q_half + kv_half), f32),
            V((8, rows), f32),
            V((8, rows), f32),
            V((group, width), f32),
            V((3, tok, width // 3), bf),
            V((3, tok, width // 3), bf),
            pltpu.SemaphoreType.DMA((8 * 16 * depth,)),
        ],
        compiler_params=pltpu.CompilerParams(
            collective_id=cid, has_side_effects=True, vmem_limit_bytes=56 * 2**20
        ),
        name="front",
    )(docs, x, dy, gain_a[None, :], gain_m[None, :], wq, wkv, wo, ids, shares, freq, *experts)


def experts_kernel(
    depth, b, dy_own, g_all, hid, gain_rows, dy_far, g_far, u_far, d_far,
    dh, dhr, gm, z_sums, z_far, eg_far,
    dy_all, wg, wu, wd, z_p, eg, z_rx, b_all, act, dgate, dup, dyr, db_p, rx, rz, db, turned, sems,
):
    f32, bf = jnp.float32, jnp.bfloat16
    p = Place(depth)
    p.greet()
    wires = Wires(sems)
    tok, width = b.shape
    hidden_units = wg.shape[1]
    expert = p.blk // 2
    pair = 2 * tok
    pieces = 2
    piece = tok // pieces

    rows = [
        Gather(
            p, wires, b.at[pl.ds(k * piece, piece)],
            lambda z, x, c, k=k: b_all.at[pl.ds(pl.multiple_of((z * 2 + x) * tok + k * piece, piece), piece)],
            False, chain=True,
        )
        for k in range(pieces)
    ]

    def cut(ref, k):
        return ref.at[pl.ds(k * piece, piece)]

    sums = Scatter(
        p, wires,
        lambda zz, xx, k: cut(db_p.at[zz * 2 + xx], k),
        lambda k: cut(db, k),
        lambda zz, k: cut(rx.at[zz], k),
        lambda slot, k: cut(rz.at[slot], k),
        pieces,
    )
    ls = wires.take(4)
    loads = [
        pltpu.make_async_copy(r, v, ls(i)) for i, (r, v) in enumerate(((dy_far, dy_all), (g_far, wg), (u_far, wu), (d_far, wd)))
    ]
    os_ = wires.take(3)
    stores = [
        pltpu.make_async_copy(v, r, os_(i))
        for i, (v, r) in enumerate(((z_p, z_far), (eg.at[pl.ds(0, 2)], eg_far.at[pl.ds(0, 2)]), (eg.at[2], eg_far.at[2])))
    ]
    each(lambda load: load.start(), loads)
    each(lambda g: g.start(), rows)
    spread = lax.broadcasted_iota(jnp.int32, (tok, 8), 1)

    def weight(slot):
        return jnp.sum(jnp.where(spread == expert, g_all[slot].T, 0.0), axis=1, keepdims=True)

    def nth(i):
        inner = jnp.where(i == 0, 1, jnp.where(i == 1, 0, i))
        other = jnp.where(i == 0, 2, jnp.where(i == 1, 1, jnp.where(i == 2, 3, 0)))
        return jnp.where(p.z == 0, i, jnp.where(p.z == depth - 1, depth - 1 - i, jnp.where(p.z == 1, inner, other)))

    def block(i, carry):
        for d in range(1, depth):
            pl.when(i == d - 1)(lambda d=d: each(lambda g: g.hop(d), rows))
        each(lambda g: g.crossed(nth(i)), rows)
        pl.when(i == 0)(lambda: each(lambda load: load.wait(), loads))
        zz = nth(i)
        at = pl.ds(pl.multiple_of(zz * pair, pair), pair)
        for xx in range(2):
            half = pl.ds(pl.multiple_of(zz * pair + xx * tok, tok), tok)
            dyr[half, :] = (weight(zz * 2 + xx) * dy_all[zz * 2 + xx].astype(f32)).astype(bf)
        for cb in range(0, hidden_units, 256):
            cs = slice(cb, cb + 256)
            gate = mm(b_all[at, :], wg[:, cs])
            up = mm(b_all[at, :], wu[:, cs])
            sig = jax.nn.sigmoid(gate)
            act[at, cs] = (gate * sig * up).astype(bf)
            dact = mm(dyr[at, :], wd[:, cs])
            dgate[at, cs] = (dact * up * sig * (1.0 + gate * (1.0 - sig))).astype(bf)
            dup[at, cs] = (dact * gate * sig).astype(bf)
        for cb in range(0, width, 512):
            cs = slice(cb, cb + 512)
            part = contract(dgate[at, :], wg[cs, :], 1, 1) + contract(dup[at, :], wu[cs, :], 1, 1)
            for xx in range(2):
                db_p[zz * 2 + xx, :, cs] = part[xx * tok : (xx + 1) * tok, :].astype(bf)
        pl.when(i == depth - 2)(lambda: sums.send(nth(2)))
        pl.when(i == depth - 1)(lambda: each(lambda n: sums.send(nth(n)), (3, 1)))
        for cb in range(0, width, 512):
            cs = slice(cb, cb + 512)
            part = contract(act[at, :], wd[cs, :], 1, 1)
            for xx in range(2):
                z_p[zz * 2 + xx, :, cs] = (
                    weight(zz * 2 + xx) * part[xx * tok : (xx + 1) * tok, :]
                ).astype(bf)
        return carry

    lax.fori_loop(0, depth, block, 0)

    stores[0].start()
    zs_, zr_ = wires.take(2 * len(EARLY)), wires.take(2 * len(EARLY))

    def z_send(n, k):
        return remote(
            cut(z_p.at[EARLY[n] * 2 + 1 - p.x], k), cut(z_rx.at[n], k), zs_(2 * n + k), zr_(2 * n + k), p.across
        )

    z_pieces = [(n, k) for n in range(len(EARLY)) for k in range(pieces)]

    wide = 256

    def grads(n):
        cs = slice(n * wide, (n + 1) * wide)
        turned[...] = flip(b_all[:, cs])
        eg[0, cs, :] = mm(turned[...], dgate[...]).astype(bf)
        eg[1, cs, :] = mm(turned[...], dup[...]).astype(bf)

    def grads_down(n):
        cs = slice(n * wide, (n + 1) * wide)
        turned[...] = flip(dyr[:, cs])
        eg[2, cs, :] = mm(turned[...], act[...]).astype(bf)

    work = [lambda n=n: grads(n) for n in range(width // wide)]
    work += [lambda n=n: grads_down(n) for n in range(width // wide)]
    events = []
    for n in (2, 3, 1, 0):
        for k in range(pieces):
            events.append(lambda n=n, k=k: sums.take(nth(n), k))
        if n == 2:
            events.append(lambda: sums.send(nth(0)))
        if n == 1:
            events.append(lambda: each(lambda piece_: z_send(*piece_).start(), z_pieces[:2]))
    done = 0
    for t, event in enumerate(events):
        while done < len(work) and done * len(events) <= t * len(work):
            work[done]()
            done += 1
        event()
    for act_ in work[done:]:
        act_()
    stores[1].start()
    stores[2].start()
    each(lambda piece_: z_send(*piece_).start(), z_pieces[2:])
    sums.finish()
    each(lambda g: g.finish(), rows)

    h = hid[...]
    r2 = lax.rsqrt(jnp.mean(h * h, -1, keepdims=True) + EPS)
    weighted = db[...] * gain_rows[1:2, :]
    inner = jnp.mean(weighted * h, -1, keepdims=True)
    total = dy_own[...].astype(f32) + r2 * weighted - h * (r2 * r2 * r2 * inner)
    dh[...] = total
    dhr[...] = total.astype(bf)
    column = jnp.sum((db[...] * h * r2).T, axis=1, keepdims=True)
    lane = lax.broadcasted_iota(jnp.int32, (width, LANES), 1)
    gm[...] = jnp.where(lane == 1, column, 0.0)
    for n, zz in enumerate(EARLY):
        for k in range(pieces):
            z_send(n, k).wait()
        z_sums[n] = (z_p[zz * 2 + p.x].astype(f32) + z_rx[n].astype(f32)).astype(bf)
    each(lambda store: store.wait(), stores)


def run_experts(b, dy_own, dy_all, g_all, weights, hid, gain_rows, depth, cid):
    f32, bf = jnp.float32, jnp.bfloat16
    shape = jax.ShapeDtypeStruct
    vmem = pl.BlockSpec(memory_space=pltpu.VMEM)
    hbm = pl.BlockSpec(memory_space=pl.ANY)
    V = pltpu.VMEM
    tok, width = b.shape
    units = weights[0].shape[1]
    rows = 2 * depth * tok
    return pl.pallas_call(
        functools.partial(experts_kernel, depth),
        out_shape=(
            shape((tok, width), f32),
            shape((tok, width), bf),
            shape((width, LANES), f32),
            shape((len(EARLY), tok, width), bf),
            shape((2 * depth, tok, width), bf),
            shape((3, width, units), bf),
        ),
        in_specs=[vmem] * 5 + [hbm] * 4,
        out_specs=tuple([vmem] * 4 + [hbm] * 2),
        scratch_shapes=[
            V((2 * depth, tok, width), bf),
            V((width, units), bf),
            V((width, units), bf),
            V((width, units), bf),
            V((2 * depth, tok, width), bf),
            V((3, width, units), bf),
            V((len(EARLY), tok, width), bf),
            V((rows, width), bf),
            V((rows, units), bf),
            V((rows, units), bf),
            V((rows, units), bf),
            V((rows, width), bf),
            V((2 * depth, tok, width), bf),
            V((depth, tok, width), bf),
            V((depth, tok, width), bf),
            V((tok, width), f32),
            V((256, rows), bf),
            pltpu.SemaphoreType.DMA((2 * 5 * depth + 8 * depth + 8 + 4 * len(EARLY),)),
        ],
        compiler_params=pltpu.CompilerParams(
            collective_id=cid, has_side_effects=True, vmem_limit_bytes=58 * 2**20
        ),
        name="experts",
    )(b, dy_own, g_all, hid, gain_rows, dy_all, *weights)


def closing_kernel(
    depth, scale, attn_sq, dhr, gain, begin, lse, cosine, sine,
    z_sums, zp_far, wo_far, ot_far, o_far, q_far, qt_far, kv_far, w_far, at_far, x_far, hid_far, dh_far, gm_far, eg,
    out, gin, gq, go, gkv, gg, f0, f1, f2, rms,
    zp, wo, ot, o, q_rows, qt, kv, w, at, x_all, hid, dh, gm,
    dhr_all, dot_, dqt, delta, dkv, do_rows, dq, att, acc,
    z_sum, z_rx, z_rz, go_p, go_rc, go_rx, go_rz, kv_sum, kv_rc, kv_rx, kv_rz,
    gq_p, gq_rc, gq_rx, gq_rz, gk_p, gk_sum, gk_rc, gk_rx, gk_rz,
    e_own, e_core, e_low, e_peer, da_out, da_in, t_out, t_in, sq, square, sems,
):
    f32, bf = jnp.float32, jnp.bfloat16
    p = Place(depth)
    p.greet(sibling=True, other=True)
    wires = Wires(sems)
    u, blk = p.u, p.blk
    tok = dhr.shape[0]
    group, q_half = o.shape
    heads = q_half // HEAD_DIM
    kv_half = 2 * HEAD_DIM
    blocks = kv.shape[0]
    rows_blk = gq.shape[0]

    cols = f0.shape[1]
    rows_e = f0.shape[0]
    es, er, el, ps, pr = (wires.take(1)(0) for _ in range(5))

    def e_cols(core):
        return eg.at[:, :, pl.ds(pl.multiple_of(core * cols, LANES), cols)]

    def e_rows(member):
        return pl.ds(pl.multiple_of(member * rows_e, rows_e), rows_e)

    e_trade = remote(e_cols(1 - p.c), e_core, es, er, p.sibling)
    e_keep = [pltpu.make_async_copy(e_cols(p.c).at[i], e_own, el) for i in range(3)]
    e_swap = remote(e_low, e_peer, ps, pr, p.other)

    def e_join():
        e_trade.wait_recv()
        theirs, mine = e_rows(1 - u), e_rows(u)
        for i in range(3):
            e_keep[i].wait()
            e_low[i] = (e_own[theirs, :].astype(f32) + e_core[i, theirs, :].astype(f32)).astype(bf)
            (f0, f1, f2)[i][...] = e_own[mine, :].astype(f32) + e_core[i, mine, :].astype(f32)
            if i < 2:
                e_keep[i + 1].start()
        e_swap.start()

    def e_done():
        e_swap.wait_recv()
        for i in range(3):
            (f0, f1, f2)[i][...] += e_peer[i].astype(f32)

    ds, dr = wires.take(1)(0), wires.take(1)(0)
    swap = remote(dhr, dhr_all.at[u], ds, dr, p.other)

    pieces = 2
    z_rows = tok // pieces

    def cut(ref, k):
        return ref.at[pl.ds(k * z_rows, z_rows)]

    zs = Scatter(
        p, wires,
        lambda zz, xx, k: cut(zp.at[zz * 2 + xx], k),
        lambda k: cut(z_sum, k),
        lambda zz, k: cut(z_rx.at[zz], k),
        lambda slot, k: cut(z_rz.at[slot], k),
        pieces, ready=EARLY,
    )
    gos = CoreScatter(p, wires, go_p, go_rc, go, go_rx, go_rz)
    kvs = CoreScatter(p, wires, dkv, kv_rc, kv_sum, kv_rx, kv_rz, down_only=True)
    gqs = CoreScatter(p, wires, gq_p, gq_rc, gq, gq_rx, gq_rz)
    gks = CoreScatter(p, wires, gk_p, gk_rc, gk_sum, gk_rx, gk_rz)
    qs, qr = wires.take(3 + depth), wires.take(3 + depth)
    sq_here = sq.at[p.z, p.x, u, p.c]
    sq_core = remote(sq_here, sq_here, qs(0), qr(0), p.sibling)
    sq_other = remote(sq.at[:, :, u], sq.at[:, :, u], qs(1), qr(1), p.other)
    sq_across = remote(sq.at[p.z, p.x, u], sq.at[p.z, p.x, u], qs(2), qr(2), p.across)

    def sq_along(z, to):
        return remote(sq.at[z, :, u], sq.at[z, :, u], qs(3 + to), qr(3 + z), p.along(to))

    ls = wires.take(13)
    loads = [
        pltpu.make_async_copy(r, v, ls(i))
        for i, (r, v) in enumerate(
            (
                (zp_far, zp), (wo_far, wo), (ot_far, ot), (o_far, o), (q_far, q_rows), (qt_far, qt), (kv_far, kv),
                (w_far, w), (at_far, at), (x_far, x_all), (hid_far, hid), (dh_far, dh), (gm_far, gm),
            )
        )
    ]
    zl = wires.take(len(EARLY))
    z_loads = [pltpu.make_async_copy(z_sums.at[n], z_rx.at[zz], zl(n)) for n, zz in enumerate(EARLY)]
    swap.start()
    each(lambda load: load.start(), z_loads)
    each(lambda load: load.start(), loads)
    e_trade.start()
    e_keep[0].start()
    loads[0].wait()
    ahead = 2
    for t in range(ahead):
        zs.begin(t)

    each(lambda load: load.wait(), z_loads)
    zs.forward()
    dqt[...] = jnp.zeros(dqt.shape, f32)
    dkv[...] = jnp.zeros(dkv.shape, bf)
    dhr_all[u] = dhr[...]
    e_join()
    zs.land(0)
    zs.begin(ahead)
    each(lambda load: load.wait(), loads[1:])
    swap.wait_recv()

    for m in range(2):
        part = mm(dhr_all[m], wo[...]).astype(bf)
        for h in range(heads):
            do_rows[h * group + m * tok : h * group + (m + 1) * tok, :] = part[:, h * HEAD_DIM : (h + 1) * HEAD_DIM]
    for h in range(heads):
        hs = slice(h * group, (h + 1) * group)
        part = do_rows[hs, :]
        turned = part.astype(f32).T
        dot_[:, hs] = turned.astype(bf)
        delta[0:1, hs] = jnp.sum(turned * ot[:, hs], axis=0, keepdims=True)

    def spread_rows(payload, turned, right, cols=None):
        some = 4

        def rows(i, carry):
            at_rows = pl.ds(pl.multiple_of(i * some * rows_blk, some * rows_blk), some * rows_blk)
            part = mm(turned[at_rows, :], right).astype(bf)
            for n in range(some):
                piece = part[n * rows_blk : (n + 1) * rows_blk, :]
                if cols is None:
                    payload[i * 2 + n // 2, n % 2] = piece
                else:
                    payload[i * 2 + n // 2, n % 2, :, :cols] = piece
            return carry

        lax.fori_loop(0, blocks // some, rows, 0)

    for m in range(2):
        att[:, m * tok : (m + 1) * tok] = flip(dhr_all[m])

    spread_rows(go_p, att, o[...])
    gos.trade()

    background = {}

    def at_tile(j, act):
        background.setdefault(j, []).append(act)

    def z_step(t):
        zs.land(t)
        zs.begin(t + ahead)

    for t in range(1, len(zs.items)):
        at_tile((0, 0, 2, 4, 6, 9, 12, 15)[t], lambda t=t: z_step(t))
    for t in range(depth):
        at_tile((5, 8, 11, 14)[t], lambda t=t: gos.join(t))
    for t in range(3):
        at_tile((11, 14, 15)[t], lambda t=t: gos.land(t))
    for t in range(depth - 1):
        last = 4 * t + 3
        at_tile(last, lambda t=t: kvs.trade(t))
        at_tile(last + 1, lambda t=t: kvs.join(t))
        if t < depth - 2:
            at_tile(last + 6, lambda t=t: kvs.land(t))

    def tile(j, carry):
        def work():
            k = kv[j, :, :HEAD_DIM]
            v = kv[j, :, HEAD_DIM:]
            kt = flip(k)
            bias = hidden_bias(j * group, blk * group, begin[0:1, :], group)
            at_ = [slice(h * group, (h + 1) * group) for h in range(heads)]
            sc = [mm(k, qt[:, hs]) * (scale * LOG2E) + bias for hs in at_]
            dp = [mm(v, dot_[:, hs]) for hs in at_]
            e = [jnp.exp2(s_ - lse[0:1, hs]) for s_, hs in zip(sc, at_)]
            g = [(e_ * (d_ - delta[0:1, hs])).astype(bf) for e_, d_, hs in zip(e, dp, at_)]
            wide_g = jnp.concatenate(g, 1)
            dk = mm(wide_g, q_rows[...])
            dv = mm(jnp.concatenate([e_.astype(bf) for e_ in e], 1), do_rows[...])
            dqt[...] += mm(kt, wide_g)
            dkv[j // 2, j % 2, :, :HEAD_DIM] = (dk * scale).astype(bf)
            dkv[j // 2, j % 2, :, HEAD_DIM:] = dv.astype(bf)

        pl.when(j <= blk)(work)
        for when, acts in background.items():
            pl.when(j == when)(lambda acts=acts: each(lambda act: act(), acts))
        return carry

    lax.fori_loop(0, blocks, tile, 0)

    kvs.trade(depth - 1)

    def back_turn(values):
        return values * cosine[...] - pltpu.roll(values, HEAD_DIM // 2, 1) * sine[...]

    for h in range(heads):
        hs = slice(h * group, (h + 1) * group)
        cs = slice(h * HEAD_DIM, (h + 1) * HEAD_DIM)
        dq[:, cs] = back_turn((dqt[:, hs] * scale).T.astype(bf).astype(f32)).astype(bf)
    kvs.join(depth - 1)

    zs.finish()
    result = hid[...] + z_sum[...]
    out[...] = result.astype(bf)
    spread = lax.broadcasted_iota(jnp.int32, (8, LANES), 1)
    z_sq = jnp.sum(z_sum[...] * z_sum[...])
    r_sq = jnp.sum(result * result)
    sq_here[...] = jnp.where(
        spread == 0, attn_sq[...], jnp.where(spread == 1, z_sq, jnp.where(spread == 2, r_sq, 0.0))
    )
    sq_core.start()

    spread_rows(gq_p, at, dq[...])
    gqs.trade()
    sq_core.wait_recv()
    sq_across.start()
    kvs.land(depth - 2)
    gqs.join(0)
    gqs.join(1)
    for m in range(2):
        for cb in range(0, D, 512):
            acc[m * tok : (m + 1) * tok, cb : cb + 512] = contract(
                dq[m * tok : (m + 1) * tok, :], w[cb : cb + 512, :q_half], 1, 1
            )
    kvs.land(depth - 1)
    kvs.release()
    kvs.finish()
    sq_across.wait_recv()
    for d in range(1, depth):
        pl.when(p.z >= d)(lambda d=d: sq_along(p.z, p.z - d).start())
        pl.when(p.z + d < depth)(lambda d=d: sq_along(p.z, p.z + d).start())
    kv_low = kv_sum[...].astype(bf).astype(f32)
    kv_pre = jnp.concatenate([back_turn(kv_low[:, :HEAD_DIM]).astype(bf), kv_low[:, HEAD_DIM:].astype(bf)], 1)

    da_s, da_r = wires.take(3), wires.take(3)
    wide = D // 3
    da_swaps = []
    for i in range(3):
        cb = i * wide
        part = contract(kv_pre, w[cb : cb + wide, q_half : q_half + kv_half], 1, 1)
        acc[:, cb : cb + wide] += part
        theirs = pl.ds(pl.multiple_of((1 - u) * tok, tok), tok)
        da_out[i] = acc[theirs, cb : cb + wide].astype(bf)
        da_swaps.append(remote(da_out.at[i], da_in.at[i], da_s(i), da_r(i), p.other))
        da_swaps[i].start()

    column = jnp.zeros((D, 1), f32)
    for m in range(2):
        xf = x_all[m].astype(f32)
        r1 = lax.rsqrt(jnp.mean(xf * xf, -1, keepdims=True) + EPS)
        terms = acc[m * tok : (m + 1) * tok, :] * xf * r1
        column = column + jnp.sum(terms.T, axis=1, keepdims=True)
    lane = lax.broadcasted_iota(jnp.int32, (D, LANES), 1)
    gain_cols = (jnp.where(lane == 0, column, 0.0) + gm[...]).astype(bf)
    for i in range(blocks):
        gk_p[i // 2, i % 2, :, kv_half:] = gain_cols[i * rows_blk : (i + 1) * rows_blk, :]

    spread_rows(gk_p, at, kv_pre, kv_half)
    gqs.land(0)
    gqs.land(1)
    gks.trade()
    for t in range(depth):
        gks.join(t)
    for t in range(2, depth):
        gqs.join(t)
    gqs.release()

    for t in range(depth):
        gks.land(t)
    gos.land(3)
    for z in range(depth):
        pl.when(p.z != z)(lambda z=z: sq_along(z, z).wait_recv())
    sq_other.start()

    mine = pl.ds(pl.multiple_of(u * tok, tok), tok)
    for i in range(3):
        da_swaps[i].wait_recv()
        acc[mine, i * wide : (i + 1) * wide] += da_in[i].astype(f32)
    da = acc[mine, :]
    xf = x_all[u].astype(f32)
    r1 = lax.rsqrt(jnp.mean(xf * xf, -1, keepdims=True) + EPS)
    weighted = da * gain[0:1, :]
    inner = jnp.mean(weighted * xf, -1, keepdims=True)
    gin[...] = dh[...] + r1 * weighted - xf * (r1 * r1 * r1 * inner)
    for t in range(2, depth):
        gqs.land(t)
    gks.release()
    gks.finish()
    rows_dev = gkv.shape[0]
    theirs = pl.ds(pl.multiple_of((1 - u) * rows_dev, rows_dev), rows_dev)
    own = pl.ds(pl.multiple_of(u * rows_dev, rows_dev), rows_dev)
    t_out[...] = gk_sum[theirs, :]
    ts, tr = wires.take(1)(0), wires.take(1)(0)
    t_swap = remote(t_out, t_in, ts, tr, p.other)
    t_swap.start()
    e_done()
    gos.release()
    gos.finish()
    gqs.finish()
    t_swap.wait_recv()
    for part in range(2):
        here = slice(part * HEAD_DIM, (part + 1) * HEAD_DIM)
        base = part * kv_half
        gkv[:, pl.ds(pl.multiple_of(base + u * HEAD_DIM, LANES), HEAD_DIM)] = gk_sum[own, here]
        gkv[:, pl.ds(pl.multiple_of(base + (1 - u) * HEAD_DIM, LANES), HEAD_DIM)] = t_in[:, here]
    square[...] = jnp.zeros(square.shape, f32)
    square[:rows_dev, :] = gk_sum[own, kv_half:] + t_in[:, kv_half:]
    gg[...] = square[...].T[:8, :]
    sq_core.wait_send()
    sq_other.wait()
    sq_across.wait_send()
    for z in range(depth):
        pl.when(p.z != z)(lambda z=z: sq_along(p.z, z).wait_send())
    squares = jnp.zeros((8, LANES), f32)
    for z in range(depth):
        for n in range(8):
            squares = squares + sq[z, n // 4, n // 2 % 2, n % 2]
    rms[...] = jnp.sqrt(squares / (8 * depth * tok * D))
    t_swap.wait_send()
    swap.wait_send()
    e_trade.wait_send()
    e_swap.wait_send()
    for i in range(3):
        da_swaps[i].wait_send()


def closing(attn_sq, dhr, gain, begin, lse, cosine, sine, z_sums, large, eg, depth, scale, cid):
    f32, bf = jnp.float32, jnp.bfloat16
    tok, width = dhr.shape
    group, q_half = large[3].shape
    blocks = large[6].shape[0]
    kv_block = large[6].shape[1:]
    rows_blk = width // blocks
    rows_e, cols = eg.shape[1] // 2, eg.shape[2] // 2
    kv_half = 2 * HEAD_DIM
    shape = jax.ShapeDtypeStruct
    vmem = pl.BlockSpec(memory_space=pltpu.VMEM)
    hbm = pl.BlockSpec(memory_space=pl.ANY)
    V = pltpu.VMEM

    def buffers(block):
        return [
            V((blocks // 2,) + block, bf),
            V((depth,) + block, bf),
            V((depth,) + block, bf),
        ]

    grad = shape((rows_e, cols), f32)
    rows = q_half // HEAD_DIM * group
    return pl.pallas_call(
        functools.partial(closing_kernel, depth, scale),
        out_shape=(
            shape((tok, width), bf),
            shape((tok, width), f32),
            shape((rows_blk, q_half), f32),
            shape((rows_blk, q_half), f32),
            shape((rows_blk // 2, 2 * kv_half), f32),
            shape((8, LANES), f32),
            grad,
            grad,
            grad,
            shape((8, LANES), f32),
        ),
        in_specs=[vmem] * 7 + [hbm] * 15,
        out_specs=tuple([vmem] * 10),
        scratch_shapes=[V(array.shape, array.dtype) for array in large]
        + [
            V((2, tok, width), bf),
            V((HEAD_DIM, rows), bf),
            V((HEAD_DIM, rows), f32),
            V((8, rows), f32),
            V((blocks // 2, 2) + kv_block, bf),
            V((rows, HEAD_DIM), bf),
            V((group, q_half), bf),
            V((width, group), bf),
            V((group, width), f32),
            V((tok, width), f32),
            V((depth, tok, width), bf),
            V((depth, tok, width), bf),
            V((blocks // 2, 2, rows_blk, q_half), bf),
        ]
        + buffers((rows_blk, q_half))
        + [V((group, kv_half), f32)]
        + buffers((group, kv_half))
        + [V((blocks // 2, 2, rows_blk, q_half), bf)]
        + buffers((rows_blk, q_half))
        + [V((blocks // 2, 2, rows_blk, kv_half + LANES), bf), V((rows_blk, kv_half + LANES), f32)]
        + buffers((rows_blk, kv_half + LANES))
        + [
            V((2 * rows_e, cols), bf),
            V((3, 2 * rows_e, cols), bf),
            V((3, rows_e, cols), bf),
            V((3, rows_e, cols), bf),
            V((3, tok, width // 3), bf),
            V((3, tok, width // 3), bf),
            V((rows_blk // 2, kv_half + LANES), f32),
            V((rows_blk // 2, kv_half + LANES), f32),
            V((depth, 2, 2, 2, 8, LANES), f32),
            V((LANES, LANES), f32),
            pltpu.SemaphoreType.DMA((320,)),
        ],
        compiler_params=pltpu.CompilerParams(
            collective_id=cid, has_side_effects=True, vmem_limit_bytes=60 * 2**20
        ),
        name="closing",
    )(attn_sq, dhr, gain, begin, lse, cosine, sine, z_sums, *large, eg)


def deliver_kernel(count, gains, rms, *refs):
    ins, (gain_a, gain_m, rms_out) = refs[:count], refs[count : count + 3]
    outs, held, sems = refs[count + 3 : 2 * count + 3], refs[2 * count + 3 : 3 * count + 3], refs[3 * count + 3]
    loads = [pltpu.make_async_copy(ins[i], held[i], sems.at[i]) for i in range(count)]
    stores = [pltpu.make_async_copy(held[i], outs[i], sems.at[count + i]) for i in range(count)]
    each(lambda load: load.start(), loads)
    gain_a[...] = gains[0:1, : gain_a.shape[1]]
    gain_m[...] = gains[1:2, : gain_m.shape[1]]
    rms_out[...] = rms[0:1, : rms_out.shape[1]]
    for load, store in zip(loads, stores):
        load.wait()
        store.start()
    each(lambda store: store.wait(), stores)


def deliver(gains, rms, arrays, rows):
    count = len(arrays)
    hbm = pl.BlockSpec(memory_space=pl.ANY)
    vmem = pl.BlockSpec(memory_space=pltpu.VMEM)
    small = [jax.ShapeDtypeStruct((1, n), jnp.float32) for n in (rows, rows, 3)]
    return pl.pallas_call(
        functools.partial(deliver_kernel, count),
        out_shape=tuple(small + [jax.ShapeDtypeStruct(a.shape, a.dtype) for a in arrays]),
        in_specs=[vmem] * 2 + [hbm] * count,
        out_specs=tuple([vmem] * 3 + [hbm] * count),
        scratch_shapes=[pltpu.VMEM(a.shape, a.dtype) for a in arrays] + [pltpu.SemaphoreType.DMA((2 * count,))],
        compiler_params=pltpu.CompilerParams(vmem_limit_bytes=60 * 2**20),
        name="deliver",
    )(gains, rms, *arrays)


def planned(
    layer_input,
    grad_output,
    gain_attn,
    gain_moe,
    w_query,
    w_keyval,
    w_out,
    w_gate,
    w_up,
    w_down,
    gate_weights,
    expert_ids,
    doc_starts,
):
    depth = lax.axis_size("blk") // 4
    scale = 1.0 / math.sqrt(HEAD_DIM)
    (
        normed_m, hidden, attn_sq, normed_t, query_rows, query_t, mixed, mixed_t, lse, gain_rows, g_all, inputs,
        begin_rows, cosine, sine, kv_all, w_all, out_w, dy_all, gate_w, up_w, down_w,
    ) = front(
        doc_starts, layer_input, grad_output, gain_attn, gain_moe, w_query, w_keyval, w_out, expert_ids.T, gate_weights.T,
        (w_gate, w_up, w_down), depth, scale, 1,
    )
    grad_hidden, grad_hidden_low, gain_terms, z_sums, z_part, expert_grads = run_experts(
        normed_m, grad_output, dy_all, g_all, (gate_w, up_w, down_w), hidden, gain_rows, depth, 2
    )
    large = (
        z_part, out_w, mixed_t, mixed, query_rows, query_t, kv_all, w_all, normed_t, inputs, hidden, grad_hidden, gain_terms
    )
    results = closing(
        attn_sq, grad_hidden_low, gain_rows, begin_rows, lse, cosine, sine, z_sums, large, expert_grads, depth, scale, 3
    )
    (
        gain_a, gain_m, rms, layer_output, grad_input, part_query, part_out, part_keyval, grad_gate, grad_up, grad_down
    ) = deliver(results[5], results[9], results[:5] + results[6:9], gain_attn.shape[0])
    return (
        layer_output,
        grad_input,
        gain_a.reshape(-1),
        gain_m.reshape(-1),
        part_query,
        part_keyval,
        part_out,
        grad_gate,
        grad_up,
        grad_down,
        rms.reshape(-1),
    )


def solution(mesh):
    in_specs = (
        P(("blk", "ulysses"), None),
        P(("blk", "ulysses"), None),
        P(("blk", "ulysses")),
        P(("blk", "ulysses")),
        P(("blk", "ulysses"), None),
        P(("blk", "ulysses"), None),
        P(("blk", "ulysses"), None),
        P("ulysses", "blk"),
        P("ulysses", "blk"),
        P("ulysses", "blk"),
        P(("blk", "ulysses"), None),
        P(("blk", "ulysses"), None),
        P(),
    )
    out_specs = (
        P(("blk", "ulysses"), None),
        P(("blk", "ulysses"), None),
        P(("blk", "ulysses")),
        P(("blk", "ulysses")),
        P("blk", "ulysses"),
        P(("blk", "ulysses"), None),
        P("blk", "ulysses"),
        P("ulysses", "blk"),
        P("ulysses", "blk"),
        P("ulysses", "blk"),
        P(),
    )
    blocks, members = mesh.shape["blk"], mesh.shape["ulysses"]
    body = planned if blocks == 16 and members == KV_HEADS else local
    return jax.shard_map(body, mesh=mesh, in_specs=in_specs, out_specs=out_specs, check_vma=False)
```

```python
import functools
import math

import jax
import jax.numpy as jnp
import numpy as np
from jax import lax
from jax.experimental import pallas as pl
from jax.experimental.pallas import tpu as pltpu
from jax.sharding import PartitionSpec as P

D = 1536
HEADS = 12
KV_HEADS = 2
HEAD_DIM = 128
TOP = 4


EPS = 1e-06
ROPE_BASE = 1000000.0
NEG = -1e30
EARLY = (0,)


def rotate(values, positions, sign):
    half = values.shape[-1] // 2
    freq = ROPE_BASE ** (-jnp.arange(half, dtype=jnp.float32) * 2.0 / values.shape[-1])
    angle = positions.astype(jnp.float32)[:, None] * freq[None, :]
    cosine = jnp.cos(angle)[:, None, :]
    sine = sign * jnp.sin(angle)[:, None, :]
    first = values[..., :half]
    second = values[..., half:]
    return jnp.concatenate([first * cosine - second * sine, second * cosine + first * sine], -1)


def doc_begin(positions, doc_starts):
    return jnp.max(
        jnp.where(doc_starts[None, :] <= positions[:, None], doc_starts[None, :], 0), axis=1
    )


def norm_back(values, factor, gain, grad):
    weighted = grad * gain
    inner = jnp.mean(weighted * values, -1, keepdims=True)
    return factor * weighted - values * factor * factor * factor * inner


def visible_mask(q_pos, q_begin, k_pos):
    return (k_pos[None, :] >= q_begin[:, None]) & (k_pos[None, :] <= q_pos[:, None])


def split_blocks(array):
    rows = array.shape[0]
    size = min(rows, 512)
    return (array.reshape((rows // size, size) + array.shape[1:]), size)


def contract(left, right, left_dim, right_dim):
    return lax.dot_general(
        left, right, (((left_dim,), (right_dim,)), ((), ())), preferred_element_type=jnp.float32
    )


def reorder_rows(array, outer, inner):
    rows = array.shape[0]
    shaped = array.reshape((outer, inner, rows // (outer * inner)) + array.shape[1:])
    return jnp.swapaxes(shaped, 0, 1).reshape(array.shape)


def route(payload):
    return lax.all_to_all(payload, "blk", split_axis=0, concat_axis=0, tiled=True)


def backward_block(queries, grads, lse, delta, q_pos, q_begin, keys, values, k_start, scale):
    k_pos = k_start + jnp.arange(keys.shape[0], dtype=jnp.int32)
    visible = visible_mask(q_pos, q_begin, k_pos)[None]
    scores = jnp.einsum("qhd,kd->hqk", queries, keys, preferred_element_type=jnp.float32) * scale
    probs = jnp.where(visible, jnp.exp(scores - lse[:, :, None]), 0.0)
    probs_low = probs.astype(jnp.bfloat16)
    grad_probs = jnp.einsum("qhd,kd->hqk", grads, values, preferred_element_type=jnp.float32)
    grad_scores = (probs * (grad_probs - delta[:, :, None])).astype(jnp.bfloat16)
    part_q = (
        jnp.einsum("hqk,kd->qhd", grad_scores, keys, preferred_element_type=jnp.float32) * scale
    )
    part_k = (
        jnp.einsum("hqk,qhd->kd", grad_scores, queries, preferred_element_type=jnp.float32) * scale
    )
    part_v = jnp.einsum("hqk,qhd->kd", probs_low, grads, preferred_element_type=jnp.float32)
    return (part_q, part_k, part_v)


def local(
    layer_input,
    grad_output,
    gain_attn,
    gain_moe,
    w_query,
    w_keyval,
    w_out,
    w_gate,
    w_up,
    w_down,
    gate_weights,
    expert_ids,
    doc_starts,
):
    n_blk = lax.axis_size("blk")
    n_uly = lax.axis_size("ulysses")
    tok = layer_input.shape[0]
    group = tok * n_uly
    heads_dev = HEADS // n_uly
    per_kv = HEADS // KV_HEADS
    which = [c * heads_dev // per_kv for c in range(n_uly)]
    kv_width = KV_HEADS * HEAD_DIM
    q_width = HEADS * HEAD_DIM
    scale = 1.0 / math.sqrt(HEAD_DIM)
    blk_index = lax.axis_index("blk")
    device = blk_index * n_uly + lax.axis_index("ulysses")
    tok_pos = device * tok + jnp.arange(tok, dtype=jnp.int32)
    places = tok_pos - doc_begin(tok_pos, doc_starts)
    gain_a, gain_m, query_w, keyval_w, out_w = (
        lax.all_gather(gain_attn, ("blk", "ulysses"), axis=0, tiled=True),
        lax.all_gather(gain_moe, ("blk", "ulysses"), axis=0, tiled=True),
        lax.all_gather(w_query, ("blk", "ulysses"), axis=0, tiled=True),
        lax.all_gather(w_keyval, ("blk", "ulysses"), axis=0, tiled=True),
        lax.all_gather(w_out, ("blk", "ulysses"), axis=0, tiled=True),
    )
    gate_w, up_w, down_w = (
        lax.all_gather(w_gate, "ulysses", axis=0, tiled=True),
        lax.all_gather(w_up, "ulysses", axis=0, tiled=True),
        lax.all_gather(w_down, "ulysses", axis=0, tiled=True),
    )
    gain_a = gain_a.astype(jnp.float32)
    gain_m = gain_m.astype(jnp.float32)
    inputs = layer_input.astype(jnp.float32)
    factor_a = lax.rsqrt(jnp.mean(inputs * inputs, -1, keepdims=True) + EPS)
    normed_a = (inputs * factor_a * gain_a).astype(jnp.bfloat16)
    query_raw = jnp.dot(normed_a, query_w, preferred_element_type=jnp.float32)
    keyval_raw = jnp.dot(normed_a, keyval_w, preferred_element_type=jnp.float32)
    queries = rotate(query_raw.reshape(tok, HEADS, HEAD_DIM), places, 1.0).astype(jnp.bfloat16)
    keys = rotate(keyval_raw[:, :kv_width].reshape(tok, KV_HEADS, HEAD_DIM), places, 1.0).astype(
        jnp.bfloat16
    )
    values = keyval_raw[:, kv_width:].reshape(tok, KV_HEADS, HEAD_DIM).astype(jnp.bfloat16)
    key_copies = jnp.stack([keys[:, j] for j in which], 1)
    value_copies = jnp.stack([values[:, j] for j in which], 1)
    spread_normed = jnp.broadcast_to(normed_a[:, None, :], (tok, n_uly, D))
    head_q, head_k, head_v, head_normed = (
        lax.all_to_all(queries, "ulysses", split_axis=1, concat_axis=0, tiled=True),
        lax.all_to_all(key_copies, "ulysses", split_axis=1, concat_axis=0, tiled=True),
        lax.all_to_all(value_copies, "ulysses", split_axis=1, concat_axis=0, tiled=True),
        lax.all_to_all(spread_normed, "ulysses", split_axis=1, concat_axis=0, tiled=True),
    )
    key_local = head_k[:, 0, :]
    value_local = head_v[:, 0, :]
    normed_group = head_normed[:, 0, :]
    q_pos = blk_index * group + jnp.arange(group, dtype=jnp.int32)
    q_begin = doc_begin(q_pos, doc_starts)
    start_state = (
        jnp.full((heads_dev, group), NEG, jnp.float32),
        jnp.zeros((heads_dev, group), jnp.float32),
        jnp.zeros((group, heads_dev, HEAD_DIM), jnp.float32),
    )
    state = start_state
    key_rows = lax.all_gather(key_local, "blk", axis=0, tiled=True)
    value_rows = lax.all_gather(value_local, "blk", axis=0, tiled=True)
    key_blocks, size = split_blocks(key_rows)
    value_blocks, _ = split_blocks(value_rows)

    def attend_step(inner, item):
        key_blk, value_blk, number = item
        k_start = number * size
        live = (k_start <= q_pos[-1]) & (k_start + size - 1 >= q_begin[0])

        def attend_work(current):
            top, total, acc = current
            k_pos = k_start + jnp.arange(size, dtype=jnp.int32)
            visible = visible_mask(q_pos, q_begin, k_pos)[None]
            scores = (
                jnp.einsum("qhd,kd->hqk", head_q, key_blk, preferred_element_type=jnp.float32)
                * scale
            )
            scores = jnp.where(visible, scores, NEG)
            new_top = jnp.maximum(top, jnp.max(scores, -1))
            weights = jnp.where(visible, jnp.exp(scores - new_top[:, :, None]), 0.0)
            keep = jnp.exp(top - new_top)
            total = total * keep + jnp.sum(weights, -1)
            acc = acc * jnp.transpose(keep)[:, :, None] + jnp.einsum(
                "hqk,kd->qhd",
                weights.astype(jnp.bfloat16),
                value_blk,
                preferred_element_type=jnp.float32,
            )
            return (new_top, total, acc)

        return (lax.cond(live, attend_work, lambda current: current, inner), None)

    state, _ = lax.scan(
        attend_step,
        state,
        (key_blocks, value_blocks, jnp.arange(key_blocks.shape[0], dtype=jnp.int32)),
    )
    top, total, acc = state
    mixed = acc / jnp.transpose(total)[:, :, None]
    mixed_low = mixed.astype(jnp.bfloat16)
    lse = top + jnp.log(total)
    attended = lax.all_to_all(
        mixed_low, "ulysses", split_axis=0, concat_axis=1, tiled=True
    ).reshape(tok, q_width)
    attn_branch = contract(attended, out_w, 1, 1)
    hidden = inputs + attn_branch
    factor_m = lax.rsqrt(jnp.mean(hidden * hidden, -1, keepdims=True) + EPS)
    normed_m = (hidden * factor_m * gain_m).astype(jnp.bfloat16)
    experts = n_blk // 2
    capacity = min(tok, 2 * tok * TOP // experts)
    flat_ids = expert_ids.reshape(-1)
    picks = (flat_ids[:, None] == jnp.arange(experts, dtype=jnp.int32)[None, :]).astype(jnp.int32)
    slots = jnp.sum((jnp.cumsum(picks, 0) - 1) * picks, -1)

    def dispatch(rows):
        buffer = jnp.zeros((experts, capacity, D), jnp.bfloat16).at[flat_ids, slots].set(rows)
        return route(jnp.repeat(buffer, 2, axis=0)).reshape(n_blk * capacity, D)

    def collect(rows):
        back = route(rows.astype(jnp.bfloat16).reshape(n_blk, capacity, D))
        return back[2 * flat_ids, slots].astype(jnp.float32) + back[2 * flat_ids + 1, slots].astype(
            jnp.float32
        )

    expert_in = dispatch(jnp.repeat(normed_m, TOP, axis=0))
    gate_pre = jnp.dot(expert_in, gate_w, preferred_element_type=jnp.float32)
    up_pre = jnp.dot(expert_in, up_w, preferred_element_type=jnp.float32)
    act = (jax.nn.silu(gate_pre) * up_pre).astype(jnp.bfloat16)
    expert_out = contract(act, down_w, 1, 1)
    returned = collect(expert_out).reshape(tok, TOP, D)
    moe_branch = jnp.sum(gate_weights[:, :, None] * returned, 1)
    result = hidden + moe_branch
    layer_output = result.astype(jnp.bfloat16)
    grad_res = grad_output.astype(jnp.float32)
    routed_grad = (
        (gate_weights[:, :, None] * grad_res[:, None, :]).reshape(tok * TOP, D).astype(jnp.bfloat16)
    )
    expert_grad = dispatch(routed_grad)
    grad_act = jnp.dot(expert_grad, down_w, preferred_element_type=jnp.float32)
    grad_down = contract(expert_grad, act, 0, 0)
    sig = jax.nn.sigmoid(gate_pre)
    grad_gate_pre = (grad_act * up_pre * sig * (1.0 + gate_pre * (1.0 - sig))).astype(jnp.bfloat16)
    grad_up_pre = (grad_act * gate_pre * sig).astype(jnp.bfloat16)
    grad_gate = contract(expert_in, grad_gate_pre, 0, 0)
    grad_up = contract(expert_in, grad_up_pre, 0, 0)
    grad_in = contract(grad_gate_pre, gate_w, 1, 1) + contract(grad_up_pre, up_w, 1, 1)
    grad_normed_m = jnp.sum(collect(grad_in).reshape(tok, TOP, D), 1)
    grad_gain_m = jnp.sum(grad_normed_m * hidden * factor_m, 0)
    grad_hidden = grad_res + norm_back(hidden, factor_m, gain_m, grad_normed_m)
    grad_hidden_low = grad_hidden.astype(jnp.bfloat16)
    grad_attended = jnp.dot(grad_hidden_low, out_w, preferred_element_type=jnp.float32).astype(
        jnp.bfloat16
    )
    spread_hidden = jnp.broadcast_to(grad_hidden_low[:, None, :], (tok, n_uly, D))
    head_grad, head_hidden = (
        lax.all_to_all(
            grad_attended.reshape(tok, HEADS, HEAD_DIM),
            "ulysses",
            split_axis=1,
            concat_axis=0,
            tiled=True,
        ),
        lax.all_to_all(spread_hidden, "ulysses", split_axis=1, concat_axis=0, tiled=True),
    )
    grad_out_slice = contract(
        head_hidden[:, 0, :], mixed_low.reshape(group, heads_dev * HEAD_DIM), 0, 0
    )
    delta = jnp.transpose(jnp.sum(head_grad.astype(jnp.float32) * mixed, -1))
    total_keys = group * n_blk
    zero_q = jnp.zeros((group, heads_dev, HEAD_DIM), jnp.float32)
    fold_start = (
        zero_q,
        jnp.zeros((total_keys, HEAD_DIM), jnp.float32),
        jnp.zeros((total_keys, HEAD_DIM), jnp.float32),
    )
    state = fold_start
    key_rows = lax.all_gather(key_local, "blk", axis=0, tiled=True)
    value_rows = lax.all_gather(value_local, "blk", axis=0, tiled=True)
    key_blocks, grads_size = split_blocks(key_rows)
    value_blocks, _ = split_blocks(value_rows)

    def grads_step(inner, item):
        key_blk, value_blk, number = item
        k_start = number * grads_size
        live = (k_start <= q_pos[-1]) & (k_start + grads_size - 1 >= q_begin[0])

        def grads_work(current):
            part_q, part_k, part_v = backward_block(
                head_q, head_grad, lse, delta, q_pos, q_begin, key_blk, value_blk, k_start, scale
            )
            grad_q, grad_keys, grad_values = current
            grad_keys = lax.dynamic_update_slice_in_dim(
                grad_keys,
                lax.dynamic_slice_in_dim(grad_keys, k_start, grads_size, 0) + part_k,
                k_start,
                0,
            )
            grad_values = lax.dynamic_update_slice_in_dim(
                grad_values,
                lax.dynamic_slice_in_dim(grad_values, k_start, grads_size, 0) + part_v,
                k_start,
                0,
            )
            return (grad_q + part_q, grad_keys, grad_values)

        return (lax.cond(live, grads_work, lambda current: current, inner), None)

    state, _ = lax.scan(
        grads_step,
        state,
        (key_blocks, value_blocks, jnp.arange(key_blocks.shape[0], dtype=jnp.int32)),
    )
    grad_q = state[0]
    grad_k, grad_v = (
        lax.psum_scatter(state[1], "blk", scatter_dimension=0, tiled=True),
        lax.psum_scatter(state[2], "blk", scatter_dimension=0, tiled=True),
    )
    group_places = q_pos - q_begin
    grad_q_pre = rotate(grad_q.astype(jnp.bfloat16).astype(jnp.float32), group_places, -1.0).astype(
        jnp.bfloat16
    )
    grad_query_slice = contract(normed_group, grad_q_pre.reshape(group, heads_dev * HEAD_DIM), 0, 0)
    token_q, token_k, token_v = (
        lax.all_to_all(grad_q_pre, "ulysses", split_axis=0, concat_axis=1, tiled=True),
        lax.all_to_all(
            grad_k.astype(jnp.bfloat16)[:, None, :],
            "ulysses",
            split_axis=0,
            concat_axis=1,
            tiled=True,
        ),
        lax.all_to_all(
            grad_v.astype(jnp.bfloat16)[:, None, :],
            "ulysses",
            split_axis=0,
            concat_axis=1,
            tiled=True,
        ),
    )
    summed_k = []
    summed_v = []
    for head in range(KV_HEADS):
        members = [c for c in range(n_uly) if which[c] == head]
        summed_k.append(sum((token_k[:, c].astype(jnp.float32) for c in members)))
        summed_v.append(sum((token_v[:, c].astype(jnp.float32) for c in members)))
    grad_key_heads = jnp.stack(summed_k, 1)
    grad_value_heads = jnp.stack(summed_v, 1)
    grad_query_pre = token_q.reshape(tok, q_width)
    grad_key_pre = rotate(grad_key_heads, places, -1.0).reshape(tok, kv_width)
    grad_keyval_pre = jnp.concatenate(
        [grad_key_pre, grad_value_heads.reshape(tok, kv_width)], 1
    ).astype(jnp.bfloat16)
    grad_normed_a = contract(grad_query_pre, query_w, 1, 1) + contract(
        grad_keyval_pre, keyval_w, 1, 1
    )
    grad_keyval_w = contract(normed_a, grad_keyval_pre, 0, 0)
    grad_gain_a = jnp.sum(grad_normed_a * inputs * factor_a, 0)
    grad_input = grad_hidden + norm_back(inputs, factor_a, gain_a, grad_normed_a)
    n_dev = n_blk * n_uly
    squares = jnp.stack(
        [
            jnp.sum(attn_branch * attn_branch),
            jnp.sum(moe_branch * moe_branch),
            jnp.sum(result * result),
        ]
    )
    square_rows = jnp.broadcast_to(squares[None, :], (n_dev, 3))
    part_gate, part_up, part_down, uly_gain_a, uly_gain_m, uly_keyval, uly_squares = (
        lax.psum_scatter(
            grad_gate.astype(jnp.bfloat16), "ulysses", scatter_dimension=0, tiled=True
        ).astype(jnp.float32),
        lax.psum_scatter(
            grad_up.astype(jnp.bfloat16), "ulysses", scatter_dimension=0, tiled=True
        ).astype(jnp.float32),
        lax.psum_scatter(
            grad_down.astype(jnp.bfloat16), "ulysses", scatter_dimension=0, tiled=True
        ).astype(jnp.float32),
        lax.psum_scatter(
            reorder_rows(grad_gain_a, n_blk, n_uly).astype(jnp.bfloat16),
            "ulysses",
            scatter_dimension=0,
            tiled=True,
        ).astype(jnp.float32),
        lax.psum_scatter(
            reorder_rows(grad_gain_m, n_blk, n_uly).astype(jnp.bfloat16),
            "ulysses",
            scatter_dimension=0,
            tiled=True,
        ).astype(jnp.float32),
        lax.psum_scatter(
            reorder_rows(grad_keyval_w, n_blk, n_uly).astype(jnp.bfloat16),
            "ulysses",
            scatter_dimension=0,
            tiled=True,
        ).astype(jnp.float32),
        lax.psum_scatter(
            square_rows.astype(jnp.bfloat16), "ulysses", scatter_dimension=0, tiled=True
        ).astype(jnp.float32),
    )
    part_outw, part_query, part_gain_a, part_gain_m, part_keyval, square_row = (
        lax.psum_scatter(grad_out_slice, "blk", scatter_dimension=0, tiled=True),
        lax.psum_scatter(grad_query_slice, "blk", scatter_dimension=0, tiled=True),
        lax.psum_scatter(uly_gain_a, "blk", scatter_dimension=0, tiled=True),
        lax.psum_scatter(uly_gain_m, "blk", scatter_dimension=0, tiled=True),
        lax.psum_scatter(uly_keyval, "blk", scatter_dimension=0, tiled=True),
        lax.psum_scatter(uly_squares, "blk", scatter_dimension=0, tiled=True),
    )
    branch_rms = jnp.sqrt(square_row[0] / (tok * n_dev * D))
    return (
        layer_output,
        grad_input,
        part_gain_a,
        part_gain_m,
        part_query,
        part_keyval,
        part_outw,
        part_gate,
        part_up,
        part_down,
        branch_rms,
    )


MESH = pl.DeviceIdType.MESH
LANES = 128
LOG2E = 1.4426950408889634


class Place:
    def __init__(self, depth):
        self.blk = lax.axis_index("blk")
        self.u = lax.axis_index("ulysses")
        self.depth = depth
        self.z = self.blk // 4
        self.x = (self.blk // 2) % 2
        self.c = self.blk % 2
        self.up = (self.blk + 4, self.u)
        self.down = (self.blk - 4, self.u)
        self.across = (self.blk + 2 - 4 * self.x, self.u)
        self.sibling = (self.blk + 1 - 2 * self.c, self.u)
        self.other = (self.blk, 1 - self.u)
        self.has_up = self.z < depth - 1
        self.has_down = self.z > 0

    def along(self, z):
        return (self.blk + 4 * (z - self.z), self.u)

    def slot(self, z, x, c):
        return z * 4 + x * 2 + c

    def greet(self, sibling=False, other=False, plane=True):
        barrier = pltpu.get_barrier_semaphore()

        def hail(device):
            pl.semaphore_signal(barrier, inc=1, device_id=device, device_id_type=MESH)

        count = 0
        if plane:
            hail(self.across)
            for d in range(1, self.depth):
                pl.when(self.z >= d)(lambda d=d: hail(self.along(self.z - d)))
                pl.when(self.z + d < self.depth)(lambda d=d: hail(self.along(self.z + d)))
            count = self.depth
        if sibling:
            hail(self.sibling)
            count = count + 1
        if other:
            hail(self.other)
            count = count + 1
        pl.semaphore_wait(barrier, count)


class Wires:
    def __init__(self, sems):
        self.sems = sems
        self.used = 0

    def take(self, count):
        base = self.used
        self.used += count
        return lambda index: self.sems.at[base + index]


def each(act, items):
    for item in items:
        act(item)


def remote(src, dst, send, recv, device):
    return pltpu.make_async_remote_copy(
        src_ref=src, dst_ref=dst, send_sem=send, recv_sem=recv, device_id=device, device_id_type=MESH
    )


class Gather:
    def __init__(self, place, wires, src, out, cores, up_only=False, chain=False, far=False):
        self.p, self.src, self.out, self.cores, self.up_only, self.chain = place, src, out, cores, up_only, chain
        n = place.depth
        self.s_z = [wires.take(n) for _ in range(2 if chain else 1)]
        self.s_across = wires.take(n)
        self.r_z, self.r_x = wires.take(n), wires.take(n)
        if cores:
            self.s_core, self.r_core = wires.take(2 * n), wires.take(2 * n)
        self.far = wires.take(1)(0) if far else None

    def _across(self, zz, xx, src=None):
        dst = self.out(zz, xx, self.p.c)
        return remote(dst if src is None else src, dst, self.s_across(zz), self.r_x(zz), self.p.across)

    def _core(self, zz, xx, src=None):
        dst = self.out(zz, xx, self.p.c)
        at = zz * 2 + xx
        return remote(dst if src is None else src, dst, self.s_core(at), self.r_core(at), self.p.sibling)

    def _along(self, zz, to, src=None):
        p = self.p
        dst = self.out(zz, p.x, p.c)
        return remote(dst if src is None else src, dst, self.s_z[0](to), self.r_z(zz), p.along(to))

    def _next(self, zz, up, src=None):
        p = self.p
        dst = self.out(zz, p.x, p.c)
        return remote(
            dst if src is None else src, dst, self.s_z[up](zz), self.r_z(zz), p.along(p.z + (1 if up else -1))
        )

    def start_z(self, in_place=False):
        p = self.p
        src = None if in_place else self.src
        if self.chain:
            pl.when(p.has_up)(lambda: self._next(p.z, 1, src).start())
            pl.when(p.has_down)(lambda: self._next(p.z, 0, src).start())
            return
        for d in range(1, p.depth):
            pl.when(p.z + d < p.depth)(lambda d=d: self._along(p.z, p.z + d, src).start())
            if not self.up_only:
                pl.when(p.z >= d)(lambda d=d: self._along(p.z, p.z - d, src).start())

    def start_x(self, in_place=False):
        p = self.p
        src = None if in_place else self.src
        self._across(p.z, p.x, src).start()
        if self.cores:
            self._core(p.z, p.x, src).start()
        if self.far is not None:
            pltpu.make_async_copy(self.src, self.out(p.z, p.x, p.c), self.far).start()
        elif not in_place:
            self.out(p.z, p.x, p.c)[...] = self.src[...]

    def start(self, in_place=False):
        self.start_z(in_place)
        self.start_x(in_place)

    def hop(self, d):
        p = self.p

        def take(zz, up):
            remote(
                self.out(zz, p.x, p.c), self.out(zz, p.x, p.c), self.s_z[0](0), self.r_z(zz), p.across
            ).wait_recv()
            if self.chain:
                pl.when(p.has_up if up else p.has_down)(lambda: self._next(zz, up).start())
            self._across(zz, p.x).start()
            if self.cores:
                self._core(zz, p.x).start()

        pl.when(p.z >= d)(lambda: take(p.z - d, 1))
        if not self.up_only:
            pl.when(p.z + d < p.depth)(lambda: take(p.z + d, 0))

    def cross(self, d):
        p = self.p

        def take(zz):
            self._across(zz, 1 - p.x).wait_recv()
            if self.cores:
                self._core(zz, 1 - p.x).start()

        if isinstance(d, int) and d == 0:
            take(p.z)
        else:
            pl.when(p.z >= d)(lambda: take(p.z - d))
            if not self.up_only:
                pl.when(p.z + d < p.depth)(lambda: take(p.z + d))

    def crossed(self, zz):
        self._across(zz, 1 - self.p.x).wait_recv()

    def core(self, zz, xx):
        self._core(zz, xx).wait_recv()

    def finish(self, cores_taken=False):
        p = self.p
        for zz in range(p.depth):

            def ends(zz=zz):
                if self.cores:
                    for xx in range(2):
                        if not cores_taken:
                            self._core(zz, xx).wait_recv()
                        self._core(zz, xx).wait_send()
                self._across(zz, p.x).wait_send()

            if self.up_only and zz > 0:
                pl.when(p.z >= zz)(ends)
            else:
                ends()
            if self.chain:
                pl.when(p.has_up & (p.z >= zz))(lambda zz=zz: self._next(zz, 1).wait_send())
                pl.when(p.has_down & (p.z <= zz))(lambda zz=zz: self._next(zz, 0).wait_send())
            else:
                away = (p.z < zz) if self.up_only else (p.z != zz)
                pl.when(away)(lambda zz=zz: self._along(p.z, zz).wait_send())
        if self.far is not None:
            pltpu.make_async_copy(self.src, self.out(p.z, p.x, p.c), self.far).wait()


class Scatter:
    def __init__(self, place, wires, part, out, rx, rz, pieces, down_only=False, ready=()):
        self.ready = ready
        self.p, self.part, self.out, self.rx, self.rz = place, part, out, rx, rz
        n = place.depth
        total = n * pieces
        self.pieces, self.down_only = pieces, down_only
        self.sx, self.cx = wires.take(total), wires.take(total)
        self.sz, self.cz = wires.take(total), wires.take(total)
        if down_only:
            self.order = list(range(n))
        else:
            self.order = [n - 1] + list(range(n - 1))
        self.items = [(zz, k) for zz in self.order if zz not in ready for k in range(pieces)]

    def _x(self, zz, k):
        i = zz * self.pieces + k
        return remote(self.part(zz, 1 - self.p.x, k), self.rx(zz, k), self.sx(i), self.cx(i), self.p.across)

    def _z(self, zz, k, source=None):
        p = self.p
        source = p.z if source is None else source
        return remote(
            self.rx(zz, k),
            self.rz(source, k),
            self.sz(zz * self.pieces + k),
            self.cz(source * self.pieces + k),
            p.along(zz),
        )

    def _live(self, zz, act):
        if self.down_only and zz > 0:
            pl.when(self.p.z >= zz)(act)
        else:
            act()

    def begin(self, t):
        if t < len(self.items):
            zz, k = self.items[t]
            self._live(zz, lambda: self._x(zz, k).start())

    def send(self, zz):
        for k in range(self.pieces):
            self._x(zz, k).start()

    def take(self, zz, k):
        p = self.p

        def act():
            self._x(zz, k).wait_recv()

            def forward():
                total = self.part(zz, p.x, k)[...].astype(jnp.float32)
                total = total + self.rx(zz, k)[...].astype(jnp.float32)
                self.rx(zz, k)[...] = total.astype(jnp.bfloat16)
                self._z(zz, k).start()

            pl.when(p.z != zz)(forward)

        self._live(zz, act)

    def land(self, t):
        self.take(*self.items[t])

    def forward(self):
        for zz in self.ready:
            for k in range(self.pieces):
                pl.when(self.p.z != zz)(lambda zz=zz, k=k: self._z(zz, k).start())

    def finish(self):
        p = self.p
        n = p.depth
        for zz, k in [(zz, k) for zz in self.order for k in range(self.pieces)]:
            if zz not in self.ready:
                self._live(zz, lambda zz=zz, k=k: self._x(zz, k).wait_send())
            away = (p.z > zz) if self.down_only else (p.z != zz)
            pl.when(away)(lambda zz=zz, k=k: self._z(zz, k).wait_send())

            def store(zz=zz, k=k):
                total = self.rx(zz, k)[...].astype(jnp.float32)
                if zz not in self.ready:
                    total = total + self.part(zz, p.x, k)[...].astype(jnp.float32)
                for source in range(zz + 1 if self.down_only else 0, n):
                    if source != zz:
                        self._z(zz, k, source).wait_recv()
                        total = total + self.rz(source, k)[...].astype(jnp.float32)
                self.out(k)[...] = total

            pl.when(p.z == zz)(store)


class CoreScatter:
    def __init__(self, place, wires, src, rc, out, rx, rz, down_only=False):
        self.p, self.src, self.rc, self.down_only = place, src, rc, down_only
        n = place.depth
        self.sc, self.cc = wires.take(n), wires.take(n)
        self.plane = Scatter(
            place, wires, lambda zz, xx, k: rc.at[zz * 2 + xx], lambda k: out,
            lambda zz, k: rx.at[zz], lambda source, k: rz.at[source], 1, down_only,
        )
        self.order = self.plane.order

    def _trade(self, zz):
        p = self.p
        if self.down_only:
            at = pl.ds(2 * zz, 2)
            return remote(self.src.at[at, 1 - p.c], self.rc.at[at], self.sc(zz), self.cc(zz), p.sibling)
        return remote(self.src.at[:, 1 - p.c], self.rc, self.sc(0), self.cc(0), p.sibling)

    def trade(self, t=0):
        zz = self.order[t]
        self.plane._live(zz, lambda: self._trade(zz).start())

    def join(self, t):
        p = self.p
        zz = self.order[t]

        def act():
            if self.down_only or t == 0:
                self._trade(zz).wait_recv()
            for xx in range(2):
                at = zz * 2 + xx
                self.rc[at] = (
                    self.src[at, p.c].astype(jnp.float32) + self.rc[at].astype(jnp.float32)
                ).astype(jnp.bfloat16)

        self.plane._live(zz, act)
        self.plane.begin(t)

    def land(self, t):
        self.plane.land(t)

    def release(self):
        for t, zz in enumerate(self.order):
            if self.down_only or t == 0:
                self.plane._live(zz, lambda zz=zz: self._trade(zz).wait_send())

    def finish(self):
        self.plane.finish()


def mm(left, right):
    return jnp.dot(left, right, preferred_element_type=jnp.float32)


def flip(tile):
    return tile.astype(jnp.float32).T.astype(jnp.bfloat16)


def hidden_bias(first_key, first_query, begin, keys):
    queries = begin.shape[1]
    k_pos = first_key + lax.broadcasted_iota(jnp.int32, (keys, queries), 0)
    q_pos = first_query + lax.broadcasted_iota(jnp.int32, (keys, queries), 1)
    return jnp.where((k_pos >= begin) & (k_pos <= q_pos), 0.0, NEG)


def front_kernel(
    depth, scale, docs, x, dy, gain_a, gain_m, wq, wkv, wo, ids, shares_of, freq, e0, e1, e2,
    b, hid, attn_sq, normed_t, q_rows, qt, o, ot, lse, gain_rows, g_all, x_all, begin, cosine, sine,
    kv_out, w_out, wo_out, dy_all, f0, f1, f2,
    kv, w_all, wo_all, own, square, g_own, wa_own, normed, raw, top, total, acc, p_out, p_in, sems,
):
    f32, bf = jnp.float32, jnp.bfloat16
    p = Place(depth)
    p.greet(sibling=True, other=True)
    wires = Wires(sems)
    u, blk = p.u, p.blk
    tok, width = x.shape
    group, q_half = o.shape
    heads = q_half // HEAD_DIM
    kv_half = 2 * HEAD_DIM
    rows_dev = wq.shape[0]
    half, cols = e0.shape
    experts = 2 * depth

    def rows_of(ref, z, xx, c, member):
        row = (p.slot(z, xx, c) * 2 + member) * rows_dev
        return ref.at[pl.ds(pl.multiple_of(row, 16), rows_dev)]

    wa_mine = Gather(p, wires, wa_own.at[u], lambda z, xx, c: rows_of(w_all, z, xx, c, u), True, chain=True)
    wa_peer = Gather(p, wires, None, lambda z, xx, c: rows_of(w_all, z, xx, c, 1 - u), True, chain=True)
    wos = Gather(
        p, wires, None,
        lambda z, xx, c: wo_all.at[pl.ds(pl.multiple_of(p.slot(z, xx, c) * 2 * rows_dev, 16), 2 * rows_dev)],
        True, chain=True,
    )
    kvs = Gather(p, wires, None, lambda z, xx, c: kv.at[p.slot(z, xx, c)], True, up_only=True)
    piece = tok // 2
    dys = [
        Gather(
            p, wires, dy.at[pl.ds(k * piece, piece)],
            lambda z, xx, c, k=k: dy_all.at[z * 2 + xx, pl.ds(k * piece, piece)], False, chain=True, far=True,
        )
        for k in range(2)
    ]
    gws = Gather(p, wires, g_own, lambda z, xx, c: g_all.at[z * 2 + xx], False, chain=True)
    ws, wr = wires.take(2), wires.take(2)
    xs, xr = wires.take(1)(0), wires.take(1)(0)
    es, er = wires.take(3), wires.take(3)
    cs, cr = wires.take(6), wires.take(6)
    ps, pr = wires.take(3), wires.take(3)

    for h in range(2):
        wa_own[h, :, :q_half] = wq[:, h * q_half : (h + 1) * q_half]
        for part in range(2):
            wa_own[h, :, q_half + part * HEAD_DIM : q_half + (part + 1) * HEAD_DIM] = wkv[
                :, (part * 2 + h) * HEAD_DIM : (part * 2 + h + 1) * HEAD_DIM
            ]
    square[...] = jnp.zeros(square.shape, f32)
    square[0:1, :rows_dev] = gain_a[...].astype(f32)
    square[1:2, :rows_dev] = gain_m[...].astype(f32)
    columns = square[...].T[:rows_dev, :].astype(bf)
    for h in range(2):
        wa_own[h, :, q_half + kv_half :] = columns

    wa_swap = remote(wa_own.at[1 - u], rows_of(w_all, p.z, p.x, p.c, u), ws(0), wr(0), p.other)
    wo_swap = remote(
        wo.at[:, pl.ds(pl.multiple_of((1 - u) * q_half, LANES), q_half)],
        rows_of(wo_all, p.z, p.x, p.c, u), ws(1), wr(1), p.other,
    )
    x_swap = remote(x, x_all.at[u], xs, xr, p.other)

    def part(ref, row, core):
        return ref.at[
            pl.ds(pl.multiple_of(row * half, half), half), pl.ds(pl.multiple_of(core * cols, LANES), cols)
        ]

    halves = ((e0, f0), (e1, f1), (e2, f2))
    ls, ks = wires.take(3), wires.take(3)
    loads = [pltpu.make_async_copy(e, own.at[i], ls(i)) for i, (e, f) in enumerate(halves)]
    keeps = [pltpu.make_async_copy(own.at[i], part(f, u, p.c), ks(i)) for i, (e, f) in enumerate(halves)]
    swaps = [remote(own.at[i], part(f, u, p.c), es(i), er(i), p.other) for i, (e, f) in enumerate(halves)]
    shares = [remote(own.at[i], part(f, u, p.c), cs(i), cr(i), p.sibling) for i, (e, f) in enumerate(halves)]
    passes = [
        remote(part(f, 1 - u, p.c), part(f, 1 - u, p.c), cs(3 + i), cr(3 + i), p.sibling)
        for i, (e, f) in enumerate(halves)
    ]
    os_ = wires.take(3)
    stores = [
        pltpu.make_async_copy(v, r, os_(i)) for i, (v, r) in enumerate(((kv, kv_out), (w_all, w_out), (wo_all, wo_out)))
    ]

    def expert_out(i):
        swaps[i].start()
        shares[i].start()

    def expert_in(i):
        swaps[i].wait_recv()
        passes[i].start()

    wa_swap.start()
    wa_mine.start()
    wo_swap.start()
    x_swap.start()
    each(lambda load: load.start(), loads)

    def starts(places):
        first = jnp.zeros(places.shape, jnp.int32)
        for i in range(docs.shape[0]):
            first = jnp.where(docs[i] <= places, jnp.maximum(first, docs[i]), first)
        return first

    begin[...] = starts(blk * group + lax.broadcasted_iota(jnp.int32, begin.shape, 1))
    places = blk * group + lax.broadcasted_iota(jnp.int32, cosine.shape, 0)
    angle = (places - starts(places)).astype(f32) * freq[0:1, :]
    cosine[...] = jnp.cos(angle)
    sine[...] = jnp.where(lax.broadcasted_iota(jnp.int32, sine.shape, 1) < HEAD_DIM // 2, -1.0, 1.0) * jnp.sin(angle)
    for e in range(experts):
        g_own[e : e + 1, :] = jnp.sum(jnp.where(ids[...] == e, shares_of[...], 0.0), axis=0, keepdims=True)
    wa_swap.wait_recv()
    wa_peer.start(in_place=True)
    x_all[u] = x[...]
    rows_of(wo_all, p.z, p.x, p.c, u)[...] = wo[:, pl.ds(pl.multiple_of(u * q_half, LANES), q_half)]
    for i in range(3):
        loads[i].wait()
        keeps[i].start()
    gws.start()
    for d in range(1, depth):
        for g in (wa_mine, wa_peer):
            g.hop(d)
            g.cross(d - 1)
        gws.hop(d)
        gws.cross(d - 1)
        if d == 1:
            wo_swap.wait_recv()
            wos.start(in_place=True)
            expert_out(0)
        else:
            wos.hop(d - 1)
    gws.cross(depth - 1)
    dys[0].start()
    expert_out(1)
    x_swap.wait_recv()
    for g in (wa_mine, wa_peer):
        g.cross(depth - 1)
    for g in (wa_mine, wa_peer):
        g.finish()
    stores[1].start()
    gain_rows[...] = w_all[:, q_half + kv_half :].astype(f32).T[:8, :]
    for m in range(2):
        xf = x_all[m].astype(f32)
        r1 = lax.rsqrt(jnp.mean(xf * xf, -1, keepdims=True) + EPS)
        normed[m * tok : (m + 1) * tok, :] = (xf * r1 * gain_rows[0:1, :]).astype(bf)
    raw[...] = mm(normed[...], w_all[:, : q_half + kv_half])

    def rope(values):
        return values * cosine[...] + pltpu.roll(values, HEAD_DIM // 2, 1) * sine[...]

    here = p.slot(p.z, p.x, p.c)
    kv[here, :, :HEAD_DIM] = rope(raw[:, q_half : q_half + HEAD_DIM]).astype(bf)
    kv[here, :, HEAD_DIM:] = raw[:, q_half + HEAD_DIM :].astype(bf)
    kvs.start(in_place=True)
    for h in range(heads):
        hs = slice(h * HEAD_DIM, (h + 1) * HEAD_DIM)
        turned = rope(raw[:, hs])
        q_rows[h * group : (h + 1) * group, :] = turned.astype(bf)
        qt[:, h * group : (h + 1) * group] = turned.T.astype(bf)
    for j in range(0, width, 256):
        normed_t[j : j + 256, :] = flip(normed[:, j : j + 256])
    top[...] = jnp.full(top.shape, NEG, f32)
    total[...] = jnp.zeros(total.shape, f32)
    ot[...] = jnp.zeros(ot.shape, f32)

    background = {}

    def at_step(s, act):
        background.setdefault(s, []).append(act)

    at_step(0, lambda: kvs.cross(0))
    at_step(0, lambda: kvs.hop(1))
    at_step(0, dys[1].start_z)
    at_step(1, lambda: wos.hop(3))
    at_step(1, lambda: dys[0].hop(1))
    at_step(2, lambda: kvs.hop(2))
    at_step(3, lambda: kvs.cross(1))
    at_step(2, dys[1].start_x)
    at_step(3, lambda: wos.cross(0))
    at_step(3, lambda: dys[1].hop(1))
    at_step(4, lambda: kvs.hop(3))
    at_step(5, lambda: kvs.cross(2))
    at_step(5, lambda: wos.cross(1))
    at_step(2, lambda: expert_in(0))
    at_step(2, lambda: expert_out(2))
    at_step(5, lambda: dys[0].hop(2))
    at_step(6, lambda: kvs.cross(3))
    at_step(6, lambda: dys[1].hop(2))
    at_step(7, lambda: wos.cross(2))
    at_step(7, lambda: wos.cross(3))

    def step(s, carry):
        d = jnp.where(s < 3, s // 2, jnp.where(s % 2 == 1, (s + 1) // 2, (s - 2) // 2))
        d = jnp.where(s == 7, 3, d)
        crossed = (s == 1) | (s == 4) | (s == 6) | (s == 7)
        zz = p.z - d
        xx = jnp.where(crossed, 1 - p.x, p.x)
        j = p.slot(zz, xx, 0)

        pl.when(zz >= 0)(lambda: kvs.core(zz, xx))

        def work():
            pair = kv[pl.ds(j, 2)].reshape(2 * group, kv_half)
            k = pair[:, :HEAD_DIM]
            vt = flip(pair[:, HEAD_DIM:])
            bias = hidden_bias(j * group, blk * group, begin[0:1, :], 2 * group)
            at = [slice(h * group, (h + 1) * group) for h in range(heads)]
            sc = [mm(k, qt[:, hs]) * (scale * LOG2E) + bias for hs in at]
            old = [top[0:1, hs] for hs in at]
            new = [jnp.maximum(o_, jnp.max(s_, axis=0, keepdims=True)) for o_, s_ in zip(old, sc)]
            e = [jnp.exp2(s_ - n_) for s_, n_ in zip(sc, new)]
            part = [jnp.sum(e_, axis=0, keepdims=True) for e_ in e]
            mixed = [mm(vt, e_.astype(bf)) for e_ in e]
            for h, hs in enumerate(at):
                keep = jnp.exp2(old[h] - new[h])
                total[0:1, hs] = total[0:1, hs] * keep + part[h]
                ot[:, hs] = ot[:, hs] * keep + mixed[h]
                top[0:1, hs] = new[h]

        pl.when((zz >= 0) & (j <= blk))(work)
        for when, acts in background.items():
            pl.when(s == when)(lambda acts=acts: each(lambda act: act(), acts))
        return carry

    lax.fori_loop(0, 2 * depth, step, 0)

    wos.finish()
    stores[2].start()
    sums = total[0:1, :]
    lse[...] = jnp.broadcast_to(top[0:1, :] + jnp.log2(sums), lse.shape)
    for h in range(heads):
        at = slice(h * group, (h + 1) * group)
        mixed = ot[:, at] / sums[:, at]
        ot[:, at] = mixed
        o[:, h * HEAD_DIM : (h + 1) * HEAD_DIM] = mixed.T.astype(bf)

    wide = width // 3
    p_swaps = []
    for i in range(3):
        cb = i * wide
        acc[:, cb : cb + wide] = contract(o[...], wo_all[cb : cb + wide, :], 1, 1)
        theirs = pl.ds(pl.multiple_of((1 - u) * tok, tok), tok)
        p_out[i] = acc[theirs, cb : cb + wide].astype(bf)
        p_swaps.append(remote(p_out.at[i], p_in.at[i], ps(i), pr(i), p.other))
        p_swaps[i].start()
    each(lambda g: g.hop(3), dys)
    expert_in(1)
    for d in range(2):
        each(lambda g: g.cross(d), dys)
    mine = pl.ds(pl.multiple_of(u * tok, tok), tok)
    for i in range(3):
        p_swaps[i].wait_recv()
        acc[mine, i * wide : (i + 1) * wide] += p_in[i].astype(f32)
    branch = acc[mine, :]
    hidden = x[...].astype(f32) + branch
    hid[...] = hidden
    r2 = lax.rsqrt(jnp.mean(hidden * hidden, -1, keepdims=True) + EPS)
    b[...] = (hidden * r2 * gain_rows[1:2, :]).astype(bf)
    attn_sq[...] = jnp.broadcast_to(jnp.sum(branch * branch).reshape(1, 1), attn_sq.shape)
    for d in range(2, depth):
        each(lambda g: g.cross(d), dys)
    expert_in(2)
    kvs.finish(cores_taken=True)
    stores[0].start()
    each(lambda g: g.finish(), dys)
    gws.finish()
    wa_swap.wait_send()
    wo_swap.wait_send()
    x_swap.wait_send()
    for i in range(3):
        swaps[i].wait_send()
        keeps[i].wait()
        shares[i].wait()
        passes[i].wait()
        p_swaps[i].wait_send()
        stores[i].wait()


def front(docs, x, dy, gain_a, gain_m, wq, wkv, wo, ids, shares, experts, depth, scale, cid):
    f32, bf = jnp.float32, jnp.bfloat16
    shape = jax.ShapeDtypeStruct
    vmem = pl.BlockSpec(memory_space=pltpu.VMEM)
    hbm = pl.BlockSpec(memory_space=pl.ANY)
    V = pltpu.VMEM
    tok, width = x.shape
    group = 2 * tok
    q_half = wq.shape[1] // 2
    kv_half = 2 * HEAD_DIM
    wide = q_half + kv_half + LANES
    rows = q_half // HEAD_DIM * group
    rows_dev = wq.shape[0]
    expert = shape((2 * experts[0].shape[0], 2 * experts[0].shape[1]), bf)
    half = HEAD_DIM // 2
    freq = np.power(np.float32(ROPE_BASE), -np.arange(half, dtype=np.float32) * np.float32(2.0 / HEAD_DIM))
    freq = jnp.asarray(np.tile(freq.astype(np.float32), (8, 2)))
    return pl.pallas_call(
        functools.partial(front_kernel, depth, scale),
        out_shape=(
            shape((tok, width), bf),
            shape((tok, width), f32),
            shape((8, LANES), f32),
            shape((width, group), bf),
            shape((rows, HEAD_DIM), bf),
            shape((HEAD_DIM, rows), bf),
            shape((group, q_half), bf),
            shape((HEAD_DIM, rows), f32),
            shape((8, rows), f32),
            shape((8, width), f32),
            shape((2 * depth, 2 * depth, tok), f32),
            shape((2, tok, width), bf),
            shape((8, group), jnp.int32),
            shape((group, HEAD_DIM), f32),
            shape((group, HEAD_DIM), f32),
            shape((4 * depth, group, kv_half), bf),
            shape((width, wide), bf),
            shape((width, q_half), bf),
            shape((2 * depth, tok, width), bf),
            expert,
            expert,
            expert,
        ),
        in_specs=[pl.BlockSpec(memory_space=pltpu.SMEM)] + [vmem] * 10 + [hbm] * 3,
        out_specs=tuple([vmem] * 15 + [hbm] * 7),
        scratch_shapes=[
            V((4 * depth, group, kv_half), bf),
            V((width, wide), bf),
            V((width, q_half), bf),
            V((3,) + experts[0].shape, bf),
            V((LANES, LANES), f32),
            V((2 * depth, tok), f32),
            V((2, rows_dev, wide), bf),
            V((group, width), bf),
            V((group, q_half + kv_half), f32),
            V((8, rows), f32),
            V((8, rows), f32),
            V((group, width), f32),
            V((3, tok, width // 3), bf),
            V((3, tok, width // 3), bf),
            pltpu.SemaphoreType.DMA((8 * 16 * depth,)),
        ],
        compiler_params=pltpu.CompilerParams(
            collective_id=cid, has_side_effects=True, vmem_limit_bytes=56 * 2**20
        ),
        name="front",
    )(docs, x, dy, gain_a[None, :], gain_m[None, :], wq, wkv, wo, ids, shares, freq, *experts)


def experts_kernel(
    depth, b, dy_own, g_all, hid, gain_rows, dy_far, g_far, u_far, d_far,
    dh, dhr, gm, z_sums, z_far, eg_far,
    dy_all, wg, wu, wd, z_p, eg, z_rx, b_all, act, dgate, dup, dyr, db_p, rx, rz, db, turned, sems,
):
    f32, bf = jnp.float32, jnp.bfloat16
    p = Place(depth)
    p.greet()
    wires = Wires(sems)
    tok, width = b.shape
    hidden_units = wg.shape[1]
    expert = p.blk // 2
    pair = 2 * tok
    pieces = 2
    piece = tok // pieces

    rows = [
        Gather(
            p, wires, b.at[pl.ds(k * piece, piece)],
            lambda z, x, c, k=k: b_all.at[pl.ds(pl.multiple_of((z * 2 + x) * tok + k * piece, piece), piece)],
            False, chain=True,
        )
        for k in range(pieces)
    ]

    def cut(ref, k):
        return ref.at[pl.ds(k * piece, piece)]

    sums = Scatter(
        p, wires,
        lambda zz, xx, k: cut(db_p.at[zz * 2 + xx], k),
        lambda k: cut(db, k),
        lambda zz, k: cut(rx.at[zz], k),
        lambda slot, k: cut(rz.at[slot], k),
        pieces,
    )
    ls = wires.take(4)
    loads = [
        pltpu.make_async_copy(r, v, ls(i)) for i, (r, v) in enumerate(((dy_far, dy_all), (g_far, wg), (u_far, wu), (d_far, wd)))
    ]
    os_ = wires.take(3)
    stores = [
        pltpu.make_async_copy(v, r, os_(i))
        for i, (v, r) in enumerate(((z_p, z_far), (eg.at[pl.ds(0, 2)], eg_far.at[pl.ds(0, 2)]), (eg.at[2], eg_far.at[2])))
    ]
    each(lambda load: load.start(), loads)
    each(lambda g: g.start(), rows)
    spread = lax.broadcasted_iota(jnp.int32, (tok, 8), 1)

    def weight(slot):
        return jnp.sum(jnp.where(spread == expert, g_all[slot].T, 0.0), axis=1, keepdims=True)

    def nth(i):
        inner = jnp.where(i == 0, 1, jnp.where(i == 1, 0, i))
        other = jnp.where(i == 0, 2, jnp.where(i == 1, 1, jnp.where(i == 2, 3, 0)))
        return jnp.where(p.z == 0, i, jnp.where(p.z == depth - 1, depth - 1 - i, jnp.where(p.z == 1, inner, other)))

    def block(i, carry):
        for d in range(1, depth):
            pl.when(i == d - 1)(lambda d=d: each(lambda g: g.hop(d), rows))
        each(lambda g: g.crossed(nth(i)), rows)
        pl.when(i == 0)(lambda: each(lambda load: load.wait(), loads))
        zz = nth(i)
        at = pl.ds(pl.multiple_of(zz * pair, pair), pair)
        for xx in range(2):
            half = pl.ds(pl.multiple_of(zz * pair + xx * tok, tok), tok)
            dyr[half, :] = (weight(zz * 2 + xx) * dy_all[zz * 2 + xx].astype(f32)).astype(bf)
        for cb in range(0, hidden_units, 256):
            cs = slice(cb, cb + 256)
            gate = mm(b_all[at, :], wg[:, cs])
            up = mm(b_all[at, :], wu[:, cs])
            sig = jax.nn.sigmoid(gate)
            act[at, cs] = (gate * sig * up).astype(bf)
            dact = mm(dyr[at, :], wd[:, cs])
            dgate[at, cs] = (dact * up * sig * (1.0 + gate * (1.0 - sig))).astype(bf)
            dup[at, cs] = (dact * gate * sig).astype(bf)
        for cb in range(0, width, 512):
            cs = slice(cb, cb + 512)
            part = contract(dgate[at, :], wg[cs, :], 1, 1) + contract(dup[at, :], wu[cs, :], 1, 1)
            for xx in range(2):
                db_p[zz * 2 + xx, :, cs] = part[xx * tok : (xx + 1) * tok, :].astype(bf)
        pl.when(i == depth - 2)(lambda: sums.send(nth(2)))
        pl.when(i == depth - 1)(lambda: each(lambda n: sums.send(nth(n)), (3, 1)))
        for cb in range(0, width, 512):
            cs = slice(cb, cb + 512)
            part = contract(act[at, :], wd[cs, :], 1, 1)
            for xx in range(2):
                z_p[zz * 2 + xx, :, cs] = (
                    weight(zz * 2 + xx) * part[xx * tok : (xx + 1) * tok, :]
                ).astype(bf)
        return carry

    lax.fori_loop(0, depth, block, 0)

    stores[0].start()
    zs_, zr_ = wires.take(2 * len(EARLY)), wires.take(2 * len(EARLY))

    def z_send(n, k):
        return remote(
            cut(z_p.at[EARLY[n] * 2 + 1 - p.x], k), cut(z_rx.at[n], k), zs_(2 * n + k), zr_(2 * n + k), p.across
        )

    z_pieces = [(n, k) for n in range(len(EARLY)) for k in range(pieces)]

    wide = 256

    def grads(n):
        cs = slice(n * wide, (n + 1) * wide)
        turned[...] = flip(b_all[:, cs])
        eg[0, cs, :] = mm(turned[...], dgate[...]).astype(bf)
        eg[1, cs, :] = mm(turned[...], dup[...]).astype(bf)

    def grads_down(n):
        cs = slice(n * wide, (n + 1) * wide)
        turned[...] = flip(dyr[:, cs])
        eg[2, cs, :] = mm(turned[...], act[...]).astype(bf)

    work = [lambda n=n: grads(n) for n in range(width // wide)]
    work += [lambda n=n: grads_down(n) for n in range(width // wide)]
    events = []
    for n in (2, 3, 1, 0):
        for k in range(pieces):
            events.append(lambda n=n, k=k: sums.take(nth(n), k))
        if n == 2:
            events.append(lambda: sums.send(nth(0)))
        if n == 1:
            events.append(lambda: each(lambda piece_: z_send(*piece_).start(), z_pieces[:2]))
    done = 0
    for t, event in enumerate(events):
        while done < len(work) and done * len(events) <= t * len(work):
            work[done]()
            done += 1
        event()
    for act_ in work[done:]:
        act_()
    stores[1].start()
    stores[2].start()
    each(lambda piece_: z_send(*piece_).start(), z_pieces[2:])
    sums.finish()
    each(lambda g: g.finish(), rows)

    h = hid[...]
    r2 = lax.rsqrt(jnp.mean(h * h, -1, keepdims=True) + EPS)
    weighted = db[...] * gain_rows[1:2, :]
    inner = jnp.mean(weighted * h, -1, keepdims=True)
    total = dy_own[...].astype(f32) + r2 * weighted - h * (r2 * r2 * r2 * inner)
    dh[...] = total
    dhr[...] = total.astype(bf)
    column = jnp.sum((db[...] * h * r2).T, axis=1, keepdims=True)
    lane = lax.broadcasted_iota(jnp.int32, (width, LANES), 1)
    gm[...] = jnp.where(lane == 1, column, 0.0)
    for n, zz in enumerate(EARLY):
        for k in range(pieces):
            z_send(n, k).wait()
        z_sums[n] = (z_p[zz * 2 + p.x].astype(f32) + z_rx[n].astype(f32)).astype(bf)
    each(lambda store: store.wait(), stores)


def run_experts(b, dy_own, dy_all, g_all, weights, hid, gain_rows, depth, cid):
    f32, bf = jnp.float32, jnp.bfloat16
    shape = jax.ShapeDtypeStruct
    vmem = pl.BlockSpec(memory_space=pltpu.VMEM)
    hbm = pl.BlockSpec(memory_space=pl.ANY)
    V = pltpu.VMEM
    tok, width = b.shape
    units = weights[0].shape[1]
    rows = 2 * depth * tok
    return pl.pallas_call(
        functools.partial(experts_kernel, depth),
        out_shape=(
            shape((tok, width), f32),
            shape((tok, width), bf),
            shape((width, LANES), f32),
            shape((len(EARLY), tok, width), bf),
            shape((2 * depth, tok, width), bf),
            shape((3, width, units), bf),
        ),
        in_specs=[vmem] * 5 + [hbm] * 4,
        out_specs=tuple([vmem] * 4 + [hbm] * 2),
        scratch_shapes=[
            V((2 * depth, tok, width), bf),
            V((width, units), bf),
            V((width, units), bf),
            V((width, units), bf),
            V((2 * depth, tok, width), bf),
            V((3, width, units), bf),
            V((len(EARLY), tok, width), bf),
            V((rows, width), bf),
            V((rows, units), bf),
            V((rows, units), bf),
            V((rows, units), bf),
            V((rows, width), bf),
            V((2 * depth, tok, width), bf),
            V((depth, tok, width), bf),
            V((depth, tok, width), bf),
            V((tok, width), f32),
            V((256, rows), bf),
            pltpu.SemaphoreType.DMA((2 * 5 * depth + 8 * depth + 8 + 4 * len(EARLY),)),
        ],
        compiler_params=pltpu.CompilerParams(
            collective_id=cid, has_side_effects=True, vmem_limit_bytes=58 * 2**20
        ),
        name="experts",
    )(b, dy_own, g_all, hid, gain_rows, dy_all, *weights)


def closing_kernel(
    depth, scale, attn_sq, dhr, gain, begin, lse, cosine, sine,
    z_sums, zp_far, wo_far, ot_far, o_far, q_far, qt_far, kv_far, w_far, at_far, x_far, hid_far, dh_far, gm_far, eg,
    gin, gq, go, gkv, gg, rms, f0_far, f1_far, f2_far, out_far,
    f0, f1, f2, out, zp, wo, ot, o, q_rows, qt, kv, w, at, x_all, hid, dh, gm,
    dhr_all, dot_, dqt, delta, dkv, do_rows, dq, att, acc,
    z_sum, z_rx, z_rz, go_p, go_rc, go_rx, go_rz, kv_sum, kv_rc, kv_rx, kv_rz,
    gq_p, gq_rc, gq_rx, gq_rz, gk_p, gk_sum, gk_rc, gk_rx, gk_rz,
    e_own, e_core, e_low, e_peer, da_out, da_in, t_out, t_in, sq, square, sems,
):
    f32, bf = jnp.float32, jnp.bfloat16
    p = Place(depth)
    p.greet(sibling=True, other=True)
    wires = Wires(sems)
    u, blk = p.u, p.blk
    tok = dhr.shape[0]
    group, q_half = o.shape
    heads = q_half // HEAD_DIM
    kv_half = 2 * HEAD_DIM
    blocks = kv.shape[0]
    rows_blk = gq.shape[0]

    cols = f0.shape[1]
    rows_e = f0.shape[0]
    es, er, el, ps, pr = (wires.take(1)(0) for _ in range(5))

    def e_cols(core):
        return eg.at[:, :, pl.ds(pl.multiple_of(core * cols, LANES), cols)]

    def e_rows(member):
        return pl.ds(pl.multiple_of(member * rows_e, rows_e), rows_e)

    fs = wires.take(4)
    f_stores = [
        pltpu.make_async_copy(v, r, fs(i))
        for i, (v, r) in enumerate(((f0, f0_far), (f1, f1_far), (f2, f2_far), (out, out_far)))
    ]
    e_trade = remote(e_cols(1 - p.c), e_core, es, er, p.sibling)
    e_keep = [pltpu.make_async_copy(e_cols(p.c).at[i], e_own, el) for i in range(3)]
    e_swap = remote(e_low, e_peer, ps, pr, p.other)

    def e_join():
        e_trade.wait_recv()
        theirs, mine = e_rows(1 - u), e_rows(u)
        for i in range(3):
            e_keep[i].wait()
            e_low[i] = (e_own[theirs, :].astype(f32) + e_core[i, theirs, :].astype(f32)).astype(bf)
            (f0, f1, f2)[i][...] = e_own[mine, :].astype(f32) + e_core[i, mine, :].astype(f32)
            if i < 2:
                e_keep[i + 1].start()
        e_swap.start()

    def e_done():
        e_swap.wait_recv()
        for i in range(3):
            (f0, f1, f2)[i][...] += e_peer[i].astype(f32)

    ds, dr = wires.take(1)(0), wires.take(1)(0)
    swap = remote(dhr, dhr_all.at[u], ds, dr, p.other)

    pieces = 2
    z_rows = tok // pieces

    def cut(ref, k):
        return ref.at[pl.ds(k * z_rows, z_rows)]

    zs = Scatter(
        p, wires,
        lambda zz, xx, k: cut(zp.at[zz * 2 + xx], k),
        lambda k: cut(z_sum, k),
        lambda zz, k: cut(z_rx.at[zz], k),
        lambda slot, k: cut(z_rz.at[slot], k),
        pieces, ready=EARLY,
    )
    gos = CoreScatter(p, wires, go_p, go_rc, go, go_rx, go_rz)
    kvs = CoreScatter(p, wires, dkv, kv_rc, kv_sum, kv_rx, kv_rz, down_only=True)
    gqs = CoreScatter(p, wires, gq_p, gq_rc, gq, gq_rx, gq_rz)
    gks = CoreScatter(p, wires, gk_p, gk_rc, gk_sum, gk_rx, gk_rz)
    qs, qr = wires.take(3 + depth), wires.take(3 + depth)
    sq_here = sq.at[p.z, p.x, u, p.c]
    sq_core = remote(sq_here, sq_here, qs(0), qr(0), p.sibling)
    sq_other = remote(sq.at[:, :, u], sq.at[:, :, u], qs(1), qr(1), p.other)
    sq_across = remote(sq.at[p.z, p.x, u], sq.at[p.z, p.x, u], qs(2), qr(2), p.across)

    def sq_along(z, to):
        return remote(sq.at[z, :, u], sq.at[z, :, u], qs(3 + to), qr(3 + z), p.along(to))

    ls = wires.take(13)
    loads = [
        pltpu.make_async_copy(r, v, ls(i))
        for i, (r, v) in enumerate(
            (
                (zp_far, zp), (wo_far, wo), (ot_far, ot), (o_far, o), (q_far, q_rows), (qt_far, qt), (kv_far, kv),
                (w_far, w), (at_far, at), (x_far, x_all), (hid_far, hid), (dh_far, dh), (gm_far, gm),
            )
        )
    ]
    zl = wires.take(len(EARLY))
    z_loads = [pltpu.make_async_copy(z_sums.at[n], z_rx.at[zz], zl(n)) for n, zz in enumerate(EARLY)]
    swap.start()
    each(lambda load: load.start(), z_loads)
    each(lambda load: load.start(), loads)
    e_trade.start()
    e_keep[0].start()
    loads[0].wait()
    ahead = 2
    for t in range(ahead):
        zs.begin(t)

    each(lambda load: load.wait(), z_loads)
    zs.forward()
    dqt[...] = jnp.zeros(dqt.shape, f32)
    dkv[...] = jnp.zeros(dkv.shape, bf)
    dhr_all[u] = dhr[...]
    e_join()
    zs.land(0)
    zs.begin(ahead)
    each(lambda load: load.wait(), loads[1:])
    swap.wait_recv()

    for m in range(2):
        part = mm(dhr_all[m], wo[...]).astype(bf)
        for h in range(heads):
            do_rows[h * group + m * tok : h * group + (m + 1) * tok, :] = part[:, h * HEAD_DIM : (h + 1) * HEAD_DIM]
    for h in range(heads):
        hs = slice(h * group, (h + 1) * group)
        part = do_rows[hs, :]
        turned = part.astype(f32).T
        dot_[:, hs] = turned.astype(bf)
        delta[0:1, hs] = jnp.sum(turned * ot[:, hs], axis=0, keepdims=True)

    def spread_rows(payload, turned, right, cols=None):
        some = 4

        def rows(i, carry):
            at_rows = pl.ds(pl.multiple_of(i * some * rows_blk, some * rows_blk), some * rows_blk)
            part = mm(turned[at_rows, :], right).astype(bf)
            for n in range(some):
                piece = part[n * rows_blk : (n + 1) * rows_blk, :]
                if cols is None:
                    payload[i * 2 + n // 2, n % 2] = piece
                else:
                    payload[i * 2 + n // 2, n % 2, :, :cols] = piece
            return carry

        lax.fori_loop(0, blocks // some, rows, 0)

    for m in range(2):
        att[:, m * tok : (m + 1) * tok] = flip(dhr_all[m])

    spread_rows(go_p, att, o[...])
    gos.trade()

    background = {}

    def at_tile(j, act):
        background.setdefault(j, []).append(act)

    def z_step(t):
        zs.land(t)
        zs.begin(t + ahead)

    for t in range(1, len(zs.items)):
        at_tile((0, 0, 2, 4, 6, 9, 12, 15)[t], lambda t=t: z_step(t))
    for t in range(depth):
        at_tile((5, 8, 11, 14)[t], lambda t=t: gos.join(t))
    for t in range(3):
        at_tile((11, 14, 15)[t], lambda t=t: gos.land(t))
    for t in range(depth - 1):
        last = 4 * t + 3
        at_tile(last, lambda t=t: kvs.trade(t))
        at_tile(last + 1, lambda t=t: kvs.join(t))
        if t < depth - 2:
            at_tile(last + 6, lambda t=t: kvs.land(t))

    def tile(j, carry):
        def work():
            k = kv[j, :, :HEAD_DIM]
            v = kv[j, :, HEAD_DIM:]
            kt = flip(k)
            bias = hidden_bias(j * group, blk * group, begin[0:1, :], group)
            at_ = [slice(h * group, (h + 1) * group) for h in range(heads)]
            sc = [mm(k, qt[:, hs]) * (scale * LOG2E) + bias for hs in at_]
            dp = [mm(v, dot_[:, hs]) for hs in at_]
            e = [jnp.exp2(s_ - lse[0:1, hs]) for s_, hs in zip(sc, at_)]
            g = [(e_ * (d_ - delta[0:1, hs])).astype(bf) for e_, d_, hs in zip(e, dp, at_)]
            wide_g = jnp.concatenate(g, 1)
            dk = mm(wide_g, q_rows[...])
            dv = mm(jnp.concatenate([e_.astype(bf) for e_ in e], 1), do_rows[...])
            dqt[...] += mm(kt, wide_g)
            dkv[j // 2, j % 2, :, :HEAD_DIM] = (dk * scale).astype(bf)
            dkv[j // 2, j % 2, :, HEAD_DIM:] = dv.astype(bf)

        pl.when(j <= blk)(work)
        for when, acts in background.items():
            pl.when(j == when)(lambda acts=acts: each(lambda act: act(), acts))
        return carry

    lax.fori_loop(0, blocks, tile, 0)

    kvs.trade(depth - 1)

    def back_turn(values):
        return values * cosine[...] - pltpu.roll(values, HEAD_DIM // 2, 1) * sine[...]

    for h in range(heads):
        hs = slice(h * group, (h + 1) * group)
        cs = slice(h * HEAD_DIM, (h + 1) * HEAD_DIM)
        dq[:, cs] = back_turn((dqt[:, hs] * scale).T.astype(bf).astype(f32)).astype(bf)
    kvs.join(depth - 1)

    zs.finish()
    result = hid[...] + z_sum[...]
    out[...] = result.astype(bf)
    spread = lax.broadcasted_iota(jnp.int32, (8, LANES), 1)
    z_sq = jnp.sum(z_sum[...] * z_sum[...])
    r_sq = jnp.sum(result * result)
    sq_here[...] = jnp.where(
        spread == 0, attn_sq[...], jnp.where(spread == 1, z_sq, jnp.where(spread == 2, r_sq, 0.0))
    )
    sq_core.start()

    spread_rows(gq_p, at, dq[...])
    gqs.trade()
    sq_core.wait_recv()
    sq_across.start()
    kvs.land(depth - 2)
    gqs.join(0)
    gqs.join(1)
    for m in range(2):
        for cb in range(0, D, 512):
            acc[m * tok : (m + 1) * tok, cb : cb + 512] = contract(
                dq[m * tok : (m + 1) * tok, :], w[cb : cb + 512, :q_half], 1, 1
            )
    kvs.land(depth - 1)
    kvs.release()
    kvs.finish()
    sq_across.wait_recv()
    for d in range(1, depth):
        pl.when(p.z >= d)(lambda d=d: sq_along(p.z, p.z - d).start())
        pl.when(p.z + d < depth)(lambda d=d: sq_along(p.z, p.z + d).start())
    kv_low = kv_sum[...].astype(bf).astype(f32)
    kv_pre = jnp.concatenate([back_turn(kv_low[:, :HEAD_DIM]).astype(bf), kv_low[:, HEAD_DIM:].astype(bf)], 1)

    da_s, da_r = wires.take(3), wires.take(3)
    wide = D // 3
    da_swaps = []
    for i in range(3):
        cb = i * wide
        part = contract(kv_pre, w[cb : cb + wide, q_half : q_half + kv_half], 1, 1)
        acc[:, cb : cb + wide] += part
        theirs = pl.ds(pl.multiple_of((1 - u) * tok, tok), tok)
        da_out[i] = acc[theirs, cb : cb + wide].astype(bf)
        da_swaps.append(remote(da_out.at[i], da_in.at[i], da_s(i), da_r(i), p.other))
        da_swaps[i].start()

    column = jnp.zeros((D, 1), f32)
    for m in range(2):
        xf = x_all[m].astype(f32)
        r1 = lax.rsqrt(jnp.mean(xf * xf, -1, keepdims=True) + EPS)
        terms = acc[m * tok : (m + 1) * tok, :] * xf * r1
        column = column + jnp.sum(terms.T, axis=1, keepdims=True)
    lane = lax.broadcasted_iota(jnp.int32, (D, LANES), 1)
    gain_cols = (jnp.where(lane == 0, column, 0.0) + gm[...]).astype(bf)
    for i in range(blocks):
        gk_p[i // 2, i % 2, :, kv_half:] = gain_cols[i * rows_blk : (i + 1) * rows_blk, :]

    spread_rows(gk_p, at, kv_pre, kv_half)
    gqs.land(0)
    gqs.land(1)
    gks.trade()
    for t in range(depth):
        gks.join(t)
    for t in range(2, depth):
        gqs.join(t)
    gqs.release()

    for t in range(depth):
        gks.land(t)
    gos.land(3)
    for z in range(depth):
        pl.when(p.z != z)(lambda z=z: sq_along(z, z).wait_recv())
    sq_other.start()
    e_done()
    each(lambda store: store.start(), f_stores)

    mine = pl.ds(pl.multiple_of(u * tok, tok), tok)
    for i in range(3):
        da_swaps[i].wait_recv()
        acc[mine, i * wide : (i + 1) * wide] += da_in[i].astype(f32)
    da = acc[mine, :]
    xf = x_all[u].astype(f32)
    r1 = lax.rsqrt(jnp.mean(xf * xf, -1, keepdims=True) + EPS)
    weighted = da * gain[0:1, :]
    inner = jnp.mean(weighted * xf, -1, keepdims=True)
    gin[...] = dh[...] + r1 * weighted - xf * (r1 * r1 * r1 * inner)
    for t in range(2, depth):
        gqs.land(t)
    gks.release()
    gks.finish()
    rows_dev = gkv.shape[0]
    theirs = pl.ds(pl.multiple_of((1 - u) * rows_dev, rows_dev), rows_dev)
    own = pl.ds(pl.multiple_of(u * rows_dev, rows_dev), rows_dev)
    t_out[...] = gk_sum[theirs, :]
    ts, tr = wires.take(1)(0), wires.take(1)(0)
    t_swap = remote(t_out, t_in, ts, tr, p.other)
    t_swap.start()
    gos.release()
    gos.finish()
    gqs.finish()
    t_swap.wait_recv()
    for part in range(2):
        here = slice(part * HEAD_DIM, (part + 1) * HEAD_DIM)
        base = part * kv_half
        gkv[:, pl.ds(pl.multiple_of(base + u * HEAD_DIM, LANES), HEAD_DIM)] = gk_sum[own, here]
        gkv[:, pl.ds(pl.multiple_of(base + (1 - u) * HEAD_DIM, LANES), HEAD_DIM)] = t_in[:, here]
    square[...] = jnp.zeros(square.shape, f32)
    square[:rows_dev, :] = gk_sum[own, kv_half:] + t_in[:, kv_half:]
    gg[...] = square[...].T[:8, :]
    sq_core.wait_send()
    sq_other.wait()
    sq_across.wait_send()
    for z in range(depth):
        pl.when(p.z != z)(lambda z=z: sq_along(p.z, z).wait_send())
    squares = jnp.zeros((8, LANES), f32)
    for z in range(depth):
        for n in range(8):
            squares = squares + sq[z, n // 4, n // 2 % 2, n % 2]
    rms[...] = jnp.sqrt(squares / (8 * depth * tok * D))
    each(lambda store: store.wait(), f_stores)
    t_swap.wait_send()
    swap.wait_send()
    e_trade.wait_send()
    e_swap.wait_send()
    for i in range(3):
        da_swaps[i].wait_send()


def closing(attn_sq, dhr, gain, begin, lse, cosine, sine, z_sums, large, eg, depth, scale, cid):
    f32, bf = jnp.float32, jnp.bfloat16
    tok, width = dhr.shape
    group, q_half = large[3].shape
    blocks = large[6].shape[0]
    kv_block = large[6].shape[1:]
    rows_blk = width // blocks
    rows_e, cols = eg.shape[1] // 2, eg.shape[2] // 2
    kv_half = 2 * HEAD_DIM
    shape = jax.ShapeDtypeStruct
    vmem = pl.BlockSpec(memory_space=pltpu.VMEM)
    hbm = pl.BlockSpec(memory_space=pl.ANY)
    V = pltpu.VMEM

    def buffers(block):
        return [
            V((blocks // 2,) + block, bf),
            V((depth,) + block, bf),
            V((depth,) + block, bf),
        ]

    grad = shape((rows_e, cols), f32)
    rows = q_half // HEAD_DIM * group
    return pl.pallas_call(
        functools.partial(closing_kernel, depth, scale),
        out_shape=(
            shape((tok, width), f32),
            shape((rows_blk, q_half), f32),
            shape((rows_blk, q_half), f32),
            shape((rows_blk // 2, 2 * kv_half), f32),
            shape((8, LANES), f32),
            shape((8, LANES), f32),
            grad,
            grad,
            grad,
            shape((tok, width), bf),
        ),
        in_specs=[vmem] * 7 + [hbm] * 15,
        out_specs=tuple([vmem] * 6 + [hbm] * 4),
        scratch_shapes=[V((rows_e, cols), f32)] * 3
        + [V((tok, width), bf)]
        + [V(array.shape, array.dtype) for array in large]
        + [
            V((2, tok, width), bf),
            V((HEAD_DIM, rows), bf),
            V((HEAD_DIM, rows), f32),
            V((8, rows), f32),
            V((blocks // 2, 2) + kv_block, bf),
            V((rows, HEAD_DIM), bf),
            V((group, q_half), bf),
            V((width, group), bf),
            V((group, width), f32),
            V((tok, width), f32),
            V((depth, tok, width), bf),
            V((depth, tok, width), bf),
            V((blocks // 2, 2, rows_blk, q_half), bf),
        ]
        + buffers((rows_blk, q_half))
        + [V((group, kv_half), f32)]
        + buffers((group, kv_half))
        + [V((blocks // 2, 2, rows_blk, q_half), bf)]
        + buffers((rows_blk, q_half))
        + [V((blocks // 2, 2, rows_blk, kv_half + LANES), bf), V((rows_blk, kv_half + LANES), f32)]
        + buffers((rows_blk, kv_half + LANES))
        + [
            V((2 * rows_e, cols), bf),
            V((3, 2 * rows_e, cols), bf),
            V((3, rows_e, cols), bf),
            V((3, rows_e, cols), bf),
            V((3, tok, width // 3), bf),
            V((3, tok, width // 3), bf),
            V((rows_blk // 2, kv_half + LANES), f32),
            V((rows_blk // 2, kv_half + LANES), f32),
            V((depth, 2, 2, 2, 8, LANES), f32),
            V((LANES, LANES), f32),
            pltpu.SemaphoreType.DMA((320,)),
        ],
        compiler_params=pltpu.CompilerParams(
            collective_id=cid, has_side_effects=True, vmem_limit_bytes=60 * 2**20
        ),
        name="closing",
    )(attn_sq, dhr, gain, begin, lse, cosine, sine, z_sums, *large, eg)


def deliver_kernel(count, rows, gains, rms, *refs):
    ins, outs = refs[:count], refs[count : 2 * count + 3]
    held, sems = refs[2 * count + 3 : 3 * count + 3], refs[3 * count + 6]
    small = refs[3 * count + 3 : 3 * count + 6]
    loads = [pltpu.make_async_copy(ins[i], held[i], sems.at[i]) for i in range(count)]
    stores = [pltpu.make_async_copy(held[i], outs[i + 3], sems.at[count + i]) for i in range(count)]
    notes = [pltpu.make_async_copy(small[i], outs[i], sems.at[2 * count + i]) for i in range(3)]
    each(lambda load: load.start(), loads)
    small[0][...] = gains[0:1, :rows]
    small[1][...] = gains[1:2, :rows]
    small[2][...] = rms[0:1, :3]
    each(lambda note: note.start(), notes)
    for load, store in zip(loads, stores):
        load.wait()
        store.start()
    each(lambda store: store.wait(), stores)
    each(lambda note: note.wait(), notes)


def deliver(gains, rms, arrays, rows):
    count = len(arrays)
    hbm = pl.BlockSpec(memory_space=pl.ANY)
    vmem = pl.BlockSpec(memory_space=pltpu.VMEM)
    small = [jax.ShapeDtypeStruct((1, n), jnp.float32) for n in (rows, rows, 3)]
    return pl.pallas_call(
        functools.partial(deliver_kernel, count, rows),
        out_shape=tuple(small + [jax.ShapeDtypeStruct(a.shape, a.dtype) for a in arrays]),
        in_specs=[vmem] * 2 + [hbm] * count,
        out_specs=tuple([hbm] * (count + 3)),
        scratch_shapes=[pltpu.VMEM(a.shape, a.dtype) for a in arrays]
        + [pltpu.VMEM(a.shape, a.dtype) for a in small]
        + [pltpu.SemaphoreType.DMA((2 * count + 3,))],
        compiler_params=pltpu.CompilerParams(vmem_limit_bytes=60 * 2**20),
        name="deliver",
    )(gains, rms, *arrays)


def planned(
    layer_input,
    grad_output,
    gain_attn,
    gain_moe,
    w_query,
    w_keyval,
    w_out,
    w_gate,
    w_up,
    w_down,
    gate_weights,
    expert_ids,
    doc_starts,
):
    depth = lax.axis_size("blk") // 4
    scale = 1.0 / math.sqrt(HEAD_DIM)
    (
        normed_m, hidden, attn_sq, normed_t, query_rows, query_t, mixed, mixed_t, lse, gain_rows, g_all, inputs,
        begin_rows, cosine, sine, kv_all, w_all, out_w, dy_all, gate_w, up_w, down_w,
    ) = front(
        doc_starts, layer_input, grad_output, gain_attn, gain_moe, w_query, w_keyval, w_out, expert_ids.T, gate_weights.T,
        (w_gate, w_up, w_down), depth, scale, 1,
    )
    grad_hidden, grad_hidden_low, gain_terms, z_sums, z_part, expert_grads = run_experts(
        normed_m, grad_output, dy_all, g_all, (gate_w, up_w, down_w), hidden, gain_rows, depth, 2
    )
    large = (
        z_part, out_w, mixed_t, mixed, query_rows, query_t, kv_all, w_all, normed_t, inputs, hidden, grad_hidden, gain_terms
    )
    results = closing(
        attn_sq, grad_hidden_low, gain_rows, begin_rows, lse, cosine, sine, z_sums, large, expert_grads, depth, scale, 3
    )
    (
        gain_a, gain_m, rms, layer_output, grad_input, part_query, part_out, part_keyval, grad_gate, grad_up, grad_down
    ) = deliver(results[4], results[5], results[9:] + results[:4] + results[6:9], gain_attn.shape[0])
    return (
        layer_output,
        grad_input,
        gain_a.reshape(-1),
        gain_m.reshape(-1),
        part_query,
        part_keyval,
        part_out,
        grad_gate,
        grad_up,
        grad_down,
        rms.reshape(-1),
    )


def solution(mesh):
    in_specs = (
        P(("blk", "ulysses"), None),
        P(("blk", "ulysses"), None),
        P(("blk", "ulysses")),
        P(("blk", "ulysses")),
        P(("blk", "ulysses"), None),
        P(("blk", "ulysses"), None),
        P(("blk", "ulysses"), None),
        P("ulysses", "blk"),
        P("ulysses", "blk"),
        P("ulysses", "blk"),
        P(("blk", "ulysses"), None),
        P(("blk", "ulysses"), None),
        P(),
    )
    out_specs = (
        P(("blk", "ulysses"), None),
        P(("blk", "ulysses"), None),
        P(("blk", "ulysses")),
        P(("blk", "ulysses")),
        P("blk", "ulysses"),
        P(("blk", "ulysses"), None),
        P("blk", "ulysses"),
        P("ulysses", "blk"),
        P("ulysses", "blk"),
        P("ulysses", "blk"),
        P(),
    )
    blocks, members = mesh.shape["blk"], mesh.shape["ulysses"]
    body = planned if blocks == 16 and members == KV_HEADS else local
    return jax.shard_map(body, mesh=mesh, in_specs=in_specs, out_specs=out_specs, check_vma=False)
```
